32 devices in a mesh: dp: 8 (over z, core), chan: 4 (over y, x).
Axes of the slice: x: 2, y: 2, z: 4, core: 2. Of those that a mesh axis runs over, the one named last changes fastest.
Arguments:
- volume: bfloat16 [8, 512, 1024], P('dp', 'chan'), may hold values from -16 to 16
- w_first: bfloat16 [27, 512, 512], P(None, 'chan'), may hold values from -0.0546875 to 0.0546875
- gain: float32 [512], replicated, may hold values from 0.1 to 1.9
- w_second: bfloat16 [27, 512, 512], P(None, None, 'chan'), may hold values from -0.0546875 to 0.0546875
- cotangent: bfloat16 [8, 512, 1024], P('dp', 'chan'), may hold values from -8 to 8
Outputs:
- output: bfloat16 [8, 512, 1024], P('dp', 'chan')
- grad_volume: bfloat16 [8, 512, 1024], P('dp', 'chan')
- grad_w_first: float32 [27, 512, 512], P(None, 'chan')
- grad_gain: float32 [512], P('chan')
- grad_w_second: float32 [27, 512, 512], P(None, None, 'chan')
The draws below stay inside these ranges and needn't reach their ends.
All inputs are finite; a program needn't handle non-finite values.
Results may differ from the reference program's by a relative error of at most 0.005.
Values may be sent and summed in bfloat16 or wider, within the bound.
No kernel may reach another device: no remote copies, remote signals or barrier semaphores. Data moves between devices by JAX's collectives and lax.ppermute only.
A program may use at most 128 MiB of HBM per device.

```python
import math
import jax
import jax.numpy as jnp
from jax import lax

CHANNELS = 512
DEPTH = 4
HEIGHT = 16
WIDTH = 16
VOXELS = 1024
SUBVOLUMES = 8


def draw_volume(key, part):
    subkeys = jax.random.split(key, 3)
    shape_all = (SUBVOLUMES, CHANNELS, VOXELS)
    chan_scale = jnp.exp(jax.random.uniform(subkeys[0], (1, CHANNELS, 1), jnp.float32, 0.0, 1.0) * (0.5 * math.log(10.0)))
    cell_scale = jnp.exp(jax.random.uniform(subkeys[1], (SUBVOLUMES, 1, VOXELS), jnp.float32, 0.0, 1.0) * (0.5 * math.log(10.0)))
    shrink = 1.0 / math.sqrt(10.0)
    entries = jnp.clip(jax.random.normal(subkeys[2], shape_all, jnp.float32), -5.0, 5.0)
    field = entries * chan_scale * cell_scale * shrink
    return field.astype(jnp.bfloat16)


def draw_cotangent(key, part):
    subkeys = jax.random.split(key, 1)
    shape_all = (SUBVOLUMES, CHANNELS, VOXELS)
    growth = 1.0 + 2.0 * jnp.arange(SUBVOLUMES, dtype=jnp.float32)[:, None, None] / max(SUBVOLUMES - 1, 1)
    entries = jnp.clip(jax.random.normal(subkeys[0], shape_all, jnp.float32), -5.0, 5.0)
    field = entries * growth * 0.5
    return field.astype(jnp.bfloat16)


def block_scale(stream_key, dims, shards, smallest, largest):
    level, own = 1.0, jax.random.fold_in(stream_key, 6)
    for axis_at, blocks in shards:
        heights = jnp.exp(jax.random.uniform(jax.random.fold_in(own, axis_at), (blocks,), jnp.float32, smallest / len(shards), largest / len(shards)))
        level = level * jnp.repeat(heights, dims[axis_at] // blocks).reshape([-1 if axis == axis_at else 1 for axis in range(len(dims))])
    return level


def bell_draw(own_key, extent, scale, most, cuts=(), kind=jnp.bfloat16):
    values = jax.random.normal(own_key, extent, jnp.float32) * scale
    if len(cuts) > 0:
        values = block_scale(own_key, extent, cuts, -0.22, 0.18) * values
    return jnp.clip(values, min=-most, max=most).astype(kind)


def setup_inputs(seed: int = 0) -> dict:
    keys = jax.random.split(jax.random.key(seed), 6)
    return {
        "volume": draw_volume(jax.random.fold_in(keys[5], 71), 0),
        "w_first": bell_draw(keys[1], (27, CHANNELS, CHANNELS), (27 * CHANNELS) ** -0.5, 0.0546875, ((1, 4),)),
        "gain": jnp.clip(1.0 + 0.18 * jax.random.normal(keys[2], (CHANNELS,), jnp.float32), 0.1, 1.9),
        "w_second": bell_draw(keys[3], (27, CHANNELS, CHANNELS), (27 * CHANNELS) ** -0.5, 0.0546875, ((2, 4),)),
        "cotangent": draw_cotangent(jax.random.fold_in(keys[5], 71), 0),
    }


TAP_OFFSETS = [(plane_off, row_off, col_off) for plane_off in (-1, 0, 1) for row_off in (-1, 0, 1) for col_off in (-1, 0, 1)]
NORM_EPS = 1e-05

def shifted(field, plane_off, row_off, col_off):
    shaped = field.reshape(field.shape[0], field.shape[1], DEPTH, HEIGHT, WIDTH)
    padded = jnp.pad(shaped, ((0, 0), (0, 0), (1, 1), (1, 1), (1, 1)))
    window = padded[:, :, 1 + plane_off:1 + plane_off + DEPTH, 1 + row_off:1 + row_off + HEIGHT, 1 + col_off:1 + col_off + WIDTH]
    return window.reshape(field.shape)

def forward_conv(field, weights):
    result = jnp.zeros((field.shape[0], weights.shape[2], field.shape[2]), jnp.float32)
    for index, offsets in enumerate(TAP_OFFSETS):
        moved = shifted(field, offsets[0], offsets[1], offsets[2]).astype(jnp.float32)
        result = result + jnp.einsum('bcp,cf->bfp', moved, weights[index].astype(jnp.float32))
    return result

def backward_conv(field, weights):
    result = jnp.zeros((field.shape[0], weights.shape[1], field.shape[2]), jnp.float32)
    for index, offsets in enumerate(TAP_OFFSETS):
        moved = shifted(field, -offsets[0], -offsets[1], -offsets[2]).astype(jnp.float32)
        result = result + jnp.einsum('bfp,cf->bcp', moved, weights[index].astype(jnp.float32))
    return result

def weight_grad(field, other):
    other_wide = other.astype(jnp.float32)
    layers = []
    for offsets in TAP_OFFSETS:
        moved = shifted(field, offsets[0], offsets[1], offsets[2]).astype(jnp.float32)
        layers.append(jnp.einsum('bcp,bfp->cf', moved, other_wide))
    return jnp.stack(layers, axis=0)

def reference(volume, w_first, gain, w_second, cotangent):
    pre = forward_conv(volume, w_first)
    center = pre - lax.optimization_barrier(jnp.mean(pre, axis=2, keepdims=True))
    inverse = lax.rsqrt(lax.optimization_barrier(jnp.mean(center * center, axis=2, keepdims=True)) + NORM_EPS)
    normed = center * inverse
    gain_wide = gain.astype(jnp.float32)[None, :, None]
    scaled = gain_wide * normed
    act = jax.nn.silu(scaled).astype(jnp.bfloat16)
    output = forward_conv(act, w_second).astype(jnp.bfloat16)
    factor = 1.0 / math.sqrt(SUBVOLUMES * VOXELS)
    dact = backward_conv(cotangent, w_second)
    grad_w_second = weight_grad(act, cotangent) * factor
    sigma = jax.nn.sigmoid(scaled)
    dscaled = dact * sigma * (1.0 + scaled * (1.0 - sigma))
    grad_gain = lax.optimization_barrier(jnp.sum(dscaled * normed, axis=(0, 2))) * factor
    dnormed = dscaled * gain_wide
    dpre = ((dnormed - lax.optimization_barrier(jnp.mean(dnormed, axis=2, keepdims=True)) - normed * lax.optimization_barrier(jnp.mean(dnormed * normed, axis=2, keepdims=True))) * inverse).astype(jnp.bfloat16)
    grad_volume = backward_conv(dpre, w_first).astype(jnp.bfloat16)
    grad_w_first = weight_grad(volume, dpre) * factor
    return (output, grad_volume, grad_w_first, grad_gain, grad_w_second)
```

```python
import functools
import math

import jax
import jax.numpy as jnp
from jax import lax
from jax.experimental import pallas as pl
from jax.experimental.pallas import tpu as pltpu
from jax.sharding import PartitionSpec as P

DEPTH, HEIGHT, WIDTH = 4, 16, 16
PLANE = HEIGHT * WIDTH
CELLS = DEPTH * PLANE
TAPS = [(a, b, c) for a in (-1, 0, 1) for b in (-1, 0, 1) for c in (-1, 0, 1)]
NORM_EPS = 1e-05
LIMIT = 56 * 1024 * 1024
F32, BF16 = jnp.float32, jnp.bfloat16
NT = (((1,), (1,)), ((), ()))


def params():
    return pltpu.CompilerParams(
        dimension_semantics=("arbitrary",), vmem_limit_bytes=LIMIT
    )


def whole(shape):
    return pl.BlockSpec(shape, lambda *_: (0,) * len(shape))


def smem():
    return pl.BlockSpec(memory_space=pltpu.SMEM)


def fill_padded(padded, rows_first, sign):
    padded[...] = jnp.zeros_like(padded)
    cells = rows_first.astype(F32).T
    width_at = lax.broadcasted_iota(jnp.int32, cells.shape, 0) % WIDTH
    for c in (-1, 0, 1):
        off = sign * c
        moved = cells if off == 0 else pltpu.roll(cells, (-off) % CELLS, 0)
        inside = (width_at + off >= 0) & (width_at + off < WIDTH)
        moved = jnp.where(inside, moved, 0.0).astype(BF16)
        padded[1 + c, 1 : 1 + DEPTH, 1 : 1 + HEIGHT] = moved.reshape(
            DEPTH, HEIGHT, WIDTH, cells.shape[1]
        )


def tap_cells(padded, plane, tap, sign):
    a, b, c = tap
    low = 1 + sign * b
    rows = padded[1 + c, plane + (1 + sign * a), low : low + HEIGHT]
    return rows.reshape(PLANE, rows.shape[-1])


def pre_kernel(n, idx, vol, w, *refs):
    outs, padded, shares = refs[:n], refs[n], refs[n + 1]
    rows = vol.shape[0]
    plane = pl.program_id(0)

    @pl.when(plane == 0)
    def _():
        fill_padded(padded, vol[...], 1)

    lhs = jnp.concatenate([tap_cells(padded, plane, tap, 1) for tap in TAPS], axis=1)
    sums = jnp.dot(lhs, w[...], preferred_element_type=F32).astype(BF16)
    for j in range(n):
        shares[j] = sums[:, j * rows : (j + 1) * rows]
    for m in range(n):
        outs[m][...] = shares[idx[0] ^ m]


def dact_kernel(n, idx, cot, w, *refs):
    outs, padded, shares, wide = refs[:n], refs[n], refs[n + 1], refs[n + 2]
    rows = cot.shape[0]
    plane = pl.program_id(0)

    @pl.when(plane == 0)
    def _():
        fill_padded(padded, cot[...], -1)
        for t in range(27):
            wide[:, t * rows : (t + 1) * rows] = w[t]

    lhs = jnp.concatenate([tap_cells(padded, plane, tap, -1) for tap in TAPS], axis=1)
    sums = lax.dot_general(lhs, wide[...], NT, preferred_element_type=F32).astype(BF16)
    for j in range(n):
        shares[j] = sums[:, j * rows : (j + 1) * rows]
    for m in range(n):
        outs[m][...] = shares[idx[0] ^ m]


def spread_shares(kernel, name, idx, n, field, w, extra):
    rows = field.shape[0]
    return pl.pallas_call(
        functools.partial(kernel, n),
        grid=(DEPTH,),
        in_specs=[smem(), whole(field.shape), whole(w.shape)],
        out_specs=[pl.BlockSpec((PLANE, rows), lambda d: (d, 0))] * n,
        out_shape=[jax.ShapeDtypeStruct((CELLS, rows), BF16)] * n,
        scratch_shapes=[
            pltpu.VMEM((3, DEPTH + 2, HEIGHT + 2, WIDTH, rows), BF16),
            pltpu.VMEM((n, PLANE, rows), BF16),
        ]
        + extra,
        compiler_params=params(),
        cost_estimate=pl.CostEstimate(
            flops=2 * 27 * rows * rows * n * CELLS, bytes_accessed=2 * w.size, transcendentals=0
        ),
        name=name,
    )(idx, field, w)


def norm_kernel(n, gain, *refs):
    shares, act, normed_out, inverse_out = refs[:n], refs[n], refs[n + 1], refs[n + 2]
    pre = shares[0][...].astype(F32)
    for m in range(1, n):
        pre = pre + shares[m][...].astype(F32)
    center = pre - jnp.mean(pre, axis=0, keepdims=True)
    inverse = lax.rsqrt(jnp.mean(center * center, axis=0, keepdims=True) + NORM_EPS)
    normed = center * inverse
    scaled = gain[...] * normed
    act[...] = (scaled * jax.nn.sigmoid(scaled)).astype(BF16)
    normed_out[...] = normed
    inverse_out[...] = inverse


def norm_back_kernel(n, gain, normed_in, inverse, *refs):
    shares, dpre, gain_part = refs[:n], refs[n], refs[n + 1]
    dact = shares[0][...].astype(F32)
    for m in range(1, n):
        dact = dact + shares[m][...].astype(F32)
    normed = normed_in[...]
    scaled = gain[...] * normed
    sigma = jax.nn.sigmoid(scaled)
    dscaled = dact * sigma * (1.0 + scaled * (1.0 - sigma))
    product = dscaled * normed
    gain_part[...] = jnp.sum(product, axis=0, keepdims=True)
    dnormed = gain[...] * dscaled
    mean_first = jnp.mean(dnormed, axis=0, keepdims=True)
    mean_second = jnp.mean(dnormed * normed, axis=0, keepdims=True)
    dpre[...] = ((dnormed - mean_first - normed * mean_second) * inverse[...]).astype(BF16)


def conv_back_add(sums, products, plane, taps, rows, sign):
    for at, tap in enumerate(taps):
        a, b, c = tap
        a, b = sign * a, sign * b
        part = products[:, at * rows : (at + 1) * rows].reshape(HEIGHT, WIDTH, rows)
        low, high = max(0, b), HEIGHT + min(0, b)
        sums[1 + c, plane + (1 - a), low - b : high - b] += part[low:high]


def conv_finish(sums, out, sign):
    rows = out.shape[0]
    total = None
    for c in (-1, 0, 1):
        off = sign * c
        part = sums[1 + c, 1 : 1 + DEPTH].reshape(CELLS, rows)
        if off != 0:
            width_at = lax.broadcasted_iota(jnp.int32, part.shape, 0) % WIDTH
            inside = (width_at + off >= 0) & (width_at + off < WIDTH)
            part = jnp.where(inside, pltpu.roll(part, (-off) % CELLS, 0), 0.0)
        total = part if total is None else total + part
    out[...] = total.T.astype(BF16)


def conv_kernel(n, sign, transposed, idx, w, *refs):
    blocks, out, ordered, sums = refs[:n], refs[n], refs[n + 1], refs[n + 2]
    rows = out.shape[0]
    plane = pl.program_id(0)

    @pl.when(plane == 0)
    def _():
        sums[...] = jnp.zeros_like(sums)
        for m in range(n):
            ordered[idx[0] ^ m] = blocks[m][...]

    begin = pl.multiple_of(plane * PLANE, PLANE)
    lhs = jnp.concatenate([ordered[j, pl.ds(begin, PLANE)] for j in range(n)], axis=1)
    for t in range(0, 27, 2):
        taps = TAPS[t : t + 2]
        if transposed:
            rhs = w[t * rows : (t + len(taps)) * rows]
            products = lax.dot_general(lhs, rhs, NT, preferred_element_type=F32)
        else:
            rhs = jnp.concatenate([w[t + k] for k in range(len(taps))], axis=1)
            products = jnp.dot(lhs, rhs, preferred_element_type=F32)
        conv_back_add(sums, products, plane, taps, rows, sign)

    @pl.when(plane == DEPTH - 1)
    def _():
        conv_finish(sums, out, sign)


def conv_full(name, sign, transposed, idx, w, blocks):
    n, rows = len(blocks), blocks[0].shape[1]
    return pl.pallas_call(
        functools.partial(conv_kernel, n, sign, transposed),
        grid=(DEPTH,),
        in_specs=[smem(), whole(w.shape)] + [whole(blocks[0].shape)] * n,
        out_specs=whole((rows, CELLS)),
        out_shape=jax.ShapeDtypeStruct((rows, CELLS), BF16),
        scratch_shapes=[
            pltpu.VMEM((n, CELLS, rows), BF16),
            pltpu.VMEM((3, DEPTH + 2, HEIGHT, WIDTH, rows), F32),
        ],
        compiler_params=params(),
        cost_estimate=pl.CostEstimate(
            flops=2 * 27 * rows * rows * n * CELLS, bytes_accessed=2 * w.size, transcendentals=0
        ),
        name=name,
    )(idx, w, *blocks)


def grad_first_kernel(n, idx, vol, *refs):
    blocks, out, ordered, moved = refs[:n], refs[n], refs[n + 1], refs[n + 2]
    rows = vol.shape[0]
    step = pl.program_id(0)

    @pl.when(step == 0)
    def _():
        for m in range(n):
            ordered[idx[0] ^ m] = blocks[m][...]
        moved[...] = jnp.zeros_like(moved)
        cells = vol[...].astype(F32)
        at = lax.broadcasted_iota(jnp.int32, cells.shape, 1)
        height_at, width_at = at // WIDTH % HEIGHT, at % WIDTH
        for k in range(9):
            b, c = k // 3 - 1, k % 3 - 1
            off = b * WIDTH + c
            part = cells if off == 0 else pltpu.roll(cells, (-off) % CELLS, 1)
            inside = (height_at + b >= 0) & (height_at + b < HEIGHT)
            inside = inside & (width_at + c >= 0) & (width_at + c < WIDTH)
            part = jnp.where(inside, part, 0.0).astype(BF16)
            moved[k * rows : (k + 1) * rows, PLANE : PLANE + CELLS] = part

    lhs = moved[:, pl.ds(pl.multiple_of(step * PLANE, PLANE), CELLS)]
    rhs = jnp.concatenate([ordered[j] for j in range(n)], axis=1)
    grads = jnp.dot(lhs, rhs, preferred_element_type=F32).astype(BF16)
    out[...] = grads.reshape(9, rows, n * rows)


def grad_first(idx, vol, blocks):
    n, rows = len(blocks), vol.shape[0]
    return pl.pallas_call(
        functools.partial(grad_first_kernel, n),
        grid=(3,),
        in_specs=[smem(), whole(vol.shape)] + [whole(blocks[0].shape)] * n,
        out_specs=pl.BlockSpec((9, rows, n * rows), lambda a: (a, 0, 0)),
        out_shape=jax.ShapeDtypeStruct((27, rows, n * rows), BF16),
        scratch_shapes=[
            pltpu.VMEM((n, CELLS, rows), BF16),
            pltpu.VMEM((9 * rows, CELLS + 2 * PLANE), BF16),
        ],
        compiler_params=params(),
        cost_estimate=pl.CostEstimate(
            flops=2 * 27 * rows * rows * n * CELLS,
            bytes_accessed=2 * 27 * rows * rows * n,
            transcendentals=0,
        ),
        name="grad_first",
    )(idx, vol, *blocks)


def grad_second_kernel(n, idx, cot, *refs):
    blocks, out, ordered, padded = refs[:n], refs[n], refs[n + 1], refs[n + 2]
    rows = cot.shape[0]
    step = pl.program_id(0)

    @pl.when(step == 0)
    def _():
        for m in range(n):
            begin = pl.multiple_of((idx[0] ^ m) * rows, rows)
            ordered[pl.ds(begin, rows)] = blocks[m][...].astype(F32).T.astype(BF16)
        fill_padded(padded, cot[...], -1)

    lhs = ordered[...]
    for k in range(0, 9, 2):
        pieces = []
        for at in range(k, min(k + 2, 9)):
            b, c = at // 3 - 1, at % 3 - 1
            planes = padded[1 + c, pl.ds(2 - step, DEPTH), 1 - b : 1 - b + HEIGHT]
            pieces.append(planes.reshape(CELLS, rows))
        rhs = jnp.concatenate(pieces, axis=1)
        grads = jnp.dot(lhs, rhs, preferred_element_type=F32).astype(BF16)
        for at in range(len(pieces)):
            out[k + at] = grads[:, at * rows : (at + 1) * rows]


def grad_second(idx, cot, blocks):
    n, rows = len(blocks), cot.shape[0]
    return pl.pallas_call(
        functools.partial(grad_second_kernel, n),
        grid=(3,),
        in_specs=[smem(), whole(cot.shape)] + [whole(blocks[0].shape)] * n,
        out_specs=pl.BlockSpec((9, n * rows, rows), lambda a: (a, 0, 0)),
        out_shape=jax.ShapeDtypeStruct((27, n * rows, rows), BF16),
        scratch_shapes=[
            pltpu.VMEM((n * rows, CELLS), BF16),
            pltpu.VMEM((3, DEPTH + 2, HEIGHT + 2, WIDTH, rows), BF16),
        ],
        compiler_params=params(),
        cost_estimate=pl.CostEstimate(
            flops=2 * 27 * rows * rows * n * CELLS,
            bytes_accessed=2 * 27 * rows * rows * n,
            transcendentals=0,
        ),
        name="grad_second",
    )(idx, cot, *blocks)


def shards(volume, w_first, gain, w_second, cotangent):
    n = lax.axis_size("chan")
    rows = volume.shape[1]
    vol, cot = volume[0], cotangent[0]
    chan = lax.axis_index("chan")
    idx = chan.astype(jnp.int32).reshape(1)
    own_gain = lax.dynamic_slice_in_dim(gain, chan * rows, rows, 0)[None]

    def to_partner(x, m):
        return lax.ppermute(x, "chan", [(i, i ^ m) for i in range(n)])

    order = sorted(range(1, n), reverse=True)

    def swap(parts):
        got = {m: to_partner(parts[m], m) for m in order}
        return [parts[0]] + [got[m] for m in range(1, n)]

    def spread(own):
        return swap([own] * n)

    pre_shares = swap(
        spread_shares(pre_kernel, "pre", idx, n, vol, w_first.reshape(27 * rows, n * rows), [])
    )
    dact_shares = swap(
        spread_shares(
            dact_kernel, "dact", idx, n, cot, w_second, [pltpu.VMEM((n * rows, 27 * rows), BF16)]
        )
    )
    act, normed, inverse = pl.pallas_call(
        functools.partial(norm_kernel, n),
        out_shape=[
            jax.ShapeDtypeStruct((CELLS, rows), BF16),
            jax.ShapeDtypeStruct((CELLS, rows), F32),
            jax.ShapeDtypeStruct((1, rows), F32),
        ],
        compiler_params=pltpu.CompilerParams(vmem_limit_bytes=LIMIT),
        name="norm",
    )(own_gain, *pre_shares)
    act_blocks = spread(act)
    dpre, gain_part = pl.pallas_call(
        functools.partial(norm_back_kernel, n),
        out_shape=[
            jax.ShapeDtypeStruct((CELLS, rows), BF16),
            jax.ShapeDtypeStruct((1, rows), F32),
        ],
        compiler_params=pltpu.CompilerParams(vmem_limit_bytes=LIMIT),
        name="norm_back",
    )(own_gain, normed, inverse, *dact_shares)
    dpre_blocks = spread(dpre)
    factor = 1.0 / math.sqrt(lax.axis_size("dp") * CELLS)

    second_part = grad_second(idx, cot, act_blocks)
    second_total = lax.psum(second_part, "dp").astype(F32) * factor
    first_part = grad_first(idx, vol, dpre_blocks)
    first_total = lax.psum(first_part, "dp").astype(F32) * factor
    output = conv_full("output", 1, False, idx, w_second, act_blocks)
    grad_volume = conv_full(
        "grad_volume", -1, True, idx, w_first.reshape(27 * rows, n * rows), dpre_blocks
    )
    gain_total = lax.psum(gain_part[0], "dp") * factor
    return (output[None], grad_volume[None], first_total, gain_total, second_total)


def solution(mesh):
    placed = (
        P("dp", "chan", None),
        P(None, "chan", None),
        P(),
        P(None, None, "chan"),
        P("dp", "chan", None),
    )
    return jax.shard_map(
        shards,
        mesh=mesh,
        in_specs=placed,
        out_specs=(
            P("dp", "chan", None),
            P("dp", "chan", None),
            P(None, "chan", None),
            P("chan"),
            P(None, None, "chan"),
        ),
        check_vma=False,
    )
```

```python
import functools
import math

import jax
import jax.numpy as jnp
from jax import lax
from jax.experimental import pallas as pl
from jax.experimental.pallas import tpu as pltpu
from jax.sharding import PartitionSpec as P

DEPTH, HEIGHT, WIDTH = 4, 16, 16
PLANE = HEIGHT * WIDTH
CELLS = DEPTH * PLANE
TAPS = [(a, b, c) for a in (-1, 0, 1) for b in (-1, 0, 1) for c in (-1, 0, 1)]
NORM_EPS = 1e-05
LIMIT = 26 * 1024 * 1024
F32, BF16 = jnp.float32, jnp.bfloat16
NT = (((1,), (1,)), ((), ()))


def params():
    return pltpu.CompilerParams(
        dimension_semantics=("arbitrary",), vmem_limit_bytes=LIMIT
    )


def whole(shape):
    return pl.BlockSpec(shape, lambda *_: (0,) * len(shape))


def smem():
    return pl.BlockSpec(memory_space=pltpu.SMEM)


def fill_padded(padded, rows_first, sign):
    padded[...] = jnp.zeros_like(padded)
    cells = rows_first.astype(F32).T
    width_at = lax.broadcasted_iota(jnp.int32, cells.shape, 0) % WIDTH
    for c in (-1, 0, 1):
        off = sign * c
        moved = cells if off == 0 else pltpu.roll(cells, (-off) % CELLS, 0)
        inside = (width_at + off >= 0) & (width_at + off < WIDTH)
        moved = jnp.where(inside, moved, 0.0).astype(BF16)
        padded[1 + c, 1 : 1 + DEPTH, 1 : 1 + HEIGHT] = moved.reshape(
            DEPTH, HEIGHT, WIDTH, cells.shape[1]
        )


def tap_cells(padded, plane, tap, sign):
    a, b, c = tap
    low = 1 + sign * b
    rows = padded[1 + c, plane + (1 + sign * a), low : low + HEIGHT]
    return rows.reshape(PLANE, rows.shape[-1])


def pre_kernel(n, idx, vol, w, *refs):
    outs, padded, shares = refs[:n], refs[n], refs[n + 1]
    rows = vol.shape[0]
    plane = pl.program_id(0)

    @pl.when(plane == 0)
    def _():
        fill_padded(padded, vol[...], 1)

    lhs = jnp.concatenate([tap_cells(padded, plane, tap, 1) for tap in TAPS], axis=1)
    sums = jnp.dot(lhs, w[...], preferred_element_type=F32).astype(BF16)
    for j in range(n):
        shares[j] = sums[:, j * rows : (j + 1) * rows]
    for m in range(n):
        outs[m][...] = shares[idx[0] ^ m]


def dact_kernel(n, idx, cot, w, *refs):
    outs, padded, shares, wide = refs[:n], refs[n], refs[n + 1], refs[n + 2]
    rows = cot.shape[0]
    plane = pl.program_id(0)

    @pl.when(plane == 0)
    def _():
        fill_padded(padded, cot[...], -1)
        for t in range(27):
            wide[:, t * rows : (t + 1) * rows] = w[t]

    lhs = jnp.concatenate([tap_cells(padded, plane, tap, -1) for tap in TAPS], axis=1)
    sums = lax.dot_general(lhs, wide[...], NT, preferred_element_type=F32).astype(BF16)
    for j in range(n):
        shares[j] = sums[:, j * rows : (j + 1) * rows]
    for m in range(n):
        outs[m][...] = shares[idx[0] ^ m]


def spread_shares(kernel, name, idx, n, field, w, extra):
    rows = field.shape[0]
    return pl.pallas_call(
        functools.partial(kernel, n),
        grid=(DEPTH,),
        in_specs=[smem(), whole(field.shape), whole(w.shape)],
        out_specs=[pl.BlockSpec((PLANE, rows), lambda d: (d, 0))] * n,
        out_shape=[jax.ShapeDtypeStruct((CELLS, rows), BF16)] * n,
        scratch_shapes=[
            pltpu.VMEM((3, DEPTH + 2, HEIGHT + 2, WIDTH, rows), BF16),
            pltpu.VMEM((n, PLANE, rows), BF16),
        ]
        + extra,
        compiler_params=params(),
        cost_estimate=pl.CostEstimate(
            flops=2 * 27 * rows * rows * n * CELLS, bytes_accessed=2 * w.size, transcendentals=0
        ),
        name=name,
    )(idx, field, w)


def norm_kernel(n, gain, *refs):
    shares, act, normed_out, inverse_out = refs[:n], refs[n], refs[n + 1], refs[n + 2]
    pre = shares[0][...].astype(F32)
    for m in range(1, n):
        pre = pre + shares[m][...].astype(F32)
    center = pre - jnp.mean(pre, axis=0, keepdims=True)
    inverse = lax.rsqrt(jnp.mean(center * center, axis=0, keepdims=True) + NORM_EPS)
    normed = center * inverse
    scaled = gain[...] * normed
    act[...] = (scaled * jax.nn.sigmoid(scaled)).astype(BF16)
    normed_out[...] = normed
    inverse_out[...] = inverse


def norm_back_kernel(n, gain, normed_in, inverse, *refs):
    shares, dpre, gain_part = refs[:n], refs[n], refs[n + 1]
    dact = shares[0][...].astype(F32)
    for m in range(1, n):
        dact = dact + shares[m][...].astype(F32)
    normed = normed_in[...]
    scaled = gain[...] * normed
    sigma = jax.nn.sigmoid(scaled)
    dscaled = dact * sigma * (1.0 + scaled * (1.0 - sigma))
    product = dscaled * normed
    gain_part[...] = jnp.sum(product, axis=0, keepdims=True)
    dnormed = gain[...] * dscaled
    mean_first = jnp.mean(dnormed, axis=0, keepdims=True)
    mean_second = jnp.mean(dnormed * normed, axis=0, keepdims=True)
    dpre[...] = ((dnormed - mean_first - normed * mean_second) * inverse[...]).astype(BF16)


def conv_back_add(sums, products, plane, taps, rows, sign):
    for at, tap in enumerate(taps):
        a, b, c = tap
        a, b = sign * a, sign * b
        part = products[:, at * rows : (at + 1) * rows].reshape(HEIGHT, WIDTH, rows)
        low, high = max(0, b), HEIGHT + min(0, b)
        sums[1 + c, plane + (1 - a), low - b : high - b] += part[low:high]


def conv_finish(sums, out, sign):
    rows = out.shape[0]
    total = None
    for c in (-1, 0, 1):
        off = sign * c
        part = sums[1 + c, 1 : 1 + DEPTH].reshape(CELLS, rows)
        if off != 0:
            width_at = lax.broadcasted_iota(jnp.int32, part.shape, 0) % WIDTH
            inside = (width_at + off >= 0) & (width_at + off < WIDTH)
            part = jnp.where(inside, pltpu.roll(part, (-off) % CELLS, 0), 0.0)
        total = part if total is None else total + part
    out[...] = total.T.astype(BF16)


def conv_kernel(n, sign, transposed, idx, w, *refs):
    blocks, out, ordered, sums = refs[:n], refs[n], refs[n + 1], refs[n + 2]
    rows = out.shape[0]
    plane = pl.program_id(0)

    @pl.when(plane == 0)
    def _():
        sums[...] = jnp.zeros_like(sums)
        for m in range(n):
            ordered[idx[0] ^ m] = blocks[m][...]

    begin = pl.multiple_of(plane * PLANE, PLANE)
    lhs = jnp.concatenate([ordered[j, pl.ds(begin, PLANE)] for j in range(n)], axis=1)
    for t in range(0, 27, 2):
        taps = TAPS[t : t + 2]
        if transposed:
            rhs = w[t * rows : (t + len(taps)) * rows]
            products = lax.dot_general(lhs, rhs, NT, preferred_element_type=F32)
        else:
            rhs = jnp.concatenate([w[t + k] for k in range(len(taps))], axis=1)
            products = jnp.dot(lhs, rhs, preferred_element_type=F32)
        conv_back_add(sums, products, plane, taps, rows, sign)

    @pl.when(plane == DEPTH - 1)
    def _():
        conv_finish(sums, out, sign)


def conv_full(name, sign, transposed, idx, w, blocks):
    n, rows = len(blocks), blocks[0].shape[1]
    return pl.pallas_call(
        functools.partial(conv_kernel, n, sign, transposed),
        grid=(DEPTH,),
        in_specs=[smem(), whole(w.shape)] + [whole(blocks[0].shape)] * n,
        out_specs=whole((rows, CELLS)),
        out_shape=jax.ShapeDtypeStruct((rows, CELLS), BF16),
        scratch_shapes=[
            pltpu.VMEM((n, CELLS, rows), BF16),
            pltpu.VMEM((3, DEPTH + 2, HEIGHT, WIDTH, rows), F32),
        ],
        compiler_params=params(),
        cost_estimate=pl.CostEstimate(
            flops=2 * 27 * rows * rows * n * CELLS, bytes_accessed=2 * w.size, transcendentals=0
        ),
        name=name,
    )(idx, w, *blocks)


def halves_kernel(n, turned, idx, *refs):
    blocks, keep, send = refs[:n], refs[n], refs[n + 1]
    half = n // 2
    rows = blocks[0].shape[1]

    def put(out, at, block):
        if turned:
            out[pl.ds(pl.multiple_of(at * rows, rows), rows)] = block[...].astype(F32).T.astype(BF16)
        else:
            out[at] = block[...]

    def split(kept, sent):
        for m in range(half):
            at = (idx[0] ^ m) & (half - 1)
            put(keep, at, blocks[kept + m])
            put(send, at, blocks[sent + m])

    @pl.when(idx[1] == 0)
    def _():
        split(0, half)

    @pl.when(idx[1] != 0)
    def _():
        split(half, 0)


def halves(name, turned, idx, blocks):
    n, rows = len(blocks), blocks[0].shape[1]
    shape = (n // 2 * rows, CELLS) if turned else (n // 2, CELLS, rows)
    return pl.pallas_call(
        functools.partial(halves_kernel, n, turned),
        in_specs=[smem()] + [pl.BlockSpec(memory_space=pltpu.VMEM)] * n,
        out_shape=[jax.ShapeDtypeStruct(shape, BF16)] * 2,
        compiler_params=pltpu.CompilerParams(vmem_limit_bytes=LIMIT),
        name=name,
    )(idx, *blocks)


def moved_first_kernel(own, other, out):
    for which, ref in enumerate((own, other)):
        cells = ref[...].astype(F32)
        at = lax.broadcasted_iota(jnp.int32, cells.shape, 1)
        height_at, width_at = at // WIDTH % HEIGHT, at % WIDTH
        rows = cells.shape[0]
        for k in range(9):
            b, c = k // 3 - 1, k % 3 - 1
            off = b * WIDTH + c
            part = cells if off == 0 else pltpu.roll(cells, (-off) % CELLS, 1)
            inside = (height_at + b >= 0) & (height_at + b < HEIGHT)
            inside = inside & (width_at + c >= 0) & (width_at + c < WIDTH)
            out[which, k * rows : (k + 1) * rows] = jnp.where(inside, part, 0.0).astype(BF16)


def moved_second_kernel(own, other, out):
    out[...] = jnp.zeros_like(out)
    for which, ref in enumerate((own, other)):
        cells = ref[...].astype(F32).T
        width_at = lax.broadcasted_iota(jnp.int32, cells.shape, 0) % WIDTH
        for c in (-1, 0, 1):
            part = cells if c == 0 else pltpu.roll(cells, c % CELLS, 0)
            inside = (width_at - c >= 0) & (width_at - c < WIDTH)
            part = jnp.where(inside, part, 0.0).astype(BF16)
            out[which, 1 + c, :, 1 : 1 + HEIGHT] = part.reshape(
                DEPTH, HEIGHT, WIDTH, cells.shape[1]
            )


def moved_fields(kernel, name, shape, own, other):
    return pl.pallas_call(
        kernel,
        out_shape=jax.ShapeDtypeStruct(shape, BF16),
        compiler_params=pltpu.CompilerParams(vmem_limit_bytes=LIMIT),
        name=name,
    )(own, other)


def grad_first_kernel(a, moved, own, other, out):
    rows, half = out.shape[1], own.shape[0]
    begin, count = max(0, -a) * PLANE, (DEPTH - abs(a)) * PLANE
    grads = None
    for which, ref in enumerate((own, other)):
        rhs = jnp.concatenate([ref[j, begin : begin + count] for j in range(half)], axis=1)
        lhs = moved[which, :, begin + a * PLANE : begin + a * PLANE + count]
        part = jnp.dot(lhs, rhs, preferred_element_type=F32)
        grads = part if grads is None else grads + part
    out[...] = grads.astype(BF16).reshape(out.shape)


def grad_first(a, moved, own, other):
    half, cells, rows = own.shape
    return pl.pallas_call(
        functools.partial(grad_first_kernel, a),
        grid=(3,),
        in_specs=[
            pl.BlockSpec((2, 3 * rows, cells), lambda b: (0, b, 0)),
            whole(own.shape),
            whole(own.shape),
        ],
        out_specs=pl.BlockSpec((3, rows, half * rows), lambda b: (b, 0, 0)),
        out_shape=jax.ShapeDtypeStruct((9, rows, half * rows), BF16),
        compiler_params=params(),
        cost_estimate=pl.CostEstimate(
            flops=2 * 9 * rows * rows * half * 2 * (DEPTH - abs(a)) * PLANE,
            bytes_accessed=2 * moved.size,
            transcendentals=0,
        ),
        name="grad_first",
    )(moved, own, other)


def grad_second_kernel(a, moved, own, other, out):
    rows = out.shape[2]
    begin, planes = max(0, a), DEPTH - abs(a)
    lhs = [
        ref[:, begin * PLANE : (begin + planes) * PLANE] for ref in (own, other)
    ]
    for k in range(0, 9, 2):
        taps = range(k, min(k + 2, 9))
        grads = None
        for which in range(2):
            pieces = []
            for at in taps:
                b, c = at // 3 - 1, at % 3 - 1
                piece = moved[which, 1 + c, begin - a : begin - a + planes, 1 - b : 1 - b + HEIGHT]
                pieces.append(piece.reshape(planes * PLANE, rows))
            rhs = jnp.concatenate(pieces, axis=1)
            part = jnp.dot(lhs[which], rhs, preferred_element_type=F32)
            grads = part if grads is None else grads + part
        for place, at in enumerate(taps):
            out[at] = grads[:, place * rows : (place + 1) * rows].astype(BF16)


def grad_second(a, moved, own, other):
    wide, rows = own.shape[0], moved.shape[-1]
    return pl.pallas_call(
        functools.partial(grad_second_kernel, a),
        out_shape=jax.ShapeDtypeStruct((9, wide, rows), BF16),
        compiler_params=pltpu.CompilerParams(vmem_limit_bytes=LIMIT),
        cost_estimate=pl.CostEstimate(
            flops=2 * 9 * rows * wide * 2 * (DEPTH - abs(a)) * PLANE,
            bytes_accessed=2 * moved.size,
            transcendentals=0,
        ),
        name="grad_second",
    )(moved, own, other)


def finish_kernel(n, axis, factor, idx, own, other, *refs):
    out = refs[-1]
    upper = (idx[0] >= n // 2).astype(jnp.int32) ^ idx[1]
    wide = own.shape[axis]

    def put(low, high):
        parts = (low[...].astype(F32) * factor, high[...].astype(F32) * factor)
        if axis == 1:
            out[:, :wide] = parts[0]
            out[:, wide:] = parts[1]
        else:
            out[:, :, :wide] = parts[0]
            out[:, :, wide:] = parts[1]

    @pl.when(upper == 0)
    def _():
        put(own, other)

    @pl.when(upper != 0)
    def _():
        put(other, own)


def finish(name, n, axis, factor, idx, chunk, own, other, before):
    taps, height, width = own.shape
    block = (3, height * 2, width) if axis == 1 else (3, height, width * 2)
    steps = taps // 3
    part = pl.BlockSpec((3, height, width), lambda k: (k, 0, 0))
    given = [] if before is None else [before]
    return pl.pallas_call(
        functools.partial(finish_kernel, n, axis, factor),
        grid=(steps,),
        in_specs=[smem(), part, part] + [pl.BlockSpec(memory_space=pl.ANY)] * len(given),
        out_specs=pl.BlockSpec(block, lambda k: (chunk * steps + k, 0, 0)),
        out_shape=jax.ShapeDtypeStruct((27,) + block[1:], F32),
        input_output_aliases={3: 0} if given else {},
        compiler_params=params(),
        name=name,
    )(idx, own, other, *given)


def add_rounded(x, y):
    return (x.astype(F32) + y.astype(F32)).astype(BF16)


def line_sum(part):
    chips = lax.axis_size("dp") // 2
    at = lax.axis_index("dp") // 2

    def send(x, moves):
        return lax.ppermute(x, "dp", [(2 * i + k, 2 * j + k) for i, j in moves for k in (0, 1)])

    total = part
    for hop in range(chips // 2 - 1):
        got = send(total, [(hop, hop + 1), (chips - 1 - hop, chips - 2 - hop)])
        total = add_rounded(part, got)
    mid = chips // 2
    total = add_rounded(total, send(total, [(mid - 1, mid), (mid, mid - 1)]))
    for hop in reversed(range(chips // 2 - 1)):
        got = send(total, [(hop + 1, hop), (chips - 2 - hop, chips - 1 - hop)])
        total = jnp.where((at == hop) | (at == chips - 1 - hop), got, total)
    return total


def shards(volume, w_first, gain, w_second, cotangent):
    n = lax.axis_size("chan")
    rows = volume.shape[1]
    vol, cot = volume[0], cotangent[0]
    chan, place = lax.axis_index("chan"), lax.axis_index("dp")
    idx = jnp.stack([chan, place % 2]).astype(jnp.int32)
    own_gain = lax.dynamic_slice_in_dim(gain, chan * rows, rows, 0)[None]
    factor = 1.0 / math.sqrt(lax.axis_size("dp") * CELLS)

    def to_partner(x, m):
        return lax.ppermute(x, "chan", [(i, i ^ m) for i in range(n)])

    def to_core(x):
        return lax.ppermute(x, "dp", [(i, i ^ 1) for i in range(lax.axis_size("dp"))])

    def swap(parts):
        got = {m: to_partner(parts[m], m) for m in reversed(range(1, n))}
        return [parts[0]] + [got[m] for m in range(1, n)]

    pre_shares = swap(
        spread_shares(pre_kernel, "pre", idx, n, vol, w_first.reshape(27 * rows, n * rows), [])
    )
    dact_shares = swap(
        spread_shares(
            dact_kernel, "dact", idx, n, cot, w_second, [pltpu.VMEM((n * rows, 27 * rows), BF16)]
        )
    )
    moved_cot = moved_fields(
        moved_second_kernel,
        "moved_second",
        (2, 3, DEPTH, HEIGHT + 2, WIDTH, rows),
        cot,
        to_core(cot),
    )
    moved_vol = moved_fields(
        moved_first_kernel, "moved_first", (2, 9 * rows, CELLS), vol, to_core(vol)
    )
    act, normed, inverse = pl.pallas_call(
        functools.partial(norm_kernel, n),
        out_shape=[
            jax.ShapeDtypeStruct((CELLS, rows), BF16),
            jax.ShapeDtypeStruct((CELLS, rows), F32),
            jax.ShapeDtypeStruct((1, rows), F32),
        ],
        compiler_params=pltpu.CompilerParams(vmem_limit_bytes=LIMIT),
        name="norm",
    )(own_gain, *pre_shares)
    act_blocks = swap([act] * n)
    act_keep, act_send = halves("act_halves", True, idx, act_blocks)
    act_other = to_core(act_send)
    second_total = None
    for chunk, a in enumerate((-1, 0, 1)):
        summed = line_sum(grad_second(a, moved_cot, act_keep, act_other))
        second_total = finish(
            "finish_second", n, 1, factor, idx, chunk, summed, to_core(summed), second_total
        )
    output = conv_full("output", 1, False, idx, w_second, act_blocks)

    dpre, gain_part = pl.pallas_call(
        functools.partial(norm_back_kernel, n),
        out_shape=[
            jax.ShapeDtypeStruct((CELLS, rows), BF16),
            jax.ShapeDtypeStruct((1, rows), F32),
        ],
        compiler_params=pltpu.CompilerParams(vmem_limit_bytes=LIMIT),
        name="norm_back",
    )(own_gain, normed, inverse, *dact_shares)
    dpre_blocks = swap([dpre] * n)
    dpre_keep, dpre_send = halves("dpre_halves", False, idx, dpre_blocks)
    dpre_other = to_core(dpre_send)
    first_total = None
    for chunk, a in enumerate((-1, 0, 1)):
        summed = line_sum(grad_first(a, moved_vol, dpre_keep, dpre_other))
        first_total = finish(
            "finish_first", n, 2, factor, idx, chunk, summed, to_core(summed), first_total
        )
    grad_volume = conv_full(
        "grad_volume", -1, True, idx, w_first.reshape(27 * rows, n * rows), dpre_blocks
    )
    gain_total = jnp.sum(lax.all_gather(gain_part[0], "dp"), axis=0) * factor
    return (output[None], grad_volume[None], first_total, gain_total, second_total)


def solution(mesh):
    placed = (
        P("dp", "chan", None),
        P(None, "chan", None),
        P(),
        P(None, None, "chan"),
        P("dp", "chan", None),
    )
    return jax.shard_map(
        shards,
        mesh=mesh,
        in_specs=placed,
        out_specs=(
            P("dp", "chan", None),
            P("dp", "chan", None),
            P(None, "chan", None),
            P("chan"),
            P(None, None, "chan"),
        ),
        check_vma=False,
    )
```

```python
import functools
import math

import jax
import jax.numpy as jnp
from jax import lax
from jax.experimental import pallas as pl
from jax.experimental.pallas import tpu as pltpu
from jax.sharding import PartitionSpec as P

DEPTH, HEIGHT, WIDTH = 4, 16, 16
PLANE = HEIGHT * WIDTH
CELLS = DEPTH * PLANE
TAPS = [(a, b, c) for a in (-1, 0, 1) for b in (-1, 0, 1) for c in (-1, 0, 1)]
NORM_EPS = 1e-05
LIMIT = 26 * 1024 * 1024
F32, BF16 = jnp.float32, jnp.bfloat16
NT = (((1,), (1,)), ((), ()))
UNREAD = pl.BlockSpec(memory_space=pl.ANY)


def params():
    return pltpu.CompilerParams(
        dimension_semantics=("arbitrary",), vmem_limit_bytes=LIMIT
    )


def whole(shape):
    return pl.BlockSpec(shape, lambda *_: (0,) * len(shape))


def smem():
    return pl.BlockSpec(memory_space=pltpu.SMEM)


def fill_padded(padded, rows_first, sign):
    padded[...] = jnp.zeros_like(padded)
    cells = rows_first.astype(F32).T
    width_at = lax.broadcasted_iota(jnp.int32, cells.shape, 0) % WIDTH
    for c in (-1, 0, 1):
        off = sign * c
        moved = cells if off == 0 else pltpu.roll(cells, (-off) % CELLS, 0)
        inside = (width_at + off >= 0) & (width_at + off < WIDTH)
        moved = jnp.where(inside, moved, 0.0).astype(BF16)
        padded[1 + c, 1 : 1 + DEPTH, 1 : 1 + HEIGHT] = moved.reshape(
            DEPTH, HEIGHT, WIDTH, cells.shape[1]
        )


def tap_cells(padded, plane, tap, sign):
    a, b, c = tap
    low = 1 + sign * b
    rows = padded[1 + c, plane + (1 + sign * a), low : low + HEIGHT]
    return rows.reshape(PLANE, rows.shape[-1])


def pre_kernel(n, idx, vol, w, *refs):
    outs, padded, shares = refs[:n], refs[n], refs[n + 1]
    rows = vol.shape[0]
    plane = pl.program_id(0)

    @pl.when(plane == 0)
    def _():
        fill_padded(padded, vol[...], 1)

    lhs = jnp.concatenate([tap_cells(padded, plane, tap, 1) for tap in TAPS], axis=1)
    sums = jnp.dot(lhs, w[...], preferred_element_type=F32).astype(BF16)
    for j in range(n):
        shares[j] = sums[:, j * rows : (j + 1) * rows]
    for m in range(n):
        outs[m][...] = shares[idx[0] ^ m]


def dact_kernel(n, idx, cot, w, *refs):
    outs, padded, shares, wide = refs[:n], refs[n], refs[n + 1], refs[n + 2]
    rows = cot.shape[0]
    plane = pl.program_id(0)

    @pl.when(plane == 0)
    def _():
        fill_padded(padded, cot[...], -1)
        for t in range(27):
            wide[:, t * rows : (t + 1) * rows] = w[t]

    lhs = jnp.concatenate([tap_cells(padded, plane, tap, -1) for tap in TAPS], axis=1)
    sums = lax.dot_general(lhs, wide[...], NT, preferred_element_type=F32).astype(BF16)
    for j in range(n):
        shares[j] = sums[:, j * rows : (j + 1) * rows]
    for m in range(n):
        outs[m][...] = shares[idx[0] ^ m]


def spread_shares(kernel, name, idx, n, field, w, extra):
    rows = field.shape[0]
    return pl.pallas_call(
        functools.partial(kernel, n),
        grid=(DEPTH,),
        in_specs=[smem(), whole(field.shape), whole(w.shape)],
        out_specs=[pl.BlockSpec((PLANE, rows), lambda d: (d, 0))] * n,
        out_shape=[jax.ShapeDtypeStruct((CELLS, rows), BF16)] * n,
        scratch_shapes=[
            pltpu.VMEM((3, DEPTH + 2, HEIGHT + 2, WIDTH, rows), BF16),
            pltpu.VMEM((n, PLANE, rows), BF16),
        ]
        + extra,
        compiler_params=params(),
        cost_estimate=pl.CostEstimate(
            flops=2 * 27 * rows * rows * n * CELLS, bytes_accessed=2 * w.size, transcendentals=0
        ),
        name=name,
    )(idx, field, w)


def norm_kernel(n, gain, *refs):
    shares = refs[:n]
    act, normed_out, inverse_out = refs[-3:]
    pre = shares[0][...].astype(F32)
    for m in range(1, n):
        pre = pre + shares[m][...].astype(F32)
    center = pre - jnp.mean(pre, axis=0, keepdims=True)
    inverse = lax.rsqrt(jnp.mean(center * center, axis=0, keepdims=True) + NORM_EPS)
    normed = center * inverse
    scaled = gain[...] * normed
    act[...] = (scaled * jax.nn.sigmoid(scaled)).astype(BF16)
    normed_out[...] = normed
    inverse_out[...] = inverse


def norm_back_kernel(n, gain, normed_in, inverse, *refs):
    shares = refs[:n]
    dpre, gain_part = refs[-2:]
    dact = shares[0][...].astype(F32)
    for m in range(1, n):
        dact = dact + shares[m][...].astype(F32)
    normed = normed_in[...]
    scaled = gain[...] * normed
    sigma = jax.nn.sigmoid(scaled)
    dscaled = dact * sigma * (1.0 + scaled * (1.0 - sigma))
    product = dscaled * normed
    gain_part[...] = jnp.sum(product, axis=0, keepdims=True)
    dnormed = gain[...] * dscaled
    mean_first = jnp.mean(dnormed, axis=0, keepdims=True)
    mean_second = jnp.mean(dnormed * normed, axis=0, keepdims=True)
    dpre[...] = ((dnormed - mean_first - normed * mean_second) * inverse[...]).astype(BF16)


def conv_back_add(sums, products, plane, taps, rows, sign):
    for at, tap in enumerate(taps):
        a, b, c = tap
        a, b = sign * a, sign * b
        part = products[:, at * rows : (at + 1) * rows].reshape(HEIGHT, WIDTH, rows)
        low, high = max(0, b), HEIGHT + min(0, b)
        sums[1 + c, plane + (1 - a), low - b : high - b] += part[low:high]


def conv_finish(sums, out, sign):
    rows = out.shape[0]
    total = None
    for c in (-1, 0, 1):
        off = sign * c
        part = sums[1 + c, 1 : 1 + DEPTH].reshape(CELLS, rows)
        if off != 0:
            width_at = lax.broadcasted_iota(jnp.int32, part.shape, 0) % WIDTH
            inside = (width_at + off >= 0) & (width_at + off < WIDTH)
            part = jnp.where(inside, pltpu.roll(part, (-off) % CELLS, 0), 0.0)
        total = part if total is None else total + part
    out[...] = total.T.astype(BF16)


def conv_kernel(n, sign, transposed, idx, w, *refs):
    blocks = refs[:n]
    out, ordered, sums = refs[-3:]
    rows = out.shape[0]
    plane = pl.program_id(0)

    @pl.when(plane == 0)
    def _():
        sums[...] = jnp.zeros_like(sums)
        for m in range(n):
            ordered[idx[0] ^ m] = blocks[m][...]

    begin = pl.multiple_of(plane * PLANE, PLANE)
    lhs = jnp.concatenate([ordered[j, pl.ds(begin, PLANE)] for j in range(n)], axis=1)
    for t in range(0, 27, 2):
        taps = TAPS[t : t + 2]
        if transposed:
            rhs = w[t * rows : (t + len(taps)) * rows]
            products = lax.dot_general(lhs, rhs, NT, preferred_element_type=F32)
        else:
            rhs = jnp.concatenate([w[t + k] for k in range(len(taps))], axis=1)
            products = jnp.dot(lhs, rhs, preferred_element_type=F32)
        conv_back_add(sums, products, plane, taps, rows, sign)

    @pl.when(plane == DEPTH - 1)
    def _():
        conv_finish(sums, out, sign)


def conv_full(name, sign, transposed, idx, w, blocks, after):
    n, rows = len(blocks), blocks[0].shape[1]
    return pl.pallas_call(
        functools.partial(conv_kernel, n, sign, transposed),
        grid=(DEPTH,),
        in_specs=[smem(), whole(w.shape)] + [whole(blocks[0].shape)] * n + [UNREAD] * len(after),
        out_specs=whole((rows, CELLS)),
        out_shape=jax.ShapeDtypeStruct((rows, CELLS), BF16),
        scratch_shapes=[
            pltpu.VMEM((n, CELLS, rows), BF16),
            pltpu.VMEM((3, DEPTH + 2, HEIGHT, WIDTH, rows), F32),
        ],
        compiler_params=params(),
        cost_estimate=pl.CostEstimate(
            flops=2 * 27 * rows * rows * n * CELLS, bytes_accessed=2 * w.size, transcendentals=0
        ),
        name=name,
    )(idx, w, *blocks, *after)


def halves_kernel(n, held, turned, idx, *refs):
    blocks = refs[:n]
    keep, send = refs[len(refs) - held - 2], refs[len(refs) - held - 1]
    half = n // 2
    rows = blocks[0].shape[1]

    def put(out, at, block):
        if turned:
            out[pl.ds(pl.multiple_of(at * rows, rows), rows)] = block[...].astype(F32).T.astype(BF16)
        else:
            out[at] = block[...]

    def split(kept, sent):
        for m in range(half):
            at = (idx[0] ^ m) & (half - 1)
            put(keep, at, blocks[kept + m])
            put(send, at, blocks[sent + m])

    @pl.when(idx[1] == 0)
    def _():
        split(0, half)

    @pl.when(idx[1] != 0)
    def _():
        split(half, 0)


def halves(name, turned, idx, blocks, after=(), held=()):
    n, rows = len(blocks), blocks[0].shape[1]
    shape = (n // 2 * rows, CELLS) if turned else (n // 2, CELLS, rows)
    first = 1 + n + len(after)
    return pl.pallas_call(
        functools.partial(halves_kernel, n, len(held), turned),
        in_specs=[smem()]
        + [pl.BlockSpec(memory_space=pltpu.VMEM)] * n
        + [UNREAD] * (len(after) + len(held)),
        out_specs=[pl.BlockSpec(memory_space=pltpu.VMEM)] * 2 + [UNREAD] * len(held),
        out_shape=[jax.ShapeDtypeStruct(shape, BF16)] * 2
        + [jax.ShapeDtypeStruct(x.shape, x.dtype) for x in held],
        input_output_aliases={first + k: 2 + k for k in range(len(held))},
        compiler_params=pltpu.CompilerParams(vmem_limit_bytes=LIMIT),
        name=name,
    )(idx, *blocks, *after, *held)


def moved_first_kernel(own, other, _, out):
    for which, ref in enumerate((own, other)):
        cells = ref[...].astype(F32)
        at = lax.broadcasted_iota(jnp.int32, cells.shape, 1)
        height_at, width_at = at // WIDTH % HEIGHT, at % WIDTH
        rows = cells.shape[0]
        for k in range(9):
            b, c = k // 3 - 1, k % 3 - 1
            off = b * WIDTH + c
            part = cells if off == 0 else pltpu.roll(cells, (-off) % CELLS, 1)
            inside = (height_at + b >= 0) & (height_at + b < HEIGHT)
            inside = inside & (width_at + c >= 0) & (width_at + c < WIDTH)
            out[which, k * rows : (k + 1) * rows] = jnp.where(inside, part, 0.0).astype(BF16)


def moved_second_kernel(own, other, _, out):
    out[...] = jnp.zeros_like(out)
    for which, ref in enumerate((own, other)):
        cells = ref[...].astype(F32).T
        width_at = lax.broadcasted_iota(jnp.int32, cells.shape, 0) % WIDTH
        for c in (-1, 0, 1):
            part = cells if c == 0 else pltpu.roll(cells, c % CELLS, 0)
            inside = (width_at - c >= 0) & (width_at - c < WIDTH)
            part = jnp.where(inside, part, 0.0).astype(BF16)
            out[which, 1 + c, :, 1 : 1 + HEIGHT] = part.reshape(
                DEPTH, HEIGHT, WIDTH, cells.shape[1]
            )


def moved_fields(kernel, name, shape, own, other, after):
    return pl.pallas_call(
        kernel,
        in_specs=[pl.BlockSpec(memory_space=pltpu.VMEM)] * 2 + [UNREAD],
        out_shape=jax.ShapeDtypeStruct(shape, BF16),
        compiler_params=pltpu.CompilerParams(vmem_limit_bytes=LIMIT),
        name=name,
    )(own, other, after)


def grad_first_kernel(a, moved, own, other, *refs):
    out = refs[-1]
    rows, half = out.shape[1], own.shape[0]
    begin, count = max(0, -a) * PLANE, (DEPTH - abs(a)) * PLANE
    grads = None
    for which, ref in enumerate((own, other)):
        rhs = jnp.concatenate([ref[j, begin : begin + count] for j in range(half)], axis=1)
        lhs = moved[which, :, begin + a * PLANE : begin + a * PLANE + count]
        part = jnp.dot(lhs, rhs, preferred_element_type=F32)
        grads = part if grads is None else grads + part
    out[...] = grads.astype(BF16).reshape(out.shape)


def grad_first(a, moved, own, other, after):
    half, cells, rows = own.shape
    return pl.pallas_call(
        functools.partial(grad_first_kernel, a),
        grid=(3,),
        in_specs=[
            pl.BlockSpec((2, 3 * rows, cells), lambda b: (0, b, 0)),
            whole(own.shape),
            whole(own.shape),
        ]
        + [UNREAD] * len(after),
        out_specs=pl.BlockSpec((3, rows, half * rows), lambda b: (b, 0, 0)),
        out_shape=jax.ShapeDtypeStruct((9, rows, half * rows), BF16),
        compiler_params=params(),
        cost_estimate=pl.CostEstimate(
            flops=2 * 9 * rows * rows * half * 2 * (DEPTH - abs(a)) * PLANE,
            bytes_accessed=2 * moved.size,
            transcendentals=0,
        ),
        name="grad_first",
    )(moved, own, other, *after)


def grad_second_kernel(a, moved, own, other, *refs):
    out = refs[-1]
    rows = out.shape[2]
    begin, planes = max(0, a), DEPTH - abs(a)
    lhs = [
        ref[:, begin * PLANE : (begin + planes) * PLANE] for ref in (own, other)
    ]
    for k in range(0, 9, 2):
        taps = range(k, min(k + 2, 9))
        grads = None
        for which in range(2):
            pieces = []
            for at in taps:
                b, c = at // 3 - 1, at % 3 - 1
                piece = moved[which, 1 + c, begin - a : begin - a + planes, 1 - b : 1 - b + HEIGHT]
                pieces.append(piece.reshape(planes * PLANE, rows))
            rhs = jnp.concatenate(pieces, axis=1)
            part = jnp.dot(lhs[which], rhs, preferred_element_type=F32)
            grads = part if grads is None else grads + part
        for place, at in enumerate(taps):
            out[at] = grads[:, place * rows : (place + 1) * rows].astype(BF16)


def grad_second(a, moved, own, other, after):
    wide, rows = own.shape[0], moved.shape[-1]
    return pl.pallas_call(
        functools.partial(grad_second_kernel, a),
        in_specs=[pl.BlockSpec(memory_space=pltpu.VMEM)] * 3 + [UNREAD] * len(after),
        out_shape=jax.ShapeDtypeStruct((9, wide, rows), BF16),
        compiler_params=pltpu.CompilerParams(vmem_limit_bytes=LIMIT),
        cost_estimate=pl.CostEstimate(
            flops=2 * 9 * rows * wide * 2 * (DEPTH - abs(a)) * PLANE,
            bytes_accessed=2 * moved.size,
            transcendentals=0,
        ),
        name="grad_second",
    )(moved, own, other, *after)


def finish_kernel(n, axis, factor, idx, own, other, *refs):
    out, mark = refs[-2:]
    mark[...] = jnp.zeros_like(mark)
    upper = (idx[0] >= n // 2).astype(jnp.int32) ^ idx[1]
    wide = own.shape[axis]

    def put(low, high):
        parts = (low[...].astype(F32) * factor, high[...].astype(F32) * factor)
        if axis == 1:
            out[:, :wide] = parts[0]
            out[:, wide:] = parts[1]
        else:
            out[:, :, :wide] = parts[0]
            out[:, :, wide:] = parts[1]

    @pl.when(upper == 0)
    def _():
        put(own, other)

    @pl.when(upper != 0)
    def _():
        put(other, own)


def finish(name, n, axis, factor, idx, chunk, own, other, before, after):
    taps, height, width = own.shape
    block = (1, height * 2, width) if axis == 1 else (1, height, width * 2)
    part = pl.BlockSpec((1, height, width), lambda k: (k, 0, 0))
    given = [] if before is None else [before]
    return pl.pallas_call(
        functools.partial(finish_kernel, n, axis, factor),
        grid=(taps,),
        in_specs=[smem(), part, part] + [UNREAD] * (len(given) + len(after)),
        out_specs=[
            pl.BlockSpec(block, lambda k: (chunk * taps + k, 0, 0)),
            whole((8, 128)),
        ],
        out_shape=[
            jax.ShapeDtypeStruct((27,) + block[1:], F32),
            jax.ShapeDtypeStruct((8, 128), F32),
        ],
        input_output_aliases={3: 0} if given else {},
        compiler_params=params(),
        name=name,
    )(idx, own, other, *given, *after)


def add_kernel(x, y, *refs):
    out = refs[-1]
    out[...] = (x[...].astype(F32) + y[...].astype(F32)).astype(out.dtype)


def pick_kernel(idx, x, y, *refs):
    out = refs[-1]

    @pl.when(idx[2] == 0)
    def _():
        out[...] = x[...]

    @pl.when(idx[2] != 0)
    def _():
        out[...] = y[...]


def whole_call(kernel, name, x, y, after, idx=None):
    given = [] if idx is None else [idx]
    return pl.pallas_call(
        kernel,
        in_specs=[smem()] * len(given)
        + [pl.BlockSpec(memory_space=pltpu.VMEM)] * 2
        + [UNREAD] * len(after),
        out_shape=jax.ShapeDtypeStruct(x.shape, x.dtype),
        compiler_params=pltpu.CompilerParams(vmem_limit_bytes=LIMIT),
        name=name,
    )(*given, x, y, *after)


def line_moves(chips):
    inward = [[(h, h + 1), (chips - 1 - h, chips - 2 - h)] for h in range(chips // 2 - 1)]
    mid = chips // 2
    outward = [[(j, i) for i, j in moves] for moves in reversed(inward)]
    return inward + [[(mid - 1, mid), (mid, mid - 1)]], outward


def line_send(x, moves):
    pairs = [(2 * i + k, 2 * j + k) for i, j in moves for k in (0, 1)]
    return lax.ppermute(x, "dp", pairs)


def line_step(step, part, total, idx, place, after):
    sums, outward = line_moves(lax.axis_size("dp") // 2)
    if step < len(sums):
        got = line_send(total, sums[step])
        base = total if step == len(sums) - 1 else part
        return whole_call(add_kernel, "line_add", base, got, after)
    moves = outward[step - len(sums)]
    got = line_send(total, moves)
    takes = functools.reduce(jnp.logical_or, [place // 2 == j for _, j in moves])
    marked = jnp.stack([idx[0], idx[1], takes.astype(jnp.int32)])
    return whole_call(pick_kernel, "line_pick", total, got, after, marked)


def shards(volume, w_first, gain, w_second, cotangent):
    n = lax.axis_size("chan")
    rows = volume.shape[1]
    vol, cot = volume[0], cotangent[0]
    chan, place = lax.axis_index("chan"), lax.axis_index("dp")
    idx = jnp.stack([chan, place % 2]).astype(jnp.int32)
    own_gain = lax.dynamic_slice_in_dim(gain, chan * rows, rows, 0)[None]
    factor = 1.0 / math.sqrt(lax.axis_size("dp") * CELLS)

    def to_partner(x, m):
        return lax.ppermute(x, "chan", [(i, i ^ m) for i in range(n)])

    def to_core(x):
        return lax.ppermute(x, "dp", [(i, i ^ 1) for i in range(lax.axis_size("dp"))])

    def swap(parts):
        got = {m: to_partner(parts[m], m) for m in reversed(range(1, n))}
        return [parts[0]] + [got[m] for m in range(1, n)]

    first_flat = w_first.reshape(27 * rows, n * rows)
    pre_parts = spread_shares(pre_kernel, "pre", idx, n, vol, first_flat, [])
    pre_shares = swap(pre_parts)
    dact_parts = spread_shares(
        dact_kernel, "dact", idx, n, cot, w_second, [pltpu.VMEM((n * rows, 27 * rows), BF16)]
    )
    act, normed, inverse = pl.pallas_call(
        functools.partial(norm_kernel, n),
        in_specs=[pl.BlockSpec(memory_space=pltpu.VMEM)] * (1 + n) + [UNREAD],
        out_shape=[
            jax.ShapeDtypeStruct((CELLS, rows), BF16),
            jax.ShapeDtypeStruct((CELLS, rows), F32),
            jax.ShapeDtypeStruct((1, rows), F32),
        ],
        compiler_params=pltpu.CompilerParams(vmem_limit_bytes=LIMIT),
        name="norm",
    )(own_gain, *pre_shares, dact_parts[0])
    act_blocks = swap([act] * n)
    moved_cot = moved_fields(
        moved_second_kernel,
        "moved_second",
        (2, 3, DEPTH, HEIGHT + 2, WIDTH, rows),
        cot,
        to_core(cot),
        act,
    )
    moved_vol = moved_fields(
        moved_first_kernel, "moved_first", (2, 9 * rows, CELLS), vol, to_core(vol), act
    )
    act_keep, act_send, *dact_held = halves(
        "act_halves", True, idx, act_blocks, (moved_cot, moved_vol), dact_parts[1:]
    )
    act_other = to_core(act_send)
    dact_shares = swap([dact_parts[0]] + dact_held)

    second_parts = []
    for a in (-1, 0, 1):
        second_parts.append(
            grad_second(a, moved_cot, act_keep, act_other, tuple(second_parts[-1:]))
        )
    output = conv_full("output", 1, False, idx, w_second, act_blocks, (second_parts[-1],))

    dpre, gain_part = pl.pallas_call(
        functools.partial(norm_back_kernel, n),
        in_specs=[pl.BlockSpec(memory_space=pltpu.VMEM)] * (3 + n) + [UNREAD],
        out_shape=[
            jax.ShapeDtypeStruct((CELLS, rows), BF16),
            jax.ShapeDtypeStruct((1, rows), F32),
        ],
        compiler_params=pltpu.CompilerParams(vmem_limit_bytes=LIMIT),
        name="norm_back",
    )(own_gain, normed, inverse, *dact_shares, output)
    dpre_blocks = swap([dpre] * n)
    dpre_keep, dpre_send = halves("dpre_halves", False, idx, dpre_blocks)
    dpre_other = to_core(dpre_send)
    first_parts = []
    for a in (-1, 0, 1):
        first_parts.append(
            grad_first(a, moved_vol, dpre_keep, dpre_other, tuple(first_parts[-1:]))
        )
    parts = second_parts + first_parts
    totals = list(parts)
    sums, outward = line_moves(lax.axis_size("dp") // 2)
    steps = len(sums) + len(outward)
    crossed = [None] * len(parts)
    second_total = first_total = None
    last = ()
    for turn in range(len(parts) + steps + 1):
        for step in range(steps):
            chunk = turn - step
            if 0 <= chunk < len(parts):
                totals[chunk] = line_step(step, parts[chunk], totals[chunk], idx, place, last)
                last = (totals[chunk],)
                if step == steps - 1:
                    crossed[chunk] = to_core(totals[chunk])
        if turn == 5:
            grad_volume = conv_full(
                "grad_volume", -1, True, idx, first_flat, dpre_blocks, (first_parts[-1],) + last
            )
            last = (grad_volume,)
        if turn == 2:
            gain_own = whole_call(add_kernel, "gain_add", gain_part, to_core(gain_part), last)
            gain_sum = gain_own
            last = (gain_sum,)
        if 3 <= turn < 3 + steps:
            gain_sum = line_step(turn - 3, gain_own, gain_sum, idx, place, last)
            last = (gain_sum,)
        chunk = turn - steps
        if 0 <= chunk < 3:
            second_total, mark = finish(
                "finish_second", n, 1, factor, idx, chunk, totals[chunk], crossed[chunk], second_total, last
            )
            last = (mark,)
        elif 3 <= chunk < 6:
            first_total, mark = finish(
                "finish_first", n, 2, factor, idx, chunk - 3, totals[chunk], crossed[chunk], first_total, last
            )
            last = (mark,)
    gain_total = gain_sum[0] * factor
    return (output[None], grad_volume[None], first_total, gain_total, second_total)


def solution(mesh):
    placed = (
        P("dp", "chan", None),
        P(None, "chan", None),
        P(),
        P(None, None, "chan"),
        P("dp", "chan", None),
    )
    return jax.shard_map(
        shards,
        mesh=mesh,
        in_specs=placed,
        out_specs=(
            P("dp", "chan", None),
            P("dp", "chan", None),
            P(None, "chan", None),
            P("chan"),
            P(None, None, "chan"),
        ),
        check_vma=False,
    )
```

```python
import functools
import math

import jax
import jax.numpy as jnp
from jax import lax
from jax.experimental import pallas as pl
from jax.experimental.pallas import tpu as pltpu
from jax.sharding import PartitionSpec as P

DEPTH, HEIGHT, WIDTH = 4, 16, 16
PLANE = HEIGHT * WIDTH
CELLS = DEPTH * PLANE
TAPS = [(a, b, c) for a in (-1, 0, 1) for b in (-1, 0, 1) for c in (-1, 0, 1)]
NORM_EPS = 1e-05
LIMIT = 24 * 1024 * 1024
SMALL = 8 * 1024 * 1024
EXTRA = 16
F32, BF16 = jnp.float32, jnp.bfloat16
NT = (((1,), (1,)), ((), ()))
UNREAD = pl.BlockSpec(memory_space=pl.ANY)


def params():
    return pltpu.CompilerParams(
        dimension_semantics=("arbitrary",), vmem_limit_bytes=LIMIT
    )


def whole(shape):
    return pl.BlockSpec(shape, lambda *_: (0,) * len(shape))


def smem():
    return pl.BlockSpec(memory_space=pltpu.SMEM)


def fill_padded(padded, rows_first, sign):
    padded[...] = jnp.zeros_like(padded)
    cells = rows_first.astype(F32).T
    width_at = lax.broadcasted_iota(jnp.int32, cells.shape, 0) % WIDTH
    for c in (-1, 0, 1):
        off = sign * c
        moved = cells if off == 0 else pltpu.roll(cells, (-off) % CELLS, 0)
        inside = (width_at + off >= 0) & (width_at + off < WIDTH)
        moved = jnp.where(inside, moved, 0.0).astype(BF16)
        padded[1 + c, 1 : 1 + DEPTH, 1 : 1 + HEIGHT] = moved.reshape(
            DEPTH, HEIGHT, WIDTH, cells.shape[1]
        )


def tap_cells(padded, plane, tap, sign):
    a, b, c = tap
    low = 1 + sign * b
    rows = padded[1 + c, plane + (1 + sign * a), low : low + HEIGHT]
    return rows.reshape(PLANE, rows.shape[-1])


def pre_kernel(n, idx, vol, w, *refs):
    outs, padded, shares = refs[:n], refs[n], refs[n + 1]
    rows = vol.shape[0]
    plane = pl.program_id(0)

    @pl.when(plane == 0)
    def _():
        fill_padded(padded, vol[...], 1)

    lhs = jnp.concatenate([tap_cells(padded, plane, tap, 1) for tap in TAPS], axis=1)
    sums = jnp.dot(lhs, w[...], preferred_element_type=F32).astype(BF16)
    for j in range(n):
        shares[j] = sums[:, j * rows : (j + 1) * rows]
    for m in range(n):
        outs[m][...] = shares[idx[0] ^ m]


def dact_kernel(n, idx, cot, w, *refs):
    outs, padded, shares, wide = refs[:n], refs[n], refs[n + 1], refs[n + 2]
    rows = cot.shape[0]
    plane = pl.program_id(0)

    @pl.when(plane == 0)
    def _():
        fill_padded(padded, cot[...], -1)
        for t in range(27):
            wide[:, t * rows : (t + 1) * rows] = w[t]

    lhs = jnp.concatenate([tap_cells(padded, plane, tap, -1) for tap in TAPS], axis=1)
    sums = lax.dot_general(lhs, wide[...], NT, preferred_element_type=F32).astype(BF16)
    for j in range(n):
        shares[j] = sums[:, j * rows : (j + 1) * rows]
    for m in range(n):
        outs[m][...] = shares[idx[0] ^ m]


def spread_shares(kernel, name, idx, n, field, w, extra):
    rows = field.shape[0]
    return pl.pallas_call(
        functools.partial(kernel, n),
        grid=(DEPTH,),
        in_specs=[smem(), whole(field.shape), whole(w.shape)],
        out_specs=[pl.BlockSpec((PLANE, rows), lambda d: (d, 0))] * n,
        out_shape=[jax.ShapeDtypeStruct((CELLS, rows), BF16)] * n,
        scratch_shapes=[
            pltpu.VMEM((3, DEPTH + 2, HEIGHT + 2, WIDTH, rows), BF16),
            pltpu.VMEM((n, PLANE, rows), BF16),
        ]
        + extra,
        compiler_params=params(),
        cost_estimate=pl.CostEstimate(
            flops=2 * 27 * rows * rows * n * CELLS, bytes_accessed=2 * w.size, transcendentals=0
        ),
        name=name,
    )(idx, field, w)


def norm_kernel(n, gain, *refs):
    shares = refs[:n]
    act, normed_out, inverse_out = refs[-3:]
    pre = shares[0][...].astype(F32)
    for m in range(1, n):
        pre = pre + shares[m][...].astype(F32)
    center = pre - jnp.mean(pre, axis=0, keepdims=True)
    inverse = lax.rsqrt(jnp.mean(center * center, axis=0, keepdims=True) + NORM_EPS)
    normed = center * inverse
    scaled = gain[...] * normed
    act[...] = (scaled * jax.nn.sigmoid(scaled)).astype(BF16)
    normed_out[...] = normed
    inverse_out[...] = inverse


def norm_back_kernel(n, gain, normed_in, inverse, *refs):
    shares = refs[:n]
    dpre, gain_part = refs[-2:]
    dact = shares[0][...].astype(F32)
    for m in range(1, n):
        dact = dact + shares[m][...].astype(F32)
    normed = normed_in[...]
    scaled = gain[...] * normed
    sigma = jax.nn.sigmoid(scaled)
    dscaled = dact * sigma * (1.0 + scaled * (1.0 - sigma))
    product = dscaled * normed
    gain_part[...] = jnp.sum(product, axis=0, keepdims=True)
    dnormed = gain[...] * dscaled
    mean_first = jnp.mean(dnormed, axis=0, keepdims=True)
    mean_second = jnp.mean(dnormed * normed, axis=0, keepdims=True)
    dpre[...] = ((dnormed - mean_first - normed * mean_second) * inverse[...]).astype(BF16)


def conv_back_add(sums, products, plane, taps, rows, sign):
    for at, tap in enumerate(taps):
        a, b, c = tap
        a, b = sign * a, sign * b
        part = products[:, at * rows : (at + 1) * rows].reshape(HEIGHT, WIDTH, rows)
        low, high = max(0, b), HEIGHT + min(0, b)
        sums[1 + c, plane + (1 - a), low - b : high - b] += part[low:high]


def conv_finish(sums, out, sign):
    rows = out.shape[0]
    total = None
    for c in (-1, 0, 1):
        off = sign * c
        part = sums[1 + c, 1 : 1 + DEPTH].reshape(CELLS, rows)
        if off != 0:
            width_at = lax.broadcasted_iota(jnp.int32, part.shape, 0) % WIDTH
            inside = (width_at + off >= 0) & (width_at + off < WIDTH)
            part = jnp.where(inside, pltpu.roll(part, (-off) % CELLS, 0), 0.0)
        total = part if total is None else total + part
    out[...] = total.T.astype(BF16)


def conv_kernel(n, sign, transposed, idx, w, *refs):
    blocks = refs[:n]
    out, ordered, sums = refs[-3:]
    rows = out.shape[0]
    plane = pl.program_id(0)

    @pl.when(plane == 0)
    def _():
        sums[...] = jnp.zeros_like(sums)
        for m in range(n):
            ordered[idx[0] ^ m] = blocks[m][...]

    begin = pl.multiple_of(plane * PLANE, PLANE)
    lhs = jnp.concatenate([ordered[j, pl.ds(begin, PLANE)] for j in range(n)], axis=1)
    for t in range(0, 27, 2):
        taps = TAPS[t : t + 2]
        if transposed:
            rhs = w[t * rows : (t + len(taps)) * rows]
            products = lax.dot_general(lhs, rhs, NT, preferred_element_type=F32)
        else:
            rhs = jnp.concatenate([w[t + k] for k in range(len(taps))], axis=1)
            products = jnp.dot(lhs, rhs, preferred_element_type=F32)
        conv_back_add(sums, products, plane, taps, rows, sign)

    @pl.when(plane == DEPTH - 1)
    def _():
        conv_finish(sums, out, sign)


def conv_full(name, sign, transposed, idx, w, blocks, after):
    n, rows = len(blocks), blocks[0].shape[1]
    return pl.pallas_call(
        functools.partial(conv_kernel, n, sign, transposed),
        grid=(DEPTH,),
        in_specs=[smem(), whole(w.shape)] + [whole(blocks[0].shape)] * n + [UNREAD] * len(after),
        out_specs=whole((rows, CELLS)),
        out_shape=jax.ShapeDtypeStruct((rows, CELLS), BF16),
        scratch_shapes=[
            pltpu.VMEM((n, CELLS, rows), BF16),
            pltpu.VMEM((3, DEPTH + 2, HEIGHT, WIDTH, rows), F32),
        ],
        compiler_params=params(),
        cost_estimate=pl.CostEstimate(
            flops=2 * 27 * rows * rows * n * CELLS, bytes_accessed=2 * w.size, transcendentals=0
        ),
        name=name,
    )(idx, w, *blocks, *after)


def halves_kernel(n, held, turned, idx, *refs):
    blocks = refs[:n]
    keep, send = refs[len(refs) - held - 2], refs[len(refs) - held - 1]
    half = n // 2
    rows = blocks[0].shape[1]

    def put(out, at, block):
        if turned:
            out[pl.ds(pl.multiple_of(at * rows, rows), rows)] = block[...].astype(F32).T.astype(BF16)
        else:
            out[at] = block[...]

    def split(kept, sent):
        for m in range(half):
            at = (idx[0] ^ m) & (half - 1)
            put(keep, at, blocks[kept + m])
            put(send, at, blocks[sent + m])

    @pl.when(idx[1] == 0)
    def _():
        split(0, half)

    @pl.when(idx[1] != 0)
    def _():
        split(half, 0)


def halves(name, turned, idx, blocks, after=(), held=()):
    n, rows = len(blocks), blocks[0].shape[1]
    shape = (n // 2 * rows, CELLS) if turned else (n // 2, CELLS, rows)
    first = 1 + n + len(after)
    return pl.pallas_call(
        functools.partial(halves_kernel, n, len(held), turned),
        in_specs=[smem()]
        + [pl.BlockSpec(memory_space=pltpu.VMEM)] * n
        + [UNREAD] * (len(after) + len(held)),
        out_specs=[pl.BlockSpec(memory_space=pltpu.VMEM)] * 2 + [UNREAD] * len(held),
        out_shape=[jax.ShapeDtypeStruct(shape, BF16)] * 2
        + [jax.ShapeDtypeStruct(x.shape, x.dtype) for x in held],
        input_output_aliases={first + k: 2 + k for k in range(len(held))},
        compiler_params=pltpu.CompilerParams(vmem_limit_bytes=LIMIT),
        name=name,
    )(idx, *blocks, *after, *held)


def moved_first_kernel(own, other, _, out):
    for which, ref in enumerate((own, other)):
        cells = ref[...].astype(F32)
        at = lax.broadcasted_iota(jnp.int32, cells.shape, 1)
        height_at, width_at = at // WIDTH % HEIGHT, at % WIDTH
        rows = cells.shape[0]
        for k in range(9):
            b, c = k // 3 - 1, k % 3 - 1
            off = b * WIDTH + c
            part = cells if off == 0 else pltpu.roll(cells, (-off) % CELLS, 1)
            inside = (height_at + b >= 0) & (height_at + b < HEIGHT)
            inside = inside & (width_at + c >= 0) & (width_at + c < WIDTH)
            out[which, k * rows : (k + 1) * rows] = jnp.where(inside, part, 0.0).astype(BF16)


def moved_second_kernel(own, other, _, out):
    out[...] = jnp.zeros_like(out)
    for which, ref in enumerate((own, other)):
        cells = ref[...].astype(F32).T
        width_at = lax.broadcasted_iota(jnp.int32, cells.shape, 0) % WIDTH
        for c in (-1, 0, 1):
            part = cells if c == 0 else pltpu.roll(cells, c % CELLS, 0)
            inside = (width_at - c >= 0) & (width_at - c < WIDTH)
            part = jnp.where(inside, part, 0.0).astype(BF16)
            out[which, 1 + c, :, 1 : 1 + HEIGHT] = part.reshape(
                DEPTH, HEIGHT, WIDTH, cells.shape[1]
            )


def moved_fields(kernel, name, shape, own, other, after):
    return pl.pallas_call(
        kernel,
        in_specs=[pl.BlockSpec(memory_space=pltpu.VMEM)] * 2 + [UNREAD],
        out_shape=jax.ShapeDtypeStruct(shape, BF16),
        compiler_params=pltpu.CompilerParams(vmem_limit_bytes=LIMIT),
        name=name,
    )(own, other, after)


def split_rows(values):
    high = values.astype(BF16)
    low = (values - high.astype(F32)).astype(BF16)
    empty = jnp.zeros((EXTRA - 2, values.shape[1]), F32)
    return jnp.concatenate([high.astype(F32), low.astype(F32), empty], axis=0).astype(BF16)


def grad_first_kernel(a, moved, own, other, gain_part, *refs):
    out = refs[-1]
    half, rows = own.shape[0], own.shape[2]
    begin, count = max(0, -a) * PLANE, (DEPTH - abs(a)) * PLANE
    rhs = [
        jnp.concatenate([ref[j, begin : begin + count] for j in range(half)], axis=1)
        for ref in (own, other)
    ]
    for b in range(3):
        span = slice(3 * rows * b, 3 * rows * (b + 1))
        grads = None
        for which in range(2):
            lhs = moved[which, span, begin + a * PLANE : begin + a * PLANE + count]
            part = jnp.dot(lhs, rhs[which], preferred_element_type=F32)
            grads = part if grads is None else grads + part
        out[span] = grads.astype(BF16)
    filler = jnp.zeros((1, out.shape[1] - rows), F32)
    out[9 * rows :] = split_rows(jnp.concatenate([gain_part[...], filler], axis=1))


def grad_first(a, moved, own, other, gain_part, after):
    half, cells, rows = own.shape
    return pl.pallas_call(
        functools.partial(grad_first_kernel, a),
        in_specs=[pl.BlockSpec(memory_space=pltpu.VMEM)] * 4 + [UNREAD] * len(after),
        out_shape=jax.ShapeDtypeStruct((9 * rows + EXTRA, half * rows), BF16),
        compiler_params=pltpu.CompilerParams(vmem_limit_bytes=LIMIT),
        cost_estimate=pl.CostEstimate(
            flops=2 * 9 * rows * rows * half * 2 * (DEPTH - abs(a)) * PLANE,
            bytes_accessed=2 * moved.size,
            transcendentals=0,
        ),
        name="grad_first",
    )(moved, own, other, gain_part, *after)


def grad_second_kernel(a, moved, own, other, *refs):
    out = refs[-1]
    rows = out.shape[2]
    begin, planes = max(0, a), DEPTH - abs(a)
    lhs = [
        ref[:, begin * PLANE : (begin + planes) * PLANE] for ref in (own, other)
    ]
    for k in range(0, 9, 2):
        taps = range(k, min(k + 2, 9))
        grads = None
        for which in range(2):
            pieces = []
            for at in taps:
                b, c = at // 3 - 1, at % 3 - 1
                piece = moved[which, 1 + c, begin - a : begin - a + planes, 1 - b : 1 - b + HEIGHT]
                pieces.append(piece.reshape(planes * PLANE, rows))
            rhs = jnp.concatenate(pieces, axis=1)
            part = jnp.dot(lhs[which], rhs, preferred_element_type=F32)
            grads = part if grads is None else grads + part
        for place, at in enumerate(taps):
            out[at] = grads[:, place * rows : (place + 1) * rows].astype(BF16)


def grad_second(a, moved, own, other, after):
    wide, rows = own.shape[0], moved.shape[-1]
    return pl.pallas_call(
        functools.partial(grad_second_kernel, a),
        in_specs=[pl.BlockSpec(memory_space=pltpu.VMEM)] * 3 + [UNREAD] * len(after),
        out_shape=jax.ShapeDtypeStruct((9, wide, rows), BF16),
        compiler_params=pltpu.CompilerParams(vmem_limit_bytes=LIMIT),
        cost_estimate=pl.CostEstimate(
            flops=2 * 9 * rows * wide * 2 * (DEPTH - abs(a)) * PLANE,
            bytes_accessed=2 * moved.size,
            transcendentals=0,
        ),
        name="grad_second",
    )(moved, own, other, *after)


def finish_kernel(n, axis, factor, chunk, idx, own, other, *refs):
    out, mark, wide, sems = refs[-4:]
    upper = (idx[0] >= n // 2).astype(jnp.int32) ^ idx[1]
    taps, height, width = wide.shape[1:]
    copies = []
    for k, (part, place) in enumerate(((own, upper), (other, 1 - upper))):
        rows = part[: taps * height] if len(part.shape) == 2 else part[...]
        wide[k] = rows.reshape(taps, height, width).astype(F32) * factor
        size = (height, width)[axis - 1]
        span = pl.ds(pl.multiple_of(place * size, size), size)
        target = out.at[pl.ds(chunk * taps, taps)]
        target = target.at[:, span] if axis == 1 else target.at[:, :, span]
        copies.append(pltpu.make_async_copy(wide.at[k], target, sems.at[k]))
        copies[-1].start()
    mark[...] = jnp.zeros_like(mark)
    for copy in copies:
        copy.wait()


def finish(name, n, axis, factor, idx, chunk, shape, own, other, before, after):
    taps, height, width = shape
    given = [] if before is None else [before]
    full = (27, height * 2, width) if axis == 1 else (27, height, width * 2)
    return pl.pallas_call(
        functools.partial(finish_kernel, n, axis, factor, chunk),
        in_specs=[smem()]
        + [pl.BlockSpec(memory_space=pltpu.VMEM)] * 2
        + [UNREAD] * (len(given) + len(after)),
        out_specs=[UNREAD, pl.BlockSpec(memory_space=pltpu.VMEM)],
        out_shape=[jax.ShapeDtypeStruct(full, F32), jax.ShapeDtypeStruct((8, 128), F32)],
        scratch_shapes=[pltpu.VMEM((2,) + shape, F32), pltpu.SemaphoreType.DMA((2,))],
        input_output_aliases={3: 0} if given else {},
        compiler_params=pltpu.CompilerParams(vmem_limit_bytes=SMALL),
        name=name,
    )(idx, own, other, *given, *after)


def add_kernel(x, y, *refs):
    out = refs[-1]
    if len(x.shape) == 3:
        out[...] = (x[...].astype(F32) + y[...].astype(F32)).astype(BF16)
    else:
        rows = x.shape[0] - EXTRA
        out[:rows] = (x[:rows].astype(F32) + y[:rows].astype(F32)).astype(BF16)
        tail = x[rows:].astype(F32) + y[rows:].astype(F32)
        out[rows:] = split_rows(tail[:1] + tail[1:2])


def pick_kernel(idx, x, y, *refs):
    out = refs[-1]

    @pl.when(idx[2] == 0)
    def _():
        out[...] = x[...]

    @pl.when(idx[2] != 0)
    def _():
        out[...] = y[...]


def whole_call(kernel, name, x, y, after, idx=None):
    given = [] if idx is None else [idx]
    return pl.pallas_call(
        kernel,
        in_specs=[smem()] * len(given)
        + [pl.BlockSpec(memory_space=pltpu.VMEM)] * 2
        + [UNREAD] * len(after),
        out_shape=jax.ShapeDtypeStruct(x.shape, x.dtype),
        compiler_params=pltpu.CompilerParams(vmem_limit_bytes=SMALL),
        name=name,
    )(*given, x, y, *after)


def line_moves(chips):
    inward = [[(h, h + 1), (chips - 1 - h, chips - 2 - h)] for h in range(chips // 2 - 1)]
    mid = chips // 2
    outward = [[(j, i) for i, j in moves] for moves in reversed(inward)]
    return inward + [[(mid - 1, mid), (mid, mid - 1)]], outward


def line_send(x, moves):
    pairs = [(2 * i + k, 2 * j + k) for i, j in moves for k in (0, 1)]
    return lax.ppermute(x, "dp", pairs)


def line_step(step, part, total, idx, place, after):
    sums, outward = line_moves(lax.axis_size("dp") // 2)
    if step < len(sums):
        got = line_send(total, sums[step])
        base = total if step == len(sums) - 1 else part
        return whole_call(add_kernel, "line_add", base, got, after)
    moves = outward[step - len(sums)]
    got = line_send(total, moves)
    takes = functools.reduce(jnp.logical_or, [place // 2 == j for _, j in moves])
    marked = jnp.stack([idx[0], idx[1], takes.astype(jnp.int32)])
    return whole_call(pick_kernel, "line_pick", total, got, after, marked)


def shards(volume, w_first, gain, w_second, cotangent):
    n = lax.axis_size("chan")
    rows = volume.shape[1]
    vol, cot = volume[0], cotangent[0]
    chan, place = lax.axis_index("chan"), lax.axis_index("dp")
    idx = jnp.stack([chan, place % 2]).astype(jnp.int32)
    own_gain = lax.dynamic_slice_in_dim(gain, chan * rows, rows, 0)[None]
    factor = 1.0 / math.sqrt(lax.axis_size("dp") * CELLS)

    def to_partner(x, m):
        return lax.ppermute(x, "chan", [(i, i ^ m) for i in range(n)])

    def to_core(x):
        return lax.ppermute(x, "dp", [(i, i ^ 1) for i in range(lax.axis_size("dp"))])

    def swap(parts):
        got = {m: to_partner(parts[m], m) for m in reversed(range(1, n))}
        return [parts[0]] + [got[m] for m in range(1, n)]

    first_flat = w_first.reshape(27 * rows, n * rows)
    pre_parts = spread_shares(pre_kernel, "pre", idx, n, vol, first_flat, [])
    pre_shares = swap(pre_parts)
    dact_parts = spread_shares(
        dact_kernel, "dact", idx, n, cot, w_second, [pltpu.VMEM((n * rows, 27 * rows), BF16)]
    )
    act, normed, inverse = pl.pallas_call(
        functools.partial(norm_kernel, n),
        in_specs=[pl.BlockSpec(memory_space=pltpu.VMEM)] * (1 + n) + [UNREAD],
        out_shape=[
            jax.ShapeDtypeStruct((CELLS, rows), BF16),
            jax.ShapeDtypeStruct((CELLS, rows), F32),
            jax.ShapeDtypeStruct((1, rows), F32),
        ],
        compiler_params=pltpu.CompilerParams(vmem_limit_bytes=LIMIT),
        name="norm",
    )(own_gain, *pre_shares, dact_parts[0])
    act_blocks = swap([act] * n)
    moved_cot = moved_fields(
        moved_second_kernel,
        "moved_second",
        (2, 3, DEPTH, HEIGHT + 2, WIDTH, rows),
        cot,
        to_core(cot),
        act,
    )
    moved_vol = moved_fields(
        moved_first_kernel, "moved_first", (2, 9 * rows, CELLS), vol, to_core(vol), act
    )
    act_keep, act_send, *dact_held = halves(
        "act_halves", True, idx, act_blocks, (moved_cot, moved_vol), dact_parts[1:]
    )
    act_other = to_core(act_send)
    dact_shares = swap([dact_parts[0]] + dact_held)

    sums, outward = line_moves(lax.axis_size("dp") // 2)
    steps = len(sums) + len(outward)
    parts, totals, crossed = {}, {}, {}
    last = ()

    def line(chunk, step):
        nonlocal last
        before = totals.get(chunk, parts[chunk])
        totals[chunk] = line_step(step, parts[chunk], before, idx, place, last)
        last = (totals[chunk],)
        if step == steps - 1:
            crossed[chunk] = to_core(totals[chunk])

    def turn(at, written):
        nonlocal last
        for step in range(steps):
            if 0 <= at - step < 6:
                line(at - step, step)
        chunk = at - steps
        if 0 <= chunk < 6:
            name, axis = ("finish_second", 1) if chunk < 3 else ("finish_first", 2)
            shape = (9, n // 2 * rows, rows) if chunk < 3 else (9, rows, n // 2 * rows)
            written[axis], mark = finish(
                name,
                n,
                axis,
                factor,
                idx,
                chunk % 3,
                shape,
                totals[chunk],
                crossed[chunk],
                written.get(axis),
                last,
            )
            last = (mark,)

    written = {}
    for chunk in range(3):
        parts[chunk] = grad_second(chunk - 1, moved_cot, act_keep, act_other, last)
        last = (parts[chunk],)
    turn(0, written)
    dpre, gain_part = pl.pallas_call(
        functools.partial(norm_back_kernel, n),
        in_specs=[pl.BlockSpec(memory_space=pltpu.VMEM)] * (3 + n) + [UNREAD],
        out_shape=[
            jax.ShapeDtypeStruct((CELLS, rows), BF16),
            jax.ShapeDtypeStruct((1, rows), F32),
        ],
        compiler_params=pltpu.CompilerParams(vmem_limit_bytes=SMALL),
        name="norm_back",
    )(own_gain, normed, inverse, *dact_shares, *last)
    dpre_blocks = swap([dpre] * n)
    output = conv_full("output", 1, False, idx, w_second, act_blocks, (dpre,))
    last = (output,)
    turn(1, written)
    dpre_keep, dpre_send = halves("dpre_halves", False, idx, dpre_blocks, last)
    dpre_other = to_core(dpre_send)
    parts[3] = grad_first(-1, moved_vol, dpre_keep, dpre_other, gain_part, last)
    last = (parts[3],)
    turn(2, written)
    for chunk in (4, 5):
        parts[chunk] = grad_first(chunk - 4, moved_vol, dpre_keep, dpre_other, gain_part, last)
        last = (parts[chunk],)
    turn(3, written)
    grad_volume = conv_full("grad_volume", -1, True, idx, first_flat, dpre_blocks, last)
    last = (grad_volume,)
    for at in range(4, 6 + steps):
        turn(at, written)
    gain_rows = totals[3][9 * rows : 9 * rows + 2, :rows].astype(F32)
    gain_rows_other = crossed[3][9 * rows : 9 * rows + 2, :rows].astype(F32)
    gain_total = (jnp.sum(gain_rows, axis=0) + jnp.sum(gain_rows_other, axis=0)) * factor
    return (output[None], grad_volume[None], written[2], gain_total, written[1])


def solution(mesh):
    placed = (
        P("dp", "chan", None),
        P(None, "chan", None),
        P(),
        P(None, None, "chan"),
        P("dp", "chan", None),
    )
    return jax.shard_map(
        shards,
        mesh=mesh,
        in_specs=placed,
        out_specs=(
            P("dp", "chan", None),
            P("dp", "chan", None),
            P(None, "chan", None),
            P("chan"),
            P(None, None, "chan"),
        ),
        check_vma=False,
    )
```

```python
import functools
import math

import jax
import jax.numpy as jnp
from jax import lax
from jax.experimental import pallas as pl
from jax.experimental.pallas import tpu as pltpu
from jax.sharding import PartitionSpec as P

DEPTH, HEIGHT, WIDTH = 4, 16, 16
PLANE = HEIGHT * WIDTH
CELLS = DEPTH * PLANE
TAPS = [(a, b, c) for a in (-1, 0, 1) for b in (-1, 0, 1) for c in (-1, 0, 1)]
NORM_EPS = 1e-05
LIMIT = 24 * 1024 * 1024
SMALL = 8 * 1024 * 1024
LARGE = 61 * 1024 * 1024
EXTRA = 16
F32, BF16 = jnp.float32, jnp.bfloat16
NT = (((1,), (1,)), ((), ()))
UNREAD = pl.BlockSpec(memory_space=pl.ANY)
IN_HBM = pl.BlockSpec(memory_space=pltpu.HBM)
PLANE_ORDER = (0, -1, 1)
LIGHT = pl.CostEstimate(flops=1024, bytes_accessed=1024, transcendentals=0)


def params():
    return pltpu.CompilerParams(
        dimension_semantics=("arbitrary",), vmem_limit_bytes=LIMIT
    )


def whole(shape):
    return pl.BlockSpec(shape, lambda *_: (0,) * len(shape))


def smem():
    return pl.BlockSpec(memory_space=pltpu.SMEM)


def fill_padded(padded, rows_first, sign):
    padded[...] = jnp.zeros_like(padded)
    cells = rows_first.astype(F32).T
    width_at = lax.broadcasted_iota(jnp.int32, cells.shape, 0) % WIDTH
    for c in (-1, 0, 1):
        off = sign * c
        moved = cells if off == 0 else pltpu.roll(cells, (-off) % CELLS, 0)
        inside = (width_at + off >= 0) & (width_at + off < WIDTH)
        moved = jnp.where(inside, moved, 0.0).astype(BF16)
        padded[1 + c, 1 : 1 + DEPTH, 1 : 1 + HEIGHT] = moved.reshape(
            DEPTH, HEIGHT, WIDTH, cells.shape[1]
        )


def span_of(a, sign):
    return max(0, -sign * a), DEPTH - abs(a)


def start_parts(source, buffer, sems):
    size = source.shape[0] // 3
    copies = {}
    for a in PLANE_ORDER:
        span = pl.ds((a + 1) * size, size)
        copies[a] = pltpu.make_async_copy(source.at[span], buffer.at[span], sems.at[a + 1])
        copies[a].start()
    return copies


def share_kernel(n, sign, idx, field, w, *refs):
    outs = refs[:n]
    padded, sums, shares, buffer, sems = refs[n:]
    rows = field.shape[0]
    copies = start_parts(w, buffer, sems)
    fill_padded(padded, field[...], sign)
    for a in PLANE_ORDER:
        begin, planes = span_of(a, sign)
        pieces = []
        for b in (-1, 0, 1):
            for c in (-1, 0, 1):
                low, first = 1 + sign * b, 1 + begin + sign * a
                piece = padded[1 + c, first : first + planes, low : low + HEIGHT]
                pieces.append(piece.reshape(planes * PLANE, rows))
        lhs = jnp.concatenate(pieces, axis=1)
        copies[a].wait()
        if sign == 1:
            rhs = buffer[(a + 1) * 9 * rows : (a + 2) * 9 * rows]
            part = jnp.dot(lhs, rhs, preferred_element_type=F32)
        else:
            rhs = jnp.concatenate([buffer[(a + 1) * 9 + k] for k in range(9)], axis=1)
            part = lax.dot_general(lhs, rhs, NT, preferred_element_type=F32)
        span = slice(begin * PLANE, (begin + planes) * PLANE)
        if a == 0:
            sums[...] = part
        else:
            sums[span] += part
    for j in range(n):
        shares[j] = sums[:, j * rows : (j + 1) * rows].astype(BF16)
    for m in range(n):
        outs[m][...] = shares[idx[0] ^ m]


def spread_shares(sign, name, idx, n, field, w, limit):
    rows = field.shape[0]
    return pl.pallas_call(
        functools.partial(share_kernel, n, sign),
        in_specs=[smem(), pl.BlockSpec(memory_space=pltpu.VMEM), IN_HBM],
        out_specs=[pl.BlockSpec(memory_space=pltpu.VMEM)] * n,
        out_shape=[jax.ShapeDtypeStruct((CELLS, rows), BF16)] * n,
        scratch_shapes=[
            pltpu.VMEM((3, DEPTH + 2, HEIGHT + 2, WIDTH, rows), BF16),
            pltpu.VMEM((CELLS, n * rows), F32),
            pltpu.VMEM((n, CELLS, rows), BF16),
            pltpu.VMEM(w.shape, BF16),
            pltpu.SemaphoreType.DMA((3,)),
        ],
        compiler_params=pltpu.CompilerParams(vmem_limit_bytes=limit),
        cost_estimate=LIGHT,
        name=name,
    )(idx, field, w)


def norm_kernel(n, gain, *refs):
    shares = refs[:n]
    act, normed_out, inverse_out = refs[-3:]
    pre = shares[0][...].astype(F32)
    for m in range(1, n):
        pre = pre + shares[m][...].astype(F32)
    center = pre - jnp.mean(pre, axis=0, keepdims=True)
    inverse = lax.rsqrt(jnp.mean(center * center, axis=0, keepdims=True) + NORM_EPS)
    normed = center * inverse
    scaled = gain[...] * normed
    act[...] = (scaled * jax.nn.sigmoid(scaled)).astype(BF16)
    normed_out[...] = normed
    inverse_out[...] = inverse


def norm_back_kernel(n, gain, normed_in, inverse, *refs):
    shares = refs[:n]
    dpre, gain_part = refs[-2:]
    dact = shares[0][...].astype(F32)
    for m in range(1, n):
        dact = dact + shares[m][...].astype(F32)
    normed = normed_in[...]
    scaled = gain[...] * normed
    sigma = jax.nn.sigmoid(scaled)
    dscaled = dact * sigma * (1.0 + scaled * (1.0 - sigma))
    product = dscaled * normed
    gain_part[...] = jnp.sum(product, axis=0, keepdims=True)
    dnormed = gain[...] * dscaled
    mean_first = jnp.mean(dnormed, axis=0, keepdims=True)
    mean_second = jnp.mean(dnormed * normed, axis=0, keepdims=True)
    dpre[...] = ((dnormed - mean_first - normed * mean_second) * inverse[...]).astype(BF16)


def conv_back_add(sums, products, begin, planes, taps, rows, sign):
    for at, tap in enumerate(taps):
        a, b, c = tap
        a, b = sign * a, sign * b
        part = products[:, at * rows : (at + 1) * rows].reshape(planes, HEIGHT, WIDTH, rows)
        low, high = max(0, b), HEIGHT + min(0, b)
        sums[1 + c, begin - a : begin - a + planes, low - b : high - b] += part[:, low:high]


def conv_finish(sums, out, sign):
    rows = out.shape[0]
    total = None
    for c in (-1, 0, 1):
        off = sign * c
        part = sums[1 + c].reshape(CELLS, rows)
        if off != 0:
            width_at = lax.broadcasted_iota(jnp.int32, part.shape, 0) % WIDTH
            inside = (width_at + off >= 0) & (width_at + off < WIDTH)
            part = jnp.where(inside, pltpu.roll(part, (-off) % CELLS, 0), 0.0)
        total = part if total is None else total + part
    out[...] = total.T.astype(BF16)


def conv_kernel(n, sign, transposed, idx, w, *refs):
    blocks = refs[:n]
    out, ordered, sums, buffer, sems = refs[-5:]
    rows = out.shape[0]
    copies = start_parts(w, buffer, sems)
    sums[...] = jnp.zeros_like(sums)
    for m in range(n):
        ordered[idx[0] ^ m] = blocks[m][...]
    for a in PLANE_ORDER:
        begin, planes = span_of(-a, sign)
        span = slice(begin * PLANE, (begin + planes) * PLANE)
        lhs = jnp.concatenate([ordered[j, span] for j in range(n)], axis=1)
        copies[a].wait()
        for k in range(0, 9, 2):
            t = (a + 1) * 9 + k
            taps = TAPS[t : t + min(2, 9 - k)]
            if transposed:
                rhs = buffer[t * rows : (t + len(taps)) * rows]
                products = lax.dot_general(lhs, rhs, NT, preferred_element_type=F32)
            else:
                rhs = jnp.concatenate([buffer[t + at] for at in range(len(taps))], axis=1)
                products = jnp.dot(lhs, rhs, preferred_element_type=F32)
            conv_back_add(sums, products, begin, planes, taps, rows, sign)
    conv_finish(sums, out, sign)


def conv_full(name, sign, transposed, idx, w, blocks, after):
    n, rows = len(blocks), blocks[0].shape[1]
    return pl.pallas_call(
        functools.partial(conv_kernel, n, sign, transposed),
        in_specs=[smem(), IN_HBM]
        + [pl.BlockSpec(memory_space=pltpu.VMEM)] * n
        + [UNREAD] * len(after),
        out_specs=pl.BlockSpec(memory_space=pltpu.VMEM),
        out_shape=jax.ShapeDtypeStruct((rows, CELLS), BF16),
        scratch_shapes=[
            pltpu.VMEM((n, CELLS, rows), BF16),
            pltpu.VMEM((3, DEPTH, HEIGHT, WIDTH, rows), F32),
            pltpu.VMEM(w.shape, BF16),
            pltpu.SemaphoreType.DMA((3,)),
        ],
        compiler_params=pltpu.CompilerParams(vmem_limit_bytes=LIMIT),
        cost_estimate=LIGHT,
        name=name,
    )(idx, w, *blocks, *after)


def halves_kernel(n, turned, idx, *refs):
    blocks = refs[:n]
    keep, send = refs[-2:]
    half = n // 2
    rows = blocks[0].shape[1]

    def put(out, at, block):
        if turned:
            out[pl.ds(pl.multiple_of(at * rows, rows), rows)] = block[...].astype(F32).T.astype(BF16)
        else:
            out[at] = block[...]

    def split(kept, sent):
        for m in range(half):
            at = (idx[0] ^ m) & (half - 1)
            put(keep, at, blocks[kept + m])
            put(send, at, blocks[sent + m])

    @pl.when(idx[1] == 0)
    def _():
        split(0, half)

    @pl.when(idx[1] != 0)
    def _():
        split(half, 0)


def halves(name, turned, idx, blocks, after):
    n, rows = len(blocks), blocks[0].shape[1]
    shape = (n // 2 * rows, CELLS) if turned else (n // 2, CELLS, rows)
    return pl.pallas_call(
        functools.partial(halves_kernel, n, turned),
        in_specs=[smem()]
        + [pl.BlockSpec(memory_space=pltpu.VMEM)] * n
        + [UNREAD] * len(after),
        out_shape=[jax.ShapeDtypeStruct(shape, BF16)] * 2,
        compiler_params=pltpu.CompilerParams(vmem_limit_bytes=LIMIT),
        cost_estimate=LIGHT,
        name=name,
    )(idx, *blocks, *after)


def moved_first_kernel(own, other, _, out):
    for which, ref in enumerate((own, other)):
        cells = ref[...].astype(F32)
        at = lax.broadcasted_iota(jnp.int32, cells.shape, 1)
        height_at, width_at = at // WIDTH % HEIGHT, at % WIDTH
        rows = cells.shape[0]
        for k in range(9):
            b, c = k // 3 - 1, k % 3 - 1
            off = b * WIDTH + c
            part = cells if off == 0 else pltpu.roll(cells, (-off) % CELLS, 1)
            inside = (height_at + b >= 0) & (height_at + b < HEIGHT)
            inside = inside & (width_at + c >= 0) & (width_at + c < WIDTH)
            out[which, k * rows : (k + 1) * rows] = jnp.where(inside, part, 0.0).astype(BF16)


def moved_second_kernel(own, other, _, out):
    out[...] = jnp.zeros_like(out)
    for which, ref in enumerate((own, other)):
        cells = ref[...].astype(F32).T
        width_at = lax.broadcasted_iota(jnp.int32, cells.shape, 0) % WIDTH
        for c in (-1, 0, 1):
            part = cells if c == 0 else pltpu.roll(cells, c % CELLS, 0)
            inside = (width_at - c >= 0) & (width_at - c < WIDTH)
            part = jnp.where(inside, part, 0.0).astype(BF16)
            out[which, 1 + c, :, 1 : 1 + HEIGHT] = part.reshape(
                DEPTH, HEIGHT, WIDTH, cells.shape[1]
            )


def moved_fields(kernel, name, shape, own, other, after):
    return pl.pallas_call(
        kernel,
        in_specs=[pl.BlockSpec(memory_space=pltpu.VMEM)] * 2 + [UNREAD],
        out_shape=jax.ShapeDtypeStruct(shape, BF16),
        compiler_params=pltpu.CompilerParams(vmem_limit_bytes=LIMIT),
        cost_estimate=LIGHT,
        name=name,
    )(own, other, after)


def split_rows(values):
    high = values.astype(BF16)
    low = (values - high.astype(F32)).astype(BF16)
    empty = jnp.zeros((EXTRA - 2, values.shape[1]), F32)
    return jnp.concatenate([high.astype(F32), low.astype(F32), empty], axis=0).astype(BF16)


def grad_first_kernel(a, moved, own, other, gain_part, *refs):
    out = refs[-1]
    half, rows = own.shape[0], own.shape[2]
    begin, count = max(0, -a) * PLANE, (DEPTH - abs(a)) * PLANE
    rhs = [
        jnp.concatenate([ref[j, begin : begin + count] for j in range(half)], axis=1)
        for ref in (own, other)
    ]
    for b in range(3):
        span = slice(3 * rows * b, 3 * rows * (b + 1))
        grads = None
        for which in range(2):
            lhs = moved[which, span, begin + a * PLANE : begin + a * PLANE + count]
            part = jnp.dot(lhs, rhs[which], preferred_element_type=F32)
            grads = part if grads is None else grads + part
        out[span] = grads.astype(BF16)
    filler = jnp.zeros((1, out.shape[1] - rows), F32)
    out[9 * rows :] = split_rows(jnp.concatenate([gain_part[...], filler], axis=1))


def grad_first(a, moved, own, other, gain_part, after):
    half, cells, rows = own.shape
    return pl.pallas_call(
        functools.partial(grad_first_kernel, a),
        in_specs=[pl.BlockSpec(memory_space=pltpu.VMEM)] * 4 + [UNREAD] * len(after),
        out_shape=jax.ShapeDtypeStruct((9 * rows + EXTRA, half * rows), BF16),
        compiler_params=pltpu.CompilerParams(vmem_limit_bytes=LIMIT),
        cost_estimate=LIGHT,
        name="grad_first",
    )(moved, own, other, gain_part, *after)


def grad_second_kernel(a, held, moved, own, other, *refs):
    out = refs[len(refs) - held - 1]
    rows = out.shape[2]
    begin, planes = max(0, a), DEPTH - abs(a)
    lhs = [
        ref[:, begin * PLANE : (begin + planes) * PLANE] for ref in (own, other)
    ]
    for k in range(0, 9, 2):
        taps = range(k, min(k + 2, 9))
        grads = None
        for which in range(2):
            pieces = []
            for at in taps:
                b, c = at // 3 - 1, at % 3 - 1
                piece = moved[which, 1 + c, begin - a : begin - a + planes, 1 - b : 1 - b + HEIGHT]
                pieces.append(piece.reshape(planes * PLANE, rows))
            rhs = jnp.concatenate(pieces, axis=1)
            part = jnp.dot(lhs[which], rhs, preferred_element_type=F32)
            grads = part if grads is None else grads + part
        for place, at in enumerate(taps):
            out[at] = grads[:, place * rows : (place + 1) * rows].astype(BF16)


def grad_second(a, moved, own, other, after, held=()):
    wide, rows = own.shape[0], moved.shape[-1]
    first = 3 + len(after)
    return pl.pallas_call(
        functools.partial(grad_second_kernel, a, len(held)),
        in_specs=[pl.BlockSpec(memory_space=pltpu.VMEM)] * 3 + [UNREAD] * (len(after) + len(held)),
        out_specs=[pl.BlockSpec(memory_space=pltpu.VMEM)] + [UNREAD] * len(held),
        out_shape=[jax.ShapeDtypeStruct((9, wide, rows), BF16)]
        + [jax.ShapeDtypeStruct(x.shape, x.dtype) for x in held],
        input_output_aliases={first + k: 1 + k for k in range(len(held))},
        compiler_params=pltpu.CompilerParams(vmem_limit_bytes=LIMIT),
        cost_estimate=LIGHT,
        name="grad_second",
    )(moved, own, other, *after, *held)


def finish_kernel(n, axis, factor, chunk, idx, own, other, *refs):
    out, mark, wide, sems = refs[-4:]
    upper = (idx[0] >= n // 2).astype(jnp.int32) ^ idx[1]
    taps, height, width = wide.shape[1:]
    copies = []
    for k, (part, place) in enumerate(((own, upper), (other, 1 - upper))):
        rows = part[: taps * height] if len(part.shape) == 2 else part[...]
        wide[k] = rows.reshape(taps, height, width).astype(F32) * factor
        size = (height, width)[axis - 1]
        span = pl.ds(pl.multiple_of(place * size, size), size)
        target = out.at[pl.ds(chunk * taps, taps)]
        target = target.at[:, span] if axis == 1 else target.at[:, :, span]
        copies.append(pltpu.make_async_copy(wide.at[k], target, sems.at[k]))
        copies[-1].start()
    mark[...] = jnp.zeros_like(mark)
    for copy in copies:
        copy.wait()


def finish(name, n, axis, factor, idx, chunk, shape, own, other, before, after):
    taps, height, width = shape
    given = [] if before is None else [before]
    full = (27, height * 2, width) if axis == 1 else (27, height, width * 2)
    return pl.pallas_call(
        functools.partial(finish_kernel, n, axis, factor, chunk),
        in_specs=[smem()]
        + [pl.BlockSpec(memory_space=pltpu.VMEM)] * 2
        + [UNREAD] * (len(given) + len(after)),
        out_specs=[UNREAD, pl.BlockSpec(memory_space=pltpu.VMEM)],
        out_shape=[jax.ShapeDtypeStruct(full, F32), jax.ShapeDtypeStruct((8, 128), F32)],
        scratch_shapes=[pltpu.VMEM((2,) + shape, F32), pltpu.SemaphoreType.DMA((2,))],
        input_output_aliases={3: 0} if given else {},
        compiler_params=pltpu.CompilerParams(vmem_limit_bytes=SMALL),
        cost_estimate=LIGHT,
        name=name,
    )(idx, own, other, *given, *after)


def add_kernel(x, y, *refs):
    out = refs[-1]
    if len(x.shape) == 3:
        out[...] = (x[...].astype(F32) + y[...].astype(F32)).astype(BF16)
    else:
        rows = x.shape[0] - EXTRA
        out[:rows] = (x[:rows].astype(F32) + y[:rows].astype(F32)).astype(BF16)
        tail = x[rows:].astype(F32) + y[rows:].astype(F32)
        out[rows:] = split_rows(tail[:1] + tail[1:2])


def pick_kernel(idx, x, y, *refs):
    out = refs[-1]

    @pl.when(idx[2] == 0)
    def _():
        out[...] = x[...]

    @pl.when(idx[2] != 0)
    def _():
        out[...] = y[...]


def whole_call(kernel, name, x, y, after, idx=None):
    given = [] if idx is None else [idx]
    return pl.pallas_call(
        kernel,
        in_specs=[smem()] * len(given)
        + [pl.BlockSpec(memory_space=pltpu.VMEM)] * 2
        + [UNREAD] * len(after),
        out_shape=jax.ShapeDtypeStruct(x.shape, x.dtype),
        compiler_params=pltpu.CompilerParams(vmem_limit_bytes=SMALL),
        cost_estimate=LIGHT,
        name=name,
    )(*given, x, y, *after)


def line_moves(chips):
    inward = [[(h, h + 1), (chips - 1 - h, chips - 2 - h)] for h in range(chips // 2 - 1)]
    mid = chips // 2
    outward = [[(j, i) for i, j in moves] for moves in reversed(inward)]
    return inward + [[(mid - 1, mid), (mid, mid - 1)]], outward


def line_send(x, moves):
    pairs = [(2 * i + k, 2 * j + k) for i, j in moves for k in (0, 1)]
    return lax.ppermute(x, "dp", pairs)


def line_step(step, part, total, idx, place, after):
    sums, outward = line_moves(lax.axis_size("dp") // 2)
    if step < len(sums):
        got = line_send(total, sums[step])
        base = total if step == len(sums) - 1 else part
        return whole_call(add_kernel, "line_add", base, got, after)
    moves = outward[step - len(sums)]
    got = line_send(total, moves)
    takes = functools.reduce(jnp.logical_or, [place // 2 == j for _, j in moves])
    marked = jnp.stack([idx[0], idx[1], takes.astype(jnp.int32)])
    return whole_call(pick_kernel, "line_pick", total, got, after, marked)


def shards(volume, w_first, gain, w_second, cotangent):
    n = lax.axis_size("chan")
    rows = volume.shape[1]
    vol, cot = volume[0], cotangent[0]
    chan, place = lax.axis_index("chan"), lax.axis_index("dp")
    idx = jnp.stack([chan, place % 2]).astype(jnp.int32)
    own_gain = lax.dynamic_slice_in_dim(gain, chan * rows, rows, 0)[None]
    factor = 1.0 / math.sqrt(lax.axis_size("dp") * CELLS)

    def to_partner(x, m):
        return lax.ppermute(x, "chan", [(i, i ^ m) for i in range(n)])

    def to_core(x):
        return lax.ppermute(x, "dp", [(i, i ^ 1) for i in range(lax.axis_size("dp"))])

    def swap(parts):
        got = {m: to_partner(parts[m], m) for m in reversed(range(1, n))}
        return [parts[0]] + [got[m] for m in range(1, n)]

    first_flat = w_first.reshape(27 * rows, n * rows)
    pre_shares = swap(spread_shares(1, "pre", idx, n, vol, first_flat, LARGE))
    dact_parts = spread_shares(-1, "dact", idx, n, cot, w_second, LIMIT)
    act, normed, inverse = pl.pallas_call(
        functools.partial(norm_kernel, n),
        in_specs=[pl.BlockSpec(memory_space=pltpu.VMEM)] * (1 + n) + [UNREAD],
        out_shape=[
            jax.ShapeDtypeStruct((CELLS, rows), BF16),
            jax.ShapeDtypeStruct((CELLS, rows), F32),
            jax.ShapeDtypeStruct((1, rows), F32),
        ],
        compiler_params=pltpu.CompilerParams(vmem_limit_bytes=LIMIT),
        cost_estimate=LIGHT,
        name="norm",
    )(own_gain, *pre_shares, dact_parts[0])
    act_blocks = swap([act] * n)
    moved_cot = moved_fields(
        moved_second_kernel,
        "moved_second",
        (2, 3, DEPTH, HEIGHT + 2, WIDTH, rows),
        cot,
        to_core(cot),
        act,
    )
    moved_vol = moved_fields(
        moved_first_kernel, "moved_first", (2, 9 * rows, CELLS), vol, to_core(vol), act
    )
    act_keep, act_send = halves("act_halves", True, idx, act_blocks, (moved_cot, moved_vol))
    act_other = to_core(act_send)

    sums, outward = line_moves(lax.axis_size("dp") // 2)
    steps = len(sums) + len(outward)
    parts, totals, crossed = {}, {}, {}
    last = ()

    def line(chunk, step):
        nonlocal last
        before = totals.get(chunk, parts[chunk])
        totals[chunk] = line_step(step, parts[chunk], before, idx, place, last)
        last = (totals[chunk],)
        if step == steps - 1:
            crossed[chunk] = to_core(totals[chunk])

    def write(chunk):
        nonlocal last
        name, axis = ("finish_second", 1) if chunk < 3 else ("finish_first", 2)
        shape = (9, n // 2 * rows, rows) if chunk < 3 else (9, rows, n // 2 * rows)
        written[axis], mark = finish(
            name,
            n,
            axis,
            factor,
            idx,
            chunk % 3,
            shape,
            totals[chunk],
            crossed[chunk],
            written.get(axis),
            last,
        )
        last = (mark,)

    def second_part(chunk):
        nonlocal last
        held = tuple(dact_parts[1:]) if chunk == 0 else ()
        parts[chunk], *passed = grad_second(
            chunk - 1, moved_cot, act_keep, act_other, last, held
        )
        last = (parts[chunk],)
        if chunk == 0:
            done["dact"] = swap([dact_parts[0]] + passed)

    def first_part(chunk):
        nonlocal last
        own, other = done["dpre_halves"]
        parts[chunk] = grad_first(chunk - 4, moved_vol, own, other, done["gain"], last)
        last = (parts[chunk],)

    def norm_back():
        nonlocal last
        dpre, done["gain"] = pl.pallas_call(
            functools.partial(norm_back_kernel, n),
            in_specs=[pl.BlockSpec(memory_space=pltpu.VMEM)] * (3 + n) + [UNREAD],
            out_shape=[
                jax.ShapeDtypeStruct((CELLS, rows), BF16),
                jax.ShapeDtypeStruct((1, rows), F32),
            ],
            compiler_params=pltpu.CompilerParams(vmem_limit_bytes=SMALL),
            cost_estimate=LIGHT,
            name="norm_back",
        )(own_gain, normed, inverse, *done["dact"], *last)
        done["dpre"] = swap([dpre] * n)
        last = (dpre,)

    def dpre_halves():
        nonlocal last
        keep, send = halves("dpre_halves", False, idx, done["dpre"], last)
        done["dpre_halves"] = keep, to_core(send)
        last = (keep,)

    def output():
        nonlocal last
        done["output"] = conv_full("output", 1, False, idx, w_second, act_blocks, last)
        last = (done["output"],)

    def grad_volume():
        nonlocal last
        done["grad_volume"] = conv_full(
            "grad_volume", -1, True, idx, first_flat, done["dpre"], last
        )
        last = (done["grad_volume"],)

    def wave(at):
        for step in range(steps):
            if 0 <= at - step < 6:
                line(at - step, step)
        if 0 <= at - steps < 6:
            write(at - steps)

    written, done = {}, {}
    second_part(0)
    output()
    second_part(1)
    norm_back()
    line(0, 0)
    second_part(2)
    line(1, 0)
    line(0, 1)
    dpre_halves()
    line(2, 0)
    line(1, 1)
    first_part(3)
    for step in range(2, steps):
        line(0, step)
    first_part(4)
    first_part(5)
    wave(3)
    grad_volume()
    for at in range(4, 6 + steps):
        wave(at)
    gain_rows = totals[3][9 * rows : 9 * rows + 2, :rows].astype(F32)
    gain_rows_other = crossed[3][9 * rows : 9 * rows + 2, :rows].astype(F32)
    gain_total = (jnp.sum(gain_rows, axis=0) + jnp.sum(gain_rows_other, axis=0)) * factor
    return (done["output"][None], done["grad_volume"][None], written[2], gain_total, written[1])


def solution(mesh):
    placed = (
        P("dp", "chan", None),
        P(None, "chan", None),
        P(),
        P(None, None, "chan"),
        P("dp", "chan", None),
    )
    return jax.shard_map(
        shards,
        mesh=mesh,
        in_specs=placed,
        out_specs=(
            P("dp", "chan", None),
            P("dp", "chan", None),
            P(None, "chan", None),
            P("chan"),
            P(None, None, "chan"),
        ),
        check_vma=False,
    )
```

```python
import functools
import math

import jax
import jax.numpy as jnp
from jax import lax
from jax.experimental import pallas as pl
from jax.experimental.pallas import tpu as pltpu
from jax.sharding import PartitionSpec as P

DEPTH, HEIGHT, WIDTH = 4, 16, 16
PLANE = HEIGHT * WIDTH
CELLS = DEPTH * PLANE
TAPS = [(a, b, c) for a in (-1, 0, 1) for b in (-1, 0, 1) for c in (-1, 0, 1)]
NORM_EPS = 1e-05
LIMIT = 16 * 1024 * 1024
SMALL = 8 * 1024 * 1024
LARGE = 61 * 1024 * 1024
EXTRA = 16
F32, BF16 = jnp.float32, jnp.bfloat16
NT = (((1,), (1,)), ((), ()))
UNREAD = pl.BlockSpec(memory_space=pl.ANY)
IN_HBM = pl.BlockSpec(memory_space=pltpu.HBM)
PLANE_ORDER = (0, -1, 1)
LIGHT = pl.CostEstimate(flops=1024, bytes_accessed=1024, transcendentals=0)


def params():
    return pltpu.CompilerParams(
        dimension_semantics=("arbitrary",), vmem_limit_bytes=LIMIT
    )


def whole(shape):
    return pl.BlockSpec(shape, lambda *_: (0,) * len(shape))


def smem():
    return pl.BlockSpec(memory_space=pltpu.SMEM)


def fill_padded(padded, rows_first, sign):
    padded[...] = jnp.zeros_like(padded)
    cells = rows_first.astype(F32).T
    width_at = lax.broadcasted_iota(jnp.int32, cells.shape, 0) % WIDTH
    for c in (-1, 0, 1):
        off = sign * c
        moved = cells if off == 0 else pltpu.roll(cells, (-off) % CELLS, 0)
        inside = (width_at + off >= 0) & (width_at + off < WIDTH)
        moved = jnp.where(inside, moved, 0.0).astype(BF16)
        padded[1 + c, 1 : 1 + DEPTH, 1 : 1 + HEIGHT] = moved.reshape(
            DEPTH, HEIGHT, WIDTH, cells.shape[1]
        )


def span_of(a, sign):
    return max(0, -sign * a), DEPTH - abs(a)


def start_parts(source, buffer, sems):
    size = source.shape[0] // 3
    copies = {}
    for a in PLANE_ORDER:
        span = pl.ds((a + 1) * size, size)
        copies[a] = pltpu.make_async_copy(source.at[span], buffer.at[span], sems.at[a + 1])
        copies[a].start()
    return copies


def share_kernel(n, sign, idx, field, w, *refs):
    outs = refs[:n]
    padded, sums, shares, buffer, sems = refs[n:]
    rows = field.shape[0]
    copies = start_parts(w, buffer, sems)
    fill_padded(padded, field[...], sign)
    for a in PLANE_ORDER:
        begin, planes = span_of(a, sign)
        pieces = []
        for b in (-1, 0, 1):
            for c in (-1, 0, 1):
                low, first = 1 + sign * b, 1 + begin + sign * a
                piece = padded[1 + c, first : first + planes, low : low + HEIGHT]
                pieces.append(piece.reshape(planes * PLANE, rows))
        lhs = jnp.concatenate(pieces, axis=1)
        copies[a].wait()
        if sign == 1:
            rhs = buffer[(a + 1) * 9 * rows : (a + 2) * 9 * rows]
            part = jnp.dot(lhs, rhs, preferred_element_type=F32)
        else:
            rhs = jnp.concatenate([buffer[(a + 1) * 9 + k] for k in range(9)], axis=1)
            part = lax.dot_general(lhs, rhs, NT, preferred_element_type=F32)
        span = slice(begin * PLANE, (begin + planes) * PLANE)
        if a == 0:
            sums[...] = part
        else:
            sums[span] += part
    for j in range(n):
        shares[j] = sums[:, j * rows : (j + 1) * rows].astype(BF16)
    for m in range(n):
        outs[m][...] = shares[idx[0] ^ m]


def spread_shares(sign, name, idx, n, field, w, limit):
    rows = field.shape[0]
    return pl.pallas_call(
        functools.partial(share_kernel, n, sign),
        in_specs=[smem(), pl.BlockSpec(memory_space=pltpu.VMEM), IN_HBM],
        out_specs=[pl.BlockSpec(memory_space=pltpu.VMEM)] * n,
        out_shape=[jax.ShapeDtypeStruct((CELLS, rows), BF16)] * n,
        scratch_shapes=[
            pltpu.VMEM((3, DEPTH + 2, HEIGHT + 2, WIDTH, rows), BF16),
            pltpu.VMEM((CELLS, n * rows), F32),
            pltpu.VMEM((n, CELLS, rows), BF16),
            pltpu.VMEM(w.shape, BF16),
            pltpu.SemaphoreType.DMA((3,)),
        ],
        compiler_params=pltpu.CompilerParams(vmem_limit_bytes=limit),
        cost_estimate=LIGHT,
        name=name,
    )(idx, field, w)


def norm_kernel(n, gain, *refs):
    shares = refs[:n]
    act, normed_out, inverse_out = refs[2 * n - 1 : 2 * n + 2]
    pre = shares[0][...].astype(F32)
    for m in range(1, n):
        pre = pre + shares[m][...].astype(F32)
    center = pre - jnp.mean(pre, axis=0, keepdims=True)
    inverse = lax.rsqrt(jnp.mean(center * center, axis=0, keepdims=True) + NORM_EPS)
    normed = center * inverse
    scaled = gain[...] * normed
    act[...] = (scaled * jax.nn.sigmoid(scaled)).astype(BF16)
    normed_out[...] = normed
    inverse_out[...] = inverse


def norm_back_kernel(n, gain, normed_in, inverse, *refs):
    shares = refs[:n]
    dpre, gain_part = refs[-2:]
    dact = shares[0][...].astype(F32)
    for m in range(1, n):
        dact = dact + shares[m][...].astype(F32)
    normed = normed_in[...]
    scaled = gain[...] * normed
    sigma = jax.nn.sigmoid(scaled)
    dscaled = dact * sigma * (1.0 + scaled * (1.0 - sigma))
    product = dscaled * normed
    gain_part[...] = jnp.sum(product, axis=0, keepdims=True)
    dnormed = gain[...] * dscaled
    mean_first = jnp.mean(dnormed, axis=0, keepdims=True)
    mean_second = jnp.mean(dnormed * normed, axis=0, keepdims=True)
    dpre[...] = ((dnormed - mean_first - normed * mean_second) * inverse[...]).astype(BF16)


def conv_back_add(sums, products, begin, planes, taps, rows, sign):
    for at, tap in enumerate(taps):
        a, b, c = tap
        a, b = sign * a, sign * b
        part = products[:, at * rows : (at + 1) * rows].reshape(planes, HEIGHT, WIDTH, rows)
        low, high = max(0, b), HEIGHT + min(0, b)
        sums[1 + c, begin - a : begin - a + planes, low - b : high - b] += part[:, low:high]


def conv_finish(sums, out, sign):
    rows = out.shape[0]
    total = None
    for c in (-1, 0, 1):
        off = sign * c
        part = sums[1 + c].reshape(CELLS, rows)
        if off != 0:
            width_at = lax.broadcasted_iota(jnp.int32, part.shape, 0) % WIDTH
            inside = (width_at + off >= 0) & (width_at + off < WIDTH)
            part = jnp.where(inside, pltpu.roll(part, (-off) % CELLS, 0), 0.0)
        total = part if total is None else total + part
    out[...] = total.T.astype(BF16)


def conv_kernel(n, sign, transposed, idx, w, *refs):
    blocks = refs[:n]
    out, mark, ordered, sums, buffer, sems = refs[-6:]
    mark[...] = jnp.zeros_like(mark)
    rows = out.shape[0]
    copies = start_parts(w, buffer, sems)
    sums[...] = jnp.zeros_like(sums)
    for m in range(n):
        ordered[idx[0] ^ m] = blocks[m][...]
    for a in PLANE_ORDER:
        begin, planes = span_of(-a, sign)
        span = slice(begin * PLANE, (begin + planes) * PLANE)
        lhs = jnp.concatenate([ordered[j, span] for j in range(n)], axis=1)
        copies[a].wait()
        for k in range(0, 9, 2):
            t = (a + 1) * 9 + k
            taps = TAPS[t : t + min(2, 9 - k)]
            if transposed:
                rhs = buffer[t * rows : (t + len(taps)) * rows]
                products = lax.dot_general(lhs, rhs, NT, preferred_element_type=F32)
            else:
                rhs = jnp.concatenate([buffer[t + at] for at in range(len(taps))], axis=1)
                products = jnp.dot(lhs, rhs, preferred_element_type=F32)
            conv_back_add(sums, products, begin, planes, taps, rows, sign)
    conv_finish(sums, out, sign)


def conv_full(name, sign, transposed, idx, w, blocks, after):
    n, rows = len(blocks), blocks[0].shape[1]
    return pl.pallas_call(
        functools.partial(conv_kernel, n, sign, transposed),
        in_specs=[smem(), IN_HBM]
        + [pl.BlockSpec(memory_space=pltpu.VMEM)] * n
        + [UNREAD] * len(after),
        out_specs=[pl.BlockSpec(memory_space=pltpu.VMEM)] * 2,
        out_shape=[
            jax.ShapeDtypeStruct((rows, CELLS), BF16),
            jax.ShapeDtypeStruct((8, 128), F32),
        ],
        scratch_shapes=[
            pltpu.VMEM((n, CELLS, rows), BF16),
            pltpu.VMEM((3, DEPTH, HEIGHT, WIDTH, rows), F32),
            pltpu.VMEM(w.shape, BF16),
            pltpu.SemaphoreType.DMA((3,)),
        ],
        compiler_params=pltpu.CompilerParams(vmem_limit_bytes=LIMIT),
        cost_estimate=LIGHT,
        name=name,
    )(idx, w, *blocks, *after)


def halves_kernel(n, turned, idx, *refs):
    blocks = refs[:n]
    keep, send = refs[-2:]
    half = n // 2
    rows = blocks[0].shape[1]

    def put(out, at, block):
        if turned:
            out[pl.ds(pl.multiple_of(at * rows, rows), rows)] = block[...].astype(F32).T.astype(BF16)
        else:
            out[at] = block[...]

    def split(kept, sent):
        for m in range(half):
            at = (idx[0] ^ m) & (half - 1)
            put(keep, at, blocks[kept + m])
            put(send, at, blocks[sent + m])

    @pl.when(idx[1] == 0)
    def _():
        split(0, half)

    @pl.when(idx[1] != 0)
    def _():
        split(half, 0)


def halves(name, turned, idx, blocks, after):
    n, rows = len(blocks), blocks[0].shape[1]
    shape = (n // 2 * rows, CELLS) if turned else (n // 2, CELLS, rows)
    return pl.pallas_call(
        functools.partial(halves_kernel, n, turned),
        in_specs=[smem()]
        + [pl.BlockSpec(memory_space=pltpu.VMEM)] * n
        + [UNREAD] * len(after),
        out_shape=[jax.ShapeDtypeStruct(shape, BF16)] * 2,
        compiler_params=pltpu.CompilerParams(vmem_limit_bytes=LIMIT),
        cost_estimate=LIGHT,
        name=name,
    )(idx, *blocks, *after)


def moved_first_kernel(own, other, _, out):
    for which, ref in enumerate((own, other)):
        cells = ref[...].astype(F32)
        at = lax.broadcasted_iota(jnp.int32, cells.shape, 1)
        height_at, width_at = at // WIDTH % HEIGHT, at % WIDTH
        rows = cells.shape[0]
        for k in range(9):
            b, c = k // 3 - 1, k % 3 - 1
            off = b * WIDTH + c
            part = cells if off == 0 else pltpu.roll(cells, (-off) % CELLS, 1)
            inside = (height_at + b >= 0) & (height_at + b < HEIGHT)
            inside = inside & (width_at + c >= 0) & (width_at + c < WIDTH)
            out[which, k * rows : (k + 1) * rows] = jnp.where(inside, part, 0.0).astype(BF16)


def moved_second_kernel(own, other, _, out):
    out[...] = jnp.zeros_like(out)
    for which, ref in enumerate((own, other)):
        cells = ref[...].astype(F32).T
        width_at = lax.broadcasted_iota(jnp.int32, cells.shape, 0) % WIDTH
        for c in (-1, 0, 1):
            part = cells if c == 0 else pltpu.roll(cells, c % CELLS, 0)
            inside = (width_at - c >= 0) & (width_at - c < WIDTH)
            part = jnp.where(inside, part, 0.0).astype(BF16)
            out[which, 1 + c, :, 1 : 1 + HEIGHT] = part.reshape(
                DEPTH, HEIGHT, WIDTH, cells.shape[1]
            )


def moved_fields(kernel, name, shape, own, other, after):
    return pl.pallas_call(
        kernel,
        in_specs=[pl.BlockSpec(memory_space=pltpu.VMEM)] * 2 + [UNREAD],
        out_shape=jax.ShapeDtypeStruct(shape, BF16),
        compiler_params=pltpu.CompilerParams(vmem_limit_bytes=LIMIT),
        cost_estimate=LIGHT,
        name=name,
    )(own, other, after)


def split_rows(values):
    high = values.astype(BF16)
    low = (values - high.astype(F32)).astype(BF16)
    empty = jnp.zeros((EXTRA - 2, values.shape[1]), F32)
    return jnp.concatenate([high.astype(F32), low.astype(F32), empty], axis=0).astype(BF16)


def grad_first_kernel(a, moved, own, other, gain_part, *refs):
    out = refs[-1]
    half, rows = own.shape[0], own.shape[2]
    begin, count = max(0, -a) * PLANE, (DEPTH - abs(a)) * PLANE
    rhs = [
        jnp.concatenate([ref[j, begin : begin + count] for j in range(half)], axis=1)
        for ref in (own, other)
    ]
    for b in range(3):
        span = slice(3 * rows * b, 3 * rows * (b + 1))
        grads = None
        for which in range(2):
            lhs = moved[which, span, begin + a * PLANE : begin + a * PLANE + count]
            part = jnp.dot(lhs, rhs[which], preferred_element_type=F32)
            grads = part if grads is None else grads + part
        out[span] = grads.astype(BF16)
    filler = jnp.zeros((1, out.shape[1] - rows), F32)
    out[9 * rows :] = split_rows(jnp.concatenate([gain_part[...], filler], axis=1))


def grad_first(a, moved, own, other, gain_part, after):
    half, cells, rows = own.shape
    return pl.pallas_call(
        functools.partial(grad_first_kernel, a),
        in_specs=[pl.BlockSpec(memory_space=pltpu.VMEM)] * 4 + [UNREAD] * len(after),
        out_shape=jax.ShapeDtypeStruct((9 * rows + EXTRA, half * rows), BF16),
        compiler_params=pltpu.CompilerParams(vmem_limit_bytes=LIMIT),
        cost_estimate=LIGHT,
        name="grad_first",
    )(moved, own, other, gain_part, *after)


def grad_second_kernel(a, moved, own, other, *refs):
    out = refs[-1]
    rows = out.shape[2]
    begin, planes = max(0, a), DEPTH - abs(a)
    lhs = [
        ref[:, begin * PLANE : (begin + planes) * PLANE] for ref in (own, other)
    ]
    for k in range(0, 9, 2):
        taps = range(k, min(k + 2, 9))
        grads = None
        for which in range(2):
            pieces = []
            for at in taps:
                b, c = at // 3 - 1, at % 3 - 1
                piece = moved[which, 1 + c, begin - a : begin - a + planes, 1 - b : 1 - b + HEIGHT]
                pieces.append(piece.reshape(planes * PLANE, rows))
            rhs = jnp.concatenate(pieces, axis=1)
            part = jnp.dot(lhs[which], rhs, preferred_element_type=F32)
            grads = part if grads is None else grads + part
        for place, at in enumerate(taps):
            out[at] = grads[:, place * rows : (place + 1) * rows].astype(BF16)


def grad_second(a, moved, own, other, after):
    wide, rows = own.shape[0], moved.shape[-1]
    return pl.pallas_call(
        functools.partial(grad_second_kernel, a),
        in_specs=[pl.BlockSpec(memory_space=pltpu.VMEM)] * 3 + [UNREAD] * len(after),
        out_shape=jax.ShapeDtypeStruct((9, wide, rows), BF16),
        compiler_params=pltpu.CompilerParams(vmem_limit_bytes=LIMIT),
        cost_estimate=LIGHT,
        name="grad_second",
    )(moved, own, other, *after)


def finish_kernel(n, axis, factor, chunk, idx, own, other, *refs):
    out, mark, wide, sems = refs[-4:]
    upper = (idx[0] >= n // 2).astype(jnp.int32) ^ idx[1]
    taps, height, width = wide.shape[1:]
    copies = []
    for k, (part, place) in enumerate(((own, upper), (other, 1 - upper))):
        size = (height, width)[axis - 1]
        span = pl.ds(pl.multiple_of(place * size, size), size)
        for third in range(3):
            at = slice(3 * third, 3 * third + 3)
            if len(part.shape) == 2:
                rows = part[3 * third * height : (3 * third + 3) * height]
                rows = rows.reshape(3, height, width)
            else:
                rows = part[at]
            wide[k, at] = rows.astype(F32) * factor
            target = out.at[pl.ds(chunk * taps + 3 * third, 3)]
            target = target.at[:, span] if axis == 1 else target.at[:, :, span]
            copies.append(
                pltpu.make_async_copy(wide.at[k, at], target, sems.at[3 * k + third])
            )
            copies[-1].start()
    mark[...] = jnp.zeros_like(mark)
    for copy in copies:
        copy.wait()


def finish(name, n, axis, factor, idx, chunk, shape, own, other, before, after):
    taps, height, width = shape
    given = [] if before is None else [before]
    full = (27, height * 2, width) if axis == 1 else (27, height, width * 2)
    return pl.pallas_call(
        functools.partial(finish_kernel, n, axis, factor, chunk),
        in_specs=[smem()]
        + [pl.BlockSpec(memory_space=pltpu.VMEM)] * 2
        + [UNREAD] * (len(given) + len(after)),
        out_specs=[UNREAD, pl.BlockSpec(memory_space=pltpu.VMEM)],
        out_shape=[jax.ShapeDtypeStruct(full, F32), jax.ShapeDtypeStruct((8, 128), F32)],
        scratch_shapes=[pltpu.VMEM((2,) + shape, F32), pltpu.SemaphoreType.DMA((6,))],
        input_output_aliases={3: 0} if given else {},
        compiler_params=pltpu.CompilerParams(vmem_limit_bytes=SMALL),
        cost_estimate=LIGHT,
        name=name,
    )(idx, own, other, *given, *after)


def add_kernel(x, y, *refs):
    out = refs[-1]
    if len(x.shape) == 3:
        out[...] = (x[...].astype(F32) + y[...].astype(F32)).astype(BF16)
    else:
        rows = x.shape[0] - EXTRA
        out[:rows] = (x[:rows].astype(F32) + y[:rows].astype(F32)).astype(BF16)
        tail = x[rows:].astype(F32) + y[rows:].astype(F32)
        out[rows:] = split_rows(tail[:1] + tail[1:2])


def pick_kernel(idx, x, y, *refs):
    out = refs[-1]

    @pl.when(idx[2] == 0)
    def _():
        out[...] = x[...]

    @pl.when(idx[2] != 0)
    def _():
        out[...] = y[...]


def whole_call(kernel, name, x, y, after, idx=None):
    given = [] if idx is None else [idx]
    return pl.pallas_call(
        kernel,
        in_specs=[smem()] * len(given)
        + [pl.BlockSpec(memory_space=pltpu.VMEM)] * 2
        + [UNREAD] * len(after),
        out_shape=jax.ShapeDtypeStruct(x.shape, x.dtype),
        compiler_params=pltpu.CompilerParams(vmem_limit_bytes=SMALL),
        cost_estimate=LIGHT,
        name=name,
    )(*given, x, y, *after)


def line_moves(chips):
    inward = [[(h, h + 1), (chips - 1 - h, chips - 2 - h)] for h in range(chips // 2 - 1)]
    mid = chips // 2
    outward = [[(j, i) for i, j in moves] for moves in reversed(inward)]
    return inward + [[(mid - 1, mid), (mid, mid - 1)]], outward


def line_send(x, moves):
    pairs = [(2 * i + k, 2 * j + k) for i, j in moves for k in (0, 1)]
    return lax.ppermute(x, "dp", pairs)


def line_step(step, part, total, idx, place, after):
    sums, outward = line_moves(lax.axis_size("dp") // 2)
    if step < len(sums):
        got = line_send(total, sums[step])
        base = total if step == len(sums) - 1 else part
        return whole_call(add_kernel, "line_add", base, got, after)
    moves = outward[step - len(sums)]
    got = line_send(total, moves)
    takes = functools.reduce(jnp.logical_or, [place // 2 == j for _, j in moves])
    marked = jnp.stack([idx[0], idx[1], takes.astype(jnp.int32)])
    return whole_call(pick_kernel, "line_pick", total, got, after, marked)


def shards(volume, w_first, gain, w_second, cotangent):
    n = lax.axis_size("chan")
    rows = volume.shape[1]
    vol, cot = volume[0], cotangent[0]
    chan, place = lax.axis_index("chan"), lax.axis_index("dp")
    idx = jnp.stack([chan, place % 2]).astype(jnp.int32)
    own_gain = lax.dynamic_slice_in_dim(gain, chan * rows, rows, 0)[None]
    factor = 1.0 / math.sqrt(lax.axis_size("dp") * CELLS)

    def to_partner(x, m):
        return lax.ppermute(x, "chan", [(i, i ^ m) for i in range(n)])

    def to_core(x):
        return lax.ppermute(x, "dp", [(i, i ^ 1) for i in range(lax.axis_size("dp"))])

    def swap(parts):
        got = {m: to_partner(parts[m], m) for m in reversed(range(1, n))}
        return [parts[0]] + [got[m] for m in range(1, n)]

    first_flat = w_first.reshape(27 * rows, n * rows)
    pre_shares = swap(spread_shares(1, "pre", idx, n, vol, first_flat, LARGE))
    dact_parts = spread_shares(-1, "dact", idx, n, cot, w_second, LIMIT)
    held = dact_parts[1:]
    act, normed, inverse, *held = pl.pallas_call(
        functools.partial(norm_kernel, n),
        in_specs=[pl.BlockSpec(memory_space=pltpu.VMEM)] * (1 + n) + [UNREAD] * len(held),
        out_specs=[pl.BlockSpec(memory_space=pltpu.VMEM)] * 3 + [UNREAD] * len(held),
        out_shape=[
            jax.ShapeDtypeStruct((CELLS, rows), BF16),
            jax.ShapeDtypeStruct((CELLS, rows), F32),
            jax.ShapeDtypeStruct((1, rows), F32),
        ]
        + [jax.ShapeDtypeStruct(x.shape, x.dtype) for x in held],
        input_output_aliases={1 + n + k: 3 + k for k in range(len(held))},
        compiler_params=pltpu.CompilerParams(vmem_limit_bytes=SMALL),
        cost_estimate=LIGHT,
        name="norm",
    )(own_gain, *pre_shares, *held)
    act_blocks = swap([act] * n)
    dact_shares = swap([dact_parts[0]] + held)
    moved_cot = moved_fields(
        moved_second_kernel,
        "moved_second",
        (2, 3, DEPTH, HEIGHT + 2, WIDTH, rows),
        cot,
        to_core(cot),
        act,
    )
    vol_other = to_core(vol)
    act_keep, act_send = halves("act_halves", True, idx, act_blocks, (moved_cot,))
    act_other = to_core(act_send)

    sums, outward = line_moves(lax.axis_size("dp") // 2)
    steps = len(sums) + len(outward)
    parts, totals, crossed = {}, {}, {}
    last = ()

    def line(chunk, step):
        nonlocal last
        before = totals.get(chunk, parts[chunk])
        totals[chunk] = line_step(step, parts[chunk], before, idx, place, last)
        last = (totals[chunk],)
        if step == steps - 1:
            crossed[chunk] = to_core(totals[chunk])

    def write(chunk):
        nonlocal last
        name, axis = ("finish_second", 1) if chunk < 3 else ("finish_first", 2)
        shape = (9, n // 2 * rows, rows) if chunk < 3 else (9, rows, n // 2 * rows)
        written[axis], mark = finish(
            name,
            n,
            axis,
            factor,
            idx,
            chunk % 3,
            shape,
            totals[chunk],
            crossed[chunk],
            written.get(axis),
            last,
        )
        last = (mark,)

    def second_part(chunk):
        nonlocal last
        parts[chunk] = grad_second(chunk - 1, moved_cot, act_keep, act_other, last)
        last = (parts[chunk],)

    def first_part(chunk):
        nonlocal last
        own, other = done["dpre_halves"]
        parts[chunk] = grad_first(chunk - 4, done["moved"], own, other, done["gain"], last)
        last = (parts[chunk],)

    def norm_back():
        nonlocal last
        dpre, done["gain"] = pl.pallas_call(
            functools.partial(norm_back_kernel, n),
            in_specs=[pl.BlockSpec(memory_space=pltpu.VMEM)] * (3 + n) + [UNREAD],
            out_shape=[
                jax.ShapeDtypeStruct((CELLS, rows), BF16),
                jax.ShapeDtypeStruct((1, rows), F32),
            ],
            compiler_params=pltpu.CompilerParams(vmem_limit_bytes=SMALL),
            cost_estimate=LIGHT,
            name="norm_back",
        )(own_gain, normed, inverse, *dact_shares, *last)
        done["dpre"] = swap([dpre] * n)
        done["moved"] = moved_fields(
            moved_first_kernel, "moved_first", (2, 9 * rows, CELLS), vol, vol_other, dpre
        )
        last = (done["moved"],)

    def dpre_halves():
        nonlocal last
        keep, send = halves("dpre_halves", False, idx, done["dpre"], last)
        done["dpre_halves"] = keep, to_core(send)
        last = (keep,)

    def output():
        nonlocal last
        done["output"], mark = conv_full("output", 1, False, idx, w_second, act_blocks, last)
        last = (mark,)

    def grad_volume():
        nonlocal last
        done["grad_volume"], mark = conv_full(
            "grad_volume", -1, True, idx, first_flat, done["dpre"], last
        )
        last = (mark,)

    def wave(at):
        for step in range(steps):
            if 0 <= at - step < 6:
                line(at - step, step)
        if 0 <= at - steps < 6:
            write(at - steps)

    written, done = {}, {}
    second_part(0)
    second_part(1)
    output()
    norm_back()
    line(0, 0)
    dpre_halves()
    second_part(2)
    line(1, 0)
    first_part(3)
    line(0, 1)
    line(2, 0)
    first_part(4)
    line(1, 1)
    for step in range(2, steps):
        line(0, step)
    line(3, 0)
    first_part(5)
    line(2, 1)
    for step in range(2, steps):
        line(1, step)
    write(0)
    line(4, 0)
    line(3, 1)
    for step in range(2, steps):
        line(2, step)
    write(1)
    line(5, 0)
    line(4, 1)
    for step in range(2, steps):
        line(3, step)
    write(2)
    grad_volume()
    line(5, 1)
    for step in range(2, steps):
        line(4, step)
    write(3)
    write(4)
    for step in range(2, steps):
        line(5, step)
    write(5)
    gain_rows = totals[3][9 * rows : 9 * rows + 2, :rows].astype(F32)
    gain_rows_other = crossed[3][9 * rows : 9 * rows + 2, :rows].astype(F32)
    gain_total = (jnp.sum(gain_rows, axis=0) + jnp.sum(gain_rows_other, axis=0)) * factor
    return (done["output"][None], done["grad_volume"][None], written[2], gain_total, written[1])


def solution(mesh):
    placed = (
        P("dp", "chan", None),
        P(None, "chan", None),
        P(),
        P(None, None, "chan"),
        P("dp", "chan", None),
    )
    return jax.shard_map(
        shards,
        mesh=mesh,
        in_specs=placed,
        out_specs=(
            P("dp", "chan", None),
            P("dp", "chan", None),
            P(None, "chan", None),
            P("chan"),
            P(None, None, "chan"),
        ),
        check_vma=False,
    )
```

```python
import functools
import math

import jax
import jax.numpy as jnp
from jax import lax
from jax.experimental import pallas as pl
from jax.experimental.pallas import tpu as pltpu
from jax.sharding import PartitionSpec as P

DEPTH, HEIGHT, WIDTH = 4, 16, 16
PLANE = HEIGHT * WIDTH
CELLS = DEPTH * PLANE
TAPS = [(a, b, c) for a in (-1, 0, 1) for b in (-1, 0, 1) for c in (-1, 0, 1)]
NORM_EPS = 1e-05
LIMIT = 16 * 1024 * 1024
SMALL = 8 * 1024 * 1024
LARGE = 59 * 1024 * 1024
EXTRA = 16
F32, BF16 = jnp.float32, jnp.bfloat16
NT = (((1,), (1,)), ((), ()))
UNREAD = pl.BlockSpec(memory_space=pl.ANY)
IN_HBM = pl.BlockSpec(memory_space=pltpu.HBM)
PLANE_ORDER = (0, -1, 1)
LIGHT = pl.CostEstimate(flops=1024, bytes_accessed=1024, transcendentals=0)


def params():
    return pltpu.CompilerParams(
        dimension_semantics=("arbitrary",), vmem_limit_bytes=LIMIT
    )


def whole(shape):
    return pl.BlockSpec(shape, lambda *_: (0,) * len(shape))


def smem():
    return pl.BlockSpec(memory_space=pltpu.SMEM)


def fill_padded(padded, rows_first, sign):
    padded[...] = jnp.zeros_like(padded)
    cells = rows_first.astype(F32).T
    width_at = lax.broadcasted_iota(jnp.int32, cells.shape, 0) % WIDTH
    for c in (-1, 0, 1):
        off = sign * c
        moved = cells if off == 0 else pltpu.roll(cells, (-off) % CELLS, 0)
        inside = (width_at + off >= 0) & (width_at + off < WIDTH)
        moved = jnp.where(inside, moved, 0.0).astype(BF16)
        padded[1 + c, 1 : 1 + DEPTH, 1 : 1 + HEIGHT] = moved.reshape(
            DEPTH, HEIGHT, WIDTH, cells.shape[1]
        )


def span_of(a, sign):
    return max(0, -sign * a), DEPTH - abs(a)


def start_parts(source, buffer, sems):
    size = source.shape[0] // 3
    copies = {}
    for a in PLANE_ORDER:
        span = pl.ds((a + 1) * size, size)
        copies[a] = pltpu.make_async_copy(source.at[span], buffer.at[span], sems.at[a + 1])
        copies[a].start()
    return copies


def share_kernel(n, sign, idx, field, w, *refs):
    outs = refs[:n]
    padded, sums, shares, buffer, sems = refs[n:]
    rows = field.shape[0]
    copies = start_parts(w, buffer, sems)
    fill_padded(padded, field[...], sign)
    for a in PLANE_ORDER:
        begin, planes = span_of(a, sign)
        pieces = []
        for b in (-1, 0, 1):
            for c in (-1, 0, 1):
                low, first = 1 + sign * b, 1 + begin + sign * a
                piece = padded[1 + c, first : first + planes, low : low + HEIGHT]
                pieces.append(piece.reshape(planes * PLANE, rows))
        lhs = jnp.concatenate(pieces, axis=1)
        copies[a].wait()
        if sign == 1:
            rhs = buffer[(a + 1) * 9 * rows : (a + 2) * 9 * rows]
            part = jnp.dot(lhs, rhs, preferred_element_type=F32)
        else:
            rhs = jnp.concatenate([buffer[(a + 1) * 9 + k] for k in range(9)], axis=1)
            part = lax.dot_general(lhs, rhs, NT, preferred_element_type=F32)
        span = slice(begin * PLANE, (begin + planes) * PLANE)
        if a == 0:
            sums[...] = part
        else:
            sums[span] += part
    for j in range(n):
        shares[j] = sums[:, j * rows : (j + 1) * rows].astype(BF16)
    for m in range(n):
        outs[m][...] = shares[idx[0] ^ m]


def spread_shares(sign, name, idx, n, field, w, limit):
    rows = field.shape[0]
    return pl.pallas_call(
        functools.partial(share_kernel, n, sign),
        in_specs=[smem(), pl.BlockSpec(memory_space=pltpu.VMEM), IN_HBM],
        out_specs=[pl.BlockSpec(memory_space=pltpu.VMEM)] * n,
        out_shape=[jax.ShapeDtypeStruct((CELLS, rows), BF16)] * n,
        scratch_shapes=[
            pltpu.VMEM((3, DEPTH + 2, HEIGHT + 2, WIDTH, rows), BF16),
            pltpu.VMEM((CELLS, n * rows), F32),
            pltpu.VMEM((n, CELLS, rows), BF16),
            pltpu.VMEM(w.shape, BF16),
            pltpu.SemaphoreType.DMA((3,)),
        ],
        compiler_params=pltpu.CompilerParams(vmem_limit_bytes=limit),
        cost_estimate=LIGHT,
        name=name,
    )(idx, field, w)


def norm_kernel(n, gain, *refs):
    shares = refs[:n]
    act, normed_out, inverse_out = refs[2 * n - 1 : 2 * n + 2]
    pre = shares[0][...].astype(F32)
    for m in range(1, n):
        pre = pre + shares[m][...].astype(F32)
    center = pre - jnp.mean(pre, axis=0, keepdims=True)
    inverse = lax.rsqrt(jnp.mean(center * center, axis=0, keepdims=True) + NORM_EPS)
    normed = center * inverse
    scaled = gain[...] * normed
    act[...] = (scaled * jax.nn.sigmoid(scaled)).astype(BF16)
    normed_out[...] = normed
    inverse_out[...] = inverse


def norm_back_kernel(n, gain, normed_in, inverse, *refs):
    shares = refs[:n]
    dpre, gain_part = refs[-2:]
    dact = shares[0][...].astype(F32)
    for m in range(1, n):
        dact = dact + shares[m][...].astype(F32)
    normed = normed_in[...]
    scaled = gain[...] * normed
    sigma = jax.nn.sigmoid(scaled)
    dscaled = dact * sigma * (1.0 + scaled * (1.0 - sigma))
    product = dscaled * normed
    gain_part[...] = jnp.sum(product, axis=0, keepdims=True)
    dnormed = gain[...] * dscaled
    mean_first = jnp.mean(dnormed, axis=0, keepdims=True)
    mean_second = jnp.mean(dnormed * normed, axis=0, keepdims=True)
    dpre[...] = ((dnormed - mean_first - normed * mean_second) * inverse[...]).astype(BF16)


def conv_back_add(sums, products, begin, planes, taps, rows, sign):
    for at, tap in enumerate(taps):
        a, b, c = tap
        a, b = sign * a, sign * b
        part = products[:, at * rows : (at + 1) * rows].reshape(planes, HEIGHT, WIDTH, rows)
        low, high = max(0, b), HEIGHT + min(0, b)
        sums[1 + c, begin - a : begin - a + planes, low - b : high - b] += part[:, low:high]


def conv_finish(sums, out, sign):
    rows = out.shape[0]
    total = None
    for c in (-1, 0, 1):
        off = sign * c
        part = sums[1 + c].reshape(CELLS, rows)
        if off != 0:
            width_at = lax.broadcasted_iota(jnp.int32, part.shape, 0) % WIDTH
            inside = (width_at + off >= 0) & (width_at + off < WIDTH)
            part = jnp.where(inside, pltpu.roll(part, (-off) % CELLS, 0), 0.0)
        total = part if total is None else total + part
    out[...] = total.T.astype(BF16)


def conv_kernel(n, sign, transposed, idx, w, *refs):
    blocks = refs[:n]
    out, mark, ordered, sums, buffer, sems = refs[-6:]
    mark[...] = jnp.zeros_like(mark)
    rows = out.shape[0]
    copies = start_parts(w, buffer, sems)
    sums[...] = jnp.zeros_like(sums)
    for m in range(n):
        ordered[idx[0] ^ m] = blocks[m][...]
    for a in PLANE_ORDER:
        begin, planes = span_of(-a, sign)
        span = slice(begin * PLANE, (begin + planes) * PLANE)
        lhs = jnp.concatenate([ordered[j, span] for j in range(n)], axis=1)
        copies[a].wait()
        for k in range(0, 9, 2):
            t = (a + 1) * 9 + k
            taps = TAPS[t : t + min(2, 9 - k)]
            if transposed:
                rhs = buffer[t * rows : (t + len(taps)) * rows]
                products = lax.dot_general(lhs, rhs, NT, preferred_element_type=F32)
            else:
                rhs = jnp.concatenate([buffer[t + at] for at in range(len(taps))], axis=1)
                products = jnp.dot(lhs, rhs, preferred_element_type=F32)
            conv_back_add(sums, products, begin, planes, taps, rows, sign)
    conv_finish(sums, out, sign)


def conv_full(name, sign, transposed, idx, w, blocks, after):
    n, rows = len(blocks), blocks[0].shape[1]
    return pl.pallas_call(
        functools.partial(conv_kernel, n, sign, transposed),
        in_specs=[smem(), IN_HBM]
        + [pl.BlockSpec(memory_space=pltpu.VMEM)] * n
        + [UNREAD] * len(after),
        out_specs=[pl.BlockSpec(memory_space=pltpu.VMEM)] * 2,
        out_shape=[
            jax.ShapeDtypeStruct((rows, CELLS), BF16),
            jax.ShapeDtypeStruct((8, 128), F32),
        ],
        scratch_shapes=[
            pltpu.VMEM((n, CELLS, rows), BF16),
            pltpu.VMEM((3, DEPTH, HEIGHT, WIDTH, rows), F32),
            pltpu.VMEM(w.shape, BF16),
            pltpu.SemaphoreType.DMA((3,)),
        ],
        compiler_params=pltpu.CompilerParams(vmem_limit_bytes=LIMIT),
        cost_estimate=LIGHT,
        name=name,
    )(idx, w, *blocks, *after)


def halves_kernel(n, turned, idx, *refs):
    blocks = refs[:n]
    keep, send = refs[-2:]
    half = n // 2
    rows = blocks[0].shape[1]

    def put(out, at, block):
        if turned:
            out[pl.ds(pl.multiple_of(at * rows, rows), rows)] = block[...].astype(F32).T.astype(BF16)
        else:
            out[at] = block[...]

    def split(kept, sent):
        for m in range(half):
            at = (idx[0] ^ m) & (half - 1)
            put(keep, at, blocks[kept + m])
            put(send, at, blocks[sent + m])

    @pl.when(idx[1] == 0)
    def _():
        split(0, half)

    @pl.when(idx[1] != 0)
    def _():
        split(half, 0)


def halves(name, turned, idx, blocks, after):
    n, rows = len(blocks), blocks[0].shape[1]
    shape = (n // 2 * rows, CELLS) if turned else (n // 2, CELLS, rows)
    return pl.pallas_call(
        functools.partial(halves_kernel, n, turned),
        in_specs=[smem()]
        + [pl.BlockSpec(memory_space=pltpu.VMEM)] * n
        + [UNREAD] * len(after),
        out_shape=[jax.ShapeDtypeStruct(shape, BF16)] * 2,
        compiler_params=pltpu.CompilerParams(vmem_limit_bytes=LIMIT),
        cost_estimate=LIGHT,
        name=name,
    )(idx, *blocks, *after)


def moved_second_kernel(own, other, _, out):
    out[...] = jnp.zeros_like(out)
    for which, ref in enumerate((own, other)):
        cells = ref[...].astype(F32).T
        width_at = lax.broadcasted_iota(jnp.int32, cells.shape, 0) % WIDTH
        for c in (-1, 0, 1):
            part = cells if c == 0 else pltpu.roll(cells, c % CELLS, 0)
            inside = (width_at - c >= 0) & (width_at - c < WIDTH)
            part = jnp.where(inside, part, 0.0).astype(BF16)
            out[which, 1 + c, :, 1 : 1 + HEIGHT] = part.reshape(
                DEPTH, HEIGHT, WIDTH, cells.shape[1]
            )


def moved_fields(kernel, name, shape, own, other, after):
    return pl.pallas_call(
        kernel,
        in_specs=[pl.BlockSpec(memory_space=pltpu.VMEM)] * 2 + [UNREAD],
        out_shape=jax.ShapeDtypeStruct(shape, BF16),
        compiler_params=pltpu.CompilerParams(vmem_limit_bytes=LIMIT),
        cost_estimate=LIGHT,
        name=name,
    )(own, other, after)


def split_rows(values):
    high = values.astype(BF16)
    low = (values - high.astype(F32)).astype(BF16)
    empty = jnp.zeros((EXTRA - 2, values.shape[1]), F32)
    return jnp.concatenate([high.astype(F32), low.astype(F32), empty], axis=0).astype(BF16)


def moved_lanes(cells, b, c):
    off = b * WIDTH + c
    if off == 0:
        return cells.astype(BF16)
    at = lax.broadcasted_iota(jnp.int32, cells.shape, 1)
    height_at, width_at = at // WIDTH % HEIGHT, at % WIDTH
    inside = (height_at + b >= 0) & (height_at + b < HEIGHT)
    inside = inside & (width_at + c >= 0) & (width_at + c < WIDTH)
    return jnp.where(inside, pltpu.roll(cells, (-off) % CELLS, 1), 0.0).astype(BF16)


def grad_first_kernel(vol_own, vol_other, own, other, gain_part, *refs):
    outs, moved = refs[-4:-1], refs[-1]
    half, rows = own.shape[0], own.shape[2]
    fields = [ref[...].astype(F32) for ref in (vol_own, vol_other)]
    rhs = [jnp.concatenate([ref[j] for j in range(half)], axis=1) for ref in (own, other)]
    for b in range(3):
        for which in range(2):
            for c in range(3):
                moved[which, c * rows : (c + 1) * rows] = moved_lanes(fields[which], b - 1, c - 1)
        for a in (-1, 0, 1):
            begin, count = max(0, -a) * PLANE, (DEPTH - abs(a)) * PLANE
            shift = begin + a * PLANE
            grads = None
            for which in range(2):
                lhs = moved[which, :, shift : shift + count]
                part = jnp.dot(lhs, rhs[which][begin : begin + count], preferred_element_type=F32)
                grads = part if grads is None else grads + part
            outs[a + 1][3 * rows * b : 3 * rows * (b + 1)] = grads.astype(BF16)
    filler = jnp.zeros((1, half * rows - rows), F32)
    outs[0][9 * rows :] = split_rows(jnp.concatenate([gain_part[...], filler], axis=1))
    for out in outs[1:]:
        out[9 * rows :] = jnp.zeros((EXTRA, half * rows), BF16)


def grad_first(vol_own, vol_other, own, other, gain_part, after):
    half, cells, rows = own.shape
    return pl.pallas_call(
        grad_first_kernel,
        in_specs=[pl.BlockSpec(memory_space=pltpu.VMEM)] * 5 + [UNREAD] * len(after),
        out_specs=[pl.BlockSpec(memory_space=pltpu.VMEM)] * 3,
        out_shape=[jax.ShapeDtypeStruct((9 * rows + EXTRA, half * rows), BF16)] * 3,
        scratch_shapes=[pltpu.VMEM((2, 3 * rows, CELLS), BF16)],
        compiler_params=pltpu.CompilerParams(vmem_limit_bytes=LIMIT),
        cost_estimate=LIGHT,
        name="grad_first",
    )(vol_own, vol_other, own, other, gain_part, *after)


def grad_second_kernel(a, moved, own, other, *refs):
    out = refs[-1]
    rows = out.shape[2]
    begin, planes = max(0, a), DEPTH - abs(a)
    lhs = [
        ref[:, begin * PLANE : (begin + planes) * PLANE] for ref in (own, other)
    ]
    for k in range(0, 9, 2):
        taps = range(k, min(k + 2, 9))
        grads = None
        for which in range(2):
            pieces = []
            for at in taps:
                b, c = at // 3 - 1, at % 3 - 1
                piece = moved[which, 1 + c, begin - a : begin - a + planes, 1 - b : 1 - b + HEIGHT]
                pieces.append(piece.reshape(planes * PLANE, rows))
            rhs = jnp.concatenate(pieces, axis=1)
            part = jnp.dot(lhs[which], rhs, preferred_element_type=F32)
            grads = part if grads is None else grads + part
        for place, at in enumerate(taps):
            out[at] = grads[:, place * rows : (place + 1) * rows].astype(BF16)


def grad_second(a, moved, own, other, after):
    wide, rows = own.shape[0], moved.shape[-1]
    return pl.pallas_call(
        functools.partial(grad_second_kernel, a),
        in_specs=[pl.BlockSpec(memory_space=pltpu.VMEM)] * 3 + [UNREAD] * len(after),
        out_shape=jax.ShapeDtypeStruct((9, wide, rows), BF16),
        compiler_params=pltpu.CompilerParams(vmem_limit_bytes=LIMIT),
        cost_estimate=LIGHT,
        name="grad_second",
    )(moved, own, other, *after)


def finish_kernel(n, axis, factor, chunk, idx, own, other, *refs):
    out, mark, wide, sems = refs[-4:]
    upper = (idx[0] >= n // 2).astype(jnp.int32) ^ idx[1]
    taps, height, width = wide.shape[1:]
    copies = []
    for k, (part, place) in enumerate(((own, upper), (other, 1 - upper))):
        size = (height, width)[axis - 1]
        span = pl.ds(pl.multiple_of(place * size, size), size)
        for third in range(3):
            at = slice(3 * third, 3 * third + 3)
            if len(part.shape) == 2:
                rows = part[3 * third * height : (3 * third + 3) * height]
                rows = rows.reshape(3, height, width)
            else:
                rows = part[at]
            wide[k, at] = rows.astype(F32) * factor
            target = out.at[pl.ds(chunk * taps + 3 * third, 3)]
            target = target.at[:, span] if axis == 1 else target.at[:, :, span]
            copies.append(
                pltpu.make_async_copy(wide.at[k, at], target, sems.at[3 * k + third])
            )
            copies[-1].start()
    mark[...] = jnp.zeros_like(mark)
    for copy in copies:
        copy.wait()


def finish(name, n, axis, factor, idx, chunk, shape, own, other, before, after):
    taps, height, width = shape
    given = [] if before is None else [before]
    full = (27, height * 2, width) if axis == 1 else (27, height, width * 2)
    return pl.pallas_call(
        functools.partial(finish_kernel, n, axis, factor, chunk),
        in_specs=[smem()]
        + [pl.BlockSpec(memory_space=pltpu.VMEM)] * 2
        + [UNREAD] * (len(given) + len(after)),
        out_specs=[UNREAD, pl.BlockSpec(memory_space=pltpu.VMEM)],
        out_shape=[jax.ShapeDtypeStruct(full, F32), jax.ShapeDtypeStruct((8, 128), F32)],
        scratch_shapes=[pltpu.VMEM((2,) + shape, F32), pltpu.SemaphoreType.DMA((6,))],
        input_output_aliases={3: 0} if given else {},
        compiler_params=pltpu.CompilerParams(vmem_limit_bytes=SMALL),
        cost_estimate=LIGHT,
        name=name,
    )(idx, own, other, *given, *after)


def add_kernel(x, y, *refs):
    out = refs[-1]
    if len(x.shape) == 3:
        out[...] = (x[...].astype(F32) + y[...].astype(F32)).astype(BF16)
    else:
        rows = x.shape[0] - EXTRA
        out[:rows] = (x[:rows].astype(F32) + y[:rows].astype(F32)).astype(BF16)
        tail = x[rows:].astype(F32) + y[rows:].astype(F32)
        out[rows:] = split_rows(tail[:1] + tail[1:2])


def pick_kernel(idx, x, y, *refs):
    out = refs[-1]

    @pl.when(idx[2] == 0)
    def _():
        out[...] = x[...]

    @pl.when(idx[2] != 0)
    def _():
        out[...] = y[...]


def whole_call(kernel, name, x, y, after, idx=None):
    given = [] if idx is None else [idx]
    return pl.pallas_call(
        kernel,
        in_specs=[smem()] * len(given)
        + [pl.BlockSpec(memory_space=pltpu.VMEM)] * 2
        + [UNREAD] * len(after),
        out_shape=jax.ShapeDtypeStruct(x.shape, x.dtype),
        compiler_params=pltpu.CompilerParams(vmem_limit_bytes=SMALL),
        cost_estimate=LIGHT,
        name=name,
    )(*given, x, y, *after)


def line_moves(chips):
    inward = [[(h, h + 1), (chips - 1 - h, chips - 2 - h)] for h in range(chips // 2 - 1)]
    mid = chips // 2
    outward = [[(j, i) for i, j in moves] for moves in reversed(inward)]
    return inward + [[(mid - 1, mid), (mid, mid - 1)]], outward


def line_send(x, moves):
    pairs = [(2 * i + k, 2 * j + k) for i, j in moves for k in (0, 1)]
    return lax.ppermute(x, "dp", pairs)


def line_step(step, part, total, idx, place, after):
    sums, outward = line_moves(lax.axis_size("dp") // 2)
    if step < len(sums):
        got = line_send(total, sums[step])
        base = total if step == len(sums) - 1 else part
        return whole_call(add_kernel, "line_add", base, got, after)
    moves = outward[step - len(sums)]
    got = line_send(total, moves)
    takes = functools.reduce(jnp.logical_or, [place // 2 == j for _, j in moves])
    marked = jnp.stack([idx[0], idx[1], takes.astype(jnp.int32)])
    return whole_call(pick_kernel, "line_pick", total, got, after, marked)


def shards(volume, w_first, gain, w_second, cotangent):
    n = lax.axis_size("chan")
    rows = volume.shape[1]
    vol, cot = volume[0], cotangent[0]
    chan, place = lax.axis_index("chan"), lax.axis_index("dp")
    idx = jnp.stack([chan, place % 2]).astype(jnp.int32)
    own_gain = lax.dynamic_slice_in_dim(gain, chan * rows, rows, 0)[None]
    factor = 1.0 / math.sqrt(lax.axis_size("dp") * CELLS)

    def to_partner(x, m):
        return lax.ppermute(x, "chan", [(i, i ^ m) for i in range(n)])

    def to_core(x):
        return lax.ppermute(x, "dp", [(i, i ^ 1) for i in range(lax.axis_size("dp"))])

    def swap(parts):
        got = {m: to_partner(parts[m], m) for m in reversed(range(1, n))}
        return [parts[0]] + [got[m] for m in range(1, n)]

    first_flat = w_first.reshape(27 * rows, n * rows)
    pre_shares = swap(spread_shares(1, "pre", idx, n, vol, first_flat, LARGE))
    dact_parts = spread_shares(-1, "dact", idx, n, cot, w_second, LIMIT)
    held = dact_parts[1:]
    act, normed, inverse, *held = pl.pallas_call(
        functools.partial(norm_kernel, n),
        in_specs=[pl.BlockSpec(memory_space=pltpu.VMEM)] * (1 + n) + [UNREAD] * len(held),
        out_specs=[pl.BlockSpec(memory_space=pltpu.VMEM)] * 3 + [UNREAD] * len(held),
        out_shape=[
            jax.ShapeDtypeStruct((CELLS, rows), BF16),
            jax.ShapeDtypeStruct((CELLS, rows), F32),
            jax.ShapeDtypeStruct((1, rows), F32),
        ]
        + [jax.ShapeDtypeStruct(x.shape, x.dtype) for x in held],
        input_output_aliases={1 + n + k: 3 + k for k in range(len(held))},
        compiler_params=pltpu.CompilerParams(vmem_limit_bytes=SMALL),
        cost_estimate=LIGHT,
        name="norm",
    )(own_gain, *pre_shares, *held)
    act_blocks = swap([act] * n)
    dact_shares = swap([dact_parts[0]] + held)
    moved_cot = moved_fields(
        moved_second_kernel,
        "moved_second",
        (2, 3, DEPTH, HEIGHT + 2, WIDTH, rows),
        cot,
        to_core(cot),
        act,
    )
    vol_other = to_core(vol)
    act_keep, act_send = halves("act_halves", True, idx, act_blocks, (moved_cot, vol_other))
    act_other = to_core(act_send)

    sums, outward = line_moves(lax.axis_size("dp") // 2)
    steps = len(sums) + len(outward)
    parts, totals, crossed = {}, {}, {}
    last = ()

    def line(chunk, step):
        nonlocal last
        before = totals.get(chunk, parts[chunk])
        totals[chunk] = line_step(step, parts[chunk], before, idx, place, last)
        last = (totals[chunk],)
        if step == steps - 1:
            crossed[chunk] = to_core(totals[chunk])

    def write(chunk):
        nonlocal last
        name, axis = ("finish_second", 1) if chunk < 3 else ("finish_first", 2)
        shape = (9, n // 2 * rows, rows) if chunk < 3 else (9, rows, n // 2 * rows)
        written[axis], mark = finish(
            name,
            n,
            axis,
            factor,
            idx,
            chunk % 3,
            shape,
            totals[chunk],
            crossed[chunk],
            written.get(axis),
            last,
        )
        last = (mark,)

    def second_part(chunk):
        nonlocal last
        parts[chunk] = grad_second(chunk - 1, moved_cot, act_keep, act_other, last)
        last = (parts[chunk],)

    def first_parts():
        nonlocal last
        own, other = done["dpre_halves"]
        parts[3], parts[4], parts[5] = grad_first(
            vol, vol_other, own, other, done["gain"], last
        )
        last = (parts[3],)

    def norm_back():
        nonlocal last
        dpre, done["gain"] = pl.pallas_call(
            functools.partial(norm_back_kernel, n),
            in_specs=[pl.BlockSpec(memory_space=pltpu.VMEM)] * (3 + n) + [UNREAD],
            out_shape=[
                jax.ShapeDtypeStruct((CELLS, rows), BF16),
                jax.ShapeDtypeStruct((1, rows), F32),
            ],
            compiler_params=pltpu.CompilerParams(vmem_limit_bytes=SMALL),
            cost_estimate=LIGHT,
            name="norm_back",
        )(own_gain, normed, inverse, *dact_shares, *last)
        done["dpre"] = swap([dpre] * n)
        last = (dpre,)

    def dpre_halves():
        nonlocal last
        keep, send = halves("dpre_halves", False, idx, done["dpre"], last)
        done["dpre_halves"] = keep, to_core(send)
        last = (keep,)

    def output():
        nonlocal last
        done["output"], mark = conv_full("output", 1, False, idx, w_second, act_blocks, last)
        last = (mark,)

    def grad_volume():
        nonlocal last
        done["grad_volume"], mark = conv_full(
            "grad_volume", -1, True, idx, first_flat, done["dpre"], last
        )
        last = (mark,)

    def wave(at):
        for step in range(steps):
            if 0 <= at - step < 6:
                line(at - step, step)
        if 0 <= at - steps < 6:
            write(at - steps)

    written, done = {}, {}
    second_part(0)
    second_part(1)
    output()
    norm_back()
    line(0, 0)
    second_part(2)
    line(1, 0)
    line(0, 1)
    dpre_halves()
    first_parts()
    wave(2)
    wave(3)
    wave(4)
    wave(5)
    grad_volume()
    for at in range(6, 6 + steps):
        wave(at)
    gain_rows = totals[3][9 * rows : 9 * rows + 2, :rows].astype(F32)
    gain_rows_other = crossed[3][9 * rows : 9 * rows + 2, :rows].astype(F32)
    gain_total = (jnp.sum(gain_rows, axis=0) + jnp.sum(gain_rows_other, axis=0)) * factor
    return (done["output"][None], done["grad_volume"][None], written[2], gain_total, written[1])


def solution(mesh):
    placed = (
        P("dp", "chan", None),
        P(None, "chan", None),
        P(),
        P(None, None, "chan"),
        P("dp", "chan", None),
    )
    return jax.shard_map(
        shards,
        mesh=mesh,
        in_specs=placed,
        out_specs=(
            P("dp", "chan", None),
            P("dp", "chan", None),
            P(None, "chan", None),
            P("chan"),
            P(None, None, "chan"),
        ),
        check_vma=False,
    )
```

```python
import functools
import math

import jax
import jax.numpy as jnp
from jax import lax
from jax.experimental import pallas as pl
from jax.experimental.pallas import tpu as pltpu
from jax.sharding import PartitionSpec as P

DEPTH, HEIGHT, WIDTH = 4, 16, 16
PLANE = HEIGHT * WIDTH
CELLS = DEPTH * PLANE
TAPS = [(a, b, c) for a in (-1, 0, 1) for b in (-1, 0, 1) for c in (-1, 0, 1)]
NORM_EPS = 1e-05
LIMIT = 16 * 1024 * 1024
SMALL = 8 * 1024 * 1024
LARGE = 59 * 1024 * 1024
EXTRA = 16
F32, BF16 = jnp.float32, jnp.bfloat16
NT = (((1,), (1,)), ((), ()))
UNREAD = pl.BlockSpec(memory_space=pl.ANY)
IN_HBM = pl.BlockSpec(memory_space=pltpu.HBM)
PLANE_ORDER = (0, -1, 1)
LIGHT = pl.CostEstimate(flops=1024, bytes_accessed=1024, transcendentals=0)


def params():
    return pltpu.CompilerParams(
        dimension_semantics=("arbitrary",), vmem_limit_bytes=LIMIT
    )


def whole(shape):
    return pl.BlockSpec(shape, lambda *_: (0,) * len(shape))


def smem():
    return pl.BlockSpec(memory_space=pltpu.SMEM)


def fill_padded(padded, rows_first, sign):
    padded[...] = jnp.zeros_like(padded)
    cells = rows_first.astype(F32).T
    width_at = lax.broadcasted_iota(jnp.int32, cells.shape, 0) % WIDTH
    for c in (-1, 0, 1):
        off = sign * c
        moved = cells if off == 0 else pltpu.roll(cells, (-off) % CELLS, 0)
        inside = (width_at + off >= 0) & (width_at + off < WIDTH)
        moved = jnp.where(inside, moved, 0.0).astype(BF16)
        padded[1 + c, 1 : 1 + DEPTH, 1 : 1 + HEIGHT] = moved.reshape(
            DEPTH, HEIGHT, WIDTH, cells.shape[1]
        )


def span_of(a, sign):
    return max(0, -sign * a), DEPTH - abs(a)


def start_parts(source, buffer, sems):
    size = source.shape[0] // 3
    copies = {}
    for a in PLANE_ORDER:
        span = pl.ds((a + 1) * size, size)
        copies[a] = pltpu.make_async_copy(source.at[span], buffer.at[span], sems.at[a + 1])
        copies[a].start()
    return copies


def share_kernel(n, sign, wanted, idx, field, w, *refs):
    outs = refs[len(refs) - 4 - len(wanted) : -4]
    padded, sums, buffer, sems = refs[-4:]
    rows, wide = field.shape[0], sums.shape[1]
    split = len(wanted) < n
    half = (idx[0] >= n // 2).astype(jnp.int32) ^ (wanted[0] // (n // 2))
    if split:
        source = w.at[:, pl.ds(pl.multiple_of(half * wide, wide), wide)]
    else:
        source = w
    copies = start_parts(source, buffer, sems)
    fill_padded(padded, field[...], sign)
    for a in PLANE_ORDER:
        begin, planes = span_of(a, sign)
        pieces = []
        for b in (-1, 0, 1):
            for c in (-1, 0, 1):
                low, first = 1 + sign * b, 1 + begin + sign * a
                piece = padded[1 + c, first : first + planes, low : low + HEIGHT]
                pieces.append(piece.reshape(planes * PLANE, rows))
        lhs = jnp.concatenate(pieces, axis=1)
        copies[a].wait()
        if sign == 1:
            rhs = buffer[(a + 1) * 9 * rows : (a + 2) * 9 * rows]
            part = jnp.dot(lhs, rhs, preferred_element_type=F32)
        else:
            rhs = jnp.concatenate([buffer[(a + 1) * 9 + k] for k in range(9)], axis=1)
            part = lax.dot_general(lhs, rhs, NT, preferred_element_type=F32)
        span = slice(begin * PLANE, (begin + planes) * PLANE)
        if a == 0:
            sums[...] = part
        else:
            sums[span] += part
    count = len(wanted)

    def put(out, j):
        out[...] = sums[:, j * rows : (j + 1) * rows].astype(BF16)

    for out, m in zip(outs, wanted):
        at = (idx[0] ^ m) & (count - 1)
        for j in range(count):
            pl.when(at == j)(functools.partial(put, out, j))


def spread_shares(sign, name, idx, n, field, w, wanted, limit, after=()):
    rows, count = field.shape[0], len(wanted)
    wide = count * rows
    kept = (w.shape[0], wide) if count < n else w.shape
    return pl.pallas_call(
        functools.partial(share_kernel, n, sign, wanted),
        in_specs=[smem(), pl.BlockSpec(memory_space=pltpu.VMEM), IN_HBM]
        + [UNREAD] * len(after),
        out_specs=[pl.BlockSpec(memory_space=pltpu.VMEM)] * count,
        out_shape=[jax.ShapeDtypeStruct((CELLS, rows), BF16)] * count,
        scratch_shapes=[
            pltpu.VMEM((3, DEPTH + 2, HEIGHT + 2, WIDTH, rows), BF16),
            pltpu.VMEM((CELLS, wide), F32),
            pltpu.VMEM(kept, BF16),
            pltpu.SemaphoreType.DMA((3,)),
        ],
        compiler_params=pltpu.CompilerParams(vmem_limit_bytes=limit),
        cost_estimate=LIGHT,
        name=name,
    )(idx, field, w, *after)


def sum_kernel(x, y, *refs):
    out = refs[-1]
    out[...] = x[...].astype(F32) + y[...].astype(F32)


def sum_shares(name, x, y, after):
    return pl.pallas_call(
        sum_kernel,
        in_specs=[pl.BlockSpec(memory_space=pltpu.VMEM)] * 2 + [UNREAD] * len(after),
        out_shape=jax.ShapeDtypeStruct(x.shape, F32),
        compiler_params=pltpu.CompilerParams(vmem_limit_bytes=SMALL),
        cost_estimate=LIGHT,
        name=name,
    )(x, y, *after)


def norm_kernel(n, gain, *refs):
    shares = refs[: n - 1]
    act, normed_out, inverse_out = refs[-3:]
    pre = shares[0][...].astype(F32)
    for m in range(1, n - 1):
        pre = pre + shares[m][...].astype(F32)
    center = pre - jnp.mean(pre, axis=0, keepdims=True)
    inverse = lax.rsqrt(jnp.mean(center * center, axis=0, keepdims=True) + NORM_EPS)
    normed = center * inverse
    scaled = gain[...] * normed
    act[...] = (scaled * jax.nn.sigmoid(scaled)).astype(BF16)
    normed_out[...] = normed
    inverse_out[...] = inverse


def norm_back_kernel(n, gain, normed_in, inverse, *refs):
    shares = refs[: n - 1]
    dpre, gain_part = refs[-2:]
    dact = shares[0][...].astype(F32)
    for m in range(1, n - 1):
        dact = dact + shares[m][...].astype(F32)
    normed = normed_in[...]
    scaled = gain[...] * normed
    sigma = jax.nn.sigmoid(scaled)
    dscaled = dact * sigma * (1.0 + scaled * (1.0 - sigma))
    product = dscaled * normed
    gain_part[...] = jnp.sum(product, axis=0, keepdims=True)
    dnormed = gain[...] * dscaled
    mean_first = jnp.mean(dnormed, axis=0, keepdims=True)
    mean_second = jnp.mean(dnormed * normed, axis=0, keepdims=True)
    dpre[...] = ((dnormed - mean_first - normed * mean_second) * inverse[...]).astype(BF16)


def conv_back_add(sums, products, begin, planes, taps, rows, sign):
    for at, tap in enumerate(taps):
        a, b, c = tap
        a, b = sign * a, sign * b
        part = products[:, at * rows : (at + 1) * rows].reshape(planes, HEIGHT, WIDTH, rows)
        low, high = max(0, b), HEIGHT + min(0, b)
        sums[1 + c, begin - a : begin - a + planes, low - b : high - b] += part[:, low:high]


def conv_finish(sums, out, sign):
    rows = out.shape[0]
    total = None
    for c in (-1, 0, 1):
        off = sign * c
        part = sums[1 + c].reshape(CELLS, rows)
        if off != 0:
            width_at = lax.broadcasted_iota(jnp.int32, part.shape, 0) % WIDTH
            inside = (width_at + off >= 0) & (width_at + off < WIDTH)
            part = jnp.where(inside, pltpu.roll(part, (-off) % CELLS, 0), 0.0)
        total = part if total is None else total + part
    out[...] = total.T.astype(BF16)


def conv_kernel(n, sign, transposed, idx, w, *refs):
    blocks = refs[:n]
    out, mark, ordered, sums, buffer, sems = refs[-6:]
    mark[...] = jnp.zeros_like(mark)
    rows = out.shape[0]
    copies = start_parts(w, buffer, sems)
    sums[...] = jnp.zeros_like(sums)
    for m in range(n):
        ordered[idx[0] ^ m] = blocks[m][...]
    for a in PLANE_ORDER:
        begin, planes = span_of(-a, sign)
        span = slice(begin * PLANE, (begin + planes) * PLANE)
        lhs = jnp.concatenate([ordered[j, span] for j in range(n)], axis=1)
        copies[a].wait()
        for k in range(0, 9, 2):
            t = (a + 1) * 9 + k
            taps = TAPS[t : t + min(2, 9 - k)]
            if transposed:
                rhs = buffer[t * rows : (t + len(taps)) * rows]
                products = lax.dot_general(lhs, rhs, NT, preferred_element_type=F32)
            else:
                rhs = jnp.concatenate([buffer[t + at] for at in range(len(taps))], axis=1)
                products = jnp.dot(lhs, rhs, preferred_element_type=F32)
            conv_back_add(sums, products, begin, planes, taps, rows, sign)
    conv_finish(sums, out, sign)


def conv_full(name, sign, transposed, idx, w, blocks, after):
    n, rows = len(blocks), blocks[0].shape[1]
    return pl.pallas_call(
        functools.partial(conv_kernel, n, sign, transposed),
        in_specs=[smem(), IN_HBM]
        + [pl.BlockSpec(memory_space=pltpu.VMEM)] * n
        + [UNREAD] * len(after),
        out_specs=[pl.BlockSpec(memory_space=pltpu.VMEM)] * 2,
        out_shape=[
            jax.ShapeDtypeStruct((rows, CELLS), BF16),
            jax.ShapeDtypeStruct((8, 128), F32),
        ],
        scratch_shapes=[
            pltpu.VMEM((n, CELLS, rows), BF16),
            pltpu.VMEM((3, DEPTH, HEIGHT, WIDTH, rows), F32),
            pltpu.VMEM(w.shape, BF16),
            pltpu.SemaphoreType.DMA((3,)),
        ],
        compiler_params=pltpu.CompilerParams(vmem_limit_bytes=LIMIT),
        cost_estimate=LIGHT,
        name=name,
    )(idx, w, *blocks, *after)


def halves_kernel(n, turned, idx, *refs):
    blocks = refs[:n]
    keep, send = refs[-2:]
    half = n // 2
    rows = blocks[0].shape[1]

    def put(out, at, block):
        if turned:
            out[pl.ds(pl.multiple_of(at * rows, rows), rows)] = block[...].astype(F32).T.astype(BF16)
        else:
            out[at] = block[...]

    def split(kept, sent):
        for m in range(half):
            at = (idx[0] ^ m) & (half - 1)
            put(keep, at, blocks[kept + m])
            put(send, at, blocks[sent + m])

    @pl.when(idx[1] == 0)
    def _():
        split(0, half)

    @pl.when(idx[1] != 0)
    def _():
        split(half, 0)


def halves(name, turned, idx, blocks, after):
    n, rows = len(blocks), blocks[0].shape[1]
    shape = (n // 2 * rows, CELLS) if turned else (n // 2, CELLS, rows)
    return pl.pallas_call(
        functools.partial(halves_kernel, n, turned),
        in_specs=[smem()]
        + [pl.BlockSpec(memory_space=pltpu.VMEM)] * n
        + [UNREAD] * len(after),
        out_shape=[jax.ShapeDtypeStruct(shape, BF16)] * 2,
        compiler_params=pltpu.CompilerParams(vmem_limit_bytes=LIMIT),
        cost_estimate=LIGHT,
        name=name,
    )(idx, *blocks, *after)


def moved_second_kernel(own, other, _, out):
    out[...] = jnp.zeros_like(out)
    for which, ref in enumerate((own, other)):
        cells = ref[...].astype(F32).T
        width_at = lax.broadcasted_iota(jnp.int32, cells.shape, 0) % WIDTH
        for c in (-1, 0, 1):
            part = cells if c == 0 else pltpu.roll(cells, c % CELLS, 0)
            inside = (width_at - c >= 0) & (width_at - c < WIDTH)
            part = jnp.where(inside, part, 0.0).astype(BF16)
            out[which, 1 + c, :, 1 : 1 + HEIGHT] = part.reshape(
                DEPTH, HEIGHT, WIDTH, cells.shape[1]
            )


def moved_fields(kernel, name, shape, own, other, after):
    return pl.pallas_call(
        kernel,
        in_specs=[pl.BlockSpec(memory_space=pltpu.VMEM)] * 2 + [UNREAD],
        out_shape=jax.ShapeDtypeStruct(shape, BF16),
        compiler_params=pltpu.CompilerParams(vmem_limit_bytes=LIMIT),
        cost_estimate=LIGHT,
        name=name,
    )(own, other, after)


def split_rows(values):
    high = values.astype(BF16)
    low = (values - high.astype(F32)).astype(BF16)
    empty = jnp.zeros((EXTRA - 2, values.shape[1]), F32)
    return jnp.concatenate([high.astype(F32), low.astype(F32), empty], axis=0).astype(BF16)


def moved_lanes(cells, b, c):
    off = b * WIDTH + c
    if off == 0:
        return cells.astype(BF16)
    at = lax.broadcasted_iota(jnp.int32, cells.shape, 1)
    height_at, width_at = at // WIDTH % HEIGHT, at % WIDTH
    inside = (height_at + b >= 0) & (height_at + b < HEIGHT)
    inside = inside & (width_at + c >= 0) & (width_at + c < WIDTH)
    return jnp.where(inside, pltpu.roll(cells, (-off) % CELLS, 1), 0.0).astype(BF16)


def grad_first_kernel(vol_own, vol_other, own, other, gain_part, *refs):
    outs, moved = refs[-4:-1], refs[-1]
    half, rows = own.shape[0], own.shape[2]
    fields = [ref[...].astype(F32) for ref in (vol_own, vol_other)]
    rhs = [jnp.concatenate([ref[j] for j in range(half)], axis=1) for ref in (own, other)]
    for b in range(3):
        for which in range(2):
            for c in range(3):
                moved[which, c * rows : (c + 1) * rows] = moved_lanes(fields[which], b - 1, c - 1)
        for a in (-1, 0, 1):
            begin, count = max(0, -a) * PLANE, (DEPTH - abs(a)) * PLANE
            shift = begin + a * PLANE
            grads = None
            for which in range(2):
                lhs = moved[which, :, shift : shift + count]
                part = jnp.dot(lhs, rhs[which][begin : begin + count], preferred_element_type=F32)
                grads = part if grads is None else grads + part
            outs[a + 1][3 * rows * b : 3 * rows * (b + 1)] = grads.astype(BF16)
    filler = jnp.zeros((1, half * rows - rows), F32)
    outs[0][9 * rows :] = split_rows(jnp.concatenate([gain_part[...], filler], axis=1))
    for out in outs[1:]:
        out[9 * rows :] = jnp.zeros((EXTRA, half * rows), BF16)


def grad_first(vol_own, vol_other, own, other, gain_part, after):
    half, cells, rows = own.shape
    return pl.pallas_call(
        grad_first_kernel,
        in_specs=[pl.BlockSpec(memory_space=pltpu.VMEM)] * 5 + [UNREAD] * len(after),
        out_specs=[pl.BlockSpec(memory_space=pltpu.VMEM)] * 3,
        out_shape=[jax.ShapeDtypeStruct((9 * rows + EXTRA, half * rows), BF16)] * 3,
        scratch_shapes=[pltpu.VMEM((2, 3 * rows, CELLS), BF16)],
        compiler_params=pltpu.CompilerParams(vmem_limit_bytes=LIMIT),
        cost_estimate=LIGHT,
        name="grad_first",
    )(vol_own, vol_other, own, other, gain_part, *after)


def grad_second_kernel(offsets, moved, own, other, *refs):
    out = refs[-1]
    rows = out.shape[2]
    for which_a, a in enumerate(offsets):
        begin, planes = max(0, a), DEPTH - abs(a)
        lhs = [ref[:, begin * PLANE : (begin + planes) * PLANE] for ref in (own, other)]
        for k in range(0, 9, 2):
            taps = range(k, min(k + 2, 9))
            grads = None
            for which in range(2):
                pieces = []
                for at in taps:
                    b, c = at // 3 - 1, at % 3 - 1
                    first = begin - a
                    piece = moved[which, 1 + c, first : first + planes, 1 - b : 1 - b + HEIGHT]
                    pieces.append(piece.reshape(planes * PLANE, rows))
                rhs = jnp.concatenate(pieces, axis=1)
                part = jnp.dot(lhs[which], rhs, preferred_element_type=F32)
                grads = part if grads is None else grads + part
            for place, at in enumerate(taps):
                piece = grads[:, place * rows : (place + 1) * rows]
                out[9 * which_a + at] = piece.astype(BF16)


def grad_second(offsets, moved, own, other, after):
    wide, rows = own.shape[0], moved.shape[-1]
    return pl.pallas_call(
        functools.partial(grad_second_kernel, offsets),
        in_specs=[pl.BlockSpec(memory_space=pltpu.VMEM)] * 3 + [UNREAD] * len(after),
        out_shape=jax.ShapeDtypeStruct((9 * len(offsets), wide, rows), BF16),
        compiler_params=pltpu.CompilerParams(vmem_limit_bytes=LIMIT),
        cost_estimate=LIGHT,
        name="grad_second",
    )(moved, own, other, *after)


def finish_kernel(n, axis, factor, chunk, idx, own, other, *refs):
    out, mark, wide, sems = refs[-4:]
    upper = (idx[0] >= n // 2).astype(jnp.int32) ^ idx[1]
    taps, height, width = wide.shape[1:]
    copies = []
    for k, (part, place) in enumerate(((own, upper), (other, 1 - upper))):
        size = (height, width)[axis - 1]
        span = pl.ds(pl.multiple_of(place * size, size), size)
        for third in range(3):
            at = slice(3 * third, 3 * third + 3)
            if len(part.shape) == 2:
                rows = part[3 * third * height : (3 * third + 3) * height]
                rows = rows.reshape(3, height, width)
            else:
                rows = part[at]
            wide[k, at] = rows.astype(F32) * factor
            target = out.at[pl.ds(chunk * taps + 3 * third, 3)]
            target = target.at[:, span] if axis == 1 else target.at[:, :, span]
            copies.append(
                pltpu.make_async_copy(wide.at[k, at], target, sems.at[3 * k + third])
            )
            copies[-1].start()
    mark[...] = jnp.zeros_like(mark)
    for copy in copies:
        copy.wait()


def finish(name, n, axis, factor, idx, chunk, shape, own, other, before, after):
    taps, height, width = shape
    given = [] if before is None else [before]
    full = (27, height * 2, width) if axis == 1 else (27, height, width * 2)
    return pl.pallas_call(
        functools.partial(finish_kernel, n, axis, factor, chunk),
        in_specs=[smem()]
        + [pl.BlockSpec(memory_space=pltpu.VMEM)] * 2
        + [UNREAD] * (len(given) + len(after)),
        out_specs=[UNREAD, pl.BlockSpec(memory_space=pltpu.VMEM)],
        out_shape=[jax.ShapeDtypeStruct(full, F32), jax.ShapeDtypeStruct((8, 128), F32)],
        scratch_shapes=[pltpu.VMEM((2,) + shape, F32), pltpu.SemaphoreType.DMA((6,))],
        input_output_aliases={3: 0} if given else {},
        compiler_params=pltpu.CompilerParams(vmem_limit_bytes=SMALL),
        cost_estimate=LIGHT,
        name=name,
    )(idx, own, other, *given, *after)


def add_kernel(first, x, y, *refs):
    out = refs[-1]
    if len(x.shape) == 3:
        span = slice(first, first + out.shape[0])
        out[...] = (x[span].astype(F32) + y[span].astype(F32)).astype(BF16)
    else:
        rows = x.shape[0] - EXTRA
        out[:rows] = (x[:rows].astype(F32) + y[:rows].astype(F32)).astype(BF16)
        tail = x[rows:].astype(F32) + y[rows:].astype(F32)
        out[rows:] = split_rows(tail[:1] + tail[1:2])


def pick_kernel(idx, x, y, *refs):
    out = refs[-1]

    @pl.when(idx[2] == 0)
    def _():
        out[...] = x[...]

    @pl.when(idx[2] != 0)
    def _():
        out[...] = y[...]


def whole_call(kernel, name, shape, x, y, after, idx=None):
    given = [] if idx is None else [idx]
    return pl.pallas_call(
        kernel,
        in_specs=[smem()] * len(given)
        + [pl.BlockSpec(memory_space=pltpu.VMEM)] * 2
        + [UNREAD] * len(after),
        out_shape=jax.ShapeDtypeStruct(shape, BF16),
        compiler_params=pltpu.CompilerParams(vmem_limit_bytes=SMALL),
        cost_estimate=LIGHT,
        name=name,
    )(*given, x, y, *after)


def line_moves(chips):
    inward = [[(h, h + 1), (chips - 1 - h, chips - 2 - h)] for h in range(chips // 2 - 1)]
    mid = chips // 2
    outward = [[(j, i) for i, j in moves] for moves in reversed(inward)]
    return inward + [[(mid - 1, mid), (mid, mid - 1)]], outward


def line_send(x, moves):
    pairs = [(2 * i + k, 2 * j + k) for i, j in moves for k in (0, 1)]
    return lax.ppermute(x, "dp", pairs)


def line_step(step, part, first, got, total, idx, place, after):
    sums, outward = line_moves(lax.axis_size("dp") // 2)
    shape = total.shape
    if step < len(sums) - 1:
        add = functools.partial(add_kernel, first)
        return whole_call(add, "line_add", shape, part, got, after)
    if step == len(sums) - 1:
        return whole_call(functools.partial(add_kernel, 0), "line_add", shape, total, got, after)
    moves = outward[step - len(sums)]
    takes = functools.reduce(jnp.logical_or, [place // 2 == j for _, j in moves])
    marked = jnp.stack([idx[0], idx[1], takes.astype(jnp.int32)])
    return whole_call(pick_kernel, "line_pick", shape, total, got, after, marked)


def shards(volume, w_first, gain, w_second, cotangent):
    n = lax.axis_size("chan")
    rows = volume.shape[1]
    vol, cot = volume[0], cotangent[0]
    chan, place = lax.axis_index("chan"), lax.axis_index("dp")
    idx = jnp.stack([chan, place % 2]).astype(jnp.int32)
    own_gain = lax.dynamic_slice_in_dim(gain, chan * rows, rows, 0)[None]
    factor = 1.0 / math.sqrt(lax.axis_size("dp") * CELLS)

    def to_partner(x, m):
        return lax.ppermute(x, "chan", [(i, i ^ m) for i in range(n)])

    def to_core(x):
        return lax.ppermute(x, "dp", [(i, i ^ 1) for i in range(lax.axis_size("dp"))])

    def swap(parts):
        got = {m: to_partner(parts[m], m) for m in reversed(range(1, n))}
        return [parts[0]] + [got[m] for m in range(1, n)]

    first_flat = w_first.reshape(27 * rows, n * rows)
    far, near = tuple(range(n // 2, n)), tuple(range(n // 2))
    pre_far = spread_shares(1, "pre_far", idx, n, vol, first_flat, far, LARGE)
    pre_near = spread_shares(
        1, "pre_near", idx, n, vol, first_flat, near, LARGE, (pre_far[0],)
    )
    pre_shares = swap(pre_near + pre_far)
    pre_first = sum_shares("pre_sum", pre_shares[0], pre_shares[-1], ())
    act, normed, inverse = pl.pallas_call(
        functools.partial(norm_kernel, n),
        out_shape=[
            jax.ShapeDtypeStruct((CELLS, rows), BF16),
            jax.ShapeDtypeStruct((CELLS, rows), F32),
            jax.ShapeDtypeStruct((1, rows), F32),
        ],
        compiler_params=pltpu.CompilerParams(vmem_limit_bytes=SMALL),
        cost_estimate=LIGHT,
        name="norm",
    )(own_gain, pre_first, *pre_shares[1:-1])
    act_blocks = swap([act] * n)
    dact_parts = spread_shares(
        -1, "dact", idx, n, cot, w_second, near + far, LIMIT, (act,)
    )
    dact_shares = swap(dact_parts)
    moved_cot = moved_fields(
        moved_second_kernel,
        "moved_second",
        (2, 3, DEPTH, HEIGHT + 2, WIDTH, rows),
        cot,
        to_core(cot),
        act,
    )
    vol_other = to_core(vol)
    act_keep, act_send = halves("act_halves", True, idx, act_blocks, (moved_cot, vol_other, dact_parts[0]))
    act_other = to_core(act_send)

    sums, outward = line_moves(lax.axis_size("dp") // 2)
    steps = len(sums) + len(outward)
    parts, totals, crossed = {}, {}, {}
    last = ()

    chunk_shape = [(9, n // 2 * rows, rows)] * 3 + [(9 * rows + EXTRA, n // 2 * rows)] * 3
    first_moves = {}

    reached = [0] * 6

    def line(chunk, step):
        nonlocal last
        if reached[chunk] > step:
            return
        if reached[chunk] < step:
            line(chunk, step - 1)
        reached[chunk] = step + 1
        part, first = parts[chunk]
        moves = (sums + outward)[step]
        if step == 0:
            if id(part) not in first_moves:
                first_moves[id(part)] = line_send(part, moves)
            got, total = first_moves[id(part)], jax.ShapeDtypeStruct(chunk_shape[chunk], BF16)
        else:
            total = totals[chunk]
            got = line_send(total, moves)
            if 0 < step < len(sums) - 1:
                part, first = part[first : first + 9] if chunk < 3 else part, 0
        totals[chunk] = line_step(step, part, first, got, total, idx, place, last)
        last = (totals[chunk],)
        if step == steps - 1:
            crossed[chunk] = to_core(totals[chunk])

    def write(chunk):
        nonlocal last
        line(chunk, steps - 1)
        name, axis = ("finish_second", 1) if chunk < 3 else ("finish_first", 2)
        shape = (9, n // 2 * rows, rows) if chunk < 3 else (9, rows, n // 2 * rows)
        written[axis], mark = finish(
            name,
            n,
            axis,
            factor,
            idx,
            chunk % 3,
            shape,
            totals[chunk],
            crossed[chunk],
            written.get(axis),
            last,
        )
        last = (mark,)

    def second_parts(offsets):
        nonlocal last
        made = grad_second(offsets, moved_cot, act_keep, act_other, last)
        for at, a in enumerate(offsets):
            parts[a + 1] = made, 9 * at
        last = (made,)

    def first_parts():
        nonlocal last
        own, other = done["dpre_halves"]
        made = grad_first(vol, vol_other, own, other, done["gain"], last)
        for at in range(3):
            parts[3 + at] = made[at], 0
        last = (made[0],)

    def norm_back():
        nonlocal last
        dpre, done["gain"] = pl.pallas_call(
            functools.partial(norm_back_kernel, n),
            in_specs=[pl.BlockSpec(memory_space=pltpu.VMEM)] * (2 + n) + [UNREAD],
            out_shape=[
                jax.ShapeDtypeStruct((CELLS, rows), BF16),
                jax.ShapeDtypeStruct((1, rows), F32),
            ],
            compiler_params=pltpu.CompilerParams(vmem_limit_bytes=SMALL),
            cost_estimate=LIGHT,
            name="norm_back",
        )(own_gain, normed, inverse, done["dact"], *dact_shares[1:-1], *last)
        done["dpre"] = swap([dpre] * n)
        last = (dpre,)

    def dpre_halves():
        nonlocal last
        keep, send = halves("dpre_halves", False, idx, done["dpre"], last)
        done["dpre_halves"] = keep, to_core(send)
        last = (keep,)

    def output():
        nonlocal last
        done["output"], mark = conv_full("output", 1, False, idx, w_second, act_blocks, last)
        last = (mark,)

    def grad_volume():
        nonlocal last
        done["grad_volume"], mark = conv_full(
            "grad_volume", -1, True, idx, first_flat, done["dpre"], last
        )
        last = (mark,)

    written, done = {}, {}
    second_parts((-1,))
    done["dact"] = sum_shares("dact_sum", dact_shares[0], dact_shares[-1], last)
    last = (done["dact"],)
    second_parts((0, 1))
    output()
    norm_back()
    line(0, 0)
    line(0, 1)
    dpre_halves()
    first_parts()
    line(1, 0)
    line(2, 0)
    line(0, 2)
    line(1, 1)
    line(3, 0)
    line(2, 1)
    line(1, 2)
    write(0)
    line(4, 0)
    line(3, 1)
    line(2, 2)
    write(1)
    line(5, 0)
    line(4, 1)
    line(3, 2)
    write(2)
    line(5, 1)
    line(4, 2)
    write(3)
    write(4)
    grad_volume()
    line(5, 2)
    write(5)
    gain_rows = totals[3][9 * rows : 9 * rows + 2, :rows].astype(F32)
    gain_rows_other = crossed[3][9 * rows : 9 * rows + 2, :rows].astype(F32)
    gain_total = (jnp.sum(gain_rows, axis=0) + jnp.sum(gain_rows_other, axis=0)) * factor
    return (done["output"][None], done["grad_volume"][None], written[2], gain_total, written[1])


def solution(mesh):
    placed = (
        P("dp", "chan", None),
        P(None, "chan", None),
        P(),
        P(None, None, "chan"),
        P("dp", "chan", None),
    )
    return jax.shard_map(
        shards,
        mesh=mesh,
        in_specs=placed,
        out_specs=(
            P("dp", "chan", None),
            P("dp", "chan", None),
            P(None, "chan", None),
            P("chan"),
            P(None, None, "chan"),
        ),
        check_vma=False,
    )
```

```python
import functools
import math

import jax
import jax.numpy as jnp
from jax import lax
from jax.experimental import pallas as pl
from jax.experimental.pallas import tpu as pltpu
from jax.sharding import PartitionSpec as P

DEPTH, HEIGHT, WIDTH = 4, 16, 16
PLANE = HEIGHT * WIDTH
CELLS = DEPTH * PLANE
TAPS = [(a, b, c) for a in (-1, 0, 1) for b in (-1, 0, 1) for c in (-1, 0, 1)]
NORM_EPS = 1e-05
LIMIT = 16 * 1024 * 1024
SMALL = 8 * 1024 * 1024
LARGE = 59 * 1024 * 1024
EXTRA = 16
F32, BF16 = jnp.float32, jnp.bfloat16
NT = (((1,), (1,)), ((), ()))
UNREAD = pl.BlockSpec(memory_space=pl.ANY)
IN_HBM = pl.BlockSpec(memory_space=pltpu.HBM)
PLANE_ORDER = (0, -1, 1)
LIGHT = pl.CostEstimate(flops=1024, bytes_accessed=1024, transcendentals=0)


def params():
    return pltpu.CompilerParams(
        dimension_semantics=("arbitrary",), vmem_limit_bytes=LIMIT
    )


def whole(shape):
    return pl.BlockSpec(shape, lambda *_: (0,) * len(shape))


def smem():
    return pl.BlockSpec(memory_space=pltpu.SMEM)


def fill_padded(padded, rows_first, sign):
    padded[...] = jnp.zeros_like(padded)
    cells = rows_first.astype(F32).T
    width_at = lax.broadcasted_iota(jnp.int32, cells.shape, 0) % WIDTH
    for c in (-1, 0, 1):
        off = sign * c
        moved = cells if off == 0 else pltpu.roll(cells, (-off) % CELLS, 0)
        inside = (width_at + off >= 0) & (width_at + off < WIDTH)
        moved = jnp.where(inside, moved, 0.0).astype(BF16)
        padded[1 + c, 1 : 1 + DEPTH, 1 : 1 + HEIGHT] = moved.reshape(
            DEPTH, HEIGHT, WIDTH, cells.shape[1]
        )


def span_of(a, sign):
    return max(0, -sign * a), DEPTH - abs(a)


def start_parts(source, buffer, sems):
    size = source.shape[0] // 3
    copies = {}
    for a in PLANE_ORDER:
        span = pl.ds((a + 1) * size, size)
        copies[a] = pltpu.make_async_copy(source.at[span], buffer.at[span], sems.at[a + 1])
        copies[a].start()
    return copies


def share_kernel(n, sign, idx, field, w, *refs):
    outs = refs[:n]
    padded, sums, shares, buffer, sems = refs[n:]
    rows = field.shape[0]
    copies = start_parts(w, buffer, sems)
    fill_padded(padded, field[...], sign)
    for a in PLANE_ORDER:
        begin, planes = span_of(a, sign)
        pieces = []
        for b in (-1, 0, 1):
            for c in (-1, 0, 1):
                low, first = 1 + sign * b, 1 + begin + sign * a
                piece = padded[1 + c, first : first + planes, low : low + HEIGHT]
                pieces.append(piece.reshape(planes * PLANE, rows))
        lhs = jnp.concatenate(pieces, axis=1)
        copies[a].wait()
        if sign == 1:
            rhs = buffer[(a + 1) * 9 * rows : (a + 2) * 9 * rows]
            part = jnp.dot(lhs, rhs, preferred_element_type=F32)
        else:
            rhs = jnp.concatenate([buffer[(a + 1) * 9 + k] for k in range(9)], axis=1)
            part = lax.dot_general(lhs, rhs, NT, preferred_element_type=F32)
        span = slice(begin * PLANE, (begin + planes) * PLANE)
        if a == 0:
            sums[...] = part
        else:
            sums[span] += part
    for j in range(n):
        shares[j] = sums[:, j * rows : (j + 1) * rows].astype(BF16)
    for m in range(n):
        outs[m][...] = shares[idx[0] ^ m]


def spread_shares(sign, name, idx, n, field, w, limit):
    rows = field.shape[0]
    return pl.pallas_call(
        functools.partial(share_kernel, n, sign),
        in_specs=[smem(), pl.BlockSpec(memory_space=pltpu.VMEM), IN_HBM],
        out_specs=[pl.BlockSpec(memory_space=pltpu.VMEM)] * n,
        out_shape=[jax.ShapeDtypeStruct((CELLS, rows), BF16)] * n,
        scratch_shapes=[
            pltpu.VMEM((3, DEPTH + 2, HEIGHT + 2, WIDTH, rows), BF16),
            pltpu.VMEM((CELLS, n * rows), F32),
            pltpu.VMEM((n, CELLS, rows), BF16),
            pltpu.VMEM(w.shape, BF16),
            pltpu.SemaphoreType.DMA((3,)),
        ],
        compiler_params=pltpu.CompilerParams(vmem_limit_bytes=limit),
        cost_estimate=LIGHT,
        name=name,
    )(idx, field, w)


def norm_kernel(n, gain, *refs):
    shares = refs[:n]
    act, normed_out, inverse_out = refs[2 * n - 1 : 2 * n + 2]
    pre = shares[0][...].astype(F32)
    for m in range(1, n):
        pre = pre + shares[m][...].astype(F32)
    center = pre - jnp.mean(pre, axis=0, keepdims=True)
    inverse = lax.rsqrt(jnp.mean(center * center, axis=0, keepdims=True) + NORM_EPS)
    normed = center * inverse
    scaled = gain[...] * normed
    act[...] = (scaled * jax.nn.sigmoid(scaled)).astype(BF16)
    normed_out[...] = normed
    inverse_out[...] = inverse


def norm_back_kernel(n, gain, normed_in, inverse, *refs):
    shares = refs[:n]
    dpre, gain_part = refs[-2:]
    dact = shares[0][...].astype(F32)
    for m in range(1, n):
        dact = dact + shares[m][...].astype(F32)
    normed = normed_in[...]
    scaled = gain[...] * normed
    sigma = jax.nn.sigmoid(scaled)
    dscaled = dact * sigma * (1.0 + scaled * (1.0 - sigma))
    product = dscaled * normed
    gain_part[...] = jnp.sum(product, axis=0, keepdims=True)
    dnormed = gain[...] * dscaled
    mean_first = jnp.mean(dnormed, axis=0, keepdims=True)
    mean_second = jnp.mean(dnormed * normed, axis=0, keepdims=True)
    dpre[...] = ((dnormed - mean_first - normed * mean_second) * inverse[...]).astype(BF16)


def conv_back_add(sums, products, begin, planes, taps, rows, sign):
    for at, tap in enumerate(taps):
        a, b, c = tap
        a, b = sign * a, sign * b
        part = products[:, at * rows : (at + 1) * rows].reshape(planes, HEIGHT, WIDTH, rows)
        low, high = max(0, b), HEIGHT + min(0, b)
        sums[1 + c, begin - a : begin - a + planes, low - b : high - b] += part[:, low:high]


def conv_finish(sums, out, sign):
    rows = out.shape[0]
    total = None
    for c in (-1, 0, 1):
        off = sign * c
        part = sums[1 + c].reshape(CELLS, rows)
        if off != 0:
            width_at = lax.broadcasted_iota(jnp.int32, part.shape, 0) % WIDTH
            inside = (width_at + off >= 0) & (width_at + off < WIDTH)
            part = jnp.where(inside, pltpu.roll(part, (-off) % CELLS, 0), 0.0)
        total = part if total is None else total + part
    out[...] = total.T.astype(BF16)


def conv_kernel(n, sign, transposed, idx, w, *refs):
    blocks = refs[:n]
    out, mark, ordered, sums, buffer, sems = refs[-6:]
    mark[...] = jnp.zeros_like(mark)
    rows = out.shape[0]
    copies = start_parts(w, buffer, sems)
    sums[...] = jnp.zeros_like(sums)
    for m in range(n):
        ordered[idx[0] ^ m] = blocks[m][...]
    for a in PLANE_ORDER:
        begin, planes = span_of(-a, sign)
        span = slice(begin * PLANE, (begin + planes) * PLANE)
        lhs = jnp.concatenate([ordered[j, span] for j in range(n)], axis=1)
        copies[a].wait()
        for k in range(0, 9, 2):
            t = (a + 1) * 9 + k
            taps = TAPS[t : t + min(2, 9 - k)]
            if transposed:
                rhs = buffer[t * rows : (t + len(taps)) * rows]
                products = lax.dot_general(lhs, rhs, NT, preferred_element_type=F32)
            else:
                rhs = jnp.concatenate([buffer[t + at] for at in range(len(taps))], axis=1)
                products = jnp.dot(lhs, rhs, preferred_element_type=F32)
            conv_back_add(sums, products, begin, planes, taps, rows, sign)
    conv_finish(sums, out, sign)


def conv_full(name, sign, transposed, idx, w, blocks, after):
    n, rows = len(blocks), blocks[0].shape[1]
    return pl.pallas_call(
        functools.partial(conv_kernel, n, sign, transposed),
        in_specs=[smem(), IN_HBM]
        + [pl.BlockSpec(memory_space=pltpu.VMEM)] * n
        + [UNREAD] * len(after),
        out_specs=[pl.BlockSpec(memory_space=pltpu.VMEM)] * 2,
        out_shape=[
            jax.ShapeDtypeStruct((rows, CELLS), BF16),
            jax.ShapeDtypeStruct((8, 128), F32),
        ],
        scratch_shapes=[
            pltpu.VMEM((n, CELLS, rows), BF16),
            pltpu.VMEM((3, DEPTH, HEIGHT, WIDTH, rows), F32),
            pltpu.VMEM(w.shape, BF16),
            pltpu.SemaphoreType.DMA((3,)),
        ],
        compiler_params=pltpu.CompilerParams(vmem_limit_bytes=LIMIT),
        cost_estimate=LIGHT,
        name=name,
    )(idx, w, *blocks, *after)


def halves_kernel(n, turned, idx, *refs):
    blocks = refs[:n]
    keep, send = refs[-2:]
    half = n // 2
    rows = blocks[0].shape[1]

    def put(out, at, block):
        if turned:
            out[pl.ds(pl.multiple_of(at * rows, rows), rows)] = block[...].astype(F32).T.astype(BF16)
        else:
            out[at] = block[...]

    def split(kept, sent):
        for m in range(half):
            at = (idx[0] ^ m) & (half - 1)
            put(keep, at, blocks[kept + m])
            put(send, at, blocks[sent + m])

    @pl.when(idx[1] == 0)
    def _():
        split(0, half)

    @pl.when(idx[1] != 0)
    def _():
        split(half, 0)


def halves(name, turned, idx, blocks, after):
    n, rows = len(blocks), blocks[0].shape[1]
    shape = (n // 2 * rows, CELLS) if turned else (n // 2, CELLS, rows)
    return pl.pallas_call(
        functools.partial(halves_kernel, n, turned),
        in_specs=[smem()]
        + [pl.BlockSpec(memory_space=pltpu.VMEM)] * n
        + [UNREAD] * len(after),
        out_shape=[jax.ShapeDtypeStruct(shape, BF16)] * 2,
        compiler_params=pltpu.CompilerParams(vmem_limit_bytes=LIMIT),
        cost_estimate=LIGHT,
        name=name,
    )(idx, *blocks, *after)


def moved_second_kernel(own, other, _, out):
    out[...] = jnp.zeros_like(out)
    for which, ref in enumerate((own, other)):
        cells = ref[...].astype(F32).T
        width_at = lax.broadcasted_iota(jnp.int32, cells.shape, 0) % WIDTH
        for c in (-1, 0, 1):
            part = cells if c == 0 else pltpu.roll(cells, c % CELLS, 0)
            inside = (width_at - c >= 0) & (width_at - c < WIDTH)
            part = jnp.where(inside, part, 0.0).astype(BF16)
            out[which, 1 + c, :, 1 : 1 + HEIGHT] = part.reshape(
                DEPTH, HEIGHT, WIDTH, cells.shape[1]
            )


def moved_fields(kernel, name, shape, own, other, after):
    return pl.pallas_call(
        kernel,
        in_specs=[pl.BlockSpec(memory_space=pltpu.VMEM)] * 2 + [UNREAD],
        out_shape=jax.ShapeDtypeStruct(shape, BF16),
        compiler_params=pltpu.CompilerParams(vmem_limit_bytes=LIMIT),
        cost_estimate=LIGHT,
        name=name,
    )(own, other, after)


def split_rows(values):
    high = values.astype(BF16)
    low = (values - high.astype(F32)).astype(BF16)
    empty = jnp.zeros((EXTRA - 2, values.shape[1]), F32)
    return jnp.concatenate([high.astype(F32), low.astype(F32), empty], axis=0).astype(BF16)


def moved_lanes(cells, b, c):
    off = b * WIDTH + c
    if off == 0:
        return cells.astype(BF16)
    at = lax.broadcasted_iota(jnp.int32, cells.shape, 1)
    height_at, width_at = at // WIDTH % HEIGHT, at % WIDTH
    inside = (height_at + b >= 0) & (height_at + b < HEIGHT)
    inside = inside & (width_at + c >= 0) & (width_at + c < WIDTH)
    return jnp.where(inside, pltpu.roll(cells, (-off) % CELLS, 1), 0.0).astype(BF16)


def grad_first_kernel(vol_own, vol_other, own, other, gain_part, *refs):
    outs, moved = refs[-4:-1], refs[-1]
    half, rows = own.shape[0], own.shape[2]
    fields = [ref[...].astype(F32) for ref in (vol_own, vol_other)]
    rhs = [jnp.concatenate([ref[j] for j in range(half)], axis=1) for ref in (own, other)]
    for b in range(3):
        for which in range(2):
            for c in range(3):
                moved[which, c * rows : (c + 1) * rows] = moved_lanes(fields[which], b - 1, c - 1)
        for a in (-1, 0, 1):
            begin, count = max(0, -a) * PLANE, (DEPTH - abs(a)) * PLANE
            shift = begin + a * PLANE
            grads = None
            for which in range(2):
                lhs = moved[which, :, shift : shift + count]
                part = jnp.dot(lhs, rhs[which][begin : begin + count], preferred_element_type=F32)
                grads = part if grads is None else grads + part
            outs[a + 1][3 * rows * b : 3 * rows * (b + 1)] = grads.astype(BF16)
    filler = jnp.zeros((1, half * rows - rows), F32)
    outs[0][9 * rows :] = split_rows(jnp.concatenate([gain_part[...], filler], axis=1))
    for out in outs[1:]:
        out[9 * rows :] = jnp.zeros((EXTRA, half * rows), BF16)


def grad_first(vol_own, vol_other, own, other, gain_part, after):
    half, cells, rows = own.shape
    return pl.pallas_call(
        grad_first_kernel,
        in_specs=[pl.BlockSpec(memory_space=pltpu.VMEM)] * 5 + [UNREAD] * len(after),
        out_specs=[pl.BlockSpec(memory_space=pltpu.VMEM)] * 3,
        out_shape=[jax.ShapeDtypeStruct((9 * rows + EXTRA, half * rows), BF16)] * 3,
        scratch_shapes=[pltpu.VMEM((2, 3 * rows, CELLS), BF16)],
        compiler_params=pltpu.CompilerParams(vmem_limit_bytes=LIMIT),
        cost_estimate=LIGHT,
        name="grad_first",
    )(vol_own, vol_other, own, other, gain_part, *after)


def grad_second_kernel(a, moved, own, other, *refs):
    out = refs[-1]
    rows = out.shape[2]
    begin, planes = max(0, a), DEPTH - abs(a)
    lhs = [
        ref[:, begin * PLANE : (begin + planes) * PLANE] for ref in (own, other)
    ]
    for k in range(0, 9, 2):
        taps = range(k, min(k + 2, 9))
        grads = None
        for which in range(2):
            pieces = []
            for at in taps:
                b, c = at // 3 - 1, at % 3 - 1
                piece = moved[which, 1 + c, begin - a : begin - a + planes, 1 - b : 1 - b + HEIGHT]
                pieces.append(piece.reshape(planes * PLANE, rows))
            rhs = jnp.concatenate(pieces, axis=1)
            part = jnp.dot(lhs[which], rhs, preferred_element_type=F32)
            grads = part if grads is None else grads + part
        for place, at in enumerate(taps):
            out[at] = grads[:, place * rows : (place + 1) * rows].astype(BF16)


def grad_second(a, moved, own, other, after):
    wide, rows = own.shape[0], moved.shape[-1]
    return pl.pallas_call(
        functools.partial(grad_second_kernel, a),
        in_specs=[pl.BlockSpec(memory_space=pltpu.VMEM)] * 3 + [UNREAD] * len(after),
        out_shape=jax.ShapeDtypeStruct((9, wide, rows), BF16),
        compiler_params=pltpu.CompilerParams(vmem_limit_bytes=LIMIT),
        cost_estimate=LIGHT,
        name="grad_second",
    )(moved, own, other, *after)


def finish_kernel(n, axis, factor, chunk, idx, own, other, *refs):
    out, mark, wide, sems = refs[-4:]
    upper = (idx[0] >= n // 2).astype(jnp.int32) ^ idx[1]
    taps, height, width = wide.shape[1:]
    copies = []
    for k, (part, place) in enumerate(((own, upper), (other, 1 - upper))):
        size = (height, width)[axis - 1]
        span = pl.ds(pl.multiple_of(place * size, size), size)
        for third in range(3):
            at = slice(3 * third, 3 * third + 3)
            if len(part.shape) == 2:
                rows = part[3 * third * height : (3 * third + 3) * height]
                rows = rows.reshape(3, height, width)
            else:
                rows = part[at]
            wide[k, at] = rows.astype(F32) * factor
            target = out.at[pl.ds(chunk * taps + 3 * third, 3)]
            target = target.at[:, span] if axis == 1 else target.at[:, :, span]
            copies.append(
                pltpu.make_async_copy(wide.at[k, at], target, sems.at[3 * k + third])
            )
            copies[-1].start()
    mark[...] = jnp.zeros_like(mark)
    for copy in copies:
        copy.wait()


def finish(name, n, axis, factor, idx, chunk, shape, own, other, before, after):
    taps, height, width = shape
    given = [] if before is None else [before]
    full = (27, height * 2, width) if axis == 1 else (27, height, width * 2)
    return pl.pallas_call(
        functools.partial(finish_kernel, n, axis, factor, chunk),
        in_specs=[smem()]
        + [pl.BlockSpec(memory_space=pltpu.VMEM)] * 2
        + [UNREAD] * (len(given) + len(after)),
        out_specs=[UNREAD, pl.BlockSpec(memory_space=pltpu.VMEM)],
        out_shape=[jax.ShapeDtypeStruct(full, F32), jax.ShapeDtypeStruct((8, 128), F32)],
        scratch_shapes=[pltpu.VMEM((2,) + shape, F32), pltpu.SemaphoreType.DMA((6,))],
        input_output_aliases={3: 0} if given else {},
        compiler_params=pltpu.CompilerParams(vmem_limit_bytes=SMALL),
        cost_estimate=LIGHT,
        name=name,
    )(idx, own, other, *given, *after)


def add_kernel(x, y, *refs):
    out = refs[-1]
    if len(x.shape) == 3:
        out[...] = (x[...].astype(F32) + y[...].astype(F32)).astype(BF16)
    else:
        rows = x.shape[0] - EXTRA
        out[:rows] = (x[:rows].astype(F32) + y[:rows].astype(F32)).astype(BF16)
        tail = x[rows:].astype(F32) + y[rows:].astype(F32)
        out[rows:] = split_rows(tail[:1] + tail[1:2])


def pick_kernel(idx, x, y, *refs):
    out = refs[-1]

    @pl.when(idx[2] == 0)
    def _():
        out[...] = x[...]

    @pl.when(idx[2] != 0)
    def _():
        out[...] = y[...]


def whole_call(kernel, name, x, y, after, idx=None):
    given = [] if idx is None else [idx]
    return pl.pallas_call(
        kernel,
        in_specs=[smem()] * len(given)
        + [pl.BlockSpec(memory_space=pltpu.VMEM)] * 2
        + [UNREAD] * len(after),
        out_shape=jax.ShapeDtypeStruct(x.shape, x.dtype),
        compiler_params=pltpu.CompilerParams(vmem_limit_bytes=SMALL),
        cost_estimate=LIGHT,
        name=name,
    )(*given, x, y, *after)


def line_moves(chips):
    inward = [[(h, h + 1), (chips - 1 - h, chips - 2 - h)] for h in range(chips // 2 - 1)]
    mid = chips // 2
    outward = [[(j, i) for i, j in moves] for moves in reversed(inward)]
    return inward + [[(mid - 1, mid), (mid, mid - 1)]], outward


def line_send(x, moves):
    pairs = [(2 * i + k, 2 * j + k) for i, j in moves for k in (0, 1)]
    return lax.ppermute(x, "dp", pairs)


def line_step(step, part, total, idx, place, after):
    sums, outward = line_moves(lax.axis_size("dp") // 2)
    if step < len(sums):
        got = line_send(total, sums[step])
        base = total if step == len(sums) - 1 else part
        return whole_call(add_kernel, "line_add", base, got, after)
    moves = outward[step - len(sums)]
    got = line_send(total, moves)
    takes = functools.reduce(jnp.logical_or, [place // 2 == j for _, j in moves])
    marked = jnp.stack([idx[0], idx[1], takes.astype(jnp.int32)])
    return whole_call(pick_kernel, "line_pick", total, got, after, marked)


def shards(volume, w_first, gain, w_second, cotangent):
    n = lax.axis_size("chan")
    rows = volume.shape[1]
    vol, cot = volume[0], cotangent[0]
    chan, place = lax.axis_index("chan"), lax.axis_index("dp")
    idx = jnp.stack([chan, place % 2]).astype(jnp.int32)
    own_gain = lax.dynamic_slice_in_dim(gain, chan * rows, rows, 0)[None]
    factor = 1.0 / math.sqrt(lax.axis_size("dp") * CELLS)

    def to_partner(x, m):
        return lax.ppermute(x, "chan", [(i, i ^ m) for i in range(n)])

    def to_core(x):
        return lax.ppermute(x, "dp", [(i, i ^ 1) for i in range(lax.axis_size("dp"))])

    def swap(parts):
        got = {m: to_partner(parts[m], m) for m in reversed(range(1, n))}
        return [parts[0]] + [got[m] for m in range(1, n)]

    first_flat = w_first.reshape(27 * rows, n * rows)
    pre_shares = swap(spread_shares(1, "pre", idx, n, vol, first_flat, LARGE))
    dact_parts = spread_shares(-1, "dact", idx, n, cot, w_second, LIMIT)
    held = dact_parts[1:]
    act, normed, inverse, *held = pl.pallas_call(
        functools.partial(norm_kernel, n),
        in_specs=[pl.BlockSpec(memory_space=pltpu.VMEM)] * (1 + n) + [UNREAD] * len(held),
        out_specs=[pl.BlockSpec(memory_space=pltpu.VMEM)] * 3 + [UNREAD] * len(held),
        out_shape=[
            jax.ShapeDtypeStruct((CELLS, rows), BF16),
            jax.ShapeDtypeStruct((CELLS, rows), F32),
            jax.ShapeDtypeStruct((1, rows), F32),
        ]
        + [jax.ShapeDtypeStruct(x.shape, x.dtype) for x in held],
        input_output_aliases={1 + n + k: 3 + k for k in range(len(held))},
        compiler_params=pltpu.CompilerParams(vmem_limit_bytes=SMALL),
        cost_estimate=LIGHT,
        name="norm",
    )(own_gain, *pre_shares, *held)
    act_blocks = swap([act] * n)
    dact_shares = swap([dact_parts[0]] + held)
    moved_cot = moved_fields(
        moved_second_kernel,
        "moved_second",
        (2, 3, DEPTH, HEIGHT + 2, WIDTH, rows),
        cot,
        to_core(cot),
        act,
    )
    vol_other = to_core(vol)
    act_keep, act_send = halves("act_halves", True, idx, act_blocks, (moved_cot, vol_other))
    act_other = to_core(act_send)

    sums, outward = line_moves(lax.axis_size("dp") // 2)
    steps = len(sums) + len(outward)
    parts, totals, crossed = {}, {}, {}
    last = ()

    reached = [0] * 6

    def line(chunk, step):
        nonlocal last
        if reached[chunk] > step:
            return
        if reached[chunk] < step:
            line(chunk, step - 1)
        reached[chunk] = step + 1
        before = totals.get(chunk, parts[chunk])
        totals[chunk] = line_step(step, parts[chunk], before, idx, place, last)
        last = (totals[chunk],)
        if step == steps - 1:
            crossed[chunk] = to_core(totals[chunk])

    def write(chunk):
        nonlocal last
        line(chunk, steps - 1)
        name, axis = ("finish_second", 1) if chunk < 3 else ("finish_first", 2)
        shape = (9, n // 2 * rows, rows) if chunk < 3 else (9, rows, n // 2 * rows)
        written[axis], mark = finish(
            name,
            n,
            axis,
            factor,
            idx,
            chunk % 3,
            shape,
            totals[chunk],
            crossed[chunk],
            written.get(axis),
            last,
        )
        last = (mark,)

    def second_part(chunk):
        nonlocal last
        parts[chunk] = grad_second(chunk - 1, moved_cot, act_keep, act_other, last)
        last = (parts[chunk],)

    def first_parts():
        nonlocal last
        own, other = done["dpre_halves"]
        parts[3], parts[4], parts[5] = grad_first(
            vol, vol_other, own, other, done["gain"], last
        )
        last = (parts[3],)

    def norm_back():
        nonlocal last
        dpre, done["gain"] = pl.pallas_call(
            functools.partial(norm_back_kernel, n),
            in_specs=[pl.BlockSpec(memory_space=pltpu.VMEM)] * (3 + n) + [UNREAD],
            out_shape=[
                jax.ShapeDtypeStruct((CELLS, rows), BF16),
                jax.ShapeDtypeStruct((1, rows), F32),
            ],
            compiler_params=pltpu.CompilerParams(vmem_limit_bytes=SMALL),
            cost_estimate=LIGHT,
            name="norm_back",
        )(own_gain, normed, inverse, *dact_shares, *last)
        done["dpre"] = swap([dpre] * n)
        last = (dpre,)

    def dpre_halves():
        nonlocal last
        keep, send = halves("dpre_halves", False, idx, done["dpre"], last)
        done["dpre_halves"] = keep, to_core(send)
        last = (keep,)

    def output():
        nonlocal last
        done["output"], mark = conv_full("output", 1, False, idx, w_second, act_blocks, last)
        last = (mark,)

    def grad_volume():
        nonlocal last
        done["grad_volume"], mark = conv_full(
            "grad_volume", -1, True, idx, first_flat, done["dpre"], last
        )
        last = (mark,)

    written, done = {}, {}
    second_part(0)
    output()
    second_part(1)
    norm_back()
    line(0, 0)
    second_part(2)
    line(1, 0)
    dpre_halves()
    first_parts()
    line(0, 1)
    line(2, 0)
    line(1, 1)
    line(0, 2)
    line(3, 0)
    line(2, 1)
    line(1, 2)
    line(4, 0)
    line(3, 1)
    write(0)
    line(5, 0)
    line(2, 2)
    line(4, 1)
    write(1)
    line(3, 2)
    write(2)
    line(5, 1)
    line(4, 2)
    write(3)
    write(4)
    grad_volume()
    line(5, 2)
    write(5)
    gain_rows = totals[3][9 * rows : 9 * rows + 2, :rows].astype(F32)
    gain_rows_other = crossed[3][9 * rows : 9 * rows + 2, :rows].astype(F32)
    gain_total = (jnp.sum(gain_rows, axis=0) + jnp.sum(gain_rows_other, axis=0)) * factor
    return (done["output"][None], done["grad_volume"][None], written[2], gain_total, written[1])


def solution(mesh):
    placed = (
        P("dp", "chan", None),
        P(None, "chan", None),
        P(),
        P(None, None, "chan"),
        P("dp", "chan", None),
    )
    return jax.shard_map(
        shards,
        mesh=mesh,
        in_specs=placed,
        out_specs=(
            P("dp", "chan", None),
            P("dp", "chan", None),
            P(None, "chan", None),
            P("chan"),
            P(None, None, "chan"),
        ),
        check_vma=False,
    )
```

```python
import functools
import math

import jax
import jax.numpy as jnp
from jax import lax
from jax.experimental import pallas as pl
from jax.experimental.pallas import tpu as pltpu
from jax.sharding import PartitionSpec as P

DEPTH, HEIGHT, WIDTH = 4, 16, 16
PLANE = HEIGHT * WIDTH
CELLS = DEPTH * PLANE
TAPS = [(a, b, c) for a in (-1, 0, 1) for b in (-1, 0, 1) for c in (-1, 0, 1)]
NORM_EPS = 1e-05
LIMIT = 16 * 1024 * 1024
SMALL = 8 * 1024 * 1024
LARGE = 59 * 1024 * 1024
EXTRA = 16
F32, BF16 = jnp.float32, jnp.bfloat16
NT = (((1,), (1,)), ((), ()))
UNREAD = pl.BlockSpec(memory_space=pl.ANY)
IN_HBM = pl.BlockSpec(memory_space=pltpu.HBM)
PLANE_ORDER = (0, -1, 1)
LIGHT = pl.CostEstimate(flops=1024, bytes_accessed=1024, transcendentals=0)


def params():
    return pltpu.CompilerParams(
        dimension_semantics=("arbitrary",), vmem_limit_bytes=LIMIT
    )


def whole(shape):
    return pl.BlockSpec(shape, lambda *_: (0,) * len(shape))


def smem():
    return pl.BlockSpec(memory_space=pltpu.SMEM)


def fill_padded(padded, rows_first, sign):
    padded[...] = jnp.zeros_like(padded)
    cells = rows_first.astype(F32).T
    width_at = lax.broadcasted_iota(jnp.int32, cells.shape, 0) % WIDTH
    for c in (-1, 0, 1):
        off = sign * c
        moved = cells if off == 0 else pltpu.roll(cells, (-off) % CELLS, 0)
        inside = (width_at + off >= 0) & (width_at + off < WIDTH)
        moved = jnp.where(inside, moved, 0.0).astype(BF16)
        padded[1 + c, 1 : 1 + DEPTH, 1 : 1 + HEIGHT] = moved.reshape(
            DEPTH, HEIGHT, WIDTH, cells.shape[1]
        )


def span_of(a, sign):
    return max(0, -sign * a), DEPTH - abs(a)


def start_parts(source, buffer, sems):
    size = source.shape[0] // 3
    copies = {}
    for a in PLANE_ORDER:
        span = pl.ds((a + 1) * size, size)
        copies[a] = pltpu.make_async_copy(source.at[span], buffer.at[span], sems.at[a + 1])
        copies[a].start()
    return copies


def share_kernel(n, sign, idx, field, w, *refs):
    outs = refs[:n]
    padded, sums, shares, buffer, sems = refs[n:]
    rows = field.shape[0]
    copies = start_parts(w, buffer, sems)
    fill_padded(padded, field[...], sign)
    for a in PLANE_ORDER:
        begin, planes = span_of(a, sign)
        pieces = []
        for b in (-1, 0, 1):
            for c in (-1, 0, 1):
                low, first = 1 + sign * b, 1 + begin + sign * a
                piece = padded[1 + c, first : first + planes, low : low + HEIGHT]
                pieces.append(piece.reshape(planes * PLANE, rows))
        lhs = jnp.concatenate(pieces, axis=1)
        copies[a].wait()
        if sign == 1:
            rhs = buffer[(a + 1) * 9 * rows : (a + 2) * 9 * rows]
            part = jnp.dot(lhs, rhs, preferred_element_type=F32)
        else:
            rhs = jnp.concatenate([buffer[(a + 1) * 9 + k] for k in range(9)], axis=1)
            part = lax.dot_general(lhs, rhs, NT, preferred_element_type=F32)
        span = slice(begin * PLANE, (begin + planes) * PLANE)
        if a == 0:
            sums[...] = part
        else:
            sums[span] += part
    for j in range(n):
        shares[j] = sums[:, j * rows : (j + 1) * rows].astype(BF16)
    for m in range(n):
        outs[m][...] = shares[idx[0] ^ m]


def spread_shares(sign, name, idx, n, field, w, limit):
    rows = field.shape[0]
    return pl.pallas_call(
        functools.partial(share_kernel, n, sign),
        in_specs=[smem(), pl.BlockSpec(memory_space=pltpu.VMEM), IN_HBM],
        out_specs=[pl.BlockSpec(memory_space=pltpu.VMEM)] * n,
        out_shape=[jax.ShapeDtypeStruct((CELLS, rows), BF16)] * n,
        scratch_shapes=[
            pltpu.VMEM((3, DEPTH + 2, HEIGHT + 2, WIDTH, rows), BF16),
            pltpu.VMEM((CELLS, n * rows), F32),
            pltpu.VMEM((n, CELLS, rows), BF16),
            pltpu.VMEM(w.shape, BF16),
            pltpu.SemaphoreType.DMA((3,)),
        ],
        compiler_params=pltpu.CompilerParams(vmem_limit_bytes=limit),
        cost_estimate=LIGHT,
        name=name,
    )(idx, field, w)


def norm_kernel(n, gain, *refs):
    shares = refs[:n]
    act, normed_out, inverse_out = refs[2 * n - 1 : 2 * n + 2]
    pre = shares[0][...].astype(F32)
    for m in range(1, n):
        pre = pre + shares[m][...].astype(F32)
    center = pre - jnp.mean(pre, axis=0, keepdims=True)
    inverse = lax.rsqrt(jnp.mean(center * center, axis=0, keepdims=True) + NORM_EPS)
    normed = center * inverse
    scaled = gain[...] * normed
    act[...] = (scaled * jax.nn.sigmoid(scaled)).astype(BF16)
    normed_out[...] = normed
    inverse_out[...] = inverse


def norm_back_kernel(n, gain, normed_in, inverse, *refs):
    shares = refs[:n]
    dpre, gain_part = refs[-2:]
    dact = shares[0][...].astype(F32)
    for m in range(1, n):
        dact = dact + shares[m][...].astype(F32)
    normed = normed_in[...]
    scaled = gain[...] * normed
    sigma = jax.nn.sigmoid(scaled)
    dscaled = dact * sigma * (1.0 + scaled * (1.0 - sigma))
    product = dscaled * normed
    gain_part[...] = jnp.sum(product, axis=0, keepdims=True)
    dnormed = gain[...] * dscaled
    mean_first = jnp.mean(dnormed, axis=0, keepdims=True)
    mean_second = jnp.mean(dnormed * normed, axis=0, keepdims=True)
    dpre[...] = ((dnormed - mean_first - normed * mean_second) * inverse[...]).astype(BF16)


def conv_back_add(sums, products, begin, planes, taps, rows, sign):
    for at, tap in enumerate(taps):
        a, b, c = tap
        a, b = sign * a, sign * b
        part = products[:, at * rows : (at + 1) * rows].reshape(planes, HEIGHT, WIDTH, rows)
        low, high = max(0, b), HEIGHT + min(0, b)
        sums[1 + c, begin - a : begin - a + planes, low - b : high - b] += part[:, low:high]


def conv_finish(sums, out, sign):
    rows = out.shape[0]
    total = None
    for c in (-1, 0, 1):
        off = sign * c
        part = sums[1 + c].reshape(CELLS, rows)
        if off != 0:
            width_at = lax.broadcasted_iota(jnp.int32, part.shape, 0) % WIDTH
            inside = (width_at + off >= 0) & (width_at + off < WIDTH)
            part = jnp.where(inside, pltpu.roll(part, (-off) % CELLS, 0), 0.0)
        total = part if total is None else total + part
    out[...] = total.T.astype(BF16)


def conv_kernel(n, sign, transposed, idx, w, *refs):
    blocks = refs[:n]
    out, mark, ordered, sums, buffer, sems = refs[-6:]
    mark[...] = jnp.zeros_like(mark)
    rows = out.shape[0]
    copies = start_parts(w, buffer, sems)
    sums[...] = jnp.zeros_like(sums)
    for m in range(n):
        ordered[idx[0] ^ m] = blocks[m][...]
    for a in PLANE_ORDER:
        begin, planes = span_of(-a, sign)
        span = slice(begin * PLANE, (begin + planes) * PLANE)
        lhs = jnp.concatenate([ordered[j, span] for j in range(n)], axis=1)
        copies[a].wait()
        for k in range(0, 9, 2):
            t = (a + 1) * 9 + k
            taps = TAPS[t : t + min(2, 9 - k)]
            if transposed:
                rhs = buffer[t * rows : (t + len(taps)) * rows]
                products = lax.dot_general(lhs, rhs, NT, preferred_element_type=F32)
            else:
                rhs = jnp.concatenate([buffer[t + at] for at in range(len(taps))], axis=1)
                products = jnp.dot(lhs, rhs, preferred_element_type=F32)
            conv_back_add(sums, products, begin, planes, taps, rows, sign)
    conv_finish(sums, out, sign)


def conv_full(name, sign, transposed, idx, w, blocks, after):
    n, rows = len(blocks), blocks[0].shape[1]
    return pl.pallas_call(
        functools.partial(conv_kernel, n, sign, transposed),
        in_specs=[smem(), IN_HBM]
        + [pl.BlockSpec(memory_space=pltpu.VMEM)] * n
        + [UNREAD] * len(after),
        out_specs=[pl.BlockSpec(memory_space=pltpu.VMEM)] * 2,
        out_shape=[
            jax.ShapeDtypeStruct((rows, CELLS), BF16),
            jax.ShapeDtypeStruct((8, 128), F32),
        ],
        scratch_shapes=[
            pltpu.VMEM((n, CELLS, rows), BF16),
            pltpu.VMEM((3, DEPTH, HEIGHT, WIDTH, rows), F32),
            pltpu.VMEM(w.shape, BF16),
            pltpu.SemaphoreType.DMA((3,)),
        ],
        compiler_params=pltpu.CompilerParams(vmem_limit_bytes=LIMIT),
        cost_estimate=LIGHT,
        name=name,
    )(idx, w, *blocks, *after)


def halves_kernel(n, turned, idx, *refs):
    blocks = refs[:n]
    keep, send = refs[-2:]
    half = n // 2
    rows = blocks[0].shape[1]

    def put(out, at, block):
        if turned:
            out[pl.ds(pl.multiple_of(at * rows, rows), rows)] = block[...].astype(F32).T.astype(BF16)
        else:
            out[at] = block[...]

    def split(kept, sent):
        for m in range(half):
            at = (idx[0] ^ m) & (half - 1)
            put(keep, at, blocks[kept + m])
            put(send, at, blocks[sent + m])

    @pl.when(idx[1] == 0)
    def _():
        split(0, half)

    @pl.when(idx[1] != 0)
    def _():
        split(half, 0)


def halves(name, turned, idx, blocks, after):
    n, rows = len(blocks), blocks[0].shape[1]
    shape = (n // 2 * rows, CELLS) if turned else (n // 2, CELLS, rows)
    return pl.pallas_call(
        functools.partial(halves_kernel, n, turned),
        in_specs=[smem()]
        + [pl.BlockSpec(memory_space=pltpu.VMEM)] * n
        + [UNREAD] * len(after),
        out_shape=[jax.ShapeDtypeStruct(shape, BF16)] * 2,
        compiler_params=pltpu.CompilerParams(vmem_limit_bytes=LIMIT),
        cost_estimate=LIGHT,
        name=name,
    )(idx, *blocks, *after)


def moved_second_kernel(own, other, _, out):
    out[...] = jnp.zeros_like(out)
    for which, ref in enumerate((own, other)):
        cells = ref[...].astype(F32).T
        width_at = lax.broadcasted_iota(jnp.int32, cells.shape, 0) % WIDTH
        for c in (-1, 0, 1):
            part = cells if c == 0 else pltpu.roll(cells, c % CELLS, 0)
            inside = (width_at - c >= 0) & (width_at - c < WIDTH)
            part = jnp.where(inside, part, 0.0).astype(BF16)
            out[which, 1 + c, :, 1 : 1 + HEIGHT] = part.reshape(
                DEPTH, HEIGHT, WIDTH, cells.shape[1]
            )


def moved_fields(kernel, name, shape, own, other, after):
    return pl.pallas_call(
        kernel,
        in_specs=[pl.BlockSpec(memory_space=pltpu.VMEM)] * 2 + [UNREAD],
        out_shape=jax.ShapeDtypeStruct(shape, BF16),
        compiler_params=pltpu.CompilerParams(vmem_limit_bytes=LIMIT),
        cost_estimate=LIGHT,
        name=name,
    )(own, other, after)


def split_rows(values):
    high = values.astype(BF16)
    low = (values - high.astype(F32)).astype(BF16)
    empty = jnp.zeros((EXTRA - 2, values.shape[1]), F32)
    return jnp.concatenate([high.astype(F32), low.astype(F32), empty], axis=0).astype(BF16)


def moved_lanes(cells, b, c):
    off = b * WIDTH + c
    if off == 0:
        return cells.astype(BF16)
    at = lax.broadcasted_iota(jnp.int32, cells.shape, 1)
    height_at, width_at = at // WIDTH % HEIGHT, at % WIDTH
    inside = (height_at + b >= 0) & (height_at + b < HEIGHT)
    inside = inside & (width_at + c >= 0) & (width_at + c < WIDTH)
    return jnp.where(inside, pltpu.roll(cells, (-off) % CELLS, 1), 0.0).astype(BF16)


def grad_first_kernel(vol_own, vol_other, own, other, gain_part, *refs):
    outs, moved = refs[-4:-1], refs[-1]
    half, rows = own.shape[0], own.shape[2]
    fields = [ref[...].astype(F32) for ref in (vol_own, vol_other)]
    rhs = [jnp.concatenate([ref[j] for j in range(half)], axis=1) for ref in (own, other)]
    for b in range(3):
        for which in range(2):
            for c in range(3):
                moved[which, c * rows : (c + 1) * rows] = moved_lanes(fields[which], b - 1, c - 1)
        for a in (-1, 0, 1):
            begin, count = max(0, -a) * PLANE, (DEPTH - abs(a)) * PLANE
            shift = begin + a * PLANE
            grads = None
            for which in range(2):
                lhs = moved[which, :, shift : shift + count]
                part = jnp.dot(lhs, rhs[which][begin : begin + count], preferred_element_type=F32)
                grads = part if grads is None else grads + part
            outs[a + 1][3 * rows * b : 3 * rows * (b + 1)] = grads.astype(BF16)
    filler = jnp.zeros((1, half * rows - rows), F32)
    outs[0][9 * rows :] = split_rows(jnp.concatenate([gain_part[...], filler], axis=1))
    for out in outs[1:]:
        out[9 * rows :] = jnp.zeros((EXTRA, half * rows), BF16)


def grad_first(vol_own, vol_other, own, other, gain_part, after):
    half, cells, rows = own.shape
    return pl.pallas_call(
        grad_first_kernel,
        in_specs=[pl.BlockSpec(memory_space=pltpu.VMEM)] * 5 + [UNREAD] * len(after),
        out_specs=[pl.BlockSpec(memory_space=pltpu.VMEM)] * 3,
        out_shape=[jax.ShapeDtypeStruct((9 * rows + EXTRA, half * rows), BF16)] * 3,
        scratch_shapes=[pltpu.VMEM((2, 3 * rows, CELLS), BF16)],
        compiler_params=pltpu.CompilerParams(vmem_limit_bytes=LIMIT),
        cost_estimate=LIGHT,
        name="grad_first",
    )(vol_own, vol_other, own, other, gain_part, *after)


def grad_second_kernel(a, moved, own, other, *refs):
    out = refs[-1]
    rows = out.shape[2]
    begin, planes = max(0, a), DEPTH - abs(a)
    lhs = [
        ref[:, begin * PLANE : (begin + planes) * PLANE] for ref in (own, other)
    ]
    for k in range(0, 9, 2):
        taps = range(k, min(k + 2, 9))
        grads = None
        for which in range(2):
            pieces = []
            for at in taps:
                b, c = at // 3 - 1, at % 3 - 1
                piece = moved[which, 1 + c, begin - a : begin - a + planes, 1 - b : 1 - b + HEIGHT]
                pieces.append(piece.reshape(planes * PLANE, rows))
            rhs = jnp.concatenate(pieces, axis=1)
            part = jnp.dot(lhs[which], rhs, preferred_element_type=F32)
            grads = part if grads is None else grads + part
        for place, at in enumerate(taps):
            out[at] = grads[:, place * rows : (place + 1) * rows].astype(BF16)


def grad_second(a, moved, own, other, after):
    wide, rows = own.shape[0], moved.shape[-1]
    return pl.pallas_call(
        functools.partial(grad_second_kernel, a),
        in_specs=[pl.BlockSpec(memory_space=pltpu.VMEM)] * 3 + [UNREAD] * len(after),
        out_shape=jax.ShapeDtypeStruct((9, wide, rows), BF16),
        compiler_params=pltpu.CompilerParams(vmem_limit_bytes=LIMIT),
        cost_estimate=LIGHT,
        name="grad_second",
    )(moved, own, other, *after)


def finish_kernel(n, axis, factor, chunk, idx, own, other, *refs):
    out, mark, wide, sems = refs[-4:]
    upper = (idx[0] >= n // 2).astype(jnp.int32) ^ idx[1]
    taps, height, width = wide.shape[1:]
    copies = []
    for k, (part, place) in enumerate(((own, upper), (other, 1 - upper))):
        size = (height, width)[axis - 1]
        span = pl.ds(pl.multiple_of(place * size, size), size)
        for third in range(3):
            at = slice(3 * third, 3 * third + 3)
            if len(part.shape) == 2:
                rows = part[3 * third * height : (3 * third + 3) * height]
                rows = rows.reshape(3, height, width)
            else:
                rows = part[at]
            wide[k, at] = rows.astype(F32) * factor
            target = out.at[pl.ds(chunk * taps + 3 * third, 3)]
            target = target.at[:, span] if axis == 1 else target.at[:, :, span]
            copies.append(
                pltpu.make_async_copy(wide.at[k, at], target, sems.at[3 * k + third])
            )
            copies[-1].start()
    mark[...] = jnp.zeros_like(mark)
    for copy in copies:
        copy.wait()


def finish(name, n, axis, factor, idx, chunk, shape, own, other, before, after):
    taps, height, width = shape
    given = [] if before is None else [before]
    full = (27, height * 2, width) if axis == 1 else (27, height, width * 2)
    return pl.pallas_call(
        functools.partial(finish_kernel, n, axis, factor, chunk),
        in_specs=[smem()]
        + [pl.BlockSpec(memory_space=pltpu.VMEM)] * 2
        + [UNREAD] * (len(given) + len(after)),
        out_specs=[UNREAD, pl.BlockSpec(memory_space=pltpu.VMEM)],
        out_shape=[jax.ShapeDtypeStruct(full, F32), jax.ShapeDtypeStruct((8, 128), F32)],
        scratch_shapes=[pltpu.VMEM((2,) + shape, F32), pltpu.SemaphoreType.DMA((6,))],
        input_output_aliases={3: 0} if given else {},
        compiler_params=pltpu.CompilerParams(vmem_limit_bytes=SMALL),
        cost_estimate=LIGHT,
        name=name,
    )(idx, own, other, *given, *after)


def add_kernel(x, y, *refs):
    out = refs[-1]
    if len(x.shape) == 3:
        out[...] = (x[...].astype(F32) + y[...].astype(F32)).astype(BF16)
    else:
        rows = x.shape[0] - EXTRA
        out[:rows] = (x[:rows].astype(F32) + y[:rows].astype(F32)).astype(BF16)
        tail = x[rows:].astype(F32) + y[rows:].astype(F32)
        out[rows:] = split_rows(tail[:1] + tail[1:2])


def pick_kernel(idx, x, y, *refs):
    out = refs[-1]

    @pl.when(idx[2] == 0)
    def _():
        out[...] = x[...]

    @pl.when(idx[2] != 0)
    def _():
        out[...] = y[...]


def whole_call(kernel, name, x, y, after, idx=None):
    given = [] if idx is None else [idx]
    return pl.pallas_call(
        kernel,
        in_specs=[smem()] * len(given)
        + [pl.BlockSpec(memory_space=pltpu.VMEM)] * 2
        + [UNREAD] * len(after),
        out_shape=jax.ShapeDtypeStruct(x.shape, x.dtype),
        compiler_params=pltpu.CompilerParams(vmem_limit_bytes=SMALL),
        cost_estimate=LIGHT,
        name=name,
    )(*given, x, y, *after)


def line_moves(chips):
    inward = [[(h, h + 1), (chips - 1 - h, chips - 2 - h)] for h in range(chips // 2 - 1)]
    mid = chips // 2
    outward = [[(j, i) for i, j in moves] for moves in reversed(inward)]
    return inward + [[(mid - 1, mid), (mid, mid - 1)]], outward


def line_send(x, moves):
    pairs = [(2 * i + k, 2 * j + k) for i, j in moves for k in (0, 1)]
    return lax.ppermute(x, "dp", pairs)


def line_step(step, part, total, idx, place, after):
    sums, outward = line_moves(lax.axis_size("dp") // 2)
    if step < len(sums):
        got = line_send(total, sums[step])
        base = total if step == len(sums) - 1 else part
        return whole_call(add_kernel, "line_add", base, got, after)
    moves = outward[step - len(sums)]
    got = line_send(total, moves)
    takes = functools.reduce(jnp.logical_or, [place // 2 == j for _, j in moves])
    marked = jnp.stack([idx[0], idx[1], takes.astype(jnp.int32)])
    return whole_call(pick_kernel, "line_pick", total, got, after, marked)


def shards(volume, w_first, gain, w_second, cotangent):
    n = lax.axis_size("chan")
    rows = volume.shape[1]
    vol, cot = volume[0], cotangent[0]
    chan, place = lax.axis_index("chan"), lax.axis_index("dp")
    idx = jnp.stack([chan, place % 2]).astype(jnp.int32)
    own_gain = lax.dynamic_slice_in_dim(gain, chan * rows, rows, 0)[None]
    factor = 1.0 / math.sqrt(lax.axis_size("dp") * CELLS)

    def to_partner(x, m):
        return lax.ppermute(x, "chan", [(i, i ^ m) for i in range(n)])

    def to_core(x):
        return lax.ppermute(x, "dp", [(i, i ^ 1) for i in range(lax.axis_size("dp"))])

    def swap(parts):
        got = {m: to_partner(parts[m], m) for m in reversed(range(1, n))}
        return [parts[0]] + [got[m] for m in range(1, n)]

    first_flat = w_first.reshape(27 * rows, n * rows)
    pre_shares = swap(spread_shares(1, "pre", idx, n, vol, first_flat, LARGE))
    dact_parts = spread_shares(-1, "dact", idx, n, cot, w_second, LIMIT)
    held = dact_parts[1:]
    act, normed, inverse, *held = pl.pallas_call(
        functools.partial(norm_kernel, n),
        in_specs=[pl.BlockSpec(memory_space=pltpu.VMEM)] * (1 + n) + [UNREAD] * len(held),
        out_specs=[pl.BlockSpec(memory_space=pltpu.VMEM)] * 3 + [UNREAD] * len(held),
        out_shape=[
            jax.ShapeDtypeStruct((CELLS, rows), BF16),
            jax.ShapeDtypeStruct((CELLS, rows), F32),
            jax.ShapeDtypeStruct((1, rows), F32),
        ]
        + [jax.ShapeDtypeStruct(x.shape, x.dtype) for x in held],
        input_output_aliases={1 + n + k: 3 + k for k in range(len(held))},
        compiler_params=pltpu.CompilerParams(vmem_limit_bytes=SMALL),
        cost_estimate=LIGHT,
        name="norm",
    )(own_gain, *pre_shares, *held)
    act_blocks = swap([act] * n)
    dact_shares = swap([dact_parts[0]] + held)
    moved_cot = moved_fields(
        moved_second_kernel,
        "moved_second",
        (2, 3, DEPTH, HEIGHT + 2, WIDTH, rows),
        cot,
        to_core(cot),
        act,
    )
    vol_other = to_core(vol)
    act_keep, act_send = halves("act_halves", True, idx, act_blocks, (moved_cot, vol_other))
    act_other = to_core(act_send)

    sums, outward = line_moves(lax.axis_size("dp") // 2)
    steps = len(sums) + len(outward)
    parts, totals, crossed = {}, {}, {}
    last = ()

    reached = [0] * 6

    def line(chunk, step):
        nonlocal last
        if reached[chunk] > step:
            return
        if reached[chunk] < step:
            line(chunk, step - 1)
        reached[chunk] = step + 1
        before = totals.get(chunk, parts[chunk])
        totals[chunk] = line_step(step, parts[chunk], before, idx, place, last)
        last = (totals[chunk],)
        if step == steps - 1:
            crossed[chunk] = to_core(totals[chunk])

    def write(chunk):
        nonlocal last
        line(chunk, steps - 1)
        name, axis = ("finish_second", 1) if chunk < 3 else ("finish_first", 2)
        shape = (9, n // 2 * rows, rows) if chunk < 3 else (9, rows, n // 2 * rows)
        written[axis], mark = finish(
            name,
            n,
            axis,
            factor,
            idx,
            chunk % 3,
            shape,
            totals[chunk],
            crossed[chunk],
            written.get(axis),
            last,
        )
        last = (mark,)

    def second_part(chunk):
        nonlocal last
        parts[chunk] = grad_second(chunk - 1, moved_cot, act_keep, act_other, last)
        last = (parts[chunk],)

    def first_parts():
        nonlocal last
        own, other = done["dpre_halves"]
        parts[3], parts[4], parts[5] = grad_first(
            vol, vol_other, own, other, done["gain"], last
        )
        last = (parts[3],)

    def norm_back():
        nonlocal last
        dpre, done["gain"] = pl.pallas_call(
            functools.partial(norm_back_kernel, n),
            in_specs=[pl.BlockSpec(memory_space=pltpu.VMEM)] * (3 + n) + [UNREAD],
            out_shape=[
                jax.ShapeDtypeStruct((CELLS, rows), BF16),
                jax.ShapeDtypeStruct((1, rows), F32),
            ],
            compiler_params=pltpu.CompilerParams(vmem_limit_bytes=SMALL),
            cost_estimate=LIGHT,
            name="norm_back",
        )(own_gain, normed, inverse, *dact_shares, *last)
        done["dpre"] = swap([dpre] * n)
        last = (dpre,)

    def dpre_halves():
        nonlocal last
        keep, send = halves("dpre_halves", False, idx, done["dpre"], last)
        done["dpre_halves"] = keep, to_core(send)
        last = (keep,)

    def output():
        nonlocal last
        done["output"], mark = conv_full("output", 1, False, idx, w_second, act_blocks, last)
        last = (mark,)

    def grad_volume():
        nonlocal last
        done["grad_volume"], mark = conv_full(
            "grad_volume", -1, True, idx, first_flat, done["dpre"], last
        )
        last = (mark,)

    written, done = {}, {}
    second_part(0)
    second_part(1)
    output()
    norm_back()
    line(0, 0)
    second_part(2)
    line(1, 0)
    line(0, 1)
    dpre_halves()
    first_parts()
    line(2, 0)
    line(1, 1)
    line(0, 2)
    line(3, 0)
    line(2, 1)
    line(1, 2)
    write(0)
    line(4, 0)
    line(3, 1)
    line(2, 2)
    line(5, 0)
    line(4, 1)
    write(1)
    line(3, 2)
    write(2)
    line(5, 1)
    line(4, 2)
    write(3)
    write(4)
    grad_volume()
    line(5, 2)
    write(5)
    gain_rows = totals[3][9 * rows : 9 * rows + 2, :rows].astype(F32)
    gain_rows_other = crossed[3][9 * rows : 9 * rows + 2, :rows].astype(F32)
    gain_total = (jnp.sum(gain_rows, axis=0) + jnp.sum(gain_rows_other, axis=0)) * factor
    return (done["output"][None], done["grad_volume"][None], written[2], gain_total, written[1])


def solution(mesh):
    placed = (
        P("dp", "chan", None),
        P(None, "chan", None),
        P(),
        P(None, None, "chan"),
        P("dp", "chan", None),
    )
    return jax.shard_map(
        shards,
        mesh=mesh,
        in_specs=placed,
        out_specs=(
            P("dp", "chan", None),
            P("dp", "chan", None),
            P(None, "chan", None),
            P("chan"),
            P(None, None, "chan"),
        ),
        check_vma=False,
    )
```

```python
import functools
import math

import jax
import jax.numpy as jnp
from jax import lax
from jax.experimental import pallas as pl
from jax.experimental.pallas import tpu as pltpu
from jax.sharding import PartitionSpec as P

DEPTH, HEIGHT, WIDTH = 4, 16, 16
PLANE = HEIGHT * WIDTH
CELLS = DEPTH * PLANE
TAPS = [(a, b, c) for a in (-1, 0, 1) for b in (-1, 0, 1) for c in (-1, 0, 1)]
NORM_EPS = 1e-05
LIMIT = 16 * 1024 * 1024
SMALL = 8 * 1024 * 1024
LARGE = 59 * 1024 * 1024
EXTRA = 16
F32, BF16 = jnp.float32, jnp.bfloat16
NT = (((1,), (1,)), ((), ()))
UNREAD = pl.BlockSpec(memory_space=pl.ANY)
IN_HBM = pl.BlockSpec(memory_space=pltpu.HBM)
PLANE_ORDER = (0, -1, 1)
LIGHT = pl.CostEstimate(flops=1024, bytes_accessed=1024, transcendentals=0)


CHAIN = (
    ("second", 0),
    ("second", 1),
    ("output",),
    ("norm_back",),
    ("line", 0, 0),
    ("second", 2),
    ("line", 1, 0),
    ("line", 0, 1),
    ("halves",),
    ("first",),
    ("line", 2, 0),
    ("line", 1, 1),
    ("line", 0, 2),
    ("line", 3, 0),
    ("line", 2, 1),
    ("line", 1, 2),
    ("write", 0),
    ("line", 4, 0),
    ("line", 3, 1),
    ("line", 2, 2),
    ("write", 1),
    ("line", 5, 0),
    ("line", 4, 1),
    ("line", 3, 2),
    ("write", 2),
    ("line", 5, 1),
    ("line", 4, 2),
    ("grad_volume",),
    ("write", 3),
    ("line", 5, 2),
    ("write", 4),
    ("write", 5),
)


def params():
    return pltpu.CompilerParams(
        dimension_semantics=("arbitrary",), vmem_limit_bytes=LIMIT
    )


def whole(shape):
    return pl.BlockSpec(shape, lambda *_: (0,) * len(shape))


def smem():
    return pl.BlockSpec(memory_space=pltpu.SMEM)


def fill_padded(padded, rows_first, sign):
    padded[...] = jnp.zeros_like(padded)
    cells = rows_first.astype(F32).T
    width_at = lax.broadcasted_iota(jnp.int32, cells.shape, 0) % WIDTH
    for c in (-1, 0, 1):
        off = sign * c
        moved = cells if off == 0 else pltpu.roll(cells, (-off) % CELLS, 0)
        inside = (width_at + off >= 0) & (width_at + off < WIDTH)
        moved = jnp.where(inside, moved, 0.0).astype(BF16)
        padded[1 + c, 1 : 1 + DEPTH, 1 : 1 + HEIGHT] = moved.reshape(
            DEPTH, HEIGHT, WIDTH, cells.shape[1]
        )


def span_of(a, sign):
    return max(0, -sign * a), DEPTH - abs(a)


def start_parts(source, buffer, sems):
    size = source.shape[0] // 3
    copies = {}
    for a in PLANE_ORDER:
        span = pl.ds((a + 1) * size, size)
        copies[a] = pltpu.make_async_copy(source.at[span], buffer.at[span], sems.at[a + 1])
        copies[a].start()
    return copies


def share_kernel(n, sign, idx, field, w, *refs):
    outs = refs[:n]
    padded, sums, shares, buffer, sems = refs[n:]
    rows = field.shape[0]
    copies = start_parts(w, buffer, sems)
    fill_padded(padded, field[...], sign)
    for a in PLANE_ORDER:
        begin, planes = span_of(a, sign)
        pieces = []
        for b in (-1, 0, 1):
            for c in (-1, 0, 1):
                low, first = 1 + sign * b, 1 + begin + sign * a
                piece = padded[1 + c, first : first + planes, low : low + HEIGHT]
                pieces.append(piece.reshape(planes * PLANE, rows))
        lhs = jnp.concatenate(pieces, axis=1)
        copies[a].wait()
        if sign == 1:
            rhs = buffer[(a + 1) * 9 * rows : (a + 2) * 9 * rows]
            part = jnp.dot(lhs, rhs, preferred_element_type=F32)
        else:
            rhs = jnp.concatenate([buffer[(a + 1) * 9 + k] for k in range(9)], axis=1)
            part = lax.dot_general(lhs, rhs, NT, preferred_element_type=F32)
        span = slice(begin * PLANE, (begin + planes) * PLANE)
        if a == 0:
            sums[...] = part
        else:
            sums[span] += part
    for j in range(n):
        shares[j] = sums[:, j * rows : (j + 1) * rows].astype(BF16)
    for m in range(n):
        outs[m][...] = shares[idx[0] ^ m]


def spread_shares(sign, name, idx, n, field, w, limit):
    rows = field.shape[0]
    return pl.pallas_call(
        functools.partial(share_kernel, n, sign),
        in_specs=[smem(), pl.BlockSpec(memory_space=pltpu.VMEM), IN_HBM],
        out_specs=[pl.BlockSpec(memory_space=pltpu.VMEM)] * n,
        out_shape=[jax.ShapeDtypeStruct((CELLS, rows), BF16)] * n,
        scratch_shapes=[
            pltpu.VMEM((3, DEPTH + 2, HEIGHT + 2, WIDTH, rows), BF16),
            pltpu.VMEM((CELLS, n * rows), F32),
            pltpu.VMEM((n, CELLS, rows), BF16),
            pltpu.VMEM(w.shape, BF16),
            pltpu.SemaphoreType.DMA((3,)),
        ],
        compiler_params=pltpu.CompilerParams(vmem_limit_bytes=limit),
        cost_estimate=LIGHT,
        name=name,
    )(idx, field, w)


def norm_kernel(n, gain, *refs):
    shares = refs[:n]
    act, normed_out, inverse_out = refs[2 * n - 1 : 2 * n + 2]
    pre = shares[0][...].astype(F32)
    for m in range(1, n):
        pre = pre + shares[m][...].astype(F32)
    center = pre - jnp.mean(pre, axis=0, keepdims=True)
    inverse = lax.rsqrt(jnp.mean(center * center, axis=0, keepdims=True) + NORM_EPS)
    normed = center * inverse
    scaled = gain[...] * normed
    act[...] = (scaled * jax.nn.sigmoid(scaled)).astype(BF16)
    normed_out[...] = normed
    inverse_out[...] = inverse


def norm_back_kernel(n, gain, normed_in, inverse, *refs):
    shares = refs[:n]
    dpre, gain_part = refs[-2:]
    dact = shares[0][...].astype(F32)
    for m in range(1, n):
        dact = dact + shares[m][...].astype(F32)
    normed = normed_in[...]
    scaled = gain[...] * normed
    sigma = jax.nn.sigmoid(scaled)
    dscaled = dact * sigma * (1.0 + scaled * (1.0 - sigma))
    product = dscaled * normed
    gain_part[...] = jnp.sum(product, axis=0, keepdims=True)
    dnormed = gain[...] * dscaled
    mean_first = jnp.mean(dnormed, axis=0, keepdims=True)
    mean_second = jnp.mean(dnormed * normed, axis=0, keepdims=True)
    dpre[...] = ((dnormed - mean_first - normed * mean_second) * inverse[...]).astype(BF16)


def conv_back_add(sums, products, begin, planes, taps, rows, sign):
    for at, tap in enumerate(taps):
        a, b, c = tap
        a, b = sign * a, sign * b
        part = products[:, at * rows : (at + 1) * rows].reshape(planes, HEIGHT, WIDTH, rows)
        low, high = max(0, b), HEIGHT + min(0, b)
        sums[1 + c, begin - a : begin - a + planes, low - b : high - b] += part[:, low:high]


def conv_finish(sums, out, sign):
    rows = out.shape[0]
    total = None
    for c in (-1, 0, 1):
        off = sign * c
        part = sums[1 + c].reshape(CELLS, rows)
        if off != 0:
            width_at = lax.broadcasted_iota(jnp.int32, part.shape, 0) % WIDTH
            inside = (width_at + off >= 0) & (width_at + off < WIDTH)
            part = jnp.where(inside, pltpu.roll(part, (-off) % CELLS, 0), 0.0)
        total = part if total is None else total + part
    out[...] = total.T.astype(BF16)


def conv_kernel(n, sign, transposed, idx, w, *refs):
    blocks = refs[:n]
    out, mark, ordered, sums, buffer, sems = refs[-6:]
    mark[...] = jnp.zeros_like(mark)
    rows = out.shape[0]
    copies = start_parts(w, buffer, sems)
    sums[...] = jnp.zeros_like(sums)
    for m in range(n):
        ordered[idx[0] ^ m] = blocks[m][...]
    for a in PLANE_ORDER:
        begin, planes = span_of(-a, sign)
        span = slice(begin * PLANE, (begin + planes) * PLANE)
        lhs = jnp.concatenate([ordered[j, span] for j in range(n)], axis=1)
        copies[a].wait()
        for k in range(0, 9, 2):
            t = (a + 1) * 9 + k
            taps = TAPS[t : t + min(2, 9 - k)]
            if transposed:
                rhs = buffer[t * rows : (t + len(taps)) * rows]
                products = lax.dot_general(lhs, rhs, NT, preferred_element_type=F32)
            else:
                rhs = jnp.concatenate([buffer[t + at] for at in range(len(taps))], axis=1)
                products = jnp.dot(lhs, rhs, preferred_element_type=F32)
            conv_back_add(sums, products, begin, planes, taps, rows, sign)
    conv_finish(sums, out, sign)


def conv_full(name, sign, transposed, idx, w, blocks, after):
    n, rows = len(blocks), blocks[0].shape[1]
    return pl.pallas_call(
        functools.partial(conv_kernel, n, sign, transposed),
        in_specs=[smem(), IN_HBM]
        + [pl.BlockSpec(memory_space=pltpu.VMEM)] * n
        + [UNREAD] * len(after),
        out_specs=[pl.BlockSpec(memory_space=pltpu.VMEM)] * 2,
        out_shape=[
            jax.ShapeDtypeStruct((rows, CELLS), BF16),
            jax.ShapeDtypeStruct((8, 128), F32),
        ],
        scratch_shapes=[
            pltpu.VMEM((n, CELLS, rows), BF16),
            pltpu.VMEM((3, DEPTH, HEIGHT, WIDTH, rows), F32),
            pltpu.VMEM(w.shape, BF16),
            pltpu.SemaphoreType.DMA((3,)),
        ],
        compiler_params=pltpu.CompilerParams(vmem_limit_bytes=LIMIT),
        cost_estimate=LIGHT,
        name=name,
    )(idx, w, *blocks, *after)


def halves_kernel(n, turned, idx, *refs):
    blocks = refs[:n]
    keep, send = refs[-2:]
    half = n // 2
    rows = blocks[0].shape[1]

    def put(out, at, block):
        if turned:
            out[pl.ds(pl.multiple_of(at * rows, rows), rows)] = block[...].astype(F32).T.astype(BF16)
        else:
            out[at] = block[...]

    def split(kept, sent):
        for m in range(half):
            at = (idx[0] ^ m) & (half - 1)
            put(keep, at, blocks[kept + m])
            put(send, at, blocks[sent + m])

    @pl.when(idx[1] == 0)
    def _():
        split(0, half)

    @pl.when(idx[1] != 0)
    def _():
        split(half, 0)


def halves(name, turned, idx, blocks, after):
    n, rows = len(blocks), blocks[0].shape[1]
    shape = (n // 2 * rows, CELLS) if turned else (n // 2, CELLS, rows)
    return pl.pallas_call(
        functools.partial(halves_kernel, n, turned),
        in_specs=[smem()]
        + [pl.BlockSpec(memory_space=pltpu.VMEM)] * n
        + [UNREAD] * len(after),
        out_shape=[jax.ShapeDtypeStruct(shape, BF16)] * 2,
        compiler_params=pltpu.CompilerParams(vmem_limit_bytes=LIMIT),
        cost_estimate=LIGHT,
        name=name,
    )(idx, *blocks, *after)


def moved_second_kernel(own, other, _, out):
    out[...] = jnp.zeros_like(out)
    for which, ref in enumerate((own, other)):
        cells = ref[...].astype(F32).T
        width_at = lax.broadcasted_iota(jnp.int32, cells.shape, 0) % WIDTH
        for c in (-1, 0, 1):
            part = cells if c == 0 else pltpu.roll(cells, c % CELLS, 0)
            inside = (width_at - c >= 0) & (width_at - c < WIDTH)
            part = jnp.where(inside, part, 0.0).astype(BF16)
            out[which, 1 + c, :, 1 : 1 + HEIGHT] = part.reshape(
                DEPTH, HEIGHT, WIDTH, cells.shape[1]
            )


def moved_fields(kernel, name, shape, own, other, after):
    return pl.pallas_call(
        kernel,
        in_specs=[pl.BlockSpec(memory_space=pltpu.VMEM)] * 2 + [UNREAD],
        out_shape=jax.ShapeDtypeStruct(shape, BF16),
        compiler_params=pltpu.CompilerParams(vmem_limit_bytes=LIMIT),
        cost_estimate=LIGHT,
        name=name,
    )(own, other, after)


def split_rows(values):
    high = values.astype(BF16)
    low = (values - high.astype(F32)).astype(BF16)
    empty = jnp.zeros((EXTRA - 2, values.shape[1]), F32)
    return jnp.concatenate([high.astype(F32), low.astype(F32), empty], axis=0).astype(BF16)


def moved_lanes(cells, b, c):
    off = b * WIDTH + c
    if off == 0:
        return cells.astype(BF16)
    at = lax.broadcasted_iota(jnp.int32, cells.shape, 1)
    height_at, width_at = at // WIDTH % HEIGHT, at % WIDTH
    inside = (height_at + b >= 0) & (height_at + b < HEIGHT)
    inside = inside & (width_at + c >= 0) & (width_at + c < WIDTH)
    return jnp.where(inside, pltpu.roll(cells, (-off) % CELLS, 1), 0.0).astype(BF16)


def grad_first_kernel(vol_own, vol_other, own, other, gain_part, *refs):
    outs, moved = refs[-4:-1], refs[-1]
    half, rows = own.shape[0], own.shape[2]
    fields = [ref[...].astype(F32) for ref in (vol_own, vol_other)]
    rhs = [jnp.concatenate([ref[j] for j in range(half)], axis=1) for ref in (own, other)]
    for b in range(3):
        for which in range(2):
            for c in range(3):
                moved[which, c * rows : (c + 1) * rows] = moved_lanes(fields[which], b - 1, c - 1)
        for a in (-1, 0, 1):
            begin, count = max(0, -a) * PLANE, (DEPTH - abs(a)) * PLANE
            shift = begin + a * PLANE
            grads = None
            for which in range(2):
                lhs = moved[which, :, shift : shift + count]
                part = jnp.dot(lhs, rhs[which][begin : begin + count], preferred_element_type=F32)
                grads = part if grads is None else grads + part
            outs[a + 1][3 * rows * b : 3 * rows * (b + 1)] = grads.astype(BF16)
    filler = jnp.zeros((1, half * rows - rows), F32)
    outs[0][9 * rows :] = split_rows(jnp.concatenate([gain_part[...], filler], axis=1))
    for out in outs[1:]:
        out[9 * rows :] = jnp.zeros((EXTRA, half * rows), BF16)


def grad_first(vol_own, vol_other, own, other, gain_part, after):
    half, cells, rows = own.shape
    return pl.pallas_call(
        grad_first_kernel,
        in_specs=[pl.BlockSpec(memory_space=pltpu.VMEM)] * 5 + [UNREAD] * len(after),
        out_specs=[pl.BlockSpec(memory_space=pltpu.VMEM)] * 3,
        out_shape=[jax.ShapeDtypeStruct((9 * rows + EXTRA, half * rows), BF16)] * 3,
        scratch_shapes=[pltpu.VMEM((2, 3 * rows, CELLS), BF16)],
        compiler_params=pltpu.CompilerParams(vmem_limit_bytes=LIMIT),
        cost_estimate=LIGHT,
        name="grad_first",
    )(vol_own, vol_other, own, other, gain_part, *after)


def grad_second_kernel(a, moved, own, other, *refs):
    out = refs[-1]
    rows = out.shape[2]
    begin, planes = max(0, a), DEPTH - abs(a)
    lhs = [
        ref[:, begin * PLANE : (begin + planes) * PLANE] for ref in (own, other)
    ]
    for k in range(0, 9, 2):
        taps = range(k, min(k + 2, 9))
        grads = None
        for which in range(2):
            pieces = []
            for at in taps:
                b, c = at // 3 - 1, at % 3 - 1
                piece = moved[which, 1 + c, begin - a : begin - a + planes, 1 - b : 1 - b + HEIGHT]
                pieces.append(piece.reshape(planes * PLANE, rows))
            rhs = jnp.concatenate(pieces, axis=1)
            part = jnp.dot(lhs[which], rhs, preferred_element_type=F32)
            grads = part if grads is None else grads + part
        for place, at in enumerate(taps):
            out[at] = grads[:, place * rows : (place + 1) * rows].astype(BF16)


def grad_second(a, moved, own, other, after):
    wide, rows = own.shape[0], moved.shape[-1]
    return pl.pallas_call(
        functools.partial(grad_second_kernel, a),
        in_specs=[pl.BlockSpec(memory_space=pltpu.VMEM)] * 3 + [UNREAD] * len(after),
        out_shape=jax.ShapeDtypeStruct((9, wide, rows), BF16),
        compiler_params=pltpu.CompilerParams(vmem_limit_bytes=LIMIT),
        cost_estimate=LIGHT,
        name="grad_second",
    )(moved, own, other, *after)


def finish_kernel(n, axis, factor, chunk, idx, own, other, *refs):
    out, mark, wide, sems = refs[-4:]
    upper = (idx[0] >= n // 2).astype(jnp.int32) ^ idx[1]
    taps, height, width = wide.shape[1:]
    copies = []
    for k, (part, place) in enumerate(((own, upper), (other, 1 - upper))):
        size = (height, width)[axis - 1]
        span = pl.ds(pl.multiple_of(place * size, size), size)
        for third in range(3):
            at = slice(3 * third, 3 * third + 3)
            if len(part.shape) == 2:
                rows = part[3 * third * height : (3 * third + 3) * height]
                rows = rows.reshape(3, height, width)
            else:
                rows = part[at]
            wide[k, at] = rows.astype(F32) * factor
            target = out.at[pl.ds(chunk * taps + 3 * third, 3)]
            target = target.at[:, span] if axis == 1 else target.at[:, :, span]
            copies.append(
                pltpu.make_async_copy(wide.at[k, at], target, sems.at[3 * k + third])
            )
            copies[-1].start()
    mark[...] = jnp.zeros_like(mark)
    for copy in copies:
        copy.wait()


def finish(name, n, axis, factor, idx, chunk, shape, own, other, before, after):
    taps, height, width = shape
    given = [] if before is None else [before]
    full = (27, height * 2, width) if axis == 1 else (27, height, width * 2)
    return pl.pallas_call(
        functools.partial(finish_kernel, n, axis, factor, chunk),
        in_specs=[smem()]
        + [pl.BlockSpec(memory_space=pltpu.VMEM)] * 2
        + [UNREAD] * (len(given) + len(after)),
        out_specs=[UNREAD, pl.BlockSpec(memory_space=pltpu.VMEM)],
        out_shape=[jax.ShapeDtypeStruct(full, F32), jax.ShapeDtypeStruct((8, 128), F32)],
        scratch_shapes=[pltpu.VMEM((2,) + shape, F32), pltpu.SemaphoreType.DMA((6,))],
        input_output_aliases={3: 0} if given else {},
        compiler_params=pltpu.CompilerParams(vmem_limit_bytes=SMALL),
        cost_estimate=LIGHT,
        name=name,
    )(idx, own, other, *given, *after)


def add_kernel(x, y, *refs):
    out = refs[-1]
    if len(x.shape) == 3:
        out[...] = (x[...].astype(F32) + y[...].astype(F32)).astype(BF16)
    else:
        rows = x.shape[0] - EXTRA
        out[:rows] = (x[:rows].astype(F32) + y[:rows].astype(F32)).astype(BF16)
        tail = x[rows:].astype(F32) + y[rows:].astype(F32)
        out[rows:] = split_rows(tail[:1] + tail[1:2])


def pick_kernel(idx, x, y, *refs):
    out = refs[-1]

    @pl.when(idx[2] == 0)
    def _():
        out[...] = x[...]

    @pl.when(idx[2] != 0)
    def _():
        out[...] = y[...]


def whole_call(kernel, name, x, y, after, idx=None):
    given = [] if idx is None else [idx]
    return pl.pallas_call(
        kernel,
        in_specs=[smem()] * len(given)
        + [pl.BlockSpec(memory_space=pltpu.VMEM)] * 2
        + [UNREAD] * len(after),
        out_shape=jax.ShapeDtypeStruct(x.shape, x.dtype),
        compiler_params=pltpu.CompilerParams(vmem_limit_bytes=SMALL),
        cost_estimate=LIGHT,
        name=name,
    )(*given, x, y, *after)


def line_moves(chips):
    inward = [[(h, h + 1), (chips - 1 - h, chips - 2 - h)] for h in range(chips // 2 - 1)]
    mid = chips // 2
    outward = [[(j, i) for i, j in moves] for moves in reversed(inward)]
    return inward + [[(mid - 1, mid), (mid, mid - 1)]], outward


def line_send(x, moves):
    pairs = [(2 * i + k, 2 * j + k) for i, j in moves for k in (0, 1)]
    return lax.ppermute(x, "dp", pairs)


def line_step(step, part, total, idx, place, after):
    sums, outward = line_moves(lax.axis_size("dp") // 2)
    if step < len(sums):
        got = line_send(total, sums[step])
        base = total if step == len(sums) - 1 else part
        return whole_call(add_kernel, "line_add", base, got, after)
    moves = outward[step - len(sums)]
    got = line_send(total, moves)
    takes = functools.reduce(jnp.logical_or, [place // 2 == j for _, j in moves])
    marked = jnp.stack([idx[0], idx[1], takes.astype(jnp.int32)])
    return whole_call(pick_kernel, "line_pick", total, got, after, marked)


def shards(volume, w_first, gain, w_second, cotangent):
    n = lax.axis_size("chan")
    rows = volume.shape[1]
    vol, cot = volume[0], cotangent[0]
    chan, place = lax.axis_index("chan"), lax.axis_index("dp")
    idx = jnp.stack([chan, place % 2]).astype(jnp.int32)
    own_gain = lax.dynamic_slice_in_dim(gain, chan * rows, rows, 0)[None]
    factor = 1.0 / math.sqrt(lax.axis_size("dp") * CELLS)

    def to_partner(x, m):
        return lax.ppermute(x, "chan", [(i, i ^ m) for i in range(n)])

    def to_core(x):
        return lax.ppermute(x, "dp", [(i, i ^ 1) for i in range(lax.axis_size("dp"))])

    def swap(parts):
        got = {m: to_partner(parts[m], m) for m in reversed(range(1, n))}
        return [parts[0]] + [got[m] for m in range(1, n)]

    first_flat = w_first.reshape(27 * rows, n * rows)
    pre_shares = swap(spread_shares(1, "pre", idx, n, vol, first_flat, LARGE))
    dact_parts = spread_shares(-1, "dact", idx, n, cot, w_second, LIMIT)
    held = dact_parts[1:]
    act, normed, inverse, *held = pl.pallas_call(
        functools.partial(norm_kernel, n),
        in_specs=[pl.BlockSpec(memory_space=pltpu.VMEM)] * (1 + n) + [UNREAD] * len(held),
        out_specs=[pl.BlockSpec(memory_space=pltpu.VMEM)] * 3 + [UNREAD] * len(held),
        out_shape=[
            jax.ShapeDtypeStruct((CELLS, rows), BF16),
            jax.ShapeDtypeStruct((CELLS, rows), F32),
            jax.ShapeDtypeStruct((1, rows), F32),
        ]
        + [jax.ShapeDtypeStruct(x.shape, x.dtype) for x in held],
        input_output_aliases={1 + n + k: 3 + k for k in range(len(held))},
        compiler_params=pltpu.CompilerParams(vmem_limit_bytes=SMALL),
        cost_estimate=LIGHT,
        name="norm",
    )(own_gain, *pre_shares, *held)
    act_blocks = swap([act] * n)
    dact_shares = swap([dact_parts[0]] + held)
    moved_cot = moved_fields(
        moved_second_kernel,
        "moved_second",
        (2, 3, DEPTH, HEIGHT + 2, WIDTH, rows),
        cot,
        to_core(cot),
        act,
    )
    vol_other = to_core(vol)
    act_keep, act_send = halves("act_halves", True, idx, act_blocks, (moved_cot, vol_other))
    act_other = to_core(act_send)

    sums, outward = line_moves(lax.axis_size("dp") // 2)
    steps = len(sums) + len(outward)
    parts, totals, crossed = {}, {}, {}
    last = ()

    reached = [0] * 6

    def line(chunk, step):
        nonlocal last
        if reached[chunk] > step:
            return
        if reached[chunk] < step:
            line(chunk, step - 1)
        reached[chunk] = step + 1
        before = totals.get(chunk, parts[chunk])
        totals[chunk] = line_step(step, parts[chunk], before, idx, place, last)
        last = (totals[chunk],)
        if step == steps - 1:
            crossed[chunk] = to_core(totals[chunk])

    def write(chunk):
        nonlocal last
        line(chunk, steps - 1)
        name, axis = ("finish_second", 1) if chunk < 3 else ("finish_first", 2)
        shape = (9, n // 2 * rows, rows) if chunk < 3 else (9, rows, n // 2 * rows)
        written[axis], mark = finish(
            name,
            n,
            axis,
            factor,
            idx,
            chunk % 3,
            shape,
            totals[chunk],
            crossed[chunk],
            written.get(axis),
            last,
        )
        last = (mark,)

    def second_part(chunk):
        nonlocal last
        parts[chunk] = grad_second(chunk - 1, moved_cot, act_keep, act_other, last)
        last = (parts[chunk],)

    def first_parts():
        nonlocal last
        own, other = done["dpre_halves"]
        parts[3], parts[4], parts[5] = grad_first(
            vol, vol_other, own, other, done["gain"], last
        )
        last = (parts[3],)

    def norm_back():
        nonlocal last
        dpre, done["gain"] = pl.pallas_call(
            functools.partial(norm_back_kernel, n),
            in_specs=[pl.BlockSpec(memory_space=pltpu.VMEM)] * (3 + n) + [UNREAD],
            out_shape=[
                jax.ShapeDtypeStruct((CELLS, rows), BF16),
                jax.ShapeDtypeStruct((1, rows), F32),
            ],
            compiler_params=pltpu.CompilerParams(vmem_limit_bytes=SMALL),
            cost_estimate=LIGHT,
            name="norm_back",
        )(own_gain, normed, inverse, *dact_shares, *last)
        done["dpre"] = swap([dpre] * n)
        last = (dpre,)

    def dpre_halves():
        nonlocal last
        keep, send = halves("dpre_halves", False, idx, done["dpre"], last)
        done["dpre_halves"] = keep, to_core(send)
        last = (keep,)

    def output():
        nonlocal last
        done["output"], mark = conv_full("output", 1, False, idx, w_second, act_blocks, last)
        last = (mark,)

    def grad_volume():
        nonlocal last
        done["grad_volume"], mark = conv_full(
            "grad_volume", -1, True, idx, first_flat, done["dpre"], last
        )
        last = (mark,)

    written, done = {}, {}
    steps_by_name = {
        "second": second_part,
        "first": first_parts,
        "output": output,
        "grad_volume": grad_volume,
        "norm_back": norm_back,
        "halves": dpre_halves,
        "line": line,
        "write": write,
    }
    for name, *at in CHAIN:
        steps_by_name[name](*at)
    gain_rows = totals[3][9 * rows : 9 * rows + 2, :rows].astype(F32)
    gain_rows_other = crossed[3][9 * rows : 9 * rows + 2, :rows].astype(F32)
    gain_total = (jnp.sum(gain_rows, axis=0) + jnp.sum(gain_rows_other, axis=0)) * factor
    return (done["output"][None], done["grad_volume"][None], written[2], gain_total, written[1])


def solution(mesh):
    placed = (
        P("dp", "chan", None),
        P(None, "chan", None),
        P(),
        P(None, None, "chan"),
        P("dp", "chan", None),
    )
    return jax.shard_map(
        shards,
        mesh=mesh,
        in_specs=placed,
        out_specs=(
            P("dp", "chan", None),
            P("dp", "chan", None),
            P(None, "chan", None),
            P("chan"),
            P(None, None, "chan"),
        ),
        check_vma=False,
    )
```

```python
import functools
import math

import jax
import jax.numpy as jnp
from jax import lax
from jax.experimental import pallas as pl
from jax.experimental.pallas import tpu as pltpu
from jax.sharding import PartitionSpec as P

DEPTH, HEIGHT, WIDTH = 4, 16, 16
PLANE = HEIGHT * WIDTH
CELLS = DEPTH * PLANE
TAPS = [(a, b, c) for a in (-1, 0, 1) for b in (-1, 0, 1) for c in (-1, 0, 1)]
NORM_EPS = 1e-05
LIMIT = 12 * 1024 * 1024
SMALL = 8 * 1024 * 1024
LARGE = 44 * 1024 * 1024
EXTRA = 16
F32, BF16 = jnp.float32, jnp.bfloat16
NT = (((1,), (1,)), ((), ()))
UNREAD = pl.BlockSpec(memory_space=pl.ANY)
IN_HBM = pl.BlockSpec(memory_space=pltpu.HBM)
PLANE_ORDER = (0, -1, 1)
LIGHT = pl.CostEstimate(flops=1024, bytes_accessed=1024, transcendentals=0)


CHAIN = (
    ("second", 0),
    ("second", 1),
    ("output",),
    ("norm_back",),
    ("line", 0, 0),
    ("second", 2),
    ("line", 1, 0),
    ("line", 0, 1),
    ("halves",),
    ("first",),
    ("line", 2, 0),
    ("line", 1, 1),
    ("line", 0, 2),
    ("line", 3, 0),
    ("line", 2, 1),
    ("line", 1, 2),
    ("write", 0),
    ("line", 4, 0),
    ("line", 3, 1),
    ("line", 2, 2),
    ("write", 1),
    ("line", 5, 0),
    ("line", 4, 1),
    ("line", 3, 2),
    ("write", 2),
    ("line", 5, 1),
    ("line", 4, 2),
    ("grad_volume",),
    ("write", 3),
    ("line", 5, 2),
    ("write", 4),
    ("write", 5),
)


def params():
    return pltpu.CompilerParams(
        dimension_semantics=("arbitrary",), vmem_limit_bytes=LIMIT
    )


def whole(shape):
    return pl.BlockSpec(shape, lambda *_: (0,) * len(shape))


def smem():
    return pl.BlockSpec(memory_space=pltpu.SMEM)


def fill_padded(padded, rows_first, sign):
    padded[...] = jnp.zeros_like(padded)
    cells = rows_first.astype(F32).T
    width_at = lax.broadcasted_iota(jnp.int32, cells.shape, 0) % WIDTH
    for c in (-1, 0, 1):
        off = sign * c
        moved = cells if off == 0 else pltpu.roll(cells, (-off) % CELLS, 0)
        inside = (width_at + off >= 0) & (width_at + off < WIDTH)
        moved = jnp.where(inside, moved, 0.0).astype(BF16)
        padded[1 + c, 1 : 1 + DEPTH, 1 : 1 + HEIGHT] = moved.reshape(
            DEPTH, HEIGHT, WIDTH, cells.shape[1]
        )


def span_of(a, sign):
    return max(0, -sign * a), DEPTH - abs(a)


def start_parts(source, buffer, sems):
    size = source.shape[0] // 3
    copies = {}
    for a in PLANE_ORDER:
        span = pl.ds((a + 1) * size, size)
        copies[a] = pltpu.make_async_copy(source.at[span], buffer.at[span], sems.at[a + 1])
        copies[a].start()
    return copies


def share_kernel(n, sign, idx, field, w, *refs):
    outs = refs[:n]
    padded, sums, shares, buffer, sems = refs[n:]
    rows = field.shape[0]
    copies = start_parts(w, buffer, sems)
    fill_padded(padded, field[...], sign)
    for a in PLANE_ORDER:
        begin, planes = span_of(a, sign)
        pieces = []
        for b in (-1, 0, 1):
            for c in (-1, 0, 1):
                low, first = 1 + sign * b, 1 + begin + sign * a
                piece = padded[1 + c, first : first + planes, low : low + HEIGHT]
                pieces.append(piece.reshape(planes * PLANE, rows))
        lhs = jnp.concatenate(pieces, axis=1)
        copies[a].wait()
        if sign == 1:
            rhs = buffer[(a + 1) * 9 * rows : (a + 2) * 9 * rows]
            part = jnp.dot(lhs, rhs, preferred_element_type=F32)
        else:
            rhs = jnp.concatenate([buffer[(a + 1) * 9 + k] for k in range(9)], axis=1)
            part = lax.dot_general(lhs, rhs, NT, preferred_element_type=F32)
        span = slice(begin * PLANE, (begin + planes) * PLANE)
        if a == 0:
            sums[...] = part
        else:
            sums[span] += part
    for j in range(n):
        shares[j] = sums[:, j * rows : (j + 1) * rows].astype(BF16)
    for m in range(n):
        outs[m][...] = shares[idx[0] ^ m]


def spread_shares(sign, name, idx, n, field, w, limit):
    rows = field.shape[0]
    return pl.pallas_call(
        functools.partial(share_kernel, n, sign),
        in_specs=[smem(), pl.BlockSpec(memory_space=pltpu.VMEM), IN_HBM],
        out_specs=[pl.BlockSpec(memory_space=pltpu.VMEM)] * n,
        out_shape=[jax.ShapeDtypeStruct((CELLS, rows), BF16)] * n,
        scratch_shapes=[
            pltpu.VMEM((3, DEPTH + 2, HEIGHT + 2, WIDTH, rows), BF16),
            pltpu.VMEM((CELLS, n * rows), F32),
            pltpu.VMEM((n, CELLS, rows), BF16),
            pltpu.VMEM(w.shape, BF16),
            pltpu.SemaphoreType.DMA((3,)),
        ],
        compiler_params=pltpu.CompilerParams(vmem_limit_bytes=limit),
        cost_estimate=LIGHT,
        name=name,
    )(idx, field, w)


def norm_kernel(n, gain, *refs):
    shares = refs[:n]
    act, normed_out, inverse_out = refs[2 * n - 1 : 2 * n + 2]
    pre = shares[0][...].astype(F32)
    for m in range(1, n):
        pre = pre + shares[m][...].astype(F32)
    center = pre - jnp.mean(pre, axis=0, keepdims=True)
    inverse = lax.rsqrt(jnp.mean(center * center, axis=0, keepdims=True) + NORM_EPS)
    normed = center * inverse
    scaled = gain[...] * normed
    act[...] = (scaled * jax.nn.sigmoid(scaled)).astype(BF16)
    normed_out[...] = normed
    inverse_out[...] = inverse


def norm_back_kernel(n, gain, normed_in, inverse, *refs):
    shares = refs[:n]
    dpre, gain_part = refs[-2:]
    dact = shares[0][...].astype(F32)
    for m in range(1, n):
        dact = dact + shares[m][...].astype(F32)
    normed = normed_in[...]
    scaled = gain[...] * normed
    sigma = jax.nn.sigmoid(scaled)
    dscaled = dact * sigma * (1.0 + scaled * (1.0 - sigma))
    product = dscaled * normed
    gain_part[...] = jnp.sum(product, axis=0, keepdims=True)
    dnormed = gain[...] * dscaled
    mean_first = jnp.mean(dnormed, axis=0, keepdims=True)
    mean_second = jnp.mean(dnormed * normed, axis=0, keepdims=True)
    dpre[...] = ((dnormed - mean_first - normed * mean_second) * inverse[...]).astype(BF16)


def conv_back_add(sums, products, begin, planes, taps, rows, sign):
    for at, tap in enumerate(taps):
        a, b, c = tap
        a, b = sign * a, sign * b
        part = products[:, at * rows : (at + 1) * rows].reshape(planes, HEIGHT, WIDTH, rows)
        low, high = max(0, b), HEIGHT + min(0, b)
        sums[1 + c, begin - a : begin - a + planes, low - b : high - b] += part[:, low:high]


def conv_finish(sums, out, sign):
    rows = out.shape[0]
    total = None
    for c in (-1, 0, 1):
        off = sign * c
        part = sums[1 + c].reshape(CELLS, rows)
        if off != 0:
            width_at = lax.broadcasted_iota(jnp.int32, part.shape, 0) % WIDTH
            inside = (width_at + off >= 0) & (width_at + off < WIDTH)
            part = jnp.where(inside, pltpu.roll(part, (-off) % CELLS, 0), 0.0)
        total = part if total is None else total + part
    out[...] = total.T.astype(BF16)


def conv_kernel(n, sign, transposed, idx, w, *refs):
    blocks = refs[:n]
    out, mark, ordered, sums, buffer, sems = refs[-6:]
    mark[...] = jnp.zeros_like(mark)
    rows = out.shape[0]
    copies = start_parts(w, buffer, sems)
    sums[...] = jnp.zeros_like(sums)
    for m in range(n):
        ordered[idx[0] ^ m] = blocks[m][...]
    for a in PLANE_ORDER:
        begin, planes = span_of(-a, sign)
        span = slice(begin * PLANE, (begin + planes) * PLANE)
        lhs = jnp.concatenate([ordered[j, span] for j in range(n)], axis=1)
        copies[a].wait()
        for k in range(0, 9, 2):
            t = (a + 1) * 9 + k
            taps = TAPS[t : t + min(2, 9 - k)]
            if transposed:
                rhs = buffer[t * rows : (t + len(taps)) * rows]
                products = lax.dot_general(lhs, rhs, NT, preferred_element_type=F32)
            else:
                rhs = jnp.concatenate([buffer[t + at] for at in range(len(taps))], axis=1)
                products = jnp.dot(lhs, rhs, preferred_element_type=F32)
            conv_back_add(sums, products, begin, planes, taps, rows, sign)
    conv_finish(sums, out, sign)


def conv_full(name, sign, transposed, idx, w, blocks, after):
    n, rows = len(blocks), blocks[0].shape[1]
    return pl.pallas_call(
        functools.partial(conv_kernel, n, sign, transposed),
        in_specs=[smem(), IN_HBM]
        + [pl.BlockSpec(memory_space=pltpu.VMEM)] * n
        + [UNREAD] * len(after),
        out_specs=[pl.BlockSpec(memory_space=pltpu.VMEM)] * 2,
        out_shape=[
            jax.ShapeDtypeStruct((rows, CELLS), BF16),
            jax.ShapeDtypeStruct((8, 128), F32),
        ],
        scratch_shapes=[
            pltpu.VMEM((n, CELLS, rows), BF16),
            pltpu.VMEM((3, DEPTH, HEIGHT, WIDTH, rows), F32),
            pltpu.VMEM(w.shape, BF16),
            pltpu.SemaphoreType.DMA((3,)),
        ],
        compiler_params=pltpu.CompilerParams(vmem_limit_bytes=LIMIT),
        cost_estimate=LIGHT,
        name=name,
    )(idx, w, *blocks, *after)


def halves_kernel(n, turned, idx, *refs):
    blocks = refs[:n]
    keep, send = refs[-2:]
    half = n // 2
    rows = blocks[0].shape[1]

    def put(out, at, block):
        if turned:
            out[pl.ds(pl.multiple_of(at * rows, rows), rows)] = block[...].astype(F32).T.astype(BF16)
        else:
            out[at] = block[...]

    def split(kept, sent):
        for m in range(half):
            at = (idx[0] ^ m) & (half - 1)
            put(keep, at, blocks[kept + m])
            put(send, at, blocks[sent + m])

    @pl.when(idx[1] == 0)
    def _():
        split(0, half)

    @pl.when(idx[1] != 0)
    def _():
        split(half, 0)


def halves(name, turned, idx, blocks, after):
    n, rows = len(blocks), blocks[0].shape[1]
    shape = (n // 2 * rows, CELLS) if turned else (n // 2, CELLS, rows)
    return pl.pallas_call(
        functools.partial(halves_kernel, n, turned),
        in_specs=[smem()]
        + [pl.BlockSpec(memory_space=pltpu.VMEM)] * n
        + [UNREAD] * len(after),
        out_shape=[jax.ShapeDtypeStruct(shape, BF16)] * 2,
        compiler_params=pltpu.CompilerParams(vmem_limit_bytes=LIMIT),
        cost_estimate=LIGHT,
        name=name,
    )(idx, *blocks, *after)


def moved_second_kernel(own, other, _, out):
    out[...] = jnp.zeros_like(out)
    for which, ref in enumerate((own, other)):
        cells = ref[...].astype(F32).T
        width_at = lax.broadcasted_iota(jnp.int32, cells.shape, 0) % WIDTH
        for c in (-1, 0, 1):
            part = cells if c == 0 else pltpu.roll(cells, c % CELLS, 0)
            inside = (width_at - c >= 0) & (width_at - c < WIDTH)
            part = jnp.where(inside, part, 0.0).astype(BF16)
            out[which, 1 + c, :, 1 : 1 + HEIGHT] = part.reshape(
                DEPTH, HEIGHT, WIDTH, cells.shape[1]
            )


def moved_fields(kernel, name, shape, own, other, after):
    return pl.pallas_call(
        kernel,
        in_specs=[pl.BlockSpec(memory_space=pltpu.VMEM)] * 2 + [UNREAD],
        out_shape=jax.ShapeDtypeStruct(shape, BF16),
        compiler_params=pltpu.CompilerParams(vmem_limit_bytes=LIMIT),
        cost_estimate=LIGHT,
        name=name,
    )(own, other, after)


def split_rows(values):
    high = values.astype(BF16)
    low = (values - high.astype(F32)).astype(BF16)
    empty = jnp.zeros((EXTRA - 2, values.shape[1]), F32)
    return jnp.concatenate([high.astype(F32), low.astype(F32), empty], axis=0).astype(BF16)


def moved_lanes(cells, b, c):
    off = b * WIDTH + c
    if off == 0:
        return cells.astype(BF16)
    at = lax.broadcasted_iota(jnp.int32, cells.shape, 1)
    height_at, width_at = at // WIDTH % HEIGHT, at % WIDTH
    inside = (height_at + b >= 0) & (height_at + b < HEIGHT)
    inside = inside & (width_at + c >= 0) & (width_at + c < WIDTH)
    return jnp.where(inside, pltpu.roll(cells, (-off) % CELLS, 1), 0.0).astype(BF16)


def grad_first_kernel(vol_own, vol_other, own, other, gain_part, *refs):
    outs, moved = refs[-4:-1], refs[-1]
    half, rows = own.shape[0], own.shape[2]
    fields = [ref[...].astype(F32) for ref in (vol_own, vol_other)]
    rhs = [jnp.concatenate([ref[j] for j in range(half)], axis=1) for ref in (own, other)]
    for b in range(3):
        for which in range(2):
            for c in range(3):
                moved[which, c * rows : (c + 1) * rows] = moved_lanes(fields[which], b - 1, c - 1)
        for a in (-1, 0, 1):
            begin, count = max(0, -a) * PLANE, (DEPTH - abs(a)) * PLANE
            shift = begin + a * PLANE
            grads = None
            for which in range(2):
                lhs = moved[which, :, shift : shift + count]
                part = jnp.dot(lhs, rhs[which][begin : begin + count], preferred_element_type=F32)
                grads = part if grads is None else grads + part
            outs[a + 1][3 * rows * b : 3 * rows * (b + 1)] = grads.astype(BF16)
    filler = jnp.zeros((1, half * rows - rows), F32)
    outs[0][9 * rows :] = split_rows(jnp.concatenate([gain_part[...], filler], axis=1))
    for out in outs[1:]:
        out[9 * rows :] = jnp.zeros((EXTRA, half * rows), BF16)


def grad_first(vol_own, vol_other, own, other, gain_part, after):
    half, cells, rows = own.shape
    return pl.pallas_call(
        grad_first_kernel,
        in_specs=[pl.BlockSpec(memory_space=pltpu.VMEM)] * 5 + [UNREAD] * len(after),
        out_specs=[pl.BlockSpec(memory_space=pltpu.VMEM)] * 3,
        out_shape=[jax.ShapeDtypeStruct((9 * rows + EXTRA, half * rows), BF16)] * 3,
        scratch_shapes=[pltpu.VMEM((2, 3 * rows, CELLS), BF16)],
        compiler_params=pltpu.CompilerParams(vmem_limit_bytes=LIMIT),
        cost_estimate=LIGHT,
        name="grad_first",
    )(vol_own, vol_other, own, other, gain_part, *after)


def grad_second_kernel(a, moved, own, other, *refs):
    out = refs[-1]
    rows = out.shape[2]
    begin, planes = max(0, a), DEPTH - abs(a)
    lhs = [
        ref[:, begin * PLANE : (begin + planes) * PLANE] for ref in (own, other)
    ]
    for k in range(0, 9, 2):
        taps = range(k, min(k + 2, 9))
        grads = None
        for which in range(2):
            pieces = []
            for at in taps:
                b, c = at // 3 - 1, at % 3 - 1
                piece = moved[which, 1 + c, begin - a : begin - a + planes, 1 - b : 1 - b + HEIGHT]
                pieces.append(piece.reshape(planes * PLANE, rows))
            rhs = jnp.concatenate(pieces, axis=1)
            part = jnp.dot(lhs[which], rhs, preferred_element_type=F32)
            grads = part if grads is None else grads + part
        for place, at in enumerate(taps):
            out[at] = grads[:, place * rows : (place + 1) * rows].astype(BF16)


def grad_second(a, moved, own, other, after):
    wide, rows = own.shape[0], moved.shape[-1]
    return pl.pallas_call(
        functools.partial(grad_second_kernel, a),
        in_specs=[pl.BlockSpec(memory_space=pltpu.VMEM)] * 3 + [UNREAD] * len(after),
        out_shape=jax.ShapeDtypeStruct((9, wide, rows), BF16),
        compiler_params=pltpu.CompilerParams(vmem_limit_bytes=LIMIT),
        cost_estimate=LIGHT,
        name="grad_second",
    )(moved, own, other, *after)


def finish_kernel(n, axis, factor, chunk, idx, own, other, *refs):
    out, mark, wide, sems = refs[-4:]
    upper = (idx[0] >= n // 2).astype(jnp.int32) ^ idx[1]
    taps, height, width = wide.shape[1:]
    copies = []
    for k, (part, place) in enumerate(((own, upper), (other, 1 - upper))):
        size = (height, width)[axis - 1]
        span = pl.ds(pl.multiple_of(place * size, size), size)
        for third in range(3):
            at = slice(3 * third, 3 * third + 3)
            if len(part.shape) == 2:
                rows = part[3 * third * height : (3 * third + 3) * height]
                rows = rows.reshape(3, height, width)
            else:
                rows = part[at]
            wide[k, at] = rows.astype(F32) * factor
            target = out.at[pl.ds(chunk * taps + 3 * third, 3)]
            target = target.at[:, span] if axis == 1 else target.at[:, :, span]
            copies.append(
                pltpu.make_async_copy(wide.at[k, at], target, sems.at[3 * k + third])
            )
            copies[-1].start()
    mark[...] = jnp.zeros_like(mark)
    for copy in copies:
        copy.wait()


def finish(name, n, axis, factor, idx, chunk, shape, own, other, before, after):
    taps, height, width = shape
    given = [] if before is None else [before]
    full = (27, height * 2, width) if axis == 1 else (27, height, width * 2)
    return pl.pallas_call(
        functools.partial(finish_kernel, n, axis, factor, chunk),
        in_specs=[smem()]
        + [pl.BlockSpec(memory_space=pltpu.VMEM)] * 2
        + [UNREAD] * (len(given) + len(after)),
        out_specs=[UNREAD, pl.BlockSpec(memory_space=pltpu.VMEM)],
        out_shape=[jax.ShapeDtypeStruct(full, F32), jax.ShapeDtypeStruct((8, 128), F32)],
        scratch_shapes=[pltpu.VMEM((2,) + shape, F32), pltpu.SemaphoreType.DMA((6,))],
        input_output_aliases={3: 0} if given else {},
        compiler_params=pltpu.CompilerParams(vmem_limit_bytes=SMALL),
        cost_estimate=LIGHT,
        name=name,
    )(idx, own, other, *given, *after)


def add_kernel(x, y, *refs):
    out = refs[-1]
    if len(x.shape) == 3:
        out[...] = (x[...].astype(F32) + y[...].astype(F32)).astype(BF16)
    else:
        rows = x.shape[0] - EXTRA
        out[:rows] = (x[:rows].astype(F32) + y[:rows].astype(F32)).astype(BF16)
        tail = x[rows:].astype(F32) + y[rows:].astype(F32)
        out[rows:] = split_rows(tail[:1] + tail[1:2])


def pick_kernel(idx, x, y, *refs):
    out = refs[-1]

    @pl.when(idx[2] == 0)
    def _():
        out[...] = x[...]

    @pl.when(idx[2] != 0)
    def _():
        out[...] = y[...]


def whole_call(kernel, name, x, y, after, idx=None):
    given = [] if idx is None else [idx]
    return pl.pallas_call(
        kernel,
        in_specs=[smem()] * len(given)
        + [pl.BlockSpec(memory_space=pltpu.VMEM)] * 2
        + [UNREAD] * len(after),
        out_shape=jax.ShapeDtypeStruct(x.shape, x.dtype),
        compiler_params=pltpu.CompilerParams(vmem_limit_bytes=SMALL),
        cost_estimate=LIGHT,
        name=name,
    )(*given, x, y, *after)


def line_moves(chips):
    inward = [[(h, h + 1), (chips - 1 - h, chips - 2 - h)] for h in range(chips // 2 - 1)]
    mid = chips // 2
    outward = [[(j, i) for i, j in moves] for moves in reversed(inward)]
    return inward + [[(mid - 1, mid), (mid, mid - 1)]], outward


def line_send(x, moves):
    pairs = [(2 * i + k, 2 * j + k) for i, j in moves for k in (0, 1)]
    return lax.ppermute(x, "dp", pairs)


def line_step(step, part, total, idx, place, after):
    sums, outward = line_moves(lax.axis_size("dp") // 2)
    if step < len(sums):
        got = line_send(total, sums[step])
        base = total if step == len(sums) - 1 else part
        return whole_call(add_kernel, "line_add", base, got, after)
    moves = outward[step - len(sums)]
    got = line_send(total, moves)
    takes = functools.reduce(jnp.logical_or, [place // 2 == j for _, j in moves])
    marked = jnp.stack([idx[0], idx[1], takes.astype(jnp.int32)])
    return whole_call(pick_kernel, "line_pick", total, got, after, marked)


def shards(volume, w_first, gain, w_second, cotangent):
    n = lax.axis_size("chan")
    rows = volume.shape[1]
    vol, cot = volume[0], cotangent[0]
    chan, place = lax.axis_index("chan"), lax.axis_index("dp")
    idx = jnp.stack([chan, place % 2]).astype(jnp.int32)
    own_gain = lax.dynamic_slice_in_dim(gain, chan * rows, rows, 0)[None]
    factor = 1.0 / math.sqrt(lax.axis_size("dp") * CELLS)

    def to_partner(x, m):
        return lax.ppermute(x, "chan", [(i, i ^ m) for i in range(n)])

    def to_core(x):
        return lax.ppermute(x, "dp", [(i, i ^ 1) for i in range(lax.axis_size("dp"))])

    def swap(parts):
        got = {m: to_partner(parts[m], m) for m in reversed(range(1, n))}
        return [parts[0]] + [got[m] for m in range(1, n)]

    first_flat = w_first.reshape(27 * rows, n * rows)
    pre_shares = swap(spread_shares(1, "pre", idx, n, vol, first_flat, LARGE))
    dact_parts = spread_shares(-1, "dact", idx, n, cot, w_second, LIMIT)
    held = dact_parts[1:]
    act, normed, inverse, *held = pl.pallas_call(
        functools.partial(norm_kernel, n),
        in_specs=[pl.BlockSpec(memory_space=pltpu.VMEM)] * (1 + n) + [UNREAD] * len(held),
        out_specs=[pl.BlockSpec(memory_space=pltpu.VMEM)] * 3 + [UNREAD] * len(held),
        out_shape=[
            jax.ShapeDtypeStruct((CELLS, rows), BF16),
            jax.ShapeDtypeStruct((CELLS, rows), F32),
            jax.ShapeDtypeStruct((1, rows), F32),
        ]
        + [jax.ShapeDtypeStruct(x.shape, x.dtype) for x in held],
        input_output_aliases={1 + n + k: 3 + k for k in range(len(held))},
        compiler_params=pltpu.CompilerParams(vmem_limit_bytes=SMALL),
        cost_estimate=LIGHT,
        name="norm",
    )(own_gain, *pre_shares, *held)
    act_blocks = swap([act] * n)
    dact_shares = swap([dact_parts[0]] + held)
    moved_cot = moved_fields(
        moved_second_kernel,
        "moved_second",
        (2, 3, DEPTH, HEIGHT + 2, WIDTH, rows),
        cot,
        to_core(cot),
        act,
    )
    vol_other = to_core(vol)
    act_keep, act_send = halves("act_halves", True, idx, act_blocks, (moved_cot, vol_other))
    act_other = to_core(act_send)

    sums, outward = line_moves(lax.axis_size("dp") // 2)
    steps = len(sums) + len(outward)
    parts, totals, crossed = {}, {}, {}
    last = ()

    reached = [0] * 6

    def line(chunk, step):
        nonlocal last
        if reached[chunk] > step:
            return
        if reached[chunk] < step:
            line(chunk, step - 1)
        reached[chunk] = step + 1
        before = totals.get(chunk, parts[chunk])
        totals[chunk] = line_step(step, parts[chunk], before, idx, place, last)
        last = (totals[chunk],)
        if step == steps - 1:
            crossed[chunk] = to_core(totals[chunk])

    def write(chunk):
        nonlocal last
        line(chunk, steps - 1)
        name, axis = ("finish_second", 1) if chunk < 3 else ("finish_first", 2)
        shape = (9, n // 2 * rows, rows) if chunk < 3 else (9, rows, n // 2 * rows)
        written[axis], mark = finish(
            name,
            n,
            axis,
            factor,
            idx,
            chunk % 3,
            shape,
            totals[chunk],
            crossed[chunk],
            written.get(axis),
            last,
        )
        last = (mark,)

    def second_part(chunk):
        nonlocal last
        parts[chunk] = grad_second(chunk - 1, moved_cot, act_keep, act_other, last)
        last = (parts[chunk],)

    def first_parts():
        nonlocal last
        own, other = done["dpre_halves"]
        parts[3], parts[4], parts[5] = grad_first(
            vol, vol_other, own, other, done["gain"], last
        )
        last = (parts[3],)

    def norm_back():
        nonlocal last
        dpre, done["gain"] = pl.pallas_call(
            functools.partial(norm_back_kernel, n),
            in_specs=[pl.BlockSpec(memory_space=pltpu.VMEM)] * (3 + n) + [UNREAD],
            out_shape=[
                jax.ShapeDtypeStruct((CELLS, rows), BF16),
                jax.ShapeDtypeStruct((1, rows), F32),
            ],
            compiler_params=pltpu.CompilerParams(vmem_limit_bytes=SMALL),
            cost_estimate=LIGHT,
            name="norm_back",
        )(own_gain, normed, inverse, *dact_shares, *last)
        done["dpre"] = swap([dpre] * n)
        last = (dpre,)

    def dpre_halves():
        nonlocal last
        keep, send = halves("dpre_halves", False, idx, done["dpre"], last)
        done["dpre_halves"] = keep, to_core(send)
        last = (keep,)

    def output():
        nonlocal last
        done["output"], mark = conv_full("output", 1, False, idx, w_second, act_blocks, last)
        last = (mark,)

    def grad_volume():
        nonlocal last
        done["grad_volume"], mark = conv_full(
            "grad_volume", -1, True, idx, first_flat, done["dpre"], last
        )
        last = (mark,)

    written, done = {}, {}
    steps_by_name = {
        "second": second_part,
        "first": first_parts,
        "output": output,
        "grad_volume": grad_volume,
        "norm_back": norm_back,
        "halves": dpre_halves,
        "line": line,
        "write": write,
    }
    for name, *at in CHAIN:
        steps_by_name[name](*at)
    gain_rows = totals[3][9 * rows : 9 * rows + 2, :rows].astype(F32)
    gain_rows_other = crossed[3][9 * rows : 9 * rows + 2, :rows].astype(F32)
    gain_total = (jnp.sum(gain_rows, axis=0) + jnp.sum(gain_rows_other, axis=0)) * factor
    return (done["output"][None], done["grad_volume"][None], written[2], gain_total, written[1])


def solution(mesh):
    placed = (
        P("dp", "chan", None),
        P(None, "chan", None),
        P(),
        P(None, None, "chan"),
        P("dp", "chan", None),
    )
    return jax.shard_map(
        shards,
        mesh=mesh,
        in_specs=placed,
        out_specs=(
            P("dp", "chan", None),
            P("dp", "chan", None),
            P(None, "chan", None),
            P("chan"),
            P(None, None, "chan"),
        ),
        check_vma=False,
    )
```

```python
import functools
import math

import jax
import jax.numpy as jnp
from jax import lax
from jax.experimental import pallas as pl
from jax.experimental.pallas import tpu as pltpu
from jax.sharding import PartitionSpec as P

DEPTH, HEIGHT, WIDTH = 4, 16, 16
PLANE = HEIGHT * WIDTH
CELLS = DEPTH * PLANE
TAPS = [(a, b, c) for a in (-1, 0, 1) for b in (-1, 0, 1) for c in (-1, 0, 1)]
NORM_EPS = 1e-05
LIMIT = 16 * 1024 * 1024
SMALL = 8 * 1024 * 1024
LARGE = 59 * 1024 * 1024
EXTRA = 16
F32, BF16 = jnp.float32, jnp.bfloat16
NT = (((1,), (1,)), ((), ()))
UNREAD = pl.BlockSpec(memory_space=pl.ANY)
IN_HBM = pl.BlockSpec(memory_space=pltpu.HBM)
PLANE_ORDER = (0, 1, -1)
LIGHT = pl.CostEstimate(flops=1024, bytes_accessed=1024, transcendentals=0)


CHAIN = (
    ("second", 0),
    ("second", 1),
    ("output",),
    ("norm_back",),
    ("line", 0, 0),
    ("second", 2),
    ("line", 1, 0),
    ("line", 0, 1),
    ("halves",),
    ("first",),
    ("line", 2, 0),
    ("line", 1, 1),
    ("line", 0, 2),
    ("line", 3, 0),
    ("line", 2, 1),
    ("line", 1, 2),
    ("write", 0),
    ("line", 4, 0),
    ("line", 3, 1),
    ("line", 2, 2),
    ("write", 1),
    ("line", 5, 0),
    ("line", 4, 1),
    ("line", 3, 2),
    ("write", 2),
    ("line", 5, 1),
    ("line", 4, 2),
    ("grad_volume",),
    ("write", 3),
    ("line", 5, 2),
    ("write", 4),
    ("write", 5),
)


def params():
    return pltpu.CompilerParams(
        dimension_semantics=("arbitrary",), vmem_limit_bytes=LIMIT
    )


def whole(shape):
    return pl.BlockSpec(shape, lambda *_: (0,) * len(shape))


def smem():
    return pl.BlockSpec(memory_space=pltpu.SMEM)


def fill_padded(padded, rows_first, sign):
    padded[...] = jnp.zeros_like(padded)
    cells = rows_first.astype(F32).T
    width_at = lax.broadcasted_iota(jnp.int32, cells.shape, 0) % WIDTH
    for c in (-1, 0, 1):
        off = sign * c
        moved = cells if off == 0 else pltpu.roll(cells, (-off) % CELLS, 0)
        inside = (width_at + off >= 0) & (width_at + off < WIDTH)
        moved = jnp.where(inside, moved, 0.0).astype(BF16)
        padded[1 + c, 1 : 1 + DEPTH, 1 : 1 + HEIGHT] = moved.reshape(
            DEPTH, HEIGHT, WIDTH, cells.shape[1]
        )


def span_of(a, sign):
    return max(0, -sign * a), DEPTH - abs(a)


def start_parts(source, buffer, sems):
    size = source.shape[0] // 3
    copies = {}
    for a in PLANE_ORDER:
        span = pl.ds((a + 1) * size, size)
        copies[a] = pltpu.make_async_copy(source.at[span], buffer.at[span], sems.at[a + 1])
        copies[a].start()
    return copies


def share_kernel(n, sign, idx, field, w, *refs):
    outs = refs[:n]
    padded, sums, shares, buffer, sems = refs[n:]
    rows = field.shape[0]
    copies = start_parts(w, buffer, sems)
    fill_padded(padded, field[...], sign)
    if sign == 1:
        for plane in range(DEPTH):
            near = [a for a in (-1, 0, 1) if 0 <= plane + a < DEPTH]
            if plane == 0:
                copies[0].wait()
                copies[1].wait()
            if plane == 1:
                copies[-1].wait()
            pieces = []
            for a in near:
                for b in (-1, 0, 1):
                    for c in (-1, 0, 1):
                        piece = padded[1 + c, 1 + plane + a, 1 + b : 1 + b + HEIGHT]
                        pieces.append(piece.reshape(PLANE, rows))
            lhs = jnp.concatenate(pieces, axis=1)
            rhs = buffer[(near[0] + 1) * 9 * rows : (near[-1] + 2) * 9 * rows]
            part = jnp.dot(lhs, rhs, preferred_element_type=F32).astype(BF16)
            for j in range(n):
                span = slice(plane * PLANE, (plane + 1) * PLANE)
                shares[j, span] = part[:, j * rows : (j + 1) * rows]
    else:
        for a in PLANE_ORDER:
            begin, planes = span_of(a, sign)
            pieces = []
            for b in (-1, 0, 1):
                for c in (-1, 0, 1):
                    low, first = 1 + sign * b, 1 + begin + sign * a
                    piece = padded[1 + c, first : first + planes, low : low + HEIGHT]
                    pieces.append(piece.reshape(planes * PLANE, rows))
            lhs = jnp.concatenate(pieces, axis=1)
            copies[a].wait()
            rhs = jnp.concatenate([buffer[(a + 1) * 9 + k] for k in range(9)], axis=1)
            part = lax.dot_general(lhs, rhs, NT, preferred_element_type=F32)
            span = slice(begin * PLANE, (begin + planes) * PLANE)
            if a == 0:
                sums[...] = part
            else:
                sums[span] += part
        for j in range(n):
            shares[j] = sums[:, j * rows : (j + 1) * rows].astype(BF16)
    for m in range(n):
        outs[m][...] = shares[idx[0] ^ m]


def spread_shares(sign, name, idx, n, field, w, limit):
    rows = field.shape[0]
    return pl.pallas_call(
        functools.partial(share_kernel, n, sign),
        in_specs=[smem(), pl.BlockSpec(memory_space=pltpu.VMEM), IN_HBM],
        out_specs=[pl.BlockSpec(memory_space=pltpu.VMEM)] * n,
        out_shape=[jax.ShapeDtypeStruct((CELLS, rows), BF16)] * n,
        scratch_shapes=[
            pltpu.VMEM((3, DEPTH + 2, HEIGHT + 2, WIDTH, rows), BF16),
            pltpu.VMEM((CELLS, n * rows), F32),
            pltpu.VMEM((n, CELLS, rows), BF16),
            pltpu.VMEM(w.shape, BF16),
            pltpu.SemaphoreType.DMA((3,)),
        ],
        compiler_params=pltpu.CompilerParams(vmem_limit_bytes=limit),
        cost_estimate=LIGHT,
        name=name,
    )(idx, field, w)


def norm_kernel(n, gain, *refs):
    shares = refs[:n]
    act, normed_out, inverse_out = refs[2 * n - 1 : 2 * n + 2]
    pre = shares[0][...].astype(F32)
    for m in range(1, n):
        pre = pre + shares[m][...].astype(F32)
    center = pre - jnp.mean(pre, axis=0, keepdims=True)
    inverse = lax.rsqrt(jnp.mean(center * center, axis=0, keepdims=True) + NORM_EPS)
    normed = center * inverse
    scaled = gain[...] * normed
    act[...] = (scaled * jax.nn.sigmoid(scaled)).astype(BF16)
    normed_out[...] = normed
    inverse_out[...] = inverse


def norm_back_kernel(n, gain, normed_in, inverse, *refs):
    shares = refs[:n]
    dpre, gain_part = refs[-2:]
    dact = shares[0][...].astype(F32)
    for m in range(1, n):
        dact = dact + shares[m][...].astype(F32)
    normed = normed_in[...]
    scaled = gain[...] * normed
    sigma = jax.nn.sigmoid(scaled)
    dscaled = dact * sigma * (1.0 + scaled * (1.0 - sigma))
    product = dscaled * normed
    gain_part[...] = jnp.sum(product, axis=0, keepdims=True)
    dnormed = gain[...] * dscaled
    mean_first = jnp.mean(dnormed, axis=0, keepdims=True)
    mean_second = jnp.mean(dnormed * normed, axis=0, keepdims=True)
    dpre[...] = ((dnormed - mean_first - normed * mean_second) * inverse[...]).astype(BF16)


def conv_back_add(sums, products, begin, planes, taps, rows, sign):
    for at, tap in enumerate(taps):
        a, b, c = tap
        a, b = sign * a, sign * b
        part = products[:, at * rows : (at + 1) * rows].reshape(planes, HEIGHT, WIDTH, rows)
        low, high = max(0, b), HEIGHT + min(0, b)
        sums[1 + c, begin - a : begin - a + planes, low - b : high - b] += part[:, low:high]


def conv_finish(sums, out, sign):
    rows = out.shape[0]
    total = None
    for c in (-1, 0, 1):
        off = sign * c
        part = sums[1 + c].reshape(CELLS, rows)
        if off != 0:
            width_at = lax.broadcasted_iota(jnp.int32, part.shape, 0) % WIDTH
            inside = (width_at + off >= 0) & (width_at + off < WIDTH)
            part = jnp.where(inside, pltpu.roll(part, (-off) % CELLS, 0), 0.0)
        total = part if total is None else total + part
    out[...] = total.T.astype(BF16)


def conv_kernel(n, sign, transposed, idx, w, *refs):
    blocks = refs[:n]
    out, mark, ordered, sums, buffer, sems = refs[-6:]
    mark[...] = jnp.zeros_like(mark)
    rows = out.shape[0]
    copies = start_parts(w, buffer, sems)
    sums[...] = jnp.zeros_like(sums)
    for m in range(n):
        ordered[idx[0] ^ m] = blocks[m][...]
    for a in PLANE_ORDER:
        begin, planes = span_of(-a, sign)
        span = slice(begin * PLANE, (begin + planes) * PLANE)
        lhs = jnp.concatenate([ordered[j, span] for j in range(n)], axis=1)
        copies[a].wait()
        for k in range(0, 9, 2):
            t = (a + 1) * 9 + k
            taps = TAPS[t : t + min(2, 9 - k)]
            if transposed:
                rhs = buffer[t * rows : (t + len(taps)) * rows]
                products = lax.dot_general(lhs, rhs, NT, preferred_element_type=F32)
            else:
                rhs = jnp.concatenate([buffer[t + at] for at in range(len(taps))], axis=1)
                products = jnp.dot(lhs, rhs, preferred_element_type=F32)
            conv_back_add(sums, products, begin, planes, taps, rows, sign)
    conv_finish(sums, out, sign)


def conv_full(name, sign, transposed, idx, w, blocks, after):
    n, rows = len(blocks), blocks[0].shape[1]
    return pl.pallas_call(
        functools.partial(conv_kernel, n, sign, transposed),
        in_specs=[smem(), IN_HBM]
        + [pl.BlockSpec(memory_space=pltpu.VMEM)] * n
        + [UNREAD] * len(after),
        out_specs=[pl.BlockSpec(memory_space=pltpu.VMEM)] * 2,
        out_shape=[
            jax.ShapeDtypeStruct((rows, CELLS), BF16),
            jax.ShapeDtypeStruct((8, 128), F32),
        ],
        scratch_shapes=[
            pltpu.VMEM((n, CELLS, rows), BF16),
            pltpu.VMEM((3, DEPTH, HEIGHT, WIDTH, rows), F32),
            pltpu.VMEM(w.shape, BF16),
            pltpu.SemaphoreType.DMA((3,)),
        ],
        compiler_params=pltpu.CompilerParams(vmem_limit_bytes=LIMIT),
        cost_estimate=LIGHT,
        name=name,
    )(idx, w, *blocks, *after)


def halves_kernel(n, turned, idx, *refs):
    blocks = refs[:n]
    keep, send = refs[-2:]
    half = n // 2
    rows = blocks[0].shape[1]

    def put(out, at, block):
        if turned:
            out[pl.ds(pl.multiple_of(at * rows, rows), rows)] = block[...].astype(F32).T.astype(BF16)
        else:
            out[at] = block[...]

    def split(kept, sent):
        for m in range(half):
            at = (idx[0] ^ m) & (half - 1)
            put(keep, at, blocks[kept + m])
            put(send, at, blocks[sent + m])

    @pl.when(idx[1] == 0)
    def _():
        split(0, half)

    @pl.when(idx[1] != 0)
    def _():
        split(half, 0)


def halves(name, turned, idx, blocks, after):
    n, rows = len(blocks), blocks[0].shape[1]
    shape = (n // 2 * rows, CELLS) if turned else (n // 2, CELLS, rows)
    return pl.pallas_call(
        functools.partial(halves_kernel, n, turned),
        in_specs=[smem()]
        + [pl.BlockSpec(memory_space=pltpu.VMEM)] * n
        + [UNREAD] * len(after),
        out_shape=[jax.ShapeDtypeStruct(shape, BF16)] * 2,
        compiler_params=pltpu.CompilerParams(vmem_limit_bytes=LIMIT),
        cost_estimate=LIGHT,
        name=name,
    )(idx, *blocks, *after)


def moved_second_kernel(own, other, _, out):
    out[...] = jnp.zeros_like(out)
    for which, ref in enumerate((own, other)):
        cells = ref[...].astype(F32).T
        width_at = lax.broadcasted_iota(jnp.int32, cells.shape, 0) % WIDTH
        for c in (-1, 0, 1):
            part = cells if c == 0 else pltpu.roll(cells, c % CELLS, 0)
            inside = (width_at - c >= 0) & (width_at - c < WIDTH)
            part = jnp.where(inside, part, 0.0).astype(BF16)
            out[which, 1 + c, :, 1 : 1 + HEIGHT] = part.reshape(
                DEPTH, HEIGHT, WIDTH, cells.shape[1]
            )


def moved_fields(kernel, name, shape, own, other, after):
    return pl.pallas_call(
        kernel,
        in_specs=[pl.BlockSpec(memory_space=pltpu.VMEM)] * 2 + [UNREAD],
        out_shape=jax.ShapeDtypeStruct(shape, BF16),
        compiler_params=pltpu.CompilerParams(vmem_limit_bytes=LIMIT),
        cost_estimate=LIGHT,
        name=name,
    )(own, other, after)


def split_rows(values):
    high = values.astype(BF16)
    low = (values - high.astype(F32)).astype(BF16)
    empty = jnp.zeros((EXTRA - 2, values.shape[1]), F32)
    return jnp.concatenate([high.astype(F32), low.astype(F32), empty], axis=0).astype(BF16)


def moved_lanes(cells, b, c):
    off = b * WIDTH + c
    if off == 0:
        return cells.astype(BF16)
    at = lax.broadcasted_iota(jnp.int32, cells.shape, 1)
    height_at, width_at = at // WIDTH % HEIGHT, at % WIDTH
    inside = (height_at + b >= 0) & (height_at + b < HEIGHT)
    inside = inside & (width_at + c >= 0) & (width_at + c < WIDTH)
    return jnp.where(inside, pltpu.roll(cells, (-off) % CELLS, 1), 0.0).astype(BF16)


def grad_first_kernel(vol_own, vol_other, own, other, gain_part, *refs):
    outs, moved = refs[-4:-1], refs[-1]
    half, rows = own.shape[0], own.shape[2]
    fields = [ref[...].astype(F32) for ref in (vol_own, vol_other)]
    rhs = [jnp.concatenate([ref[j] for j in range(half)], axis=1) for ref in (own, other)]
    for b in range(3):
        for which in range(2):
            for c in range(3):
                moved[which, c * rows : (c + 1) * rows] = moved_lanes(fields[which], b - 1, c - 1)
        for a in (-1, 0, 1):
            begin, count = max(0, -a) * PLANE, (DEPTH - abs(a)) * PLANE
            shift = begin + a * PLANE
            grads = None
            for which in range(2):
                lhs = moved[which, :, shift : shift + count]
                part = jnp.dot(lhs, rhs[which][begin : begin + count], preferred_element_type=F32)
                grads = part if grads is None else grads + part
            outs[a + 1][3 * rows * b : 3 * rows * (b + 1)] = grads.astype(BF16)
    filler = jnp.zeros((1, half * rows - rows), F32)
    outs[0][9 * rows :] = split_rows(jnp.concatenate([gain_part[...], filler], axis=1))
    for out in outs[1:]:
        out[9 * rows :] = jnp.zeros((EXTRA, half * rows), BF16)


def grad_first(vol_own, vol_other, own, other, gain_part, after):
    half, cells, rows = own.shape
    return pl.pallas_call(
        grad_first_kernel,
        in_specs=[pl.BlockSpec(memory_space=pltpu.VMEM)] * 5 + [UNREAD] * len(after),
        out_specs=[pl.BlockSpec(memory_space=pltpu.VMEM)] * 3,
        out_shape=[jax.ShapeDtypeStruct((9 * rows + EXTRA, half * rows), BF16)] * 3,
        scratch_shapes=[pltpu.VMEM((2, 3 * rows, CELLS), BF16)],
        compiler_params=pltpu.CompilerParams(vmem_limit_bytes=LIMIT),
        cost_estimate=LIGHT,
        name="grad_first",
    )(vol_own, vol_other, own, other, gain_part, *after)


def grad_second_kernel(a, moved, own, other, *refs):
    out = refs[-1]
    rows = out.shape[2]
    begin, planes = max(0, a), DEPTH - abs(a)
    lhs = [
        ref[:, begin * PLANE : (begin + planes) * PLANE] for ref in (own, other)
    ]
    for k in range(0, 9, 2):
        taps = range(k, min(k + 2, 9))
        grads = None
        for which in range(2):
            pieces = []
            for at in taps:
                b, c = at // 3 - 1, at % 3 - 1
                piece = moved[which, 1 + c, begin - a : begin - a + planes, 1 - b : 1 - b + HEIGHT]
                pieces.append(piece.reshape(planes * PLANE, rows))
            rhs = jnp.concatenate(pieces, axis=1)
            part = jnp.dot(lhs[which], rhs, preferred_element_type=F32)
            grads = part if grads is None else grads + part
        for place, at in enumerate(taps):
            out[at] = grads[:, place * rows : (place + 1) * rows].astype(BF16)


def grad_second(a, moved, own, other, after):
    wide, rows = own.shape[0], moved.shape[-1]
    return pl.pallas_call(
        functools.partial(grad_second_kernel, a),
        in_specs=[pl.BlockSpec(memory_space=pltpu.VMEM)] * 3 + [UNREAD] * len(after),
        out_shape=jax.ShapeDtypeStruct((9, wide, rows), BF16),
        compiler_params=pltpu.CompilerParams(vmem_limit_bytes=LIMIT),
        cost_estimate=LIGHT,
        name="grad_second",
    )(moved, own, other, *after)


def finish_kernel(n, axis, factor, chunk, idx, own, other, *refs):
    out, mark, wide, sems = refs[-4:]
    upper = (idx[0] >= n // 2).astype(jnp.int32) ^ idx[1]
    taps, height, width = wide.shape[1:]
    copies = []
    for k, (part, place) in enumerate(((own, upper), (other, 1 - upper))):
        size = (height, width)[axis - 1]
        span = pl.ds(pl.multiple_of(place * size, size), size)
        for third in range(3):
            at = slice(3 * third, 3 * third + 3)
            if len(part.shape) == 2:
                rows = part[3 * third * height : (3 * third + 3) * height]
                rows = rows.reshape(3, height, width)
            else:
                rows = part[at]
            wide[k, at] = rows.astype(F32) * factor
            target = out.at[pl.ds(chunk * taps + 3 * third, 3)]
            target = target.at[:, span] if axis == 1 else target.at[:, :, span]
            copies.append(
                pltpu.make_async_copy(wide.at[k, at], target, sems.at[3 * k + third])
            )
            copies[-1].start()
    mark[...] = jnp.zeros_like(mark)
    for copy in copies:
        copy.wait()


def finish(name, n, axis, factor, idx, chunk, shape, own, other, before, after):
    taps, height, width = shape
    given = [] if before is None else [before]
    full = (27, height * 2, width) if axis == 1 else (27, height, width * 2)
    return pl.pallas_call(
        functools.partial(finish_kernel, n, axis, factor, chunk),
        in_specs=[smem()]
        + [pl.BlockSpec(memory_space=pltpu.VMEM)] * 2
        + [UNREAD] * (len(given) + len(after)),
        out_specs=[UNREAD, pl.BlockSpec(memory_space=pltpu.VMEM)],
        out_shape=[jax.ShapeDtypeStruct(full, F32), jax.ShapeDtypeStruct((8, 128), F32)],
        scratch_shapes=[pltpu.VMEM((2,) + shape, F32), pltpu.SemaphoreType.DMA((6,))],
        input_output_aliases={3: 0} if given else {},
        compiler_params=pltpu.CompilerParams(vmem_limit_bytes=SMALL),
        cost_estimate=LIGHT,
        name=name,
    )(idx, own, other, *given, *after)


def add_kernel(x, y, *refs):
    out = refs[-1]
    if len(x.shape) == 3:
        out[...] = (x[...].astype(F32) + y[...].astype(F32)).astype(BF16)
    else:
        rows = x.shape[0] - EXTRA
        out[:rows] = (x[:rows].astype(F32) + y[:rows].astype(F32)).astype(BF16)
        tail = x[rows:].astype(F32) + y[rows:].astype(F32)
        out[rows:] = split_rows(tail[:1] + tail[1:2])


def pick_kernel(idx, x, y, *refs):
    out = refs[-1]

    @pl.when(idx[2] == 0)
    def _():
        out[...] = x[...]

    @pl.when(idx[2] != 0)
    def _():
        out[...] = y[...]


def whole_call(kernel, name, x, y, after, idx=None):
    given = [] if idx is None else [idx]
    return pl.pallas_call(
        kernel,
        in_specs=[smem()] * len(given)
        + [pl.BlockSpec(memory_space=pltpu.VMEM)] * 2
        + [UNREAD] * len(after),
        out_shape=jax.ShapeDtypeStruct(x.shape, x.dtype),
        compiler_params=pltpu.CompilerParams(vmem_limit_bytes=SMALL),
        cost_estimate=LIGHT,
        name=name,
    )(*given, x, y, *after)


def line_moves(chips):
    inward = [[(h, h + 1), (chips - 1 - h, chips - 2 - h)] for h in range(chips // 2 - 1)]
    mid = chips // 2
    outward = [[(j, i) for i, j in moves] for moves in reversed(inward)]
    return inward + [[(mid - 1, mid), (mid, mid - 1)]], outward


def line_send(x, moves):
    pairs = [(2 * i + k, 2 * j + k) for i, j in moves for k in (0, 1)]
    return lax.ppermute(x, "dp", pairs)


def line_step(step, part, total, idx, place, after):
    sums, outward = line_moves(lax.axis_size("dp") // 2)
    if step < len(sums):
        got = line_send(total, sums[step])
        base = total if step == len(sums) - 1 else part
        return whole_call(add_kernel, "line_add", base, got, after)
    moves = outward[step - len(sums)]
    got = line_send(total, moves)
    takes = functools.reduce(jnp.logical_or, [place // 2 == j for _, j in moves])
    marked = jnp.stack([idx[0], idx[1], takes.astype(jnp.int32)])
    return whole_call(pick_kernel, "line_pick", total, got, after, marked)


def shards(volume, w_first, gain, w_second, cotangent):
    n = lax.axis_size("chan")
    rows = volume.shape[1]
    vol, cot = volume[0], cotangent[0]
    chan, place = lax.axis_index("chan"), lax.axis_index("dp")
    idx = jnp.stack([chan, place % 2]).astype(jnp.int32)
    own_gain = lax.dynamic_slice_in_dim(gain, chan * rows, rows, 0)[None]
    factor = 1.0 / math.sqrt(lax.axis_size("dp") * CELLS)

    def to_partner(x, m):
        return lax.ppermute(x, "chan", [(i, i ^ m) for i in range(n)])

    def to_core(x):
        return lax.ppermute(x, "dp", [(i, i ^ 1) for i in range(lax.axis_size("dp"))])

    def swap(parts):
        got = {m: to_partner(parts[m], m) for m in reversed(range(1, n))}
        return [parts[0]] + [got[m] for m in range(1, n)]

    first_flat = w_first.reshape(27 * rows, n * rows)
    pre_shares = swap(spread_shares(1, "pre", idx, n, vol, first_flat, LARGE))
    dact_parts = spread_shares(-1, "dact", idx, n, cot, w_second, LIMIT)
    held = dact_parts[1:]
    act, normed, inverse, *held = pl.pallas_call(
        functools.partial(norm_kernel, n),
        in_specs=[pl.BlockSpec(memory_space=pltpu.VMEM)] * (1 + n) + [UNREAD] * len(held),
        out_specs=[pl.BlockSpec(memory_space=pltpu.VMEM)] * 3 + [UNREAD] * len(held),
        out_shape=[
            jax.ShapeDtypeStruct((CELLS, rows), BF16),
            jax.ShapeDtypeStruct((CELLS, rows), F32),
            jax.ShapeDtypeStruct((1, rows), F32),
        ]
        + [jax.ShapeDtypeStruct(x.shape, x.dtype) for x in held],
        input_output_aliases={1 + n + k: 3 + k for k in range(len(held))},
        compiler_params=pltpu.CompilerParams(vmem_limit_bytes=SMALL),
        cost_estimate=LIGHT,
        name="norm",
    )(own_gain, *pre_shares, *held)
    act_blocks = swap([act] * n)
    dact_shares = swap([dact_parts[0]] + held)
    moved_cot = moved_fields(
        moved_second_kernel,
        "moved_second",
        (2, 3, DEPTH, HEIGHT + 2, WIDTH, rows),
        cot,
        to_core(cot),
        act,
    )
    vol_other = to_core(vol)
    act_keep, act_send = halves("act_halves", True, idx, act_blocks, (moved_cot, vol_other))
    act_other = to_core(act_send)

    sums, outward = line_moves(lax.axis_size("dp") // 2)
    steps = len(sums) + len(outward)
    parts, totals, crossed = {}, {}, {}
    last = ()

    reached = [0] * 6

    def line(chunk, step):
        nonlocal last
        if reached[chunk] > step:
            return
        if reached[chunk] < step:
            line(chunk, step - 1)
        reached[chunk] = step + 1
        before = totals.get(chunk, parts[chunk])
        totals[chunk] = line_step(step, parts[chunk], before, idx, place, last)
        last = (totals[chunk],)
        if step == steps - 1:
            crossed[chunk] = to_core(totals[chunk])

    def write(chunk):
        nonlocal last
        line(chunk, steps - 1)
        name, axis = ("finish_second", 1) if chunk < 3 else ("finish_first", 2)
        shape = (9, n // 2 * rows, rows) if chunk < 3 else (9, rows, n // 2 * rows)
        written[axis], mark = finish(
            name,
            n,
            axis,
            factor,
            idx,
            chunk % 3,
            shape,
            totals[chunk],
            crossed[chunk],
            written.get(axis),
            last,
        )
        last = (mark,)

    def second_part(chunk):
        nonlocal last
        parts[chunk] = grad_second(chunk - 1, moved_cot, act_keep, act_other, last)
        last = (parts[chunk],)

    def first_parts():
        nonlocal last
        own, other = done["dpre_halves"]
        parts[3], parts[4], parts[5] = grad_first(
            vol, vol_other, own, other, done["gain"], last
        )
        last = (parts[3],)

    def norm_back():
        nonlocal last
        dpre, done["gain"] = pl.pallas_call(
            functools.partial(norm_back_kernel, n),
            in_specs=[pl.BlockSpec(memory_space=pltpu.VMEM)] * (3 + n) + [UNREAD],
            out_shape=[
                jax.ShapeDtypeStruct((CELLS, rows), BF16),
                jax.ShapeDtypeStruct((1, rows), F32),
            ],
            compiler_params=pltpu.CompilerParams(vmem_limit_bytes=SMALL),
            cost_estimate=LIGHT,
            name="norm_back",
        )(own_gain, normed, inverse, *dact_shares, *last)
        done["dpre"] = swap([dpre] * n)
        last = (dpre,)

    def dpre_halves():
        nonlocal last
        keep, send = halves("dpre_halves", False, idx, done["dpre"], last)
        done["dpre_halves"] = keep, to_core(send)
        last = (keep,)

    def output():
        nonlocal last
        done["output"], mark = conv_full("output", 1, False, idx, w_second, act_blocks, last)
        last = (mark,)

    def grad_volume():
        nonlocal last
        done["grad_volume"], mark = conv_full(
            "grad_volume", -1, True, idx, first_flat, done["dpre"], last
        )
        last = (mark,)

    written, done = {}, {}
    steps_by_name = {
        "second": second_part,
        "first": first_parts,
        "output": output,
        "grad_volume": grad_volume,
        "norm_back": norm_back,
        "halves": dpre_halves,
        "line": line,
        "write": write,
    }
    for name, *at in CHAIN:
        steps_by_name[name](*at)
    gain_rows = totals[3][9 * rows : 9 * rows + 2, :rows].astype(F32)
    gain_rows_other = crossed[3][9 * rows : 9 * rows + 2, :rows].astype(F32)
    gain_total = (jnp.sum(gain_rows, axis=0) + jnp.sum(gain_rows_other, axis=0)) * factor
    return (done["output"][None], done["grad_volume"][None], written[2], gain_total, written[1])


def solution(mesh):
    placed = (
        P("dp", "chan", None),
        P(None, "chan", None),
        P(),
        P(None, None, "chan"),
        P("dp", "chan", None),
    )
    return jax.shard_map(
        shards,
        mesh=mesh,
        in_specs=placed,
        out_specs=(
            P("dp", "chan", None),
            P("dp", "chan", None),
            P(None, "chan", None),
            P("chan"),
            P(None, None, "chan"),
        ),
        check_vma=False,
    )
```

```python
import functools
import math

import jax
import jax.numpy as jnp
from jax import lax
from jax.experimental import pallas as pl
from jax.experimental.pallas import tpu as pltpu
from jax.sharding import PartitionSpec as P

DEPTH, HEIGHT, WIDTH = 4, 16, 16
PLANE = HEIGHT * WIDTH
CELLS = DEPTH * PLANE
TAPS = [(a, b, c) for a in (-1, 0, 1) for b in (-1, 0, 1) for c in (-1, 0, 1)]
NORM_EPS = 1e-05
LIMIT = 16 * 1024 * 1024
SMALL = 8 * 1024 * 1024
LARGE = 59 * 1024 * 1024
EXTRA = 16
F32, BF16 = jnp.float32, jnp.bfloat16
NT = (((1,), (1,)), ((), ()))
UNREAD = pl.BlockSpec(memory_space=pl.ANY)
IN_HBM = pl.BlockSpec(memory_space=pltpu.HBM)
PLANE_ORDER = (0, 1, -1)
LIGHT = pl.CostEstimate(flops=1024, bytes_accessed=1024, transcendentals=0)


CHAIN = (
    ("second", 0),
    ("second", 1),
    ("output",),
    ("norm_back",),
    ("line", 0, 0),
    ("second", 2),
    ("line", 1, 0),
    ("halves",),
    ("line", 0, 1),
    ("first", -1),
    ("line", 2, 0),
    ("first", 0, 1),
    ("line", 1, 1),
    ("line", 0, 2),
    ("line", 3, 0),
    ("line", 2, 1),
    ("line", 1, 2),
    ("write", 0),
    ("line", 4, 0),
    ("line", 3, 1),
    ("line", 2, 2),
    ("write", 1),
    ("line", 5, 0),
    ("line", 4, 1),
    ("line", 3, 2),
    ("write", 2),
    ("line", 5, 1),
    ("line", 4, 2),
    ("grad_volume",),
    ("write", 3),
    ("line", 5, 2),
    ("write", 4),
    ("write", 5),
)


def params():
    return pltpu.CompilerParams(
        dimension_semantics=("arbitrary",), vmem_limit_bytes=LIMIT
    )


def whole(shape):
    return pl.BlockSpec(shape, lambda *_: (0,) * len(shape))


def smem():
    return pl.BlockSpec(memory_space=pltpu.SMEM)


def fill_padded(padded, rows_first, sign):
    padded[...] = jnp.zeros_like(padded)
    cells = rows_first.astype(F32).T
    width_at = lax.broadcasted_iota(jnp.int32, cells.shape, 0) % WIDTH
    for c in (-1, 0, 1):
        off = sign * c
        moved = cells if off == 0 else pltpu.roll(cells, (-off) % CELLS, 0)
        inside = (width_at + off >= 0) & (width_at + off < WIDTH)
        moved = jnp.where(inside, moved, 0.0).astype(BF16)
        padded[1 + c, 1 : 1 + DEPTH, 1 : 1 + HEIGHT] = moved.reshape(
            DEPTH, HEIGHT, WIDTH, cells.shape[1]
        )


def span_of(a, sign):
    return max(0, -sign * a), DEPTH - abs(a)


def start_parts(source, buffer, sems):
    size = source.shape[0] // 3
    copies = {}
    for a in PLANE_ORDER:
        span = pl.ds((a + 1) * size, size)
        copies[a] = pltpu.make_async_copy(source.at[span], buffer.at[span], sems.at[a + 1])
        copies[a].start()
    return copies


def share_kernel(n, sign, idx, field, w, *refs):
    outs = refs[:n]
    padded, sums, shares, buffer, sems = refs[n:]
    rows = field.shape[0]
    copies = start_parts(w, buffer, sems)
    fill_padded(padded, field[...], sign)
    if sign == 1:
        for plane in range(DEPTH):
            near = [a for a in (-1, 0, 1) if 0 <= plane + a < DEPTH]
            if plane == 0:
                copies[0].wait()
                copies[1].wait()
            if plane == 1:
                copies[-1].wait()
            pieces = []
            for a in near:
                for b in (-1, 0, 1):
                    for c in (-1, 0, 1):
                        piece = padded[1 + c, 1 + plane + a, 1 + b : 1 + b + HEIGHT]
                        pieces.append(piece.reshape(PLANE, rows))
            lhs = jnp.concatenate(pieces, axis=1)
            rhs = buffer[(near[0] + 1) * 9 * rows : (near[-1] + 2) * 9 * rows]
            part = jnp.dot(lhs, rhs, preferred_element_type=F32).astype(BF16)
            for j in range(n):
                span = slice(plane * PLANE, (plane + 1) * PLANE)
                shares[j, span] = part[:, j * rows : (j + 1) * rows]
    else:
        for a in PLANE_ORDER:
            begin, planes = span_of(a, sign)
            pieces = []
            for b in (-1, 0, 1):
                for c in (-1, 0, 1):
                    low, first = 1 + sign * b, 1 + begin + sign * a
                    piece = padded[1 + c, first : first + planes, low : low + HEIGHT]
                    pieces.append(piece.reshape(planes * PLANE, rows))
            lhs = jnp.concatenate(pieces, axis=1)
            copies[a].wait()
            rhs = jnp.concatenate([buffer[(a + 1) * 9 + k] for k in range(9)], axis=1)
            part = lax.dot_general(lhs, rhs, NT, preferred_element_type=F32)
            span = slice(begin * PLANE, (begin + planes) * PLANE)
            if a == 0:
                sums[...] = part
            else:
                sums[span] += part
        for j in range(n):
            shares[j] = sums[:, j * rows : (j + 1) * rows].astype(BF16)
    for m in range(n):
        outs[m][...] = shares[idx[0] ^ m]


def spread_shares(sign, name, idx, n, field, w, limit):
    rows = field.shape[0]
    return pl.pallas_call(
        functools.partial(share_kernel, n, sign),
        in_specs=[smem(), pl.BlockSpec(memory_space=pltpu.VMEM), IN_HBM],
        out_specs=[pl.BlockSpec(memory_space=pltpu.VMEM)] * n,
        out_shape=[jax.ShapeDtypeStruct((CELLS, rows), BF16)] * n,
        scratch_shapes=[
            pltpu.VMEM((3, DEPTH + 2, HEIGHT + 2, WIDTH, rows), BF16),
            pltpu.VMEM((CELLS, n * rows), F32),
            pltpu.VMEM((n, CELLS, rows), BF16),
            pltpu.VMEM(w.shape, BF16),
            pltpu.SemaphoreType.DMA((3,)),
        ],
        compiler_params=pltpu.CompilerParams(vmem_limit_bytes=limit),
        cost_estimate=LIGHT,
        name=name,
    )(idx, field, w)


def norm_kernel(n, gain, *refs):
    shares = refs[:n]
    act, normed_out, inverse_out = refs[2 * n - 1 : 2 * n + 2]
    pre = shares[0][...].astype(F32)
    for m in range(1, n):
        pre = pre + shares[m][...].astype(F32)
    center = pre - jnp.mean(pre, axis=0, keepdims=True)
    inverse = lax.rsqrt(jnp.mean(center * center, axis=0, keepdims=True) + NORM_EPS)
    normed = center * inverse
    scaled = gain[...] * normed
    act[...] = (scaled * jax.nn.sigmoid(scaled)).astype(BF16)
    normed_out[...] = normed
    inverse_out[...] = inverse


def norm_back_kernel(n, gain, normed_in, inverse, *refs):
    shares = refs[:n]
    dpre, gain_part = refs[-2:]
    dact = shares[0][...].astype(F32)
    for m in range(1, n):
        dact = dact + shares[m][...].astype(F32)
    normed = normed_in[...]
    scaled = gain[...] * normed
    sigma = jax.nn.sigmoid(scaled)
    dscaled = dact * sigma * (1.0 + scaled * (1.0 - sigma))
    product = dscaled * normed
    gain_part[...] = jnp.sum(product, axis=0, keepdims=True)
    dnormed = gain[...] * dscaled
    mean_first = jnp.mean(dnormed, axis=0, keepdims=True)
    mean_second = jnp.mean(dnormed * normed, axis=0, keepdims=True)
    dpre[...] = ((dnormed - mean_first - normed * mean_second) * inverse[...]).astype(BF16)


def conv_back_add(sums, products, begin, planes, taps, rows, sign):
    for at, tap in enumerate(taps):
        a, b, c = tap
        a, b = sign * a, sign * b
        part = products[:, at * rows : (at + 1) * rows].reshape(planes, HEIGHT, WIDTH, rows)
        low, high = max(0, b), HEIGHT + min(0, b)
        sums[1 + c, begin - a : begin - a + planes, low - b : high - b] += part[:, low:high]


def conv_finish(sums, out, sign):
    rows = out.shape[0]
    total = None
    for c in (-1, 0, 1):
        off = sign * c
        part = sums[1 + c].reshape(CELLS, rows)
        if off != 0:
            width_at = lax.broadcasted_iota(jnp.int32, part.shape, 0) % WIDTH
            inside = (width_at + off >= 0) & (width_at + off < WIDTH)
            part = jnp.where(inside, pltpu.roll(part, (-off) % CELLS, 0), 0.0)
        total = part if total is None else total + part
    out[...] = total.T.astype(BF16)


def conv_kernel(n, sign, transposed, idx, w, *refs):
    blocks = refs[:n]
    out, mark, ordered, sums, buffer, sems = refs[-6:]
    mark[...] = jnp.zeros_like(mark)
    rows = out.shape[0]
    copies = start_parts(w, buffer, sems)
    sums[...] = jnp.zeros_like(sums)
    for m in range(n):
        ordered[idx[0] ^ m] = blocks[m][...]
    for a in PLANE_ORDER:
        begin, planes = span_of(-a, sign)
        span = slice(begin * PLANE, (begin + planes) * PLANE)
        lhs = jnp.concatenate([ordered[j, span] for j in range(n)], axis=1)
        copies[a].wait()
        for k in range(0, 9, 2):
            t = (a + 1) * 9 + k
            taps = TAPS[t : t + min(2, 9 - k)]
            if transposed:
                rhs = buffer[t * rows : (t + len(taps)) * rows]
                products = lax.dot_general(lhs, rhs, NT, preferred_element_type=F32)
            else:
                rhs = jnp.concatenate([buffer[t + at] for at in range(len(taps))], axis=1)
                products = jnp.dot(lhs, rhs, preferred_element_type=F32)
            conv_back_add(sums, products, begin, planes, taps, rows, sign)
    conv_finish(sums, out, sign)


def conv_full(name, sign, transposed, idx, w, blocks, after):
    n, rows = len(blocks), blocks[0].shape[1]
    return pl.pallas_call(
        functools.partial(conv_kernel, n, sign, transposed),
        in_specs=[smem(), IN_HBM]
        + [pl.BlockSpec(memory_space=pltpu.VMEM)] * n
        + [UNREAD] * len(after),
        out_specs=[pl.BlockSpec(memory_space=pltpu.VMEM)] * 2,
        out_shape=[
            jax.ShapeDtypeStruct((rows, CELLS), BF16),
            jax.ShapeDtypeStruct((8, 128), F32),
        ],
        scratch_shapes=[
            pltpu.VMEM((n, CELLS, rows), BF16),
            pltpu.VMEM((3, DEPTH, HEIGHT, WIDTH, rows), F32),
            pltpu.VMEM(w.shape, BF16),
            pltpu.SemaphoreType.DMA((3,)),
        ],
        compiler_params=pltpu.CompilerParams(vmem_limit_bytes=LIMIT),
        cost_estimate=LIGHT,
        name=name,
    )(idx, w, *blocks, *after)


def halves_kernel(n, turned, idx, *refs):
    blocks = refs[:n]
    keep, send = refs[-2:]
    half = n // 2
    rows = blocks[0].shape[1]

    def put(out, at, block):
        if turned:
            out[pl.ds(pl.multiple_of(at * rows, rows), rows)] = block[...].astype(F32).T.astype(BF16)
        else:
            out[at] = block[...]

    def split(kept, sent):
        for m in range(half):
            at = (idx[0] ^ m) & (half - 1)
            put(keep, at, blocks[kept + m])
            put(send, at, blocks[sent + m])

    @pl.when(idx[1] == 0)
    def _():
        split(0, half)

    @pl.when(idx[1] != 0)
    def _():
        split(half, 0)


def halves(name, turned, idx, blocks, after):
    n, rows = len(blocks), blocks[0].shape[1]
    shape = (n // 2 * rows, CELLS) if turned else (n // 2, CELLS, rows)
    return pl.pallas_call(
        functools.partial(halves_kernel, n, turned),
        in_specs=[smem()]
        + [pl.BlockSpec(memory_space=pltpu.VMEM)] * n
        + [UNREAD] * len(after),
        out_shape=[jax.ShapeDtypeStruct(shape, BF16)] * 2,
        compiler_params=pltpu.CompilerParams(vmem_limit_bytes=LIMIT),
        cost_estimate=LIGHT,
        name=name,
    )(idx, *blocks, *after)


def moved_second_kernel(own, other, _, out):
    out[...] = jnp.zeros_like(out)
    for which, ref in enumerate((own, other)):
        cells = ref[...].astype(F32).T
        width_at = lax.broadcasted_iota(jnp.int32, cells.shape, 0) % WIDTH
        for c in (-1, 0, 1):
            part = cells if c == 0 else pltpu.roll(cells, c % CELLS, 0)
            inside = (width_at - c >= 0) & (width_at - c < WIDTH)
            part = jnp.where(inside, part, 0.0).astype(BF16)
            out[which, 1 + c, :, 1 : 1 + HEIGHT] = part.reshape(
                DEPTH, HEIGHT, WIDTH, cells.shape[1]
            )


def moved_fields(kernel, name, shape, own, other, after):
    return pl.pallas_call(
        kernel,
        in_specs=[pl.BlockSpec(memory_space=pltpu.VMEM)] * 2 + [UNREAD],
        out_shape=jax.ShapeDtypeStruct(shape, BF16),
        compiler_params=pltpu.CompilerParams(vmem_limit_bytes=LIMIT),
        cost_estimate=LIGHT,
        name=name,
    )(own, other, after)


def split_rows(values):
    high = values.astype(BF16)
    low = (values - high.astype(F32)).astype(BF16)
    empty = jnp.zeros((EXTRA - 2, values.shape[1]), F32)
    return jnp.concatenate([high.astype(F32), low.astype(F32), empty], axis=0).astype(BF16)


def moved_lanes(cells, b, c):
    off = b * WIDTH + c
    if off == 0:
        return cells.astype(BF16)
    at = lax.broadcasted_iota(jnp.int32, cells.shape, 1)
    height_at, width_at = at // WIDTH % HEIGHT, at % WIDTH
    inside = (height_at + b >= 0) & (height_at + b < HEIGHT)
    inside = inside & (width_at + c >= 0) & (width_at + c < WIDTH)
    return jnp.where(inside, pltpu.roll(cells, (-off) % CELLS, 1), 0.0).astype(BF16)


def grad_first_kernel(offsets, vol_own, vol_other, own, other, gain_part, *refs):
    outs, moved = refs[-1 - len(offsets) : -1], refs[-1]
    half, rows = own.shape[0], own.shape[2]
    fields = [ref[...].astype(F32) for ref in (vol_own, vol_other)]
    rhs = [jnp.concatenate([ref[j] for j in range(half)], axis=1) for ref in (own, other)]
    for b in range(3):
        for which in range(2):
            for c in range(3):
                moved[which, c * rows : (c + 1) * rows] = moved_lanes(fields[which], b - 1, c - 1)
        for out, a in zip(outs, offsets):
            begin, count = max(0, -a) * PLANE, (DEPTH - abs(a)) * PLANE
            shift = begin + a * PLANE
            grads = None
            for which in range(2):
                lhs = moved[which, :, shift : shift + count]
                part = jnp.dot(lhs, rhs[which][begin : begin + count], preferred_element_type=F32)
                grads = part if grads is None else grads + part
            out[3 * rows * b : 3 * rows * (b + 1)] = grads.astype(BF16)
    filler = jnp.zeros((1, half * rows - rows), F32)
    for out, a in zip(outs, offsets):
        if a == -1:
            extra = split_rows(jnp.concatenate([gain_part[...], filler], axis=1))
        else:
            extra = jnp.zeros((EXTRA, half * rows), BF16)
        out[9 * rows :] = extra


def grad_first(offsets, vol_own, vol_other, own, other, gain_part, after):
    half, cells, rows = own.shape
    count = len(offsets)
    return pl.pallas_call(
        functools.partial(grad_first_kernel, offsets),
        in_specs=[pl.BlockSpec(memory_space=pltpu.VMEM)] * 5 + [UNREAD] * len(after),
        out_specs=[pl.BlockSpec(memory_space=pltpu.VMEM)] * count,
        out_shape=[jax.ShapeDtypeStruct((9 * rows + EXTRA, half * rows), BF16)] * count,
        scratch_shapes=[pltpu.VMEM((2, 3 * rows, CELLS), BF16)],
        compiler_params=pltpu.CompilerParams(vmem_limit_bytes=LIMIT),
        cost_estimate=LIGHT,
        name="grad_first",
    )(vol_own, vol_other, own, other, gain_part, *after)


def grad_second_kernel(a, moved, own, other, *refs):
    out = refs[-1]
    rows = out.shape[2]
    begin, planes = max(0, a), DEPTH - abs(a)
    lhs = [
        ref[:, begin * PLANE : (begin + planes) * PLANE] for ref in (own, other)
    ]
    for k in range(0, 9, 2):
        taps = range(k, min(k + 2, 9))
        grads = None
        for which in range(2):
            pieces = []
            for at in taps:
                b, c = at // 3 - 1, at % 3 - 1
                piece = moved[which, 1 + c, begin - a : begin - a + planes, 1 - b : 1 - b + HEIGHT]
                pieces.append(piece.reshape(planes * PLANE, rows))
            rhs = jnp.concatenate(pieces, axis=1)
            part = jnp.dot(lhs[which], rhs, preferred_element_type=F32)
            grads = part if grads is None else grads + part
        for place, at in enumerate(taps):
            out[at] = grads[:, place * rows : (place + 1) * rows].astype(BF16)


def grad_second(a, moved, own, other, after):
    wide, rows = own.shape[0], moved.shape[-1]
    return pl.pallas_call(
        functools.partial(grad_second_kernel, a),
        in_specs=[pl.BlockSpec(memory_space=pltpu.VMEM)] * 3 + [UNREAD] * len(after),
        out_shape=jax.ShapeDtypeStruct((9, wide, rows), BF16),
        compiler_params=pltpu.CompilerParams(vmem_limit_bytes=LIMIT),
        cost_estimate=LIGHT,
        name="grad_second",
    )(moved, own, other, *after)


def finish_kernel(n, axis, factor, chunk, idx, own, other, *refs):
    out, mark, wide, sems = refs[-4:]
    upper = (idx[0] >= n // 2).astype(jnp.int32) ^ idx[1]
    taps, height, width = wide.shape[1:]
    copies = []
    for k, (part, place) in enumerate(((own, upper), (other, 1 - upper))):
        size = (height, width)[axis - 1]
        span = pl.ds(pl.multiple_of(place * size, size), size)
        for third in range(3):
            at = slice(3 * third, 3 * third + 3)
            if len(part.shape) == 2:
                rows = part[3 * third * height : (3 * third + 3) * height]
                rows = rows.reshape(3, height, width)
            else:
                rows = part[at]
            wide[k, at] = rows.astype(F32) * factor
            target = out.at[pl.ds(chunk * taps + 3 * third, 3)]
            target = target.at[:, span] if axis == 1 else target.at[:, :, span]
            copies.append(
                pltpu.make_async_copy(wide.at[k, at], target, sems.at[3 * k + third])
            )
            copies[-1].start()
    mark[...] = jnp.zeros_like(mark)
    for copy in copies:
        copy.wait()


def finish(name, n, axis, factor, idx, chunk, shape, own, other, before, after):
    taps, height, width = shape
    given = [] if before is None else [before]
    full = (27, height * 2, width) if axis == 1 else (27, height, width * 2)
    return pl.pallas_call(
        functools.partial(finish_kernel, n, axis, factor, chunk),
        in_specs=[smem()]
        + [pl.BlockSpec(memory_space=pltpu.VMEM)] * 2
        + [UNREAD] * (len(given) + len(after)),
        out_specs=[UNREAD, pl.BlockSpec(memory_space=pltpu.VMEM)],
        out_shape=[jax.ShapeDtypeStruct(full, F32), jax.ShapeDtypeStruct((8, 128), F32)],
        scratch_shapes=[pltpu.VMEM((2,) + shape, F32), pltpu.SemaphoreType.DMA((6,))],
        input_output_aliases={3: 0} if given else {},
        compiler_params=pltpu.CompilerParams(vmem_limit_bytes=SMALL),
        cost_estimate=LIGHT,
        name=name,
    )(idx, own, other, *given, *after)


def add_kernel(x, y, *refs):
    out = refs[-1]
    if len(x.shape) == 3:
        out[...] = (x[...].astype(F32) + y[...].astype(F32)).astype(BF16)
    else:
        rows = x.shape[0] - EXTRA
        out[:rows] = (x[:rows].astype(F32) + y[:rows].astype(F32)).astype(BF16)
        tail = x[rows:].astype(F32) + y[rows:].astype(F32)
        out[rows:] = split_rows(tail[:1] + tail[1:2])


def pick_kernel(idx, x, y, *refs):
    out = refs[-1]

    @pl.when(idx[2] == 0)
    def _():
        out[...] = x[...]

    @pl.when(idx[2] != 0)
    def _():
        out[...] = y[...]


def whole_call(kernel, name, x, y, after, idx=None):
    given = [] if idx is None else [idx]
    return pl.pallas_call(
        kernel,
        in_specs=[smem()] * len(given)
        + [pl.BlockSpec(memory_space=pltpu.VMEM)] * 2
        + [UNREAD] * len(after),
        out_shape=jax.ShapeDtypeStruct(x.shape, x.dtype),
        compiler_params=pltpu.CompilerParams(vmem_limit_bytes=SMALL),
        cost_estimate=LIGHT,
        name=name,
    )(*given, x, y, *after)


def line_moves(chips):
    inward = [[(h, h + 1), (chips - 1 - h, chips - 2 - h)] for h in range(chips // 2 - 1)]
    mid = chips // 2
    outward = [[(j, i) for i, j in moves] for moves in reversed(inward)]
    return inward + [[(mid - 1, mid), (mid, mid - 1)]], outward


def line_send(x, moves):
    pairs = [(2 * i + k, 2 * j + k) for i, j in moves for k in (0, 1)]
    return lax.ppermute(x, "dp", pairs)


def line_step(step, part, total, idx, place, after):
    sums, outward = line_moves(lax.axis_size("dp") // 2)
    if step < len(sums):
        got = line_send(total, sums[step])
        base = total if step == len(sums) - 1 else part
        return whole_call(add_kernel, "line_add", base, got, after)
    moves = outward[step - len(sums)]
    got = line_send(total, moves)
    takes = functools.reduce(jnp.logical_or, [place // 2 == j for _, j in moves])
    marked = jnp.stack([idx[0], idx[1], takes.astype(jnp.int32)])
    return whole_call(pick_kernel, "line_pick", total, got, after, marked)


def shards(volume, w_first, gain, w_second, cotangent):
    n = lax.axis_size("chan")
    rows = volume.shape[1]
    vol, cot = volume[0], cotangent[0]
    chan, place = lax.axis_index("chan"), lax.axis_index("dp")
    idx = jnp.stack([chan, place % 2]).astype(jnp.int32)
    own_gain = lax.dynamic_slice_in_dim(gain, chan * rows, rows, 0)[None]
    factor = 1.0 / math.sqrt(lax.axis_size("dp") * CELLS)

    def to_partner(x, m):
        return lax.ppermute(x, "chan", [(i, i ^ m) for i in range(n)])

    def to_core(x):
        return lax.ppermute(x, "dp", [(i, i ^ 1) for i in range(lax.axis_size("dp"))])

    def swap(parts):
        got = {m: to_partner(parts[m], m) for m in reversed(range(1, n))}
        return [parts[0]] + [got[m] for m in range(1, n)]

    first_flat = w_first.reshape(27 * rows, n * rows)
    pre_shares = swap(spread_shares(1, "pre", idx, n, vol, first_flat, LARGE))
    dact_parts = spread_shares(-1, "dact", idx, n, cot, w_second, LIMIT)
    held = dact_parts[1:]
    act, normed, inverse, *held = pl.pallas_call(
        functools.partial(norm_kernel, n),
        in_specs=[pl.BlockSpec(memory_space=pltpu.VMEM)] * (1 + n) + [UNREAD] * len(held),
        out_specs=[pl.BlockSpec(memory_space=pltpu.VMEM)] * 3 + [UNREAD] * len(held),
        out_shape=[
            jax.ShapeDtypeStruct((CELLS, rows), BF16),
            jax.ShapeDtypeStruct((CELLS, rows), F32),
            jax.ShapeDtypeStruct((1, rows), F32),
        ]
        + [jax.ShapeDtypeStruct(x.shape, x.dtype) for x in held],
        input_output_aliases={1 + n + k: 3 + k for k in range(len(held))},
        compiler_params=pltpu.CompilerParams(vmem_limit_bytes=SMALL),
        cost_estimate=LIGHT,
        name="norm",
    )(own_gain, *pre_shares, *held)
    act_blocks = swap([act] * n)
    dact_shares = swap([dact_parts[0]] + held)
    moved_cot = moved_fields(
        moved_second_kernel,
        "moved_second",
        (2, 3, DEPTH, HEIGHT + 2, WIDTH, rows),
        cot,
        to_core(cot),
        act,
    )
    vol_other = to_core(vol)
    act_keep, act_send = halves("act_halves", True, idx, act_blocks, (moved_cot, vol_other))
    act_other = to_core(act_send)

    sums, outward = line_moves(lax.axis_size("dp") // 2)
    steps = len(sums) + len(outward)
    parts, totals, crossed = {}, {}, {}
    last = ()

    reached = [0] * 6

    def line(chunk, step):
        nonlocal last
        if reached[chunk] > step:
            return
        if reached[chunk] < step:
            line(chunk, step - 1)
        reached[chunk] = step + 1
        before = totals.get(chunk, parts[chunk])
        totals[chunk] = line_step(step, parts[chunk], before, idx, place, last)
        last = (totals[chunk],)
        if step == steps - 1:
            crossed[chunk] = to_core(totals[chunk])

    def write(chunk):
        nonlocal last
        line(chunk, steps - 1)
        name, axis = ("finish_second", 1) if chunk < 3 else ("finish_first", 2)
        shape = (9, n // 2 * rows, rows) if chunk < 3 else (9, rows, n // 2 * rows)
        written[axis], mark = finish(
            name,
            n,
            axis,
            factor,
            idx,
            chunk % 3,
            shape,
            totals[chunk],
            crossed[chunk],
            written.get(axis),
            last,
        )
        last = (mark,)

    def second_part(chunk):
        nonlocal last
        parts[chunk] = grad_second(chunk - 1, moved_cot, act_keep, act_other, last)
        last = (parts[chunk],)

    def first_parts(*offsets):
        nonlocal last
        own, other = done["dpre_halves"]
        made = grad_first(offsets, vol, vol_other, own, other, done["gain"], last)
        for a, part in zip(offsets, made):
            parts[4 + a] = part
        last = (made[0],)

    def norm_back():
        nonlocal last
        dpre, done["gain"] = pl.pallas_call(
            functools.partial(norm_back_kernel, n),
            in_specs=[pl.BlockSpec(memory_space=pltpu.VMEM)] * (3 + n) + [UNREAD],
            out_shape=[
                jax.ShapeDtypeStruct((CELLS, rows), BF16),
                jax.ShapeDtypeStruct((1, rows), F32),
            ],
            compiler_params=pltpu.CompilerParams(vmem_limit_bytes=SMALL),
            cost_estimate=LIGHT,
            name="norm_back",
        )(own_gain, normed, inverse, *dact_shares, *last)
        done["dpre"] = swap([dpre] * n)
        last = (dpre,)

    def dpre_halves():
        nonlocal last
        keep, send = halves("dpre_halves", False, idx, done["dpre"], last)
        done["dpre_halves"] = keep, to_core(send)
        last = (keep,)

    def output():
        nonlocal last
        done["output"], mark = conv_full("output", 1, False, idx, w_second, act_blocks, last)
        last = (mark,)

    def grad_volume():
        nonlocal last
        done["grad_volume"], mark = conv_full(
            "grad_volume", -1, True, idx, first_flat, done["dpre"], last
        )
        last = (mark,)

    written, done = {}, {}
    steps_by_name = {
        "second": second_part,
        "first": first_parts,
        "output": output,
        "grad_volume": grad_volume,
        "norm_back": norm_back,
        "halves": dpre_halves,
        "line": line,
        "write": write,
    }
    for name, *at in CHAIN:
        steps_by_name[name](*at)
    gain_rows = totals[3][9 * rows : 9 * rows + 2, :rows].astype(F32)
    gain_rows_other = crossed[3][9 * rows : 9 * rows + 2, :rows].astype(F32)
    gain_total = (jnp.sum(gain_rows, axis=0) + jnp.sum(gain_rows_other, axis=0)) * factor
    return (done["output"][None], done["grad_volume"][None], written[2], gain_total, written[1])


def solution(mesh):
    placed = (
        P("dp", "chan", None),
        P(None, "chan", None),
        P(),
        P(None, None, "chan"),
        P("dp", "chan", None),
    )
    return jax.shard_map(
        shards,
        mesh=mesh,
        in_specs=placed,
        out_specs=(
            P("dp", "chan", None),
            P("dp", "chan", None),
            P(None, "chan", None),
            P("chan"),
            P(None, None, "chan"),
        ),
        check_vma=False,
    )
```

```python
import functools
import math

import jax
import jax.numpy as jnp
from jax import lax
from jax.experimental import pallas as pl
from jax.experimental.pallas import tpu as pltpu
from jax.sharding import PartitionSpec as P

DEPTH, HEIGHT, WIDTH = 4, 16, 16
PLANE = HEIGHT * WIDTH
CELLS = DEPTH * PLANE
TAPS = [(a, b, c) for a in (-1, 0, 1) for b in (-1, 0, 1) for c in (-1, 0, 1)]
NORM_EPS = 1e-05
LIMIT = 16 * 1024 * 1024
SMALL = 8 * 1024 * 1024
LARGE = 59 * 1024 * 1024
EXTRA = 16
F32, BF16 = jnp.float32, jnp.bfloat16
NT = (((1,), (1,)), ((), ()))
UNREAD = pl.BlockSpec(memory_space=pl.ANY)
IN_HBM = pl.BlockSpec(memory_space=pltpu.HBM)
PLANE_ORDER = (0, 1, -1)
LIGHT = pl.CostEstimate(flops=1024, bytes_accessed=1024, transcendentals=0)


CHAIN = (
    ("second", 0),
    ("second", 1),
    ("output",),
    ("norm_back",),
    ("line", 0, 0),
    ("second", 2),
    ("line", 1, 0),
    ("halves",),
    ("line", 0, 1),
    ("first", -1),
    ("line", 2, 0),
    ("first", 0, 1),
    ("line", 1, 1),
    ("line", 0, 2),
    ("line", 3, 0),
    ("line", 2, 1),
    ("line", 1, 2),
    ("write", 0),
    ("line", 4, 0),
    ("line", 3, 1),
    ("line", 2, 2),
    ("write", 1),
    ("line", 5, 0),
    ("line", 4, 1),
    ("line", 3, 2),
    ("write", 2),
    ("line", 5, 1),
    ("line", 4, 2),
    ("grad_volume",),
    ("write", 3),
    ("line", 5, 2),
    ("write", 4),
    ("write", 5),
)


def params():
    return pltpu.CompilerParams(
        dimension_semantics=("arbitrary",), vmem_limit_bytes=LIMIT
    )


def whole(shape):
    return pl.BlockSpec(shape, lambda *_: (0,) * len(shape))


def smem():
    return pl.BlockSpec(memory_space=pltpu.SMEM)


def fill_padded(padded, rows_first, sign):
    padded[...] = jnp.zeros_like(padded)
    cells = rows_first.astype(F32).T
    width_at = lax.broadcasted_iota(jnp.int32, cells.shape, 0) % WIDTH
    for c in (-1, 0, 1):
        off = sign * c
        moved = cells if off == 0 else pltpu.roll(cells, (-off) % CELLS, 0)
        inside = (width_at + off >= 0) & (width_at + off < WIDTH)
        moved = jnp.where(inside, moved, 0.0).astype(BF16)
        padded[1 + c, 1 : 1 + DEPTH, 1 : 1 + HEIGHT] = moved.reshape(
            DEPTH, HEIGHT, WIDTH, cells.shape[1]
        )


def span_of(a, sign):
    return max(0, -sign * a), DEPTH - abs(a)


def start_parts(source, buffer, sems):
    size = source.shape[0] // 3
    copies = {}
    for a in PLANE_ORDER:
        span = pl.ds((a + 1) * size, size)
        copies[a] = pltpu.make_async_copy(source.at[span], buffer.at[span], sems.at[a + 1])
        copies[a].start()
    return copies


def share_kernel(n, sign, idx, field, w, *refs):
    outs = refs[:n]
    padded, sums, shares, buffer, sems = refs[n:]
    rows = field.shape[0]
    copies = start_parts(w, buffer, sems)
    fill_padded(padded, field[...], sign)
    if sign == 1:
        for plane in range(DEPTH):
            near = [a for a in (-1, 0, 1) if 0 <= plane + a < DEPTH]
            if plane == 0:
                copies[0].wait()
                copies[1].wait()
            if plane == 1:
                copies[-1].wait()
            pieces = []
            for a in near:
                for b in (-1, 0, 1):
                    for c in (-1, 0, 1):
                        piece = padded[1 + c, 1 + plane + a, 1 + b : 1 + b + HEIGHT]
                        pieces.append(piece.reshape(PLANE, rows))
            lhs = jnp.concatenate(pieces, axis=1)
            rhs = buffer[(near[0] + 1) * 9 * rows : (near[-1] + 2) * 9 * rows]
            part = jnp.dot(lhs, rhs, preferred_element_type=F32).astype(BF16)
            for j in range(n):
                span = slice(plane * PLANE, (plane + 1) * PLANE)
                shares[j, span] = part[:, j * rows : (j + 1) * rows]
    else:
        for a in PLANE_ORDER:
            begin, planes = span_of(a, sign)
            pieces = []
            for b in (-1, 0, 1):
                for c in (-1, 0, 1):
                    low, first = 1 + sign * b, 1 + begin + sign * a
                    piece = padded[1 + c, first : first + planes, low : low + HEIGHT]
                    pieces.append(piece.reshape(planes * PLANE, rows))
            lhs = jnp.concatenate(pieces, axis=1)
            copies[a].wait()
            rhs = jnp.concatenate([buffer[(a + 1) * 9 + k] for k in range(9)], axis=1)
            part = lax.dot_general(lhs, rhs, NT, preferred_element_type=F32)
            span = slice(begin * PLANE, (begin + planes) * PLANE)
            if a == 0:
                sums[...] = part
            else:
                sums[span] += part
        for j in range(n):
            shares[j] = sums[:, j * rows : (j + 1) * rows].astype(BF16)
    for m in range(n):
        outs[m][...] = shares[idx[0] ^ m]


def spread_shares(sign, name, idx, n, field, w, limit):
    rows = field.shape[0]
    return pl.pallas_call(
        functools.partial(share_kernel, n, sign),
        in_specs=[smem(), pl.BlockSpec(memory_space=pltpu.VMEM), IN_HBM],
        out_specs=[pl.BlockSpec(memory_space=pltpu.VMEM)] * n,
        out_shape=[jax.ShapeDtypeStruct((CELLS, rows), BF16)] * n,
        scratch_shapes=[
            pltpu.VMEM((3, DEPTH + 2, HEIGHT + 2, WIDTH, rows), BF16),
            pltpu.VMEM((CELLS, n * rows), F32),
            pltpu.VMEM((n, CELLS, rows), BF16),
            pltpu.VMEM(w.shape, BF16),
            pltpu.SemaphoreType.DMA((3,)),
        ],
        compiler_params=pltpu.CompilerParams(vmem_limit_bytes=limit),
        cost_estimate=LIGHT,
        name=name,
    )(idx, field, w)


def norm_kernel(n, gain, *refs):
    shares = refs[:n]
    act, normed_out, inverse_out = refs[2 * n - 1 : 2 * n + 2]
    pre = shares[0][...].astype(F32)
    for m in range(1, n):
        pre = pre + shares[m][...].astype(F32)
    center = pre - jnp.mean(pre, axis=0, keepdims=True)
    inverse = lax.rsqrt(jnp.mean(center * center, axis=0, keepdims=True) + NORM_EPS)
    normed = center * inverse
    scaled = gain[...] * normed
    act[...] = (scaled * jax.nn.sigmoid(scaled)).astype(BF16)
    normed_out[...] = normed
    inverse_out[...] = inverse


def norm_back_kernel(n, gain, normed_in, inverse, *refs):
    shares = refs[:n]
    dpre, gain_part = refs[-2:]
    dact = shares[0][...].astype(F32)
    for m in range(1, n):
        dact = dact + shares[m][...].astype(F32)
    normed = normed_in[...]
    scaled = gain[...] * normed
    sigma = jax.nn.sigmoid(scaled)
    dscaled = dact * sigma * (1.0 + scaled * (1.0 - sigma))
    product = dscaled * normed
    gain_part[...] = jnp.sum(product, axis=0, keepdims=True)
    dnormed = gain[...] * dscaled
    mean_first = jnp.mean(dnormed, axis=0, keepdims=True)
    mean_second = jnp.mean(dnormed * normed, axis=0, keepdims=True)
    dpre[...] = ((dnormed - mean_first - normed * mean_second) * inverse[...]).astype(BF16)


def conv_back_add(sums, products, begin, planes, taps, rows, sign):
    for at, tap in enumerate(taps):
        a, b, c = tap
        a, b = sign * a, sign * b
        part = products[:, at * rows : (at + 1) * rows].reshape(planes, HEIGHT, WIDTH, rows)
        low, high = max(0, b), HEIGHT + min(0, b)
        sums[1 + c, begin - a : begin - a + planes, low - b : high - b] += part[:, low:high]


def conv_finish(sums, out, sign):
    rows = out.shape[0]
    total = None
    for c in (-1, 0, 1):
        off = sign * c
        part = sums[1 + c].reshape(CELLS, rows)
        if off != 0:
            width_at = lax.broadcasted_iota(jnp.int32, part.shape, 0) % WIDTH
            inside = (width_at + off >= 0) & (width_at + off < WIDTH)
            part = jnp.where(inside, pltpu.roll(part, (-off) % CELLS, 0), 0.0)
        total = part if total is None else total + part
    out[...] = total.T.astype(BF16)


def conv_kernel(n, sign, transposed, idx, w, *refs):
    blocks = refs[:n]
    out, mark, ordered, sums, buffer, sems = refs[-6:]
    mark[...] = jnp.zeros_like(mark)
    rows = out.shape[0]
    copies = start_parts(w, buffer, sems)
    sums[...] = jnp.zeros_like(sums)
    for m in range(n):
        ordered[idx[0] ^ m] = blocks[m][...]
    for a in PLANE_ORDER:
        begin, planes = span_of(-a, sign)
        span = slice(begin * PLANE, (begin + planes) * PLANE)
        lhs = jnp.concatenate([ordered[j, span] for j in range(n)], axis=1)
        copies[a].wait()
        for k in range(0, 9, 2):
            t = (a + 1) * 9 + k
            taps = TAPS[t : t + min(2, 9 - k)]
            if transposed:
                rhs = buffer[t * rows : (t + len(taps)) * rows]
                products = lax.dot_general(lhs, rhs, NT, preferred_element_type=F32)
            else:
                rhs = jnp.concatenate([buffer[t + at] for at in range(len(taps))], axis=1)
                products = jnp.dot(lhs, rhs, preferred_element_type=F32)
            conv_back_add(sums, products, begin, planes, taps, rows, sign)
    conv_finish(sums, out, sign)


def conv_full(name, sign, transposed, idx, w, blocks, after):
    n, rows = len(blocks), blocks[0].shape[1]
    return pl.pallas_call(
        functools.partial(conv_kernel, n, sign, transposed),
        in_specs=[smem(), IN_HBM]
        + [pl.BlockSpec(memory_space=pltpu.VMEM)] * n
        + [UNREAD] * len(after),
        out_specs=[pl.BlockSpec(memory_space=pltpu.VMEM)] * 2,
        out_shape=[
            jax.ShapeDtypeStruct((rows, CELLS), BF16),
            jax.ShapeDtypeStruct((8, 128), F32),
        ],
        scratch_shapes=[
            pltpu.VMEM((n, CELLS, rows), BF16),
            pltpu.VMEM((3, DEPTH, HEIGHT, WIDTH, rows), F32),
            pltpu.VMEM(w.shape, BF16),
            pltpu.SemaphoreType.DMA((3,)),
        ],
        compiler_params=pltpu.CompilerParams(vmem_limit_bytes=LIMIT),
        cost_estimate=LIGHT,
        name=name,
    )(idx, w, *blocks, *after)


def halves_kernel(n, turned, idx, *refs):
    blocks = refs[:n]
    keep, send = refs[-2:]
    half = n // 2
    rows = blocks[0].shape[1]

    def put(out, at, block):
        if turned:
            out[pl.ds(pl.multiple_of(at * rows, rows), rows)] = block[...].astype(F32).T.astype(BF16)
        else:
            out[at] = block[...]

    def split(kept, sent):
        for m in range(half):
            at = (idx[0] ^ m) & (half - 1)
            put(keep, at, blocks[kept + m])
            put(send, at, blocks[sent + m])

    @pl.when(idx[1] == 0)
    def _():
        split(0, half)

    @pl.when(idx[1] != 0)
    def _():
        split(half, 0)


def halves(name, turned, idx, blocks, after):
    n, rows = len(blocks), blocks[0].shape[1]
    shape = (n // 2 * rows, CELLS) if turned else (n // 2, CELLS, rows)
    return pl.pallas_call(
        functools.partial(halves_kernel, n, turned),
        in_specs=[smem()]
        + [pl.BlockSpec(memory_space=pltpu.VMEM)] * n
        + [UNREAD] * len(after),
        out_shape=[jax.ShapeDtypeStruct(shape, BF16)] * 2,
        compiler_params=pltpu.CompilerParams(vmem_limit_bytes=LIMIT),
        cost_estimate=LIGHT,
        name=name,
    )(idx, *blocks, *after)


def moved_second_kernel(own, other, _, out):
    out[...] = jnp.zeros_like(out)
    for which, ref in enumerate((own, other)):
        cells = ref[...].astype(F32).T
        width_at = lax.broadcasted_iota(jnp.int32, cells.shape, 0) % WIDTH
        for c in (-1, 0, 1):
            part = cells if c == 0 else pltpu.roll(cells, c % CELLS, 0)
            inside = (width_at - c >= 0) & (width_at - c < WIDTH)
            part = jnp.where(inside, part, 0.0).astype(BF16)
            out[which, 1 + c, :, 1 : 1 + HEIGHT] = part.reshape(
                DEPTH, HEIGHT, WIDTH, cells.shape[1]
            )


def moved_fields(kernel, name, shape, own, other, after):
    return pl.pallas_call(
        kernel,
        in_specs=[pl.BlockSpec(memory_space=pltpu.VMEM)] * 2 + [UNREAD],
        out_shape=jax.ShapeDtypeStruct(shape, BF16),
        compiler_params=pltpu.CompilerParams(vmem_limit_bytes=LIMIT),
        cost_estimate=LIGHT,
        name=name,
    )(own, other, after)


def split_rows(values):
    high = values.astype(BF16)
    low = (values - high.astype(F32)).astype(BF16)
    empty = jnp.zeros((EXTRA - 2, values.shape[1]), F32)
    return jnp.concatenate([high.astype(F32), low.astype(F32), empty], axis=0).astype(BF16)


def moved_lanes(cells, b, c):
    off = b * WIDTH + c
    if off == 0:
        return cells.astype(BF16)
    at = lax.broadcasted_iota(jnp.int32, cells.shape, 1)
    height_at, width_at = at // WIDTH % HEIGHT, at % WIDTH
    inside = (height_at + b >= 0) & (height_at + b < HEIGHT)
    inside = inside & (width_at + c >= 0) & (width_at + c < WIDTH)
    return jnp.where(inside, pltpu.roll(cells, (-off) % CELLS, 1), 0.0).astype(BF16)


def grad_first_kernel(offsets, vol_own, vol_other, own, other, gain_part, *refs):
    outs, moved = refs[-1 - len(offsets) : -1], refs[-1]
    half, rows = own.shape[0], own.shape[2]
    fields = [ref[...].astype(F32) for ref in (vol_own, vol_other)]
    rhs = [jnp.concatenate([ref[j] for j in range(half)], axis=1) for ref in (own, other)]
    for b in range(3):
        for which in range(2):
            for c in range(3):
                moved[which, c * rows : (c + 1) * rows] = moved_lanes(fields[which], b - 1, c - 1)
        for out, a in zip(outs, offsets):
            begin, count = max(0, -a) * PLANE, (DEPTH - abs(a)) * PLANE
            shift = begin + a * PLANE
            grads = None
            for which in range(2):
                lhs = moved[which, :, shift : shift + count]
                part = jnp.dot(lhs, rhs[which][begin : begin + count], preferred_element_type=F32)
                grads = part if grads is None else grads + part
            out[3 * rows * b : 3 * rows * (b + 1)] = grads.astype(BF16)
    filler = jnp.zeros((1, half * rows - rows), F32)
    for out, a in zip(outs, offsets):
        if a == -1:
            extra = split_rows(jnp.concatenate([gain_part[...], filler], axis=1))
        else:
            extra = jnp.zeros((EXTRA, half * rows), BF16)
        out[9 * rows :] = extra


def grad_first(offsets, vol_own, vol_other, own, other, gain_part, after):
    half, cells, rows = own.shape
    count = len(offsets)
    return pl.pallas_call(
        functools.partial(grad_first_kernel, offsets),
        in_specs=[pl.BlockSpec(memory_space=pltpu.VMEM)] * 5 + [UNREAD] * len(after),
        out_specs=[pl.BlockSpec(memory_space=pltpu.VMEM)] * count,
        out_shape=[jax.ShapeDtypeStruct((9 * rows + EXTRA, half * rows), BF16)] * count,
        scratch_shapes=[pltpu.VMEM((2, 3 * rows, CELLS), BF16)],
        compiler_params=pltpu.CompilerParams(vmem_limit_bytes=LIMIT),
        cost_estimate=LIGHT,
        name="grad_first",
    )(vol_own, vol_other, own, other, gain_part, *after)


def grad_second_kernel(a, moved, own, other, *refs):
    out = refs[-1]
    rows = out.shape[2]
    begin, planes = max(0, a), DEPTH - abs(a)
    lhs = [
        ref[:, begin * PLANE : (begin + planes) * PLANE] for ref in (own, other)
    ]
    for k in range(0, 9, 2):
        taps = range(k, min(k + 2, 9))
        grads = None
        for which in range(2):
            pieces = []
            for at in taps:
                b, c = at // 3 - 1, at % 3 - 1
                piece = moved[which, 1 + c, begin - a : begin - a + planes, 1 - b : 1 - b + HEIGHT]
                pieces.append(piece.reshape(planes * PLANE, rows))
            rhs = jnp.concatenate(pieces, axis=1)
            part = jnp.dot(lhs[which], rhs, preferred_element_type=F32)
            grads = part if grads is None else grads + part
        for place, at in enumerate(taps):
            out[at] = grads[:, place * rows : (place + 1) * rows].astype(BF16)


def grad_second(a, moved, own, other, after):
    wide, rows = own.shape[0], moved.shape[-1]
    return pl.pallas_call(
        functools.partial(grad_second_kernel, a),
        in_specs=[pl.BlockSpec(memory_space=pltpu.VMEM)] * 3 + [UNREAD] * len(after),
        out_shape=jax.ShapeDtypeStruct((9, wide, rows), BF16),
        compiler_params=pltpu.CompilerParams(vmem_limit_bytes=LIMIT),
        cost_estimate=LIGHT,
        name="grad_second",
    )(moved, own, other, *after)


def finish_kernel(n, axis, factor, chunk, idx, own, other, *refs):
    out, mark, wide, sems = refs[-4:]
    upper = (idx[0] >= n // 2).astype(jnp.int32) ^ idx[1]
    taps, height, width = wide.shape[1:]
    copies = []
    for k, (part, place) in enumerate(((own, upper), (other, 1 - upper))):
        size = (height, width)[axis - 1]
        span = pl.ds(pl.multiple_of(place * size, size), size)
        for third in range(3):
            at = slice(3 * third, 3 * third + 3)
            if len(part.shape) == 2:
                rows = part[3 * third * height : (3 * third + 3) * height]
                rows = rows.reshape(3, height, width)
            else:
                rows = part[at]
            wide[k, at] = rows.astype(F32) * factor
            target = out.at[pl.ds(chunk * taps + 3 * third, 3)]
            target = target.at[:, span] if axis == 1 else target.at[:, :, span]
            copies.append(
                pltpu.make_async_copy(wide.at[k, at], target, sems.at[3 * k + third])
            )
            copies[-1].start()
    mark[...] = jnp.zeros_like(mark)
    for copy in copies:
        copy.wait()


def finish(name, n, axis, factor, idx, chunk, shape, own, other, before, after):
    taps, height, width = shape
    given = [] if before is None else [before]
    full = (27, height * 2, width) if axis == 1 else (27, height, width * 2)
    return pl.pallas_call(
        functools.partial(finish_kernel, n, axis, factor, chunk),
        in_specs=[smem()]
        + [pl.BlockSpec(memory_space=pltpu.VMEM)] * 2
        + [UNREAD] * (len(given) + len(after)),
        out_specs=[UNREAD, pl.BlockSpec(memory_space=pltpu.VMEM)],
        out_shape=[jax.ShapeDtypeStruct(full, F32), jax.ShapeDtypeStruct((8, 128), F32)],
        scratch_shapes=[pltpu.VMEM((2,) + shape, F32), pltpu.SemaphoreType.DMA((6,))],
        input_output_aliases={3: 0} if given else {},
        compiler_params=pltpu.CompilerParams(vmem_limit_bytes=SMALL),
        cost_estimate=LIGHT,
        name=name,
    )(idx, own, other, *given, *after)


def add_kernel(x, y, *refs):
    out = refs[-1]
    if len(x.shape) == 3:
        out[...] = (x[...].astype(F32) + y[...].astype(F32)).astype(BF16)
    else:
        rows = x.shape[0] - EXTRA
        out[:rows] = (x[:rows].astype(F32) + y[:rows].astype(F32)).astype(BF16)
        tail = x[rows:].astype(F32) + y[rows:].astype(F32)
        out[rows:] = split_rows(tail[:1] + tail[1:2])


def pick_kernel(idx, x, y, *refs):
    out = refs[-1]

    @pl.when(idx[2] == 0)
    def _():
        out[...] = x[...]

    @pl.when(idx[2] != 0)
    def _():
        out[...] = y[...]


def whole_call(kernel, name, x, y, after, idx=None):
    given = [] if idx is None else [idx]
    return pl.pallas_call(
        kernel,
        in_specs=[smem()] * len(given)
        + [pl.BlockSpec(memory_space=pltpu.VMEM)] * 2
        + [UNREAD] * len(after),
        out_shape=jax.ShapeDtypeStruct(x.shape, x.dtype),
        compiler_params=pltpu.CompilerParams(vmem_limit_bytes=SMALL),
        cost_estimate=LIGHT,
        name=name,
    )(*given, x, y, *after)


def line_moves(chips):
    inward = [[(h, h + 1), (chips - 1 - h, chips - 2 - h)] for h in range(chips // 2 - 1)]
    mid = chips // 2
    outward = [[(j, i) for i, j in moves] for moves in reversed(inward)]
    return inward + [[(mid - 1, mid), (mid, mid - 1)]], outward


def line_send(x, moves):
    pairs = [(2 * i + k, 2 * j + k) for i, j in moves for k in (0, 1)]
    return lax.ppermute(x, "dp", pairs)


def line_step(step, part, total, idx, place, after):
    sums, outward = line_moves(lax.axis_size("dp") // 2)
    if step < len(sums):
        got = line_send(total, sums[step])
        base = total if step == len(sums) - 1 else part
        return whole_call(add_kernel, "line_add", base, got, after)
    moves = outward[step - len(sums)]
    got = line_send(total, moves)
    takes = functools.reduce(jnp.logical_or, [place // 2 == j for _, j in moves])
    marked = jnp.stack([idx[0], idx[1], takes.astype(jnp.int32)])
    return whole_call(pick_kernel, "line_pick", total, got, after, marked)


def shards(volume, w_first, gain, w_second, cotangent):
    n = lax.axis_size("chan")
    rows = volume.shape[1]
    vol, cot = volume[0], cotangent[0]
    chan, place = lax.axis_index("chan"), lax.axis_index("dp")
    idx = jnp.stack([chan, place % 2]).astype(jnp.int32)
    own_gain = lax.dynamic_slice_in_dim(gain, chan * rows, rows, 0)[None]
    factor = 1.0 / math.sqrt(lax.axis_size("dp") * CELLS)

    def to_partner(x, m):
        return lax.ppermute(x, "chan", [(i, i ^ m) for i in range(n)])

    def to_core(x):
        return lax.ppermute(x, "dp", [(i, i ^ 1) for i in range(lax.axis_size("dp"))])

    def swap(parts):
        got = {m: to_partner(parts[m], m) for m in reversed(range(1, n))}
        return [parts[0]] + [got[m] for m in range(1, n)]

    first_flat = w_first.reshape(27 * rows, n * rows)
    pre_shares = swap(spread_shares(1, "pre", chan.astype(jnp.int32).reshape(1), n, vol, first_flat, LARGE))
    dact_parts = spread_shares(-1, "dact", idx, n, cot, w_second, LIMIT)
    held = dact_parts[1:]
    act, normed, inverse, *held = pl.pallas_call(
        functools.partial(norm_kernel, n),
        in_specs=[pl.BlockSpec(memory_space=pltpu.VMEM)] * (1 + n) + [UNREAD] * len(held),
        out_specs=[pl.BlockSpec(memory_space=pltpu.VMEM)] * 3 + [UNREAD] * len(held),
        out_shape=[
            jax.ShapeDtypeStruct((CELLS, rows), BF16),
            jax.ShapeDtypeStruct((CELLS, rows), F32),
            jax.ShapeDtypeStruct((1, rows), F32),
        ]
        + [jax.ShapeDtypeStruct(x.shape, x.dtype) for x in held],
        input_output_aliases={1 + n + k: 3 + k for k in range(len(held))},
        compiler_params=pltpu.CompilerParams(vmem_limit_bytes=SMALL),
        cost_estimate=LIGHT,
        name="norm",
    )(own_gain, *pre_shares, *held)
    act_blocks = swap([act] * n)
    dact_shares = swap([dact_parts[0]] + held)
    moved_cot = moved_fields(
        moved_second_kernel,
        "moved_second",
        (2, 3, DEPTH, HEIGHT + 2, WIDTH, rows),
        cot,
        to_core(cot),
        act,
    )
    vol_other = to_core(vol)
    act_keep, act_send = halves("act_halves", True, idx, act_blocks, (moved_cot, vol_other))
    act_other = to_core(act_send)

    sums, outward = line_moves(lax.axis_size("dp") // 2)
    steps = len(sums) + len(outward)
    parts, totals, crossed = {}, {}, {}
    last = ()

    reached = [0] * 6

    def line(chunk, step):
        nonlocal last
        if reached[chunk] > step:
            return
        if reached[chunk] < step:
            line(chunk, step - 1)
        reached[chunk] = step + 1
        before = totals.get(chunk, parts[chunk])
        totals[chunk] = line_step(step, parts[chunk], before, idx, place, last)
        last = (totals[chunk],)
        if step == steps - 1:
            crossed[chunk] = to_core(totals[chunk])

    def write(chunk):
        nonlocal last
        line(chunk, steps - 1)
        name, axis = ("finish_second", 1) if chunk < 3 else ("finish_first", 2)
        shape = (9, n // 2 * rows, rows) if chunk < 3 else (9, rows, n // 2 * rows)
        written[axis], mark = finish(
            name,
            n,
            axis,
            factor,
            idx,
            chunk % 3,
            shape,
            totals[chunk],
            crossed[chunk],
            written.get(axis),
            last,
        )
        last = (mark,)

    def second_part(chunk):
        nonlocal last
        parts[chunk] = grad_second(chunk - 1, moved_cot, act_keep, act_other, last)
        last = (parts[chunk],)

    def first_parts(*offsets):
        nonlocal last
        own, other = done["dpre_halves"]
        made = grad_first(offsets, vol, vol_other, own, other, done["gain"], last)
        for a, part in zip(offsets, made):
            parts[4 + a] = part
        last = (made[0],)

    def norm_back():
        nonlocal last
        dpre, done["gain"] = pl.pallas_call(
            functools.partial(norm_back_kernel, n),
            in_specs=[pl.BlockSpec(memory_space=pltpu.VMEM)] * (3 + n) + [UNREAD],
            out_shape=[
                jax.ShapeDtypeStruct((CELLS, rows), BF16),
                jax.ShapeDtypeStruct((1, rows), F32),
            ],
            compiler_params=pltpu.CompilerParams(vmem_limit_bytes=SMALL),
            cost_estimate=LIGHT,
            name="norm_back",
        )(own_gain, normed, inverse, *dact_shares, *last)
        done["dpre"] = swap([dpre] * n)
        last = (dpre,)

    def dpre_halves():
        nonlocal last
        keep, send = halves("dpre_halves", False, idx, done["dpre"], last)
        done["dpre_halves"] = keep, to_core(send)
        last = (keep,)

    def output():
        nonlocal last
        done["output"], mark = conv_full("output", 1, False, idx, w_second, act_blocks, last)
        last = (mark,)

    def grad_volume():
        nonlocal last
        done["grad_volume"], mark = conv_full(
            "grad_volume", -1, True, idx, first_flat, done["dpre"], last
        )
        last = (mark,)

    written, done = {}, {}
    steps_by_name = {
        "second": second_part,
        "first": first_parts,
        "output": output,
        "grad_volume": grad_volume,
        "norm_back": norm_back,
        "halves": dpre_halves,
        "line": line,
        "write": write,
    }
    for name, *at in CHAIN:
        steps_by_name[name](*at)
    gain_rows = totals[3][9 * rows : 9 * rows + 2, :rows].astype(F32)
    gain_rows_other = crossed[3][9 * rows : 9 * rows + 2, :rows].astype(F32)
    gain_total = (jnp.sum(gain_rows, axis=0) + jnp.sum(gain_rows_other, axis=0)) * factor
    return (done["output"][None], done["grad_volume"][None], written[2], gain_total, written[1])


def solution(mesh):
    placed = (
        P("dp", "chan", None),
        P(None, "chan", None),
        P(),
        P(None, None, "chan"),
        P("dp", "chan", None),
    )
    return jax.shard_map(
        shards,
        mesh=mesh,
        in_specs=placed,
        out_specs=(
            P("dp", "chan", None),
            P("dp", "chan", None),
            P(None, "chan", None),
            P("chan"),
            P(None, None, "chan"),
        ),
        check_vma=False,
    )
```
